32 devices in a mesh: dp: 8 (over y, x, core), mp: 4 (over z).
Axes of the slice: x: 2, y: 2, z: 4, core: 2. Of those that a mesh axis runs over, the one named last changes fastest.
Arguments:
- hidden: float32 [8, 3072, 1024], P('dp', None, 'mp'), may hold values from -0.1875 to 0.1875
- wq: float32 [1024, 1024], P('dp', 'mp'), may hold values from -0.1875 to 0.1875
- wk: float32 [1024, 1024], P('dp', 'mp'), may hold values from -0.1875 to 0.1875
- wv: float32 [1024, 1024], P('dp', 'mp'), may hold values from -0.1875 to 0.1875
- wo: float32 [1024, 1024], P('mp', 'dp'), may hold values from -0.1875 to 0.1875
- w_up: float32 [1024, 4096], P('dp', 'mp'), may hold values from -0.1875 to 0.1875
- w_gate: float32 [1024, 4096], P('dp', 'mp'), may hold values from -0.1875 to 0.1875
- w_down: float32 [4096, 1024], P('mp', 'dp'), may hold values from -0.09375 to 0.09375
- s_qk: float32 [1024], P('mp'), may hold values from 0.5 to 2
- s_u: float32 [4096], P('mp'), may hold values from 0.5 to 2
- s_v: float32 [4096], P('mp'), may hold values from 0.5 to 2
- alpha_a: float32 [1024], P('mp'), may hold values from 0.1 to 0.5
- alpha_m: float32 [1024], P('mp'), may hold values from 0.1 to 0.5
- doc_ids: int32 [8, 3072], P('dp'), may hold values from 0 to 4, as said below
- valid: int32 [8, 3072], P('dp'), may hold values from 0 to 1, as said below
- cotangent: float32 [8, 3072, 1024], P('dp', None, 'mp'), may hold values from -6 to 6
Outputs:
- out_hidden: float32 [8, 3072, 1024], P('dp', None, 'mp')
- grad_hidden: float32 [8, 3072, 1024], P('dp', None, 'mp')
- grad_wq: float32 [1024, 1024], P('dp', 'mp')
- grad_wk: float32 [1024, 1024], P('dp', 'mp')
- grad_wv: float32 [1024, 1024], P('dp', 'mp')
- grad_wo: float32 [1024, 1024], P('mp', 'dp')
- grad_w_up: float32 [1024, 4096], P('dp', 'mp')
- grad_w_gate: float32 [1024, 4096], P('dp', 'mp')
- grad_w_down: float32 [4096, 1024], P('mp', 'dp')
- grad_s_qk: float32 [1024], P('mp')
- grad_s_u: float32 [4096], P('mp')
- grad_s_v: float32 [4096], P('mp')
- grad_alpha_a: float32 [1024], P('mp')
- grad_alpha_m: float32 [1024], P('mp')
The draws below stay inside these ranges and needn't reach their ends.
Inputs may be any that keep to these rules, and one draw needn't show every extreme that they name: `doc_ids`: within a row ids start at 0 and never fall; the first document holds 1024 to 1536 slots, and the last slot of every row has id 4. `valid`: padding is one run of 1 to 384 slots at the end of each row.
All inputs are finite; a program needn't handle non-finite values.
Results may differ from the reference program's by a relative error of at most 0.018.
The reference program's roundings to bfloat16 on the way count: a program that leaves them out, or rounds other values in their place, can miss the bound.
Values may be sent and summed in bfloat16 or wider, within the bound.
A program may use at most 256 MiB of HBM per device.

```python
import math
import jax
import jax.numpy as jnp
from jax import lax

D = 1024
HEADS = 16
DK = 64
FF = 4096
SLOTS = 3072
ROWS_ALL = 8


def draw_doc_ids(key, part):
    key = jax.random.fold_in(key, 11)
    lead_key, cut_key = jax.random.split(key)
    leading = jax.random.randint(lead_key, (ROWS_ALL, 1), SLOTS // 3, SLOTS // 2 + 1)
    spread = jax.random.randint(cut_key, (ROWS_ALL, 3), 0, 1 << 20)
    cuts = leading + spread % (SLOTS - leading)
    slot_index = jnp.arange(SLOTS, dtype=jnp.int32)
    after = (slot_index[None, None, :] >= cuts[:, :, None]).astype(jnp.int32)
    return (slot_index[None, :] >= leading).astype(jnp.int32) + jnp.sum(after, axis=1)


def draw_valid(key, part):
    key = jax.random.fold_in(key, 23)
    padding = jax.random.randint(key, (ROWS_ALL, 1), 1, SLOTS // 8 + 1)
    slot_index = jnp.arange(SLOTS, dtype=jnp.int32)
    return (slot_index[None, :] < SLOTS - padding).astype(jnp.int32)


def block_scale(rng, dims, cuts, smallest, top_value):
    def one(axis_at, shards_of):
        steps = jax.random.uniform(jax.random.fold_in(jax.random.fold_in(rng, 6), axis_at), (shards_of,), jnp.float32, smallest / len(cuts), top_value / len(cuts))
        return jnp.repeat(jnp.exp(steps), dims[axis_at] // shards_of).reshape((-1,) + (1,) * (len(dims) - axis_at - 1))

    level = one(*cuts[0])
    for cut in cuts[1:]:
        level = level * one(*cut)
    return level


def noise(stream_key, shape, deviation, reach, cuts=(), kind=jnp.bfloat16):
    values = deviation * jax.random.normal(stream_key, shape, jnp.float32)
    if cuts:
        values = values * block_scale(stream_key, shape, cuts, -0.22, 0.18)
    return jnp.clip(values, -reach, reach).astype(kind)


def setup_inputs(seed: int = 0) -> dict:
    arg_keys = jax.random.split(jax.random.key(seed), 17)
    hidden = noise(arg_keys[0], (ROWS_ALL, SLOTS, D), D ** -0.5, 0.1875, ((0, 8), (2, 4)), jnp.float32)
    wq = noise(arg_keys[1], (D, D), D ** -0.5, 0.1875, ((0, 8), (1, 4)), jnp.float32)
    wk = noise(arg_keys[2], (D, D), D ** -0.5, 0.1875, ((0, 8), (1, 4)), jnp.float32)
    wv = noise(arg_keys[3], (D, D), D ** -0.5, 0.1875, ((0, 8), (1, 4)), jnp.float32)
    wo = noise(arg_keys[4], (D, D), D ** -0.5, 0.1875, ((0, 4), (1, 8)), jnp.float32)
    w_up = noise(arg_keys[5], (D, FF), D ** -0.5, 0.1875, ((0, 8), (1, 4)), jnp.float32)
    w_gate = noise(arg_keys[6], (D, FF), D ** -0.5, 0.1875, ((0, 8), (1, 4)), jnp.float32)
    w_down = noise(arg_keys[7], (FF, D), FF ** -0.5, 0.09375, ((0, 4), (1, 8)), jnp.float32)
    s_qk = jnp.clip(jnp.exp(math.log(2.0) - 1.3862944 * jax.random.uniform(arg_keys[8], (D,), jnp.float32) ** block_scale(arg_keys[8], (D,), ((0, 4),), -0.2, 0.2)), 0.5, 2.0)
    s_u = jnp.clip(jnp.exp(math.log(2.0) - 1.3862944 * jax.random.uniform(arg_keys[9], (FF,), jnp.float32) ** block_scale(arg_keys[9], (FF,), ((0, 4),), -0.2, 0.2)), 0.5, 2.0)
    s_v = jnp.clip(jnp.exp(math.log(2.0) - 1.3862944 * jax.random.uniform(arg_keys[10], (FF,), jnp.float32) ** block_scale(arg_keys[10], (FF,), ((0, 4),), -0.2, 0.2)), 0.5, 2.0)
    alpha_a = jnp.clip(0.1 + 0.4 * jax.random.uniform(arg_keys[11], (D,), jnp.float32) ** block_scale(arg_keys[11], (D,), ((0, 4),), -0.2, 0.2), 0.1, 0.5)
    alpha_m = jnp.clip(0.1 + 0.4 * jax.random.uniform(arg_keys[12], (D,), jnp.float32) ** block_scale(arg_keys[12], (D,), ((0, 4),), -0.2, 0.2), 0.1, 0.5)
    doc_ids = draw_doc_ids(jax.random.fold_in(arg_keys[16], 71), 0)
    valid = draw_valid(jax.random.fold_in(arg_keys[16], 71), 0)
    cotangent = noise(arg_keys[15], (ROWS_ALL, SLOTS, D), 1.0, 6.0, ((0, 8), (2, 4)), jnp.float32)
    return {"hidden": hidden, "wq": wq, "wk": wk, "wv": wv, "wo": wo, "w_up": w_up, "w_gate": w_gate, "w_down": w_down, "s_qk": s_qk, "s_u": s_u, "s_v": s_v, "alpha_a": alpha_a, "alpha_m": alpha_m, "doc_ids": doc_ids, "valid": valid, "cotangent": cotangent}


EPSILON = 1e-06
ROPE_BASE = 10000.0
NEG_LARGE = -1e+30

@jax.custom_vjp
def low(v):
    return lax.optimization_barrier(v.astype(jnp.bfloat16)).astype(jnp.float32)

@jax.custom_vjp
def low_back(v):
    return v

def low_keep(v):
    return (low(v), None)

def low_pass(kept, grad):
    return (grad,)

def back_keep(v):
    return (v, None)

def back_low(kept, grad):
    return (low(grad),)
low.defvjp(low_keep, low_pass)
low_back.defvjp(back_keep, back_low)

def matmul(left, right):
    return jnp.dot(left, right, precision=lax.Precision.HIGHEST, preferred_element_type=jnp.float32)

def normalize(vector):
    return vector * lax.rsqrt(lax.optimization_barrier(jnp.sum(vector * vector, axis=-1, keepdims=True)) + EPSILON)

def residual_step(resid, branch, alpha):
    unit = normalize(branch)
    return normalize(resid + alpha * (unit - resid))

def rope_tables(positions, head_size):
    half_size = head_size // 2
    freq_index = jnp.arange(half_size, dtype=jnp.float32)
    inverse = jnp.exp(freq_index * (-2.0 * math.log(ROPE_BASE) / head_size))
    angles = positions.astype(jnp.float32)[..., None] * inverse
    return (jnp.cos(angles), jnp.sin(angles))

def rotate(vector, cosine, sine):
    half_size = vector.shape[-1] // 2
    first_half = vector[..., :half_size]
    second_half = vector[..., half_size:]
    cosine = cosine[..., None, :]
    sine = sine[..., None, :]
    return jnp.concatenate([first_half * cosine - second_half * sine, second_half * cosine + first_half * sine], axis=-1)

def positions_of(doc_ids):
    slot_index = jnp.arange(doc_ids.shape[-1], dtype=jnp.int32)
    earlier = jnp.concatenate([doc_ids[..., :1] - 1, doc_ids[..., :-1]], axis=-1)
    starts = jnp.where(doc_ids != earlier, slot_index, jnp.zeros_like(slot_index))
    return slot_index - lax.cummax(starts, axis=starts.ndim - 1)

def block_mask(seg_ids, valid_row, start, block):
    key_slot = jnp.arange(seg_ids.shape[0], dtype=jnp.int32)
    query_slot = start + jnp.arange(block, dtype=jnp.int32)
    query_ids = lax.dynamic_slice_in_dim(seg_ids, start, block, 0)
    same_doc = query_ids[:, None] == seg_ids[None, :]
    causal = key_slot[None, :] <= query_slot[:, None]
    usable = (valid_row[None, :] == 1) | (key_slot[None, :] == query_slot[:, None])
    return same_doc & causal & usable

def head_post(raw, cosine, sine, gain):
    heads_here = gain.shape[0] // DK
    shaped = raw.reshape(raw.shape[0], heads_here, DK)
    return normalize(rotate(shaped, cosine, sine)) * gain.reshape(heads_here, DK)

def attend_row(query, keys, values, seg_ids, valid_row):
    slots = query.shape[0]
    block = min(512, slots)
    scale = math.sqrt(DK)

    def one_block(start):
        query_block = lax.dynamic_slice_in_dim(query, start, block, 0)
        scores = low_back(jnp.einsum('qhd,khd->hqk', query_block, keys, precision=lax.Precision.HIGHEST) * scale)
        scores = jnp.where(block_mask(seg_ids, valid_row, start, block)[None], scores, NEG_LARGE)
        peak = lax.optimization_barrier(jnp.max(scores, axis=-1, keepdims=True))
        expo = jnp.exp(scores - peak)
        probs = low(expo / lax.optimization_barrier(jnp.sum(expo, axis=-1, keepdims=True)))
        return jnp.einsum('hqk,khd->qhd', probs, values, precision=lax.Precision.HIGHEST)
    starts = jnp.arange(slots // block, dtype=jnp.int32) * block
    blocks_out = lax.map(jax.checkpoint(one_block), starts)
    return blocks_out.reshape(slots, query.shape[1], query.shape[2])

def layer_row(resid, seg_ids, valid_row, weights, gains):
    w_query, w_keys, w_values, w_output, w_upward, w_gating, w_downward = weights
    gain_qk, gain_up, gain_gate, alpha_attn, alpha_mlp = gains
    slots = resid.shape[0]
    cosine, sine = rope_tables(positions_of(seg_ids), DK)
    wide = low(resid)
    query = low(head_post(low_back(matmul(wide, w_query)), cosine, sine, gain_qk))
    keys = low(head_post(low_back(matmul(wide, w_keys)), cosine, sine, gain_qk))
    values = low(low_back(matmul(wide, w_values))).reshape(slots, HEADS, DK)
    attended = attend_row(query, keys, values, seg_ids, valid_row)
    merged = low(low_back(attended.reshape(slots, D)))
    middle = residual_step(resid, low_back(matmul(merged, w_output)), alpha_attn)
    middle_low = low(middle)
    upward = low_back(matmul(middle_low, w_upward)) * gain_up
    gating = low_back(matmul(middle_low, w_gating)) * (gain_gate * math.sqrt(D))
    hidden_units = low(upward * jax.nn.silu(gating))
    return residual_step(middle, low_back(matmul(hidden_units, w_downward)), alpha_mlp)

def reference(hidden, wq, wk, wv, wo, w_up, w_gate, w_down, s_qk, s_u, s_v, alpha_a, alpha_m, doc_ids, valid, cotangent):

    def forward(states, weights, gains):
        lowered = tuple((low(matrix) for matrix in weights))

        def one_row(pieces):
            resid, seg_ids, valid_row = pieces
            return layer_row(resid, seg_ids, valid_row, lowered, gains)
        return lax.map(jax.checkpoint(one_row), (states, doc_ids, valid))
    result, pullback = jax.vjp(forward, hidden, (wq, wk, wv, wo, w_up, w_gate, w_down), (s_qk, s_u, s_v, alpha_a, alpha_m))
    grad_states, grad_weights, grad_gains = pullback(cotangent)
    return (result, grad_states, grad_weights[0], grad_weights[1], grad_weights[2], grad_weights[3], grad_weights[4], grad_weights[5], grad_weights[6], grad_gains[0], grad_gains[1], grad_gains[2], grad_gains[3], grad_gains[4])
```

```python
import functools
import math

import jax
import jax.numpy as jnp
import numpy as np
from jax import lax
from jax.experimental import pallas as pl
from jax.experimental.pallas import tpu as pltpu
from jax.sharding import Mesh
from jax.sharding import PartitionSpec as P

DK = 64
HALF = DK // 2
EXT = 128
EPSILON = 1e-06
ROPE_BASE = 10000.0
VMEM_LIMIT = 56 * 1024 * 1024
F32 = jnp.float32
BF16 = jnp.bfloat16
DP = ("chip", "core")


def dot(left, right, dims=((1,), (0,)), precision=None):
    return lax.dot_general(
        left, right, (dims, ((), ())), precision=precision, preferred_element_type=F32
    )


NT = ((1,), (1,))
TN = ((0,), (0,))


def grid_params(dims):
    return pltpu.CompilerParams(
        dimension_semantics=("arbitrary",) * dims, vmem_limit_bytes=VMEM_LIMIT
    )


ANY = pl.BlockSpec(memory_space=pl.ANY)


def remote_params(collective, **more):
    return pltpu.CompilerParams(
        collective_id=collective,
        has_side_effects=True,
        vmem_limit_bytes=VMEM_LIMIT,
        **more,
    )


def to_member(source, target, send, receive, member):
    return pltpu.make_async_remote_copy(
        src_ref=source,
        dst_ref=target,
        send_sem=send,
        recv_sem=receive,
        device_id={"mp": member},
        device_id_type=pl.DeviceIdType.MESH,
    )


def flip(index, mask):
    bit = 1
    while bit <= mask:
        if mask & bit:
            index = index + bit - 2 * bit * lax.rem(lax.div(index, bit), 2)
        bit *= 2
    return index


def greet(member):
    pl.semaphore_signal(
        pltpu.get_barrier_semaphore(),
        inc=1,
        device_id={"mp": member},
        device_id_type=pl.DeviceIdType.MESH,
    )


def greet_all(size):
    me = lax.axis_index("mp")
    for k in range(1, size):
        greet(flip(me, k))
    pl.semaphore_wait(pltpu.get_barrier_semaphore(), size - 1)


def greet_line(size):
    me = lax.axis_index("mp")

    @pl.when(me > 0)
    def _():
        greet(me - 1)

    @pl.when(me < size - 1)
    def _():
        greet(me + 1)

    inside = (me > 0) & (me < size - 1)

    @pl.when(inside)
    def _():
        pl.semaphore_wait(pltpu.get_barrier_semaphore(), 2)

    @pl.when(jnp.logical_not(inside))
    def _():
        pl.semaphore_wait(pltpu.get_barrier_semaphore(), 1)


class Exchange:
    def __init__(self, size, source, target, piece, place, send, receive, local):
        me = lax.axis_index("mp")
        self.local = pltpu.make_async_copy(piece(source, me), place(target, me), local)
        self.remote = [
            to_member(
                piece(source, flip(me, k)),
                place(target, me),
                send.at[k],
                receive.at[k],
                flip(me, k),
            )
            for k in range(1, size)
        ]

    def start(self):
        for copy in self.remote:
            copy.start()
        self.local.start()

    def wait(self):
        self.local.wait()
        for copy in self.remote:
            copy.wait()


def exchange_semaphores(size):
    return [
        pltpu.SemaphoreType.DMA((size,)),
        pltpu.SemaphoreType.DMA((size,)),
        pltpu.SemaphoreType.DMA,
    ]


def row_part(rows):
    return lambda ref, j: ref.at[pl.ds(pl.multiple_of(j * rows, rows), rows), :]


def column_part(columns):
    return lambda ref, j: ref.at[:, pl.ds(pl.multiple_of(j * columns, columns), columns)]


def spread_tokens_kernel(size, source, target, send, receive, local):
    greet_all(size)
    tokens, part = source.shape
    exchange = Exchange(
        size,
        source,
        target,
        row_part(tokens // size),
        column_part(part),
        send,
        receive,
        local,
    )
    exchange.start()
    exchange.wait()


def spread_tokens(value, size, collective):
    tokens, part = value.shape
    return pl.pallas_call(
        functools.partial(spread_tokens_kernel, size),
        in_specs=[ANY],
        out_specs=ANY,
        out_shape=jax.ShapeDtypeStruct((tokens // size, size * part), value.dtype),
        scratch_shapes=exchange_semaphores(size),
        compiler_params=remote_params(collective),
        name="spread_tokens",
    )(value)


def gather_parts_kernel(size, chunks, source, target, send_up, send_down, receive, local):
    me = lax.axis_index("mp")
    tokens = source.shape[0]
    rows = tokens // chunks
    greet_line(size)
    own = pltpu.make_async_copy(source, target.at[me], local)
    own.start()

    def hop(origin, chunk, ref, member, send):
        at = pl.ds(chunk * rows, rows)
        return to_member(
            ref.at[at, :],
            target.at[origin, at, :],
            send.at[origin, chunk],
            receive.at[origin, chunk],
            member,
        )

    for chunk in range(chunks):

        @pl.when(me < size - 1)
        def _():
            hop(me, chunk, source, me + 1, send_up).start()

        @pl.when(me > 0)
        def _():
            hop(me, chunk, source, me - 1, send_down).start()

    for distance in range(1, size):
        for chunk in range(chunks):
            below, above = me - distance, me + distance

            @pl.when(below >= 0)
            def _():
                hop(below, chunk, target.at[below], me, send_up).wait_recv()

                @pl.when(me < size - 1)
                def _():
                    hop(below, chunk, target.at[below], me + 1, send_up).start()

            @pl.when(above < size)
            def _():
                hop(above, chunk, target.at[above], me, send_down).wait_recv()

                @pl.when(me > 0)
                def _():
                    hop(above, chunk, target.at[above], me - 1, send_down).start()

    own.wait()
    for distance in range(size):
        for chunk in range(chunks):
            below, above = me - distance, me + distance

            @pl.when((below >= 0) & (me < size - 1))
            def _():
                hop(below, chunk, source, me + 1, send_up).wait_send()

            @pl.when((above < size) & (me > 0))
            def _():
                hop(above, chunk, source, me - 1, send_down).wait_send()


def gather_parts(value, size, collective):
    tokens, part = value.shape
    chunks = 6
    semaphores = pltpu.SemaphoreType.DMA((size, chunks))
    return pl.pallas_call(
        functools.partial(gather_parts_kernel, size, chunks),
        in_specs=[ANY],
        out_specs=ANY,
        out_shape=jax.ShapeDtypeStruct((size, tokens, part), value.dtype),
        scratch_shapes=[semaphores, semaphores, semaphores, pltpu.SemaphoreType.DMA],
        compiler_params=remote_params(collective),
        name="gather_parts",
    )(value)


def sum_parts_kernel(size, chunks, term, out, up, down, sent_up, sent_down, got_up, got_down):
    me = lax.axis_index("mp")
    rows = out.shape[0] // chunks
    greet_line(size)

    def hop(slots, goal, chunk, member, send, receive):
        at = pl.ds(chunk * rows, rows)
        return to_member(
            slots.at[goal, at, :],
            slots.at[goal, at, :],
            send.at[goal, chunk],
            receive.at[goal, chunk],
            member,
        )

    for order in range(size - 1):
        for chunk in range(chunks):
            at = pl.ds(chunk * rows, rows)
            for slots, goal, ahead, first, step, send, receive in (
                (up, size - 1 - order, me < size - 1 - order, me == 0, 1, sent_up, got_up),
                (down, order, me > order, me == size - 1, -1, sent_down, got_down),
            ):

                @pl.when(ahead & first)
                def _():
                    slots[goal, at, :] = term[goal, at, :]

                @pl.when(ahead & jnp.logical_not(first))
                def _():
                    hop(slots, goal, chunk, me, send, receive).wait_recv()
                    slots[goal, at, :] = (
                        slots[goal, at, :].astype(F32) + term[goal, at, :].astype(F32)
                    ).astype(BF16)

                @pl.when(ahead)
                def _():
                    hop(slots, goal, chunk, me + step, send, receive).start()

    for chunk in range(chunks):
        at = pl.ds(chunk * rows, rows)
        out[at, :] = term[me, at, :].astype(F32)

        @pl.when(me > 0)
        def _():
            hop(up, me, chunk, me, sent_up, got_up).wait_recv()
            out[at, :] += up[me, at, :].astype(F32)

        @pl.when(me < size - 1)
        def _():
            hop(down, me, chunk, me, sent_down, got_down).wait_recv()
            out[at, :] += down[me, at, :].astype(F32)

    for order in range(size - 1):
        for chunk in range(chunks):

            @pl.when(me < size - 1 - order)
            def _():
                hop(up, size - 1 - order, chunk, me, sent_up, got_up).wait_send()

            @pl.when(me > order)
            def _():
                hop(down, order, chunk, me, sent_down, got_down).wait_send()


def sum_parts(term, collective):
    size, tokens, part = term.shape
    chunks = 6
    semaphores = pltpu.SemaphoreType.DMA((size, chunks))
    return pl.pallas_call(
        functools.partial(sum_parts_kernel, size, chunks),
        in_specs=[pl.BlockSpec(memory_space=pltpu.VMEM)],
        out_specs=pl.BlockSpec(memory_space=pltpu.VMEM),
        out_shape=jax.ShapeDtypeStruct((tokens, part), F32),
        scratch_shapes=[pltpu.VMEM((size, tokens, part), BF16)] * 2 + [semaphores] * 4,
        compiler_params=remote_params(collective),
        name="sum_parts",
    )(term)


def paired_place(heads):
    head, feature = np.divmod(np.arange(heads * DK), DK)
    return (feature // HALF) * (heads * HALF) + head * HALF + feature % HALF


def placing_matrix(place, heads):
    head, feature = np.divmod(np.arange(heads * DK), DK)
    matrix = np.zeros((heads * DK, heads * EXT), np.float32)
    matrix[place, head * EXT + feature] = 1
    return matrix


def head_sum_matrix(heads):
    lane = np.arange(heads * HALF) // HALF
    return (lane[:, None] == lane[None, :]).astype(np.float32)


def project_kernel(
    wide, weight, cosine, sine, gain, place_pair, place_plain, sums, q, k, v, rq, rk
):
    parts = wide.shape[0]
    heads = q.shape[0]
    pair = heads * HALF
    width = heads * DK
    raw = dot(wide[0], weight[0])
    for part in range(1, parts):
        raw += dot(wide[part], weight[part])
    rows = raw.shape[0]
    lane = lax.broadcasted_iota(jnp.int32, (rows, EXT), 1)
    cos = cosine[...]
    sin = sine[...]
    gain_first = gain[:, :pair]
    gain_second = gain[:, pair:]
    for offset, out, scale_out, factor in ((0, q, rq, math.sqrt(DK)), (width, k, rk, 1.0)):
        first = raw[:, offset : offset + pair]
        second = raw[:, offset + pair : offset + width]
        turned_first = first * cos - second * sin
        turned_second = second * cos + first * sin
        total = dot(
            turned_first * turned_first + turned_second * turned_second,
            sums[...],
            precision=lax.Precision.HIGHEST,
        )
        scale = lax.rsqrt(total + EPSILON)
        scale_out[...] = scale
        both = jnp.concatenate(
            [turned_first * scale * gain_first, turned_second * scale * gain_second], axis=1
        ).astype(BF16)
        padded = dot(both, place_pair[...]) * factor
        for head in range(heads):
            piece = padded[:, head * EXT : (head + 1) * EXT]
            if factor == 1.0:
                piece = jnp.where(lane < DK, piece, 1.0)
            out[head] = piece.astype(BF16)
    padded = dot(raw[:, 2 * width :].astype(BF16), place_plain[...])
    for head in range(heads):
        piece = padded[:, head * EXT : (head + 1) * EXT]
        v[head] = jnp.where(lane < DK, piece, 1.0).astype(BF16)


def project(wide, weight, cosine, sine, gain, place_pair, place_plain, sums):
    parts, tokens, part = wide.shape
    width = gain.shape[1]
    heads = width // DK
    block = min(512, tokens)
    padded = jax.ShapeDtypeStruct((heads, tokens, EXT), BF16)
    scale = jax.ShapeDtypeStruct((tokens, heads * HALF), F32)

    def whole(array):
        return pl.BlockSpec(array.shape, lambda i: (0,) * array.ndim)

    rows = pl.BlockSpec((block, heads * HALF), lambda i: (i, 0))
    headed = pl.BlockSpec((heads, block, EXT), lambda i: (0, i, 0))
    return pl.pallas_call(
        project_kernel,
        grid=(tokens // block,),
        in_specs=[
            pl.BlockSpec((parts, block, part), lambda i: (0, i, 0)),
            whole(weight),
            rows,
            rows,
            whole(gain),
            whole(place_pair),
            whole(place_plain),
            whole(sums),
        ],
        out_specs=[headed, headed, headed, rows, rows],
        out_shape=[padded, padded, padded, scale, scale],
        compiler_params=grid_params(1),
        cost_estimate=pl.CostEstimate(
            flops=2 * tokens * parts * part * width * 3,
            bytes_accessed=20 << 20,
            transcendentals=0,
        ),
        name="project",
    )(wide, weight, cosine, sine, gain, place_pair, place_plain, sums)


def split_three(value):
    high = value.astype(BF16).astype(F32)
    rest = value - high
    middle = rest.astype(BF16).astype(F32)
    return high, middle, rest - middle


def attend_kernel(low, q, k, v, qdoc, kdoc, collect, attended, qback, acc):
    heads, rows, _ = q.shape
    block = kdoc.shape[2]
    index = pl.program_id(0)
    acc[...] = jnp.zeros_like(acc)

    def step(j, diagonal):
        slots = pl.ds(pl.multiple_of(j * block, block), block)
        mask = qdoc[...] == kdoc[j]
        if diagonal:
            row = lax.broadcasted_iota(jnp.int32, (rows, block), 0)
            column = lax.broadcasted_iota(jnp.int32, (rows, block), 1)
            mask = (mask & (column < row)) | (column == row)
        for head in range(heads):
            scores = dot(q[head], k[head, slots, :], NT)
            weight = jnp.where(mask, jnp.exp(scores), 0.0).astype(BF16)
            acc[head] += dot(weight, v[head, slots, :])

    def earlier(j, carry):
        step(j, False)
        return carry

    lax.fori_loop(low[index], index, earlier, 0)
    step(index, True)

    lane = lax.broadcasted_iota(jnp.int32, (rows, EXT), 1)
    merged = jnp.zeros((rows, heads * DK), F32)
    for head in range(heads):
        both = acc[head]
        total = pltpu.roll(both, DK, 1)
        output = jnp.where(lane < DK, both / total, 0.0).astype(BF16)
        merged += dot(output, collect[head])
        high, middle, rest = split_three(-jnp.log(both))
        qback[head] = jnp.where(
            lane < DK,
            q[head].astype(F32),
            jnp.where(
                lane == DK,
                high,
                jnp.where(lane == DK + 1, middle, jnp.where(lane == DK + 2, rest, 0.0)),
            ),
        ).astype(BF16)
    attended[...] = merged.astype(BF16)


def attend(low, q, k, v, qdoc, kdoc, collect):
    heads, tokens, _ = q.shape
    block = kdoc.shape[2]
    width = heads * DK

    def whole(array):
        return pl.BlockSpec(array.shape, lambda i, low: (0,) * array.ndim)

    headed = pl.BlockSpec((heads, block, EXT), lambda i, low: (0, i, 0))
    return pl.pallas_call(
        attend_kernel,
        grid_spec=pltpu.PrefetchScalarGridSpec(
            num_scalar_prefetch=1,
            grid=(tokens // block,),
            in_specs=[
                headed,
                whole(k),
                whole(v),
                pl.BlockSpec((block, 1), lambda i, low: (i, 0)),
                whole(kdoc),
                whole(collect),
            ],
            out_specs=[pl.BlockSpec((block, width), lambda i, low: (i, 0)), headed],
            scratch_shapes=[pltpu.VMEM((heads, block, EXT), F32)],
        ),
        out_shape=[
            jax.ShapeDtypeStruct((tokens, width), BF16),
            jax.ShapeDtypeStruct((heads, tokens, EXT), BF16),
        ],
        compiler_params=grid_params(1),
        cost_estimate=pl.CostEstimate(
            flops=40_000_000_000, bytes_accessed=16 << 20, transcendentals=0
        ),
        name="attend",
    )(low, q, k, v, qdoc, kdoc, collect)


def gather_heads(padded, matrix, heads):
    total = None
    for head in range(heads):
        value = padded[head]
        high = value.astype(BF16)
        rest = (value - high.astype(F32)).astype(BF16)
        term = dot(high, matrix[head]) + dot(rest, matrix[head])
        total = term if total is None else total + term
    return total


def unrope(grad, unit, gain, scale, cos, sin, sums):
    pair = cos.shape[1]
    grad_gain = jnp.sum(grad * unit, axis=0, keepdims=True)
    dy = grad * gain
    prod = dy * unit
    total = dot(prod[:, :pair] + prod[:, pair:], sums, precision=lax.Precision.HIGHEST)
    first = scale * (dy[:, :pair] - unit[:, :pair] * total)
    second = scale * (dy[:, pair:] - unit[:, pair:] * total)
    raw = jnp.concatenate([first * cos + second * sin, second * cos - first * sin], axis=1)
    return raw.astype(BF16), grad_gain


def attend_back_kernel(
    low,
    qback,
    dout,
    attended,
    k,
    v,
    qdoc,
    kdoc,
    cosine,
    sine,
    rq,
    rk,
    gain,
    weight,
    place_plain,
    collect_plain,
    collect_pair,
    sums,
    dq_out,
    dk_out,
    dv_out,
    term_out,
    gain_out,
    dk,
    dv,
    dq,
    dox,
    dq_low,
):
    heads, rows, _ = qback.shape
    steps = pl.num_programs(0) // 2
    step_at = pl.program_id(0)
    width = heads * DK
    scale = math.sqrt(DK)

    @pl.when(step_at == 0)
    def _():
        dk[...] = jnp.zeros_like(dk)
        dv[...] = jnp.zeros_like(dv)
        gain_out[...] = jnp.zeros_like(gain_out)

    @pl.when(step_at < steps)
    def _():
        index = step_at
        lane = lax.broadcasted_iota(jnp.int32, (rows, EXT), 1)
        spread_grad = dot(dout[...], place_plain[...])
        spread_out = dot(attended[...], place_plain[...])
        for head in range(heads):
            piece = spread_grad[:, head * EXT : (head + 1) * EXT]
            other = spread_out[:, head * EXT : (head + 1) * EXT]
            delta = jnp.sum(piece * other, axis=1, keepdims=True)
            high, middle, rest = split_three(-delta)
            dox[head] = jnp.where(
                lane < DK,
                piece,
                jnp.where(
                    lane == DK,
                    high,
                    jnp.where(lane == DK + 1, middle, jnp.where(lane == DK + 2, rest, 0.0)),
                ),
            ).astype(BF16)
        dq[...] = jnp.zeros_like(dq)

        def step(j, diagonal):
            slots = pl.ds(pl.multiple_of(j * rows, rows), rows)
            mask = kdoc[slots, :] == qdoc[0]
            if diagonal:
                key = lax.broadcasted_iota(jnp.int32, (rows, rows), 0)
                query = lax.broadcasted_iota(jnp.int32, (rows, rows), 1)
                mask = (mask & (key < query)) | (key == query)
            for head in range(heads):
                keys = k[head, slots, :]
                scores = dot(keys, qback[head], NT)
                probs = jnp.where(mask, jnp.exp(scores), 0.0)
                dv[head, slots, :] += dot(probs.astype(BF16), dox[head])
                dprobs = dot(v[head, slots, :], dox[head], NT)
                dscores = (probs * dprobs).astype(BF16)
                dk[head, slots, :] += dot(dscores, qback[head])
                dq[head] += dot(dscores, keys, TN)

        def earlier(j, carry):
            step(j, False)
            return carry

        lax.fori_loop(low[index], index, earlier, 0)
        step(index, True)

        grad = gather_heads(dq, collect_pair, heads) * scale
        query = dot(qback[0], collect_pair[0])
        for head in range(1, heads):
            query += dot(qback[head], collect_pair[head])
        unit = query * (1.0 / scale) / gain[...]
        raw, grad_gain = unrope(
            grad, unit, gain[...], rq[...], cosine[...], sine[...], sums[...]
        )
        gain_out[...] += grad_gain
        dq_out[...] = raw
        dq_low[pl.ds(pl.multiple_of(index * rows, rows), rows), :] = raw

    @pl.when(step_at >= steps)
    def _():
        index = step_at - steps
        slots = pl.ds(pl.multiple_of(index * rows, rows), rows)
        grad = gather_heads([dk[head, slots, :] for head in range(heads)], collect_pair, heads)
        keys = dot(k[0, slots, :], collect_pair[0])
        for head in range(1, heads):
            keys += dot(k[head, slots, :], collect_pair[head])
        raw, grad_gain = unrope(
            grad, keys / gain[...], gain[...], rk[...], cosine[...], sine[...], sums[...]
        )
        gain_out[...] += grad_gain
        dk_out[...] = raw
        dvalues = gather_heads(
            [dv[head, slots, :] for head in range(heads)], collect_plain, heads
        ).astype(BF16)
        dv_out[...] = dvalues
        dquery = dq_low[slots, :]
        for part in range(weight.shape[0]):
            term = dot(dquery, weight[part, :, :width], NT)
            term += dot(raw, weight[part, :, width : 2 * width], NT)
            term += dot(dvalues, weight[part, :, 2 * width :], NT)
            term_out[part] = term.astype(BF16)


def attend_back(
    low,
    qback,
    dout,
    attended,
    k,
    v,
    qdoc,
    kdoc,
    cosine,
    sine,
    rq,
    rk,
    gain,
    weight,
    place_plain,
    collect_plain,
    collect_pair,
    sums,
):
    heads, tokens, _ = k.shape
    block = qdoc.shape[2]
    width = heads * DK
    steps = tokens // block
    parts, part = weight.shape[:2]

    def whole(array):
        return pl.BlockSpec(array.shape, lambda i, low: (0,) * array.ndim)

    def now(i):
        return jnp.minimum(i, steps - 1)

    def after(i):
        return jnp.maximum(i - steps, 0)

    def both(i):
        return lax.rem(i, steps)

    def rows(columns, at):
        return pl.BlockSpec((block, columns), lambda i, low: (at(i), 0))

    return pl.pallas_call(
        attend_back_kernel,
        grid_spec=pltpu.PrefetchScalarGridSpec(
            num_scalar_prefetch=1,
            grid=(2 * steps,),
            in_specs=[
                pl.BlockSpec((heads, block, EXT), lambda i, low: (0, now(i), 0)),
                rows(width, now),
                rows(width, now),
                whole(k),
                whole(v),
                pl.BlockSpec((1, 1, block), lambda i, low: (now(i), 0, 0)),
                whole(kdoc),
                rows(width // 2, both),
                rows(width // 2, both),
                rows(width // 2, now),
                rows(width // 2, after),
                whole(gain),
                whole(weight),
                whole(place_plain),
                whole(collect_plain),
                whole(collect_pair),
                whole(sums),
            ],
            out_specs=[
                rows(width, now),
                rows(width, after),
                rows(width, after),
                pl.BlockSpec((parts, block, part), lambda i, low: (0, after(i), 0)),
                pl.BlockSpec((1, width), lambda i, low: (0, 0)),
            ],
            scratch_shapes=[
                pltpu.VMEM((heads, tokens, EXT), F32),
                pltpu.VMEM((heads, tokens, EXT), F32),
                pltpu.VMEM((heads, block, EXT), F32),
                pltpu.VMEM((heads, block, EXT), BF16),
                pltpu.VMEM((tokens, width), BF16),
            ],
        ),
        out_shape=[
            jax.ShapeDtypeStruct((tokens, width), BF16),
            jax.ShapeDtypeStruct((tokens, width), BF16),
            jax.ShapeDtypeStruct((tokens, width), BF16),
            jax.ShapeDtypeStruct((parts, tokens, part), BF16),
            jax.ShapeDtypeStruct((1, width), F32),
        ],
        compiler_params=grid_params(1),
        cost_estimate=pl.CostEstimate(
            flops=80_000_000_000, bytes_accessed=30 << 20, transcendentals=0
        ),
        name="attend_back",
    )(
        low,
        qback,
        dout,
        attended,
        k,
        v,
        qdoc,
        kdoc,
        cosine,
        sine,
        rq,
        rk,
        gain,
        weight,
        place_plain,
        collect_plain,
        collect_pair,
        sums,
    )


def whole_matrix(ref):
    _, chips, rows, units = ref.shape
    return ref[...].reshape(chips * rows, units)


def first_step():
    return (pl.program_id(0) == 0) & (pl.program_id(1) == 0)


def last_step():
    return (pl.program_id(0) == pl.num_programs(0) - 1) & (
        pl.program_id(1) == pl.num_programs(1) - 1
    )


def feed_kernel(
    size,
    x,
    w_up,
    w_gate,
    w_down,
    s_u,
    s_v,
    cotangent,
    up_out,
    gate_out,
    units_out,
    branch,
    spread,
    acc,
    send,
    receive,
    local,
):
    exchange = Exchange(
        size,
        cotangent,
        spread,
        row_part(spread.shape[0]),
        column_part(cotangent.shape[1]),
        send,
        receive,
        local,
    )

    @pl.when(first_step())
    def _():
        greet_all(size)
        exchange.start()

    part = pl.program_id(1)
    up = dot(x[...], whole_matrix(w_up))
    gate = dot(x[...], whole_matrix(w_gate))
    up_out[0] = up.astype(BF16)
    gate_out[0] = gate.astype(BF16)
    scaled = gate * s_v[0]
    units = (up * s_u[0] * (scaled / (1.0 + jnp.exp(-scaled)))).astype(BF16)
    units_out[0] = units
    term = dot(units, whole_matrix(w_down), NT)

    @pl.when(part == 0)
    def _():
        acc[...] = term

    @pl.when(part > 0)
    def _():
        acc[...] += term

    @pl.when(part == pl.num_programs(1) - 1)
    def _():
        branch[...] = acc[...].astype(BF16)

    @pl.when(last_step())
    def _():
        exchange.wait()


def packed_specs(packed, width):
    _, chips, _, units = packed.shape
    return [
        pl.BlockSpec((1, chips, width // chips, units), lambda t, m, w=w: (m, 0, w, 0))
        for w in range(3)
    ]


def feed(x, packed, s_u, s_v, cotangent, collective):
    tokens, width = x.shape
    parts, _, _, units = packed.shape
    size = parts
    block = min(512, tokens)
    rows = pl.BlockSpec((block, width), lambda t, m: (t, 0))
    vector = pl.BlockSpec((1, 1, units), lambda t, m: (m, 0, 0))
    piece = pl.BlockSpec((1, block, units), lambda t, m: (m, t, 0))
    hidden = jax.ShapeDtypeStruct((parts, tokens, units), BF16)
    slots, part = cotangent.shape
    return pl.pallas_call(
        functools.partial(feed_kernel, size),
        grid=(tokens // block, parts),
        in_specs=[rows, *packed_specs(packed, width), vector, vector, ANY],
        out_specs=[piece, piece, piece, rows, ANY],
        out_shape=[
            hidden,
            hidden,
            hidden,
            jax.ShapeDtypeStruct((tokens, width), BF16),
            jax.ShapeDtypeStruct((slots // size, size * part), BF16),
        ],
        scratch_shapes=[pltpu.VMEM((block, width), F32), *exchange_semaphores(size)],
        compiler_params=remote_params(collective),
        cost_estimate=pl.CostEstimate(
            flops=6 * tokens * width * parts * units, bytes_accessed=60 << 20, transcendentals=0
        ),
        name="feed",
    )(x, packed, packed, packed, s_u, s_v, cotangent)


def feed_back_kernel(
    size,
    dbranch,
    w_up,
    w_gate,
    w_down,
    s_u,
    s_v,
    up_in,
    gate_in,
    result,
    dup_out,
    dgate_out,
    dx,
    grad_u,
    grad_v,
    spread,
    acc,
    sum_u,
    sum_v,
    send,
    receive,
    local,
):
    exchange = Exchange(
        size,
        result,
        spread,
        column_part(spread.shape[1]),
        row_part(result.shape[0]),
        send,
        receive,
        local,
    )

    @pl.when(first_step())
    def _():
        greet_all(size)
        exchange.start()

    block = pl.program_id(0)
    part = pl.program_id(1)
    dunits = dot(dbranch[...], whole_matrix(w_down))
    up = up_in[0].astype(F32)
    gate = gate_in[0].astype(F32)
    scaled = gate * s_v[0]
    sigmoid = 1.0 / (1.0 + jnp.exp(-scaled))
    silu = scaled * sigmoid
    slope = sigmoid * (1.0 + scaled - silu)
    through_up = dunits * silu
    through_gate = dunits * up * s_u[0] * slope
    dup = (through_up * s_u[0]).astype(BF16)
    dgate = (through_gate * s_v[0]).astype(BF16)
    dup_out[0] = dup
    dgate_out[0] = dgate
    term = dot(dup, whole_matrix(w_up), NT) + dot(dgate, whole_matrix(w_gate), NT)
    part_u = jnp.sum(through_up * up, axis=0, keepdims=True)
    part_v = jnp.sum(through_gate * gate, axis=0, keepdims=True)

    @pl.when(block == 0)
    def _():
        sum_u[part] = part_u
        sum_v[part] = part_v

    @pl.when(block > 0)
    def _():
        sum_u[part] += part_u
        sum_v[part] += part_v

    @pl.when(part == 0)
    def _():
        acc[...] = term

    @pl.when(part > 0)
    def _():
        acc[...] += term

    @pl.when(part == pl.num_programs(1) - 1)
    def _():
        dx[...] = acc[...].astype(BF16)

    @pl.when(last_step())
    def _():
        grad_u[...] = sum_u[...]
        grad_v[...] = sum_v[...]
        exchange.wait()


def feed_back(dbranch, packed, s_u, s_v, up, gate, result, collective):
    tokens, width = dbranch.shape
    parts, _, _, units = packed.shape
    size = parts
    block = min(512, tokens)
    rows = pl.BlockSpec((block, width), lambda t, m: (t, 0))
    vector = pl.BlockSpec((1, 1, units), lambda t, m: (m, 0, 0))
    piece = pl.BlockSpec((1, block, units), lambda t, m: (m, t, 0))
    vectors = pl.BlockSpec((parts, 1, units), lambda t, m: (0, 0, 0))
    hidden = jax.ShapeDtypeStruct((parts, tokens, units), BF16)
    sums = jax.ShapeDtypeStruct((parts, 1, units), F32)
    mine = result.shape[0]
    return pl.pallas_call(
        functools.partial(feed_back_kernel, size),
        grid=(tokens // block, parts),
        in_specs=[rows, *packed_specs(packed, width), vector, vector, piece, piece, ANY],
        out_specs=[piece, piece, rows, vectors, vectors, ANY],
        out_shape=[
            hidden,
            hidden,
            jax.ShapeDtypeStruct((tokens, width), BF16),
            sums,
            sums,
            jax.ShapeDtypeStruct((size * mine, width // size), BF16),
        ],
        scratch_shapes=[
            pltpu.VMEM((block, width), F32),
            pltpu.VMEM((parts, 1, units), F32),
            pltpu.VMEM((parts, 1, units), F32),
            *exchange_semaphores(size),
        ],
        compiler_params=remote_params(collective),
        cost_estimate=pl.CostEstimate(
            flops=6 * tokens * width * parts * units, bytes_accessed=70 << 20, transcendentals=0
        ),
        name="feed_back",
    )(dbranch, packed, packed, packed, s_u, s_v, up, gate, result)


def feed_grads_kernel(
    size,
    x,
    dbranch,
    dup,
    dgate,
    units,
    dmerged,
    grads,
    dattended,
    x_turned,
    d_turned,
    send,
    receive,
    local,
):
    exchange = Exchange(
        size,
        dmerged,
        dattended,
        column_part(dattended.shape[1]),
        row_part(dmerged.shape[0]),
        send,
        receive,
        local,
    )

    @pl.when(first_step())
    def _():
        greet_all(size)
        exchange.start()
        x_turned[...] = x[...].T
        d_turned[...] = dbranch[...].T

    _, chips, rows, _ = grads.shape
    for which, left, right in (
        (0, x_turned, dup),
        (1, x_turned, dgate),
        (2, d_turned, units),
    ):

        @pl.when(pl.program_id(0) == which)
        def _():
            total = dot(left[...], right[0])
            grads[0] = total.astype(BF16).reshape(chips, rows, total.shape[1])

    @pl.when(last_step())
    def _():
        exchange.wait()


def feed_grads(x, dbranch, dup, dgate, units_in, dmerged, chips, collective):
    tokens, width = x.shape
    parts, _, units = dup.shape
    size = parts
    rows = width // chips
    mine = dmerged.shape[0]
    whole = pl.BlockSpec((tokens, width), lambda w, m: (0, 0))

    def piece(which):
        def at(w, m):
            return (jnp.where(w == which, m, jnp.where(w < which, 0, parts - 1)), 0, 0)

        return pl.BlockSpec((1, tokens, units), at)

    return pl.pallas_call(
        functools.partial(feed_grads_kernel, size),
        grid=(3, parts),
        in_specs=[whole, whole, piece(0), piece(1), piece(2), ANY],
        out_specs=[pl.BlockSpec((1, chips, rows, units), lambda w, m: (m, 0, w, 0)), ANY],
        out_shape=[
            jax.ShapeDtypeStruct((parts, chips, 3 * rows, units), BF16),
            jax.ShapeDtypeStruct((size * mine, width // size), BF16),
        ],
        scratch_shapes=[
            pltpu.VMEM((width, tokens), BF16),
            pltpu.VMEM((width, tokens), BF16),
            *exchange_semaphores(size),
        ],
        compiler_params=remote_params(collective),
        cost_estimate=pl.CostEstimate(
            flops=6 * tokens * width * parts * units, bytes_accessed=40 << 20, transcendentals=0
        ),
        name="feed_grads",
    )(x, dbranch, dup, dgate, units_in, dmerged)


def rope_tables(positions, head_size):
    half_size = head_size // 2
    freq_index = jnp.arange(half_size, dtype=F32)
    inverse = jnp.exp(freq_index * (-2.0 * math.log(ROPE_BASE) / head_size))
    angles = positions.astype(F32)[..., None] * inverse
    return (jnp.cos(angles), jnp.sin(angles))


def document_starts(doc_ids):
    slot_index = jnp.arange(doc_ids.shape[-1], dtype=jnp.int32)
    earlier = jnp.concatenate([doc_ids[..., :1] - 1, doc_ids[..., :-1]], axis=-1)
    starts = jnp.where(doc_ids != earlier, slot_index, jnp.zeros_like(slot_index))
    return lax.cummax(starts, axis=starts.ndim - 1)


def row_scale(value):
    return lax.rsqrt(jnp.sum(value * value, axis=-1, keepdims=True) + EPSILON)


def residual_forward(resid, branch, alpha):
    branch_scale = row_scale(branch)
    unit = branch * branch_scale
    mixed = resid + alpha * (unit - resid)
    mixed_scale = row_scale(mixed)
    return (mixed * mixed_scale, (unit, branch_scale, mixed_scale))


def residual_backward(grad_out, result, resid, alpha, kept):
    unit, branch_scale, mixed_scale = kept
    grad_mixed = mixed_scale * (
        grad_out - result * jnp.sum(grad_out * result, axis=-1, keepdims=True)
    )
    grad_alpha = jnp.sum(grad_mixed * (unit - resid), axis=0)
    grad_resid = grad_mixed * (1.0 - alpha)
    grad_unit = grad_mixed * alpha
    grad_branch = branch_scale * (
        grad_unit - unit * jnp.sum(grad_unit * unit, axis=-1, keepdims=True)
    )
    return (grad_resid, grad_branch, grad_alpha)


def other_core(value):
    return lax.ppermute(value, "core", [(0, 1), (1, 0)])


def make_on_device(chips, size):
    def on_device(
        hidden,
        wq,
        wk,
        wv,
        wo,
        w_up,
        w_gate,
        w_down,
        s_qk,
        s_u,
        s_v,
        alpha_a,
        alpha_m,
        doc_ids,
        valid,
        cotangent,
    ):
        _, slots, part = hidden.shape
        width = part * size
        heads = s_qk.shape[0] // DK
        rows = wq.shape[0]
        units = w_up.shape[1] // 2
        mine = slots // size
        block = min(512, slots)
        me = lax.axis_index("mp")
        core = lax.axis_index("core")
        everyone = ("mp", "chip", "core")

        place = paired_place(heads)
        in_pairs = (
            lambda w: w.reshape(w.shape[0], heads, 2, HALF)
            .transpose(0, 2, 1, 3)
            .reshape(w.shape[0], heads * DK)
        )
        low_qkv = jnp.concatenate([in_pairs(wq), in_pairs(wk), wv], axis=1).astype(BF16)
        full_qkv = lax.all_gather(low_qkv, DP, axis=0, tiled=True).reshape(size, part, 3 * part)

        stacked = jnp.stack([w_up, w_gate, w_down.T]).astype(BF16).reshape(3, rows, 2, units)
        keep = lax.dynamic_index_in_dim(stacked, core, 2, keepdims=False)
        give = lax.dynamic_index_in_dim(stacked, 1 - core, 2, keepdims=False)
        low_wo = wo.astype(BF16).T.reshape(rows // 2, 2 * part)
        given = jnp.concatenate([give.reshape(3 * rows, units), low_wo])
        got = other_core(given)

        def in_order(own, other):
            return jnp.where(core == 0, jnp.stack([own, other], 1), jnp.stack([other, own], 1))

        pair = in_order(keep, got[: 3 * rows].reshape(3, rows, units))
        pair_wo = in_order(low_wo[None], got[3 * rows :][None])
        packed = jnp.concatenate([pair.reshape(6 * rows, units), pair_wo.reshape(rows, units)])
        packed = lax.all_gather(packed, ("mp", "chip"), axis=0).reshape(
            size, chips, 7 * rows, units
        )
        wide = gather_parts(hidden[0].astype(BF16), size, 0)
        full_wo = packed[:, :, 6 * rows :].reshape(size, width, part)
        vectors = jnp.concatenate([s_u, s_v * math.sqrt(width), alpha_a, alpha_m])
        vectors = lax.all_gather(vectors, "mp", axis=0)
        s_up = lax.dynamic_slice_in_dim(vectors[:, : 2 * units], core * units, units, 1)
        s_gate = lax.dynamic_slice_in_dim(
            vectors[:, 2 * units : 4 * units], core * units, units, 1
        )
        s_up = s_up[:, None, :]
        s_gate = s_gate[:, None, :]
        alpha_attn = vectors[:, 4 * units : 4 * units + part].reshape(width)
        alpha_mlp = vectors[:, 4 * units + part :].reshape(width)

        docs = doc_ids[0]
        starts = document_starts(docs)
        slot = jnp.arange(slots, dtype=jnp.int32)
        cosine, sine = rope_tables(slot - starts, DK)
        cosine = jnp.tile(cosine, (1, heads))
        sine = jnp.tile(sine, (1, heads))
        low = starts[::block] // block
        key_docs = jnp.where(valid[0] == 1, docs, -1)
        to_pair = placing_matrix(place, heads)
        to_plain = placing_matrix(np.arange(heads * DK), heads)
        place_pair = jnp.asarray(to_pair, BF16)
        place_plain = jnp.asarray(to_plain, BF16)
        collect_pair = jnp.asarray(to_pair.T.reshape(heads, EXT, heads * DK), BF16)
        collect_plain = jnp.asarray(to_plain.T.reshape(heads, EXT, heads * DK), BF16)
        sums = jnp.asarray(head_sum_matrix(heads))
        gain = in_pairs(s_qk[None, :])

        q, k, v, rq, rk = project(
            wide, full_qkv, cosine, sine, gain, place_pair, place_plain, sums
        )
        attended, qback = attend(
            low,
            q,
            k,
            v,
            docs[:, None],
            key_docs.reshape(slots // block, 1, block),
            collect_plain,
        )
        merged = spread_tokens(attended, size, 1)
        resid = lax.dynamic_slice_in_dim(wide, me * mine, mine, 1)
        resid = resid.transpose(1, 0, 2).reshape(mine, width).astype(F32)
        merged_parts = merged.reshape(mine, size, part)
        branch_attn = jnp.einsum("tmh,mdh->td", merged_parts, full_wo, preferred_element_type=F32)
        middle, kept_attn = residual_forward(resid, branch_attn, alpha_attn)

        middle_low = middle.astype(BF16)
        x = jnp.concatenate([middle_low, other_core(middle_low)])
        up, gate, hidden_units, down_term, spread_cot = feed(
            x, packed, s_up, s_gate, cotangent[0].astype(BF16), 2
        )
        branch_mlp = down_term[:mine].astype(F32) + other_core(down_term[mine:]).astype(F32)
        result, kept_mlp = residual_forward(middle, branch_mlp, alpha_mlp)

        grad_middle, grad_branch_mlp, grad_alpha_mlp = residual_backward(
            spread_cot.astype(F32), result, middle, alpha_mlp, kept_mlp
        )
        grad_branch_mlp = grad_branch_mlp.astype(BF16)
        dbranch = jnp.concatenate([grad_branch_mlp, other_core(grad_branch_mlp)])
        dup, dgate, dx, grad_u, grad_v, out_low = feed_back(
            dbranch, packed, s_up, s_gate, up, gate, result.astype(BF16), 3
        )
        out_hidden = out_low.astype(F32)
        grad_middle = (
            grad_middle + dx[:mine].astype(F32) + other_core(dx[mine:]).astype(F32)
        )

        grad_resid, grad_branch_attn, grad_alpha_attn = residual_backward(
            grad_middle, middle, resid, alpha_attn, kept_attn
        )
        grad_branch_attn = grad_branch_attn.astype(BF16)
        grad_merged = jnp.einsum(
            "td,mdh->tmh", grad_branch_attn, full_wo, preferred_element_type=F32
        ).astype(BF16)
        grads, dattended = feed_grads(
            x, dbranch, dup, dgate, hidden_units, grad_merged.reshape(mine, width), chips, 4
        )
        total = lax.psum_scatter(
            grads.reshape(size * chips, 6 * rows, units), ("mp", "chip"), scatter_dimension=0
        )
        total = total.reshape(3, 2, rows, units)
        keep = lax.dynamic_index_in_dim(total, core, 1, keepdims=False)
        got = other_core(lax.dynamic_index_in_dim(total, 1 - core, 1, keepdims=False))
        owned = jnp.where(
            core == 0,
            jnp.concatenate([keep, got], axis=2),
            jnp.concatenate([got, keep], axis=2),
        ).astype(F32)
        owned_upward, owned_gating, owned_downward = owned[0], owned[1], owned[2].T
        grad_wo = jnp.einsum(
            "td,tmh->mdh", grad_branch_attn, merged_parts, preferred_element_type=F32
        ).astype(BF16)
        owned_output = lax.psum_scatter(
            grad_wo.reshape(size * chips * 2, rows, part), everyone, scatter_dimension=0
        )
        owned_output = owned_output.astype(F32).T
        dq, dk, dv, term, grad_gain = attend_back(
            low,
            qback,
            dattended,
            attended,
            k,
            v,
            docs.reshape(slots // block, 1, block),
            key_docs[:, None],
            cosine,
            sine,
            rq,
            rk,
            gain,
            full_qkv,
            place_plain,
            collect_plain,
            collect_pair,
            sums,
        )
        own = lax.dynamic_slice_in_dim(term, me * mine, mine, 1).astype(F32)
        own = own + grad_resid.reshape(mine, size, part).transpose(1, 0, 2)
        term = lax.dynamic_update_slice_in_dim(term, own.astype(BF16), me * mine, 1)
        grad_hidden = sum_parts(term, 5)

        grad_qkv = [
            jnp.einsum("mtd,tf->mdf", wide, d, preferred_element_type=F32)
            .astype(BF16)
            .reshape(width, part)
            for d in (dq, dk, dv)
        ]
        owned = lax.psum_scatter(
            jnp.concatenate(grad_qkv, axis=1), DP, scatter_dimension=0, tiled=True
        ).astype(F32)
        out_pairs = (
            lambda w: w.reshape(w.shape[0], 2, heads, HALF)
            .transpose(0, 2, 1, 3)
            .reshape(w.shape[0], heads * DK)
        )
        owned_query = out_pairs(owned[:, :part])
        owned_keys = out_pairs(owned[:, part : 2 * part])
        owned_values = owned[:, 2 * part :]

        zero = jnp.zeros((size, 2, units), F32)
        placed_u = lax.dynamic_update_slice(zero, grad_u, (0, core, 0))
        placed_v = lax.dynamic_update_slice(zero, grad_v * math.sqrt(width), (0, core, 0))
        placed_qk = lax.dynamic_update_slice(
            jnp.zeros((size, part), F32), out_pairs(grad_gain), (me, 0)
        )
        summed = lax.psum(
            jnp.concatenate(
                [
                    placed_u.reshape(size, 2 * units),
                    placed_v.reshape(size, 2 * units),
                    placed_qk,
                    grad_alpha_attn.reshape(size, part),
                    grad_alpha_mlp.reshape(size, part),
                ],
                axis=1,
            ),
            everyone,
        )
        summed = lax.dynamic_index_in_dim(summed, me, 0, keepdims=False)
        bounds = [2 * units, 4 * units, 4 * units + part, 4 * units + 2 * part]
        summed_up, summed_gate, summed_qk, summed_attn, summed_mlp = jnp.split(summed, bounds)
        return (
            out_hidden[None],
            grad_hidden[None],
            owned_query,
            owned_keys,
            owned_values,
            owned_output,
            owned_upward,
            owned_gating,
            owned_downward,
            summed_qk,
            summed_up,
            summed_gate,
            summed_attn,
            summed_mlp,
        )

    return on_device


def solution(mesh):
    rows, size = mesh.shape["dp"], mesh.shape["mp"]
    paired = Mesh(mesh.devices.reshape(rows // 2, 2, size), ("chip", "core", "mp"))
    return jax.shard_map(
        make_on_device(rows // 2, size),
        mesh=paired,
        in_specs=(
            P(DP, None, "mp"),
            P(DP, "mp"),
            P(DP, "mp"),
            P(DP, "mp"),
            P("mp", DP),
            P(DP, "mp"),
            P(DP, "mp"),
            P("mp", DP),
            P("mp"),
            P("mp"),
            P("mp"),
            P("mp"),
            P("mp"),
            P(DP, None),
            P(DP, None),
            P(DP, None, "mp"),
        ),
        out_specs=(
            P(DP, None, "mp"),
            P(DP, None, "mp"),
            P(DP, "mp"),
            P(DP, "mp"),
            P(DP, "mp"),
            P("mp", DP),
            P(DP, "mp"),
            P(DP, "mp"),
            P("mp", DP),
            P("mp"),
            P("mp"),
            P("mp"),
            P("mp"),
            P("mp"),
        ),
        check_vma=False,
    )
```

```python
import functools
import math

import jax
import jax.numpy as jnp
import numpy as np
from jax import lax
from jax.experimental import pallas as pl
from jax.experimental.pallas import tpu as pltpu
from jax.sharding import Mesh
from jax.sharding import PartitionSpec as P

DK = 64
HALF = DK // 2
EXT = 128
EPSILON = 1e-06
ROPE_BASE = 10000.0
VMEM_LIMIT = 60 * 1024 * 1024
F32 = jnp.float32
BF16 = jnp.bfloat16
DP = ("chip", "core")


def dot(left, right, dims=((1,), (0,)), precision=None):
    return lax.dot_general(
        left, right, (dims, ((), ())), precision=precision, preferred_element_type=F32
    )


NT = ((1,), (1,))
TN = ((0,), (0,))


def grid_params(dims):
    return pltpu.CompilerParams(
        dimension_semantics=("arbitrary",) * dims, vmem_limit_bytes=VMEM_LIMIT
    )


ANY = pl.BlockSpec(memory_space=pl.ANY)


def remote_params(collective, **more):
    return pltpu.CompilerParams(
        collective_id=collective,
        has_side_effects=True,
        vmem_limit_bytes=VMEM_LIMIT,
        **more,
    )


def to_device(source, target, send, receive, where):
    return pltpu.make_async_remote_copy(
        src_ref=source,
        dst_ref=target,
        send_sem=send,
        recv_sem=receive,
        device_id=where,
        device_id_type=pl.DeviceIdType.MESH,
    )


def to_member(source, target, send, receive, member):
    return to_device(source, target, send, receive, {"mp": member})


def flip(index, mask):
    bit = 1
    while bit <= mask:
        if mask & bit:
            index = index + bit - 2 * bit * lax.rem(lax.div(index, bit), 2)
        bit *= 2
    return index


def bits_below(count):
    return [1 << k for k in range(count.bit_length() - 1)]


def greet(where):
    pl.semaphore_signal(
        pltpu.get_barrier_semaphore(),
        inc=1,
        device_id=where,
        device_id_type=pl.DeviceIdType.MESH,
    )


def greet_all(size):
    me = lax.axis_index("mp")
    for k in range(1, size):
        greet({"mp": flip(me, k)})
    pl.semaphore_wait(pltpu.get_barrier_semaphore(), size - 1)


def greet_around(size, chips):
    me, chip, core = (lax.axis_index(name) for name in ("mp", "chip", "core"))
    for k in range(1, size):
        greet({"mp": flip(me, k)})
    for bit in bits_below(chips):
        greet({"chip": flip(chip, bit)})
    greet({"core": 1 - core})
    pl.semaphore_wait(pltpu.get_barrier_semaphore(), size + len(bits_below(chips)))


class Exchange:
    def __init__(self, size, source, target, piece, place, send, receive, local):
        me = lax.axis_index("mp")
        self.local = pltpu.make_async_copy(piece(source, me), place(target, me), local)
        self.remote = [
            to_member(
                piece(source, flip(me, k)),
                place(target, me),
                send.at[k],
                receive.at[k],
                flip(me, k),
            )
            for k in range(1, size)
        ]

    def start(self):
        for copy in self.remote:
            copy.start()
        self.local.start()

    def wait(self):
        self.local.wait()
        for copy in self.remote:
            copy.wait()


def exchange_semaphores(size):
    return [
        pltpu.SemaphoreType.DMA((size,)),
        pltpu.SemaphoreType.DMA((size,)),
        pltpu.SemaphoreType.DMA,
    ]


def row_part(rows):
    return lambda ref, j: ref.at[pl.ds(pl.multiple_of(j * rows, rows), rows), :]


def column_part(columns):
    return lambda ref, j: ref.at[:, pl.ds(pl.multiple_of(j * columns, columns), columns)]


def spread_tokens_kernel(size, source, target, send, receive, local):
    greet_all(size)
    tokens, part = source.shape
    exchange = Exchange(
        size,
        source,
        target,
        row_part(tokens // size),
        column_part(part),
        send,
        receive,
        local,
    )
    exchange.start()
    exchange.wait()


def spread_tokens(value, size, collective):
    tokens, part = value.shape
    return pl.pallas_call(
        functools.partial(spread_tokens_kernel, size),
        in_specs=[ANY],
        out_specs=ANY,
        out_shape=jax.ShapeDtypeStruct((tokens // size, size * part), value.dtype),
        scratch_shapes=exchange_semaphores(size),
        compiler_params=remote_params(collective),
        name="spread_tokens",
    )(value)


class Gather:
    def __init__(self, block, index, bits, where, send, receive):
        self.block, self.index, self.bits, self.where = block, index, bits, where
        self.send, self.receive = send, receive

    def copies(self, stage, incoming):
        span = [0]
        for bit in self.bits[:stage]:
            span += [held | bit for held in span]
        bit = self.bits[stage]
        for order, held in enumerate(span):
            ref = self.block(flip(self.index, held | bit if incoming else held))
            slot = (1 << stage) - 1 + order
            yield to_device(
                ref,
                ref,
                self.send(slot),
                self.receive(slot),
                self.where(flip(self.index, bit)),
            )

    def start(self, stage):
        if stage < len(self.bits):
            for copy in self.copies(stage, False):
                copy.start()

    def arrive(self, stage):
        if stage < len(self.bits):
            for copy in self.copies(stage, True):
                copy.wait_recv()

    def close(self):
        for stage in range(len(self.bits)):
            for copy in self.copies(stage, False):
                copy.wait_send()


def gather_all_kernel(
    size,
    chips,
    chunks,
    split,
    hidden,
    qkv,
    packed,
    vectors,
    wide,
    full_qkv,
    full,
    full_vectors,
    local,
    hidden_up,
    hidden_down,
    hidden_got,
    packed_up,
    packed_down,
    packed_got,
    plane_sent,
    plane_got,
    qkv_sent,
    qkv_got,
    vector_sent,
    vector_got,
):
    me, chip, core = (lax.axis_index(name) for name in ("mp", "chip", "core"))
    tokens = hidden.shape[0]
    rows = tokens // chunks
    height = packed.shape[0]
    owner = chip * 2 + core
    bits = bits_below(chips)
    stages = len(bits)
    greet_around(size, chips)

    own = [
        pltpu.make_async_copy(qkv, full_qkv.at[owner], local.at[0]),
        pltpu.make_async_copy(packed, full.at[me, chip], local.at[1]),
        pltpu.make_async_copy(vectors, full_vectors.at[me], local.at[2]),
        pltpu.make_async_copy(hidden, wide.at[me], local.at[3]),
    ]
    for copy in own:
        copy.start()

    def hidden_hop(origin, chunk, ref, member, send):
        at = pl.ds(chunk * rows, rows)
        return to_member(
            ref.at[at, :],
            wide.at[origin, at, :],
            send.at[origin, chunk],
            hidden_got.at[origin, chunk],
            member,
        )

    def packed_hop(origin, ref, member, send):
        return to_member(
            ref, full.at[origin, chip], send.at[origin], packed_got.at[origin], member
        )

    vector_copies = [
        to_member(
            vectors, full_vectors.at[me], vector_sent.at[k], vector_got.at[k], flip(me, k)
        )
        for k in range(1, size)
    ]

    def plane(origin, slot):
        return [
            Gather(
                lambda i, at=at: full.at[origin, i, at, :],
                chip,
                order,
                lambda i: {"chip": i},
                lambda k, half=half: plane_sent.at[slot, half, k],
                lambda k, half=half: plane_got.at[slot, half, k],
            )
            for half, (at, order) in enumerate(
                (
                    (pl.ds(0, split), bits),
                    (pl.ds(split, height - split), bits[::-1]),
                )
            )
        ]

    gather_qkv = Gather(
        lambda i: full_qkv.at[i],
        owner,
        [2 * bit for bit in bits] + [1],
        lambda i: {"chip": lax.div(i, 2), "core": lax.rem(i, 2)},
        lambda k: qkv_sent.at[k],
        lambda k: qkv_got.at[k],
    )

    sources = {0: [(me >= 0, me, 0, None)]}
    for distance in range(1, size):
        sources[distance] = [
            (me >= distance, me - distance, 2 * distance - 1, True),
            (me + distance < size, me + distance, 2 * distance, False),
        ]

    own[0].wait()
    gather_qkv.start(0)

    @pl.when(me < size - 1)
    def _():
        packed_hop(me, packed, me + 1, packed_up).start()

    @pl.when(me > 0)
    def _():
        packed_hop(me, packed, me - 1, packed_down).start()

    own[1].wait()
    for half in plane(me, 0):
        half.start(0)
    for chunk in range(chunks):

        @pl.when(me < size - 1)
        def _():
            hidden_hop(me, chunk, hidden, me + 1, hidden_up).start()

        @pl.when(me > 0)
        def _():
            hidden_hop(me, chunk, hidden, me - 1, hidden_down).start()

    for copy in vector_copies:
        copy.start()
    for stage in range(stages + 1):
        gather_qkv.arrive(stage)
        if stage < stages:
            gather_qkv.start(stage + 1)

    def advance(distance, stage):
        for exists, origin, slot, _ in sources[distance]:

            @pl.when(exists)
            def _():
                for half in plane(origin, slot):
                    half.arrive(stage)
                    half.start(stage + 1)

    for distance in range(1, size):
        for exists, origin, slot, upward in sources[distance]:

            @pl.when(exists)
            def _():
                block = full.at[origin, chip]
                packed_hop(origin, block, me, packed_up).wait_recv()
                if upward:

                    @pl.when(me < size - 1)
                    def _():
                        packed_hop(origin, block, me + 1, packed_up).start()
                else:

                    @pl.when(me > 0)
                    def _():
                        packed_hop(origin, block, me - 1, packed_down).start()

                for half in plane(origin, slot):
                    half.start(0)

        for chunk in range(chunks):
            for exists, origin, _, upward in sources[distance]:

                @pl.when(exists)
                def _():
                    block = wide.at[origin]
                    hidden_hop(origin, chunk, block, me, hidden_up).wait_recv()
                    if upward:

                        @pl.when(me < size - 1)
                        def _():
                            hidden_hop(origin, chunk, block, me + 1, hidden_up).start()
                    else:

                        @pl.when(me > 0)
                        def _():
                            hidden_hop(origin, chunk, block, me - 1, hidden_down).start()

            if chunk == chunks // 3:
                for stage in range(stages - 1):
                    advance(distance - 1, stage)
        advance(distance - 1, stages - 1)
    for stage in range(stages):
        advance(size - 1, stage)

    own[2].wait()
    own[3].wait()
    for copy in vector_copies:
        copy.wait()
    gather_qkv.close()
    for distance in range(size):
        for exists, origin, slot, upward in sources[distance]:

            @pl.when(exists)
            def _():
                for half in plane(origin, slot):
                    half.close()
                block = full.at[origin, chip]
                if upward is not False:

                    @pl.when(me < size - 1)
                    def _():
                        packed_hop(origin, block, me, packed_up).wait_send()
                        for chunk in range(chunks):
                            hidden_hop(origin, chunk, wide.at[origin], me, hidden_up).wait_send()

                if not upward:

                    @pl.when(me > 0)
                    def _():
                        packed_hop(origin, block, me, packed_down).wait_send()
                        for chunk in range(chunks):
                            hidden_hop(
                                origin, chunk, wide.at[origin], me, hidden_down
                            ).wait_send()


def gather_all(hidden, qkv, packed, vectors, size, chips, collective):
    chunks = 6
    height = packed.shape[0]
    dma = pltpu.SemaphoreType.DMA
    line = dma((size, chunks))
    plane = dma((2 * size - 1, 2, max(chips - 1, 1)))
    return pl.pallas_call(
        functools.partial(gather_all_kernel, size, chips, chunks, height // 32 * 16),
        in_specs=[ANY] * 4,
        out_specs=[ANY] * 4,
        out_shape=[
            jax.ShapeDtypeStruct((size, *hidden.shape), BF16),
            jax.ShapeDtypeStruct((2 * chips, *qkv.shape), BF16),
            jax.ShapeDtypeStruct((size, chips, *packed.shape), BF16),
            jax.ShapeDtypeStruct((size, *vectors.shape), F32),
        ],
        scratch_shapes=[
            dma((4,)),
            line,
            line,
            line,
            dma((size,)),
            dma((size,)),
            dma((size,)),
            plane,
            plane,
            dma((2 * chips - 1,)),
            dma((2 * chips - 1,)),
            dma((size,)),
            dma((size,)),
        ],
        compiler_params=remote_params(collective),
        name="gather_all",
    )(hidden, qkv, packed, vectors)


class LineSum:
    def __init__(self, size, chunks, term, up, down, sems):
        self.size, self.chunks = size, chunks
        self.term, self.up, self.down = term, up, down
        self.sent_up, self.sent_down, self.got_up, self.got_down = sems
        self.me = lax.axis_index("mp")
        self.rows = up.shape[1] // chunks

    def at(self, chunk):
        return pl.ds(chunk * self.rows, self.rows)

    def hop(self, upward, goal, chunk, member):
        slots = self.up if upward else self.down
        send = self.sent_up if upward else self.sent_down
        receive = self.got_up if upward else self.got_down
        ref = slots.at[goal, self.at(chunk), :]
        return to_member(ref, ref, send.at[goal, chunk], receive.at[goal, chunk], member)

    def step(self, order, chunk):
        me, last, at = self.me, self.size - 1, self.at(chunk)
        for upward, goal, ahead, first, member in (
            (True, last - order, me < last - order, me == 0, me + 1),
            (False, order, me > order, me == last, me - 1),
        ):
            slots = self.up if upward else self.down

            @pl.when(ahead & first)
            def _():
                slots[goal, at, :] = self.term(goal, at)

            @pl.when(ahead & jnp.logical_not(first))
            def _():
                self.hop(upward, goal, chunk, me).wait_recv()
                slots[goal, at, :] = (
                    slots[goal, at, :].astype(F32) + self.term(goal, at).astype(F32)
                ).astype(BF16)

            @pl.when(ahead)
            def _():
                self.hop(upward, goal, chunk, member).start()

    def result(self, chunk, out, out_at):
        me, at = self.me, self.at(chunk)
        out[out_at, :] = self.term(me, at).astype(F32)

        @pl.when(me > 0)
        def _():
            self.hop(True, me, chunk, me).wait_recv()
            out[out_at, :] += self.up[me, at, :].astype(F32)

        @pl.when(me < self.size - 1)
        def _():
            self.hop(False, me, chunk, me).wait_recv()
            out[out_at, :] += self.down[me, at, :].astype(F32)

    def close(self):
        for order in range(self.size - 1):
            for chunk in range(self.chunks):

                @pl.when(self.me < self.size - 1 - order)
                def _():
                    self.hop(True, self.size - 1 - order, chunk, self.me).wait_send()

                @pl.when(self.me > order)
                def _():
                    self.hop(False, order, chunk, self.me).wait_send()


class ChipSum:
    def __init__(self, layers, bits, source, acc, got, load, send, receive):
        self.layers, self.bits = layers, bits
        self.acc, self.got, self.chip = acc, got, lax.axis_index("chip")
        self.half = 1 << (len(bits) - 1)
        self.load = [
            pltpu.make_async_copy(
                source(layer, flip(self.chip, self.combo(slot))),
                acc.at[layer, slot],
                load.at[layer, slot],
            )
            for layer in range(layers)
            for slot in range(self.half)
        ]
        self.source, self.sent, self.received = source, send, receive

    def combo(self, slot):
        count = len(self.bits)
        return sum(self.bits[count - 1 - j] for j in range(count - 1) if slot >> j & 1)

    def copies(self, stage):
        count = self.half >> stage
        offset = 2 * self.half - 2 * count
        where = {"chip": flip(self.chip, self.bits[stage])}
        for layer in range(self.layers):
            for slot in range(count):
                if stage == 0:
                    other = flip(self.chip, self.bits[0] | self.combo(slot))
                    ref = self.source(layer, other)
                else:
                    ref = self.acc.at[layer, count + slot]
                at = offset + slot
                yield layer, slot, at, to_device(
                    ref,
                    self.got.at[layer, at],
                    self.sent.at[layer, at],
                    self.received.at[layer, at],
                    where,
                )

    def start(self, stage):
        if stage == 0:
            for copy in self.load:
                copy.start()
        for _, _, _, copy in self.copies(stage):
            copy.start()

    def add(self, stage):
        if stage == 0:
            for copy in self.load:
                copy.wait()
        for layer, slot, at, copy in self.copies(stage):
            copy.wait_recv()
            self.acc[layer, slot] = (
                self.acc[layer, slot].astype(F32) + self.got[layer, at].astype(F32)
            ).astype(BF16)

    def close(self):
        for stage in range(len(self.bits)):
            for _, _, _, copy in self.copies(stage):
                copy.wait_send()


def sum_all_kernel(
    size,
    chips,
    chunks,
    split,
    term,
    grads,
    grad_wo,
    grad_qkv,
    vectors,
    out,
    owned,
    owned_wo,
    owned_qkv,
    owned_vectors,
    term_up,
    term_down,
    acc_a,
    got_a,
    up_a,
    down_a,
    acc_b,
    got_b,
    up_b,
    down_b,
    pair_wo,
    other_wo,
    acc_wo,
    got_wo,
    up_wo,
    down_wo,
    pair_qkv,
    other_qkv,
    acc_qkv,
    got_qkv,
    whole,
    vector_sum,
    vector_got,
    vector_line,
    local,
    core_sent,
    core_got,
    vector_sent,
    vector_received,
    term_sems,
    line_sems,
    load_sems,
    chip_sent,
    chip_got,
):
    me, chip, core = (lax.axis_index(name) for name in ("mp", "chip", "core"))
    bits = bits_below(chips)
    stages = len(bits)
    greet_around(size, chips)
    other_core_is = {"core": 1 - core}

    def sems(ref, which):
        return [ref.at[which, k] for k in range(4)]

    line = LineSum(
        size, chunks, lambda goal, at: term[goal, at, :], term_up, term_down, sems(term_sems, 0)
    )
    sum_a = ChipSum(
        size,
        bits,
        lambda m, c: grads.at[m, c, pl.ds(0, split), :],
        acc_a,
        got_a,
        load_sems.at[0],
        chip_sent.at[0],
        chip_got.at[0],
    )
    sum_b = ChipSum(
        size,
        bits[::-1],
        lambda m, c: grads.at[m, c, pl.ds(split, grads.shape[2] - split), :],
        acc_b,
        got_b,
        load_sems.at[1],
        chip_sent.at[1],
        chip_got.at[1],
    )
    sum_wo = ChipSum(
        size,
        bits,
        lambda m, c: pair_wo.at[m, c],
        acc_wo,
        got_wo,
        load_sems.at[2],
        chip_sent.at[2],
        chip_got.at[2],
    )
    sum_qkv = ChipSum(
        1,
        bits,
        lambda m, c: pair_qkv.at[c],
        acc_qkv,
        got_qkv,
        load_sems.at[3],
        chip_sent.at[3],
        chip_got.at[3],
    )
    lines = [
        LineSum(
            size,
            1,
            lambda goal, at, acc=acc: acc[goal, 0, at, :],
            up,
            down,
            sems(line_sems, which),
        )
        for which, (acc, up, down) in enumerate(
            ((acc_a, up_a, down_a), (acc_b, up_b, down_b), (acc_wo, up_wo, down_wo))
        )
    ]

    own = [
        pltpu.make_async_copy(grad_wo.at[:, :, core], pair_wo, local.at[0]),
        pltpu.make_async_copy(grad_qkv.at[:, core], pair_qkv, local.at[1]),
    ]
    given = [
        to_device(
            grad_wo.at[:, :, 1 - core], other_wo, core_sent.at[0], core_got.at[0], other_core_is
        ),
        to_device(
            grad_qkv.at[:, 1 - core], other_qkv, core_sent.at[1], core_got.at[1], other_core_is
        ),
    ]
    vector_copies = [
        to_member(
            vectors.at[flip(me, k)],
            vector_line.at[k],
            vector_sent.at[k],
            vector_received.at[k],
            flip(me, k),
        )
        for k in range(1, size)
    ]
    for copy in own + given:
        copy.start()
    sum_a.start(0)
    sum_b.start(0)
    for copy in vector_copies:
        copy.start()

    owner = chip * 2 + core
    vector_bits = [1] + [2 * bit for bit in bits]

    def vector_copy(stage):
        partner = flip(owner, vector_bits[stage])
        return to_device(
            vector_sum.at[stage],
            vector_got.at[stage],
            vector_sent.at[size + stage],
            vector_received.at[size + stage],
            {"chip": lax.div(partner, 2), "core": lax.rem(partner, 2)},
        )

    def vector_step(stage):
        if stage == 0:
            total = vectors[me]
            for k, copy in enumerate(vector_copies):
                copy.wait_recv()
                total = total + vector_line[k + 1]
            vector_sum[0] = total
        else:
            vector_copy(stage - 1).wait_recv()
            vector_sum[stage] = vector_sum[stage - 1] + vector_got[stage - 1]
        if stage < len(vector_bits):
            vector_copy(stage).start()

    for chunk in range(chunks):
        line.step(0, chunk)
    for copy in own:
        copy.wait()
    for copy in given:
        copy.wait_recv()
    pair_wo[...] = (pair_wo[...].astype(F32) + other_wo[...].astype(F32)).astype(BF16)
    pair_qkv[...] = (pair_qkv[...].astype(F32) + other_qkv[...].astype(F32)).astype(BF16)
    sum_wo.start(0)
    sum_qkv.start(0)
    vector_step(0)
    vector_step(1)
    for order in range(1, size - 1):
        for chunk in range(chunks):
            line.step(order, chunk)
        if order - 1 < stages:
            for part in (sum_a, sum_b, sum_wo, sum_qkv):
                part.add(order - 1)
                if order < stages:
                    part.start(order)
    for stage in range(size - 2, stages):
        for part in (sum_a, sum_b, sum_wo, sum_qkv):
            part.add(stage)
            if stage + 1 < stages:
                part.start(stage + 1)
    lines[0].step(0, 0)
    lines[1].step(0, 0)
    lines[2].step(0, 0)
    for stage in range(2, len(vector_bits) + 1):
        vector_step(stage)
    for chunk in range(chunks):
        line.result(chunk, out, line.at(chunk))
    for order in range(1, size - 1):
        for part in lines:
            part.step(order, 0)
    owned_vectors[...] = vector_sum[len(vector_bits)]
    owned_qkv[...] = acc_qkv[0, 0].astype(F32)
    lines[0].result(0, whole, pl.ds(0, split))
    lines[1].result(0, whole, pl.ds(split, whole.shape[0] - split))
    lines[2].result(0, owned_wo, slice(None))

    matrices, rows, columns = owned.shape
    columns = columns // 2
    place = pl.ds(pl.multiple_of(core * columns, columns), columns)
    swaps = []
    for matrix in range(matrices):
        mine = pl.ds(pl.multiple_of((2 * matrix + core) * rows, rows), rows)
        theirs = pl.ds(pl.multiple_of((2 * matrix + 1 - core) * rows, rows), rows)
        swaps.append(
            to_device(
                whole.at[theirs, :],
                owned.at[matrix, :, place],
                core_sent.at[2 + matrix],
                core_got.at[2 + matrix],
                other_core_is,
            )
        )
        swaps[-1].start()
        copy = pltpu.make_async_copy(
            whole.at[mine, :], owned.at[matrix, :, place], local.at[2 + matrix]
        )
        copy.start()
        swaps.append(copy)
    for copy in swaps:
        copy.wait()

    for copy in given + vector_copies:
        copy.wait_send()
    for stage in range(len(vector_bits)):
        vector_copy(stage).wait_send()
    for part in (sum_a, sum_b, sum_wo, sum_qkv):
        part.close()
    line.close()
    for part in lines:
        part.close()


def sum_all(term, grads, grad_wo, grad_qkv, vectors, chips, collective):
    size, tokens, part = term.shape
    height, units = grads.shape[2:]
    rows = height // 6
    chunks = 6
    split = height // 32 * 16
    half, blocks = max(chips // 2, 1), max(chips - 1, 1)
    stages = chips.bit_length()
    dma = pltpu.SemaphoreType.DMA
    vmem = pl.BlockSpec(memory_space=pltpu.VMEM)
    wo_block, qkv_block = grad_wo.shape[3:], grad_qkv.shape[2:]
    long = vectors.shape[1:]

    def sums(layers, block):
        return [
            pltpu.VMEM((layers, half, *block), BF16),
            pltpu.VMEM((layers, blocks, *block), BF16),
        ]

    def line(block):
        return [pltpu.VMEM((size, *block), BF16)] * 2

    return pl.pallas_call(
        functools.partial(sum_all_kernel, size, chips, chunks, split),
        in_specs=[vmem, ANY, ANY, ANY, vmem],
        out_specs=[vmem] * 5,
        out_shape=[
            jax.ShapeDtypeStruct((tokens, part), F32),
            jax.ShapeDtypeStruct((3, rows, 2 * units), F32),
            jax.ShapeDtypeStruct(wo_block, F32),
            jax.ShapeDtypeStruct(qkv_block, F32),
            jax.ShapeDtypeStruct(long, F32),
        ],
        scratch_shapes=[
            *line((tokens, part)),
            *sums(size, (split, units)),
            *line((split, units)),
            *sums(size, (height - split, units)),
            *line((height - split, units)),
            pltpu.VMEM((size, chips, *wo_block), BF16),
            pltpu.VMEM((size, chips, *wo_block), BF16),
            *sums(size, wo_block),
            *line(wo_block),
            pltpu.VMEM((chips, *qkv_block), BF16),
            pltpu.VMEM((chips, *qkv_block), BF16),
            *sums(1, qkv_block),
            pltpu.VMEM((height, units), F32),
            pltpu.VMEM((stages + 1, *long), F32),
            pltpu.VMEM((stages + 1, *long), F32),
            pltpu.VMEM((size, *long), F32),
            dma((5,)),
            dma((5,)),
            dma((5,)),
            dma((size + stages,)),
            dma((size + stages,)),
            dma((1, 4, size, chunks)),
            dma((3, 4, size, 1)),
            dma((4, size, half)),
            dma((4, size, blocks)),
            dma((4, size, blocks)),
        ],
        compiler_params=remote_params(collective),
        name="sum_all",
    )(term, grads, grad_wo, grad_qkv, vectors)


def paired_place(heads):
    head, feature = np.divmod(np.arange(heads * DK), DK)
    return (feature // HALF) * (heads * HALF) + head * HALF + feature % HALF


def placing_matrix(place, heads):
    head, feature = np.divmod(np.arange(heads * DK), DK)
    matrix = np.zeros((heads * DK, heads * EXT), np.float32)
    matrix[place, head * EXT + feature] = 1
    return matrix


def head_sum_matrix(heads):
    lane = np.arange(heads * HALF) // HALF
    return (lane[:, None] == lane[None, :]).astype(np.float32)


def project_kernel(
    wide, weight, cosine, sine, gain, place_pair, place_plain, sums, q, k, v, rq, rk
):
    parts = wide.shape[0]
    heads = q.shape[0]
    pair = heads * HALF
    width = heads * DK
    raw = dot(wide[0], weight[0])
    for part in range(1, parts):
        raw += dot(wide[part], weight[part])
    rows = raw.shape[0]
    lane = lax.broadcasted_iota(jnp.int32, (rows, EXT), 1)
    cos = cosine[...]
    sin = sine[...]
    gain_first = gain[:, :pair]
    gain_second = gain[:, pair:]
    for offset, out, scale_out, factor in ((0, q, rq, math.sqrt(DK)), (width, k, rk, 1.0)):
        first = raw[:, offset : offset + pair]
        second = raw[:, offset + pair : offset + width]
        turned_first = first * cos - second * sin
        turned_second = second * cos + first * sin
        total = dot(
            turned_first * turned_first + turned_second * turned_second,
            sums[...],
            precision=lax.Precision.HIGHEST,
        )
        scale = lax.rsqrt(total + EPSILON)
        scale_out[...] = scale
        both = jnp.concatenate(
            [turned_first * scale * gain_first, turned_second * scale * gain_second], axis=1
        ).astype(BF16)
        padded = dot(both, place_pair[...]) * factor
        for head in range(heads):
            piece = padded[:, head * EXT : (head + 1) * EXT]
            if factor == 1.0:
                piece = jnp.where(lane < DK, piece, 1.0)
            out[head] = piece.astype(BF16)
    padded = dot(raw[:, 2 * width :].astype(BF16), place_plain[...])
    for head in range(heads):
        piece = padded[:, head * EXT : (head + 1) * EXT]
        v[head] = jnp.where(lane < DK, piece, 1.0).astype(BF16)


def project(wide, weight, cosine, sine, gain, place_pair, place_plain, sums):
    parts, tokens, part = wide.shape
    width = gain.shape[1]
    heads = width // DK
    block = min(512, tokens)
    padded = jax.ShapeDtypeStruct((heads, tokens, EXT), BF16)
    scale = jax.ShapeDtypeStruct((tokens, heads * HALF), F32)

    def whole(array):
        return pl.BlockSpec(array.shape, lambda i: (0,) * array.ndim)

    rows = pl.BlockSpec((block, heads * HALF), lambda i: (i, 0))
    headed = pl.BlockSpec((heads, block, EXT), lambda i: (0, i, 0))
    return pl.pallas_call(
        project_kernel,
        grid=(tokens // block,),
        in_specs=[
            pl.BlockSpec((parts, block, part), lambda i: (0, i, 0)),
            whole(weight),
            rows,
            rows,
            whole(gain),
            whole(place_pair),
            whole(place_plain),
            whole(sums),
        ],
        out_specs=[headed, headed, headed, rows, rows],
        out_shape=[padded, padded, padded, scale, scale],
        compiler_params=grid_params(1),
        cost_estimate=pl.CostEstimate(
            flops=2 * tokens * parts * part * width * 3,
            bytes_accessed=20 << 20,
            transcendentals=0,
        ),
        name="project",
    )(wide, weight, cosine, sine, gain, place_pair, place_plain, sums)


def split_three(value):
    high = value.astype(BF16).astype(F32)
    rest = value - high
    middle = rest.astype(BF16).astype(F32)
    return high, middle, rest - middle


def attend_kernel(low, q, k, v, qdoc, kdoc, collect, attended, qback, acc):
    heads, rows, _ = q.shape
    block = kdoc.shape[2]
    index = pl.program_id(0)
    acc[...] = jnp.zeros_like(acc)

    def step(j, diagonal):
        slots = pl.ds(pl.multiple_of(j * block, block), block)
        mask = qdoc[...] == kdoc[j]
        if diagonal:
            row = lax.broadcasted_iota(jnp.int32, (rows, block), 0)
            column = lax.broadcasted_iota(jnp.int32, (rows, block), 1)
            mask = (mask & (column < row)) | (column == row)
        for head in range(heads):
            scores = dot(q[head], k[head, slots, :], NT)
            weight = jnp.where(mask, jnp.exp(scores), 0.0).astype(BF16)
            acc[head] += dot(weight, v[head, slots, :])

    def earlier(j, carry):
        step(j, False)
        return carry

    lax.fori_loop(low[index], index, earlier, 0)
    step(index, True)

    lane = lax.broadcasted_iota(jnp.int32, (rows, EXT), 1)
    merged = jnp.zeros((rows, heads * DK), F32)
    for head in range(heads):
        both = acc[head]
        total = pltpu.roll(both, DK, 1)
        output = jnp.where(lane < DK, both / total, 0.0).astype(BF16)
        merged += dot(output, collect[head])
        high, middle, rest = split_three(-jnp.log(both))
        qback[head] = jnp.where(
            lane < DK,
            q[head].astype(F32),
            jnp.where(
                lane == DK,
                high,
                jnp.where(lane == DK + 1, middle, jnp.where(lane == DK + 2, rest, 0.0)),
            ),
        ).astype(BF16)
    attended[...] = merged.astype(BF16)


def attend(low, q, k, v, qdoc, kdoc, collect):
    heads, tokens, _ = q.shape
    block = kdoc.shape[2]
    width = heads * DK

    def whole(array):
        return pl.BlockSpec(array.shape, lambda i, low: (0,) * array.ndim)

    headed = pl.BlockSpec((heads, block, EXT), lambda i, low: (0, i, 0))
    return pl.pallas_call(
        attend_kernel,
        grid_spec=pltpu.PrefetchScalarGridSpec(
            num_scalar_prefetch=1,
            grid=(tokens // block,),
            in_specs=[
                headed,
                whole(k),
                whole(v),
                pl.BlockSpec((block, 1), lambda i, low: (i, 0)),
                whole(kdoc),
                whole(collect),
            ],
            out_specs=[pl.BlockSpec((block, width), lambda i, low: (i, 0)), headed],
            scratch_shapes=[pltpu.VMEM((heads, block, EXT), F32)],
        ),
        out_shape=[
            jax.ShapeDtypeStruct((tokens, width), BF16),
            jax.ShapeDtypeStruct((heads, tokens, EXT), BF16),
        ],
        compiler_params=grid_params(1),
        cost_estimate=pl.CostEstimate(
            flops=40_000_000_000, bytes_accessed=16 << 20, transcendentals=0
        ),
        name="attend",
    )(low, q, k, v, qdoc, kdoc, collect)


def gather_heads(padded, matrix, heads):
    total = None
    for head in range(heads):
        value = padded[head]
        high = value.astype(BF16)
        rest = (value - high.astype(F32)).astype(BF16)
        term = dot(high, matrix[head]) + dot(rest, matrix[head])
        total = term if total is None else total + term
    return total


def unrope(grad, unit, gain, scale, cos, sin, sums):
    pair = cos.shape[1]
    grad_gain = jnp.sum(grad * unit, axis=0, keepdims=True)
    dy = grad * gain
    prod = dy * unit
    total = dot(prod[:, :pair] + prod[:, pair:], sums, precision=lax.Precision.HIGHEST)
    first = scale * (dy[:, :pair] - unit[:, :pair] * total)
    second = scale * (dy[:, pair:] - unit[:, pair:] * total)
    raw = jnp.concatenate([first * cos + second * sin, second * cos - first * sin], axis=1)
    return raw.astype(BF16), grad_gain


def attend_back_kernel(
    low,
    qback,
    dout,
    attended,
    k,
    v,
    qdoc,
    kdoc,
    cosine,
    sine,
    rq,
    rk,
    gain,
    weight,
    place_plain,
    collect_plain,
    collect_pair,
    sums,
    dq_out,
    dk_out,
    dv_out,
    term_out,
    gain_out,
    dk,
    dv,
    dq,
    dox,
    dq_low,
):
    heads, rows, _ = qback.shape
    steps = pl.num_programs(0) // 2
    step_at = pl.program_id(0)
    width = heads * DK
    scale = math.sqrt(DK)

    @pl.when(step_at == 0)
    def _():
        dk[...] = jnp.zeros_like(dk)
        dv[...] = jnp.zeros_like(dv)
        gain_out[...] = jnp.zeros_like(gain_out)

    @pl.when(step_at < steps)
    def _():
        index = step_at
        lane = lax.broadcasted_iota(jnp.int32, (rows, EXT), 1)
        spread_grad = dot(dout[...], place_plain[...])
        spread_out = dot(attended[...], place_plain[...])
        for head in range(heads):
            piece = spread_grad[:, head * EXT : (head + 1) * EXT]
            other = spread_out[:, head * EXT : (head + 1) * EXT]
            delta = jnp.sum(piece * other, axis=1, keepdims=True)
            high, middle, rest = split_three(-delta)
            dox[head] = jnp.where(
                lane < DK,
                piece,
                jnp.where(
                    lane == DK,
                    high,
                    jnp.where(lane == DK + 1, middle, jnp.where(lane == DK + 2, rest, 0.0)),
                ),
            ).astype(BF16)
        dq[...] = jnp.zeros_like(dq)

        def step(j, diagonal):
            slots = pl.ds(pl.multiple_of(j * rows, rows), rows)
            mask = kdoc[slots, :] == qdoc[0]
            if diagonal:
                key = lax.broadcasted_iota(jnp.int32, (rows, rows), 0)
                query = lax.broadcasted_iota(jnp.int32, (rows, rows), 1)
                mask = (mask & (key < query)) | (key == query)
            for head in range(heads):
                keys = k[head, slots, :]
                scores = dot(keys, qback[head], NT)
                probs = jnp.where(mask, jnp.exp(scores), 0.0)
                dv[head, slots, :] += dot(probs.astype(BF16), dox[head])
                dprobs = dot(v[head, slots, :], dox[head], NT)
                dscores = (probs * dprobs).astype(BF16)
                dk[head, slots, :] += dot(dscores, qback[head])
                dq[head] += dot(dscores, keys, TN)

        def earlier(j, carry):
            step(j, False)
            return carry

        lax.fori_loop(low[index], index, earlier, 0)
        step(index, True)

        grad = gather_heads(dq, collect_pair, heads) * scale
        query = dot(qback[0], collect_pair[0])
        for head in range(1, heads):
            query += dot(qback[head], collect_pair[head])
        unit = query * (1.0 / scale) / gain[...]
        raw, grad_gain = unrope(
            grad, unit, gain[...], rq[...], cosine[...], sine[...], sums[...]
        )
        gain_out[...] += grad_gain
        dq_out[...] = raw
        dq_low[pl.ds(pl.multiple_of(index * rows, rows), rows), :] = raw

    @pl.when(step_at >= steps)
    def _():
        index = step_at - steps
        slots = pl.ds(pl.multiple_of(index * rows, rows), rows)
        grad = gather_heads([dk[head, slots, :] for head in range(heads)], collect_pair, heads)
        keys = dot(k[0, slots, :], collect_pair[0])
        for head in range(1, heads):
            keys += dot(k[head, slots, :], collect_pair[head])
        raw, grad_gain = unrope(
            grad, keys / gain[...], gain[...], rk[...], cosine[...], sine[...], sums[...]
        )
        gain_out[...] += grad_gain
        dk_out[...] = raw
        dvalues = gather_heads(
            [dv[head, slots, :] for head in range(heads)], collect_plain, heads
        ).astype(BF16)
        dv_out[...] = dvalues
        dquery = dq_low[slots, :]
        for part in range(weight.shape[0]):
            term = dot(dquery, weight[part, :, :width], NT)
            term += dot(raw, weight[part, :, width : 2 * width], NT)
            term += dot(dvalues, weight[part, :, 2 * width :], NT)
            term_out[part] = term.astype(BF16)


def attend_back(
    low,
    qback,
    dout,
    attended,
    k,
    v,
    qdoc,
    kdoc,
    cosine,
    sine,
    rq,
    rk,
    gain,
    weight,
    place_plain,
    collect_plain,
    collect_pair,
    sums,
):
    heads, tokens, _ = k.shape
    block = qdoc.shape[2]
    width = heads * DK
    steps = tokens // block
    parts, part = weight.shape[:2]

    def whole(array):
        return pl.BlockSpec(array.shape, lambda i, low: (0,) * array.ndim)

    def now(i):
        return jnp.minimum(i, steps - 1)

    def after(i):
        return jnp.maximum(i - steps, 0)

    def both(i):
        return lax.rem(i, steps)

    def rows(columns, at):
        return pl.BlockSpec((block, columns), lambda i, low: (at(i), 0))

    return pl.pallas_call(
        attend_back_kernel,
        grid_spec=pltpu.PrefetchScalarGridSpec(
            num_scalar_prefetch=1,
            grid=(2 * steps,),
            in_specs=[
                pl.BlockSpec((heads, block, EXT), lambda i, low: (0, now(i), 0)),
                rows(width, now),
                rows(width, now),
                whole(k),
                whole(v),
                pl.BlockSpec((1, 1, block), lambda i, low: (now(i), 0, 0)),
                whole(kdoc),
                rows(width // 2, both),
                rows(width // 2, both),
                rows(width // 2, now),
                rows(width // 2, after),
                whole(gain),
                whole(weight),
                whole(place_plain),
                whole(collect_plain),
                whole(collect_pair),
                whole(sums),
            ],
            out_specs=[
                rows(width, now),
                rows(width, after),
                rows(width, after),
                pl.BlockSpec((parts, block, part), lambda i, low: (0, after(i), 0)),
                pl.BlockSpec((1, width), lambda i, low: (0, 0)),
            ],
            scratch_shapes=[
                pltpu.VMEM((heads, tokens, EXT), F32),
                pltpu.VMEM((heads, tokens, EXT), F32),
                pltpu.VMEM((heads, block, EXT), F32),
                pltpu.VMEM((heads, block, EXT), BF16),
                pltpu.VMEM((tokens, width), BF16),
            ],
        ),
        out_shape=[
            jax.ShapeDtypeStruct((tokens, width), BF16),
            jax.ShapeDtypeStruct((tokens, width), BF16),
            jax.ShapeDtypeStruct((tokens, width), BF16),
            jax.ShapeDtypeStruct((parts, tokens, part), BF16),
            jax.ShapeDtypeStruct((1, width), F32),
        ],
        compiler_params=grid_params(1),
        cost_estimate=pl.CostEstimate(
            flops=80_000_000_000, bytes_accessed=30 << 20, transcendentals=0
        ),
        name="attend_back",
    )(
        low,
        qback,
        dout,
        attended,
        k,
        v,
        qdoc,
        kdoc,
        cosine,
        sine,
        rq,
        rk,
        gain,
        weight,
        place_plain,
        collect_plain,
        collect_pair,
        sums,
    )


def whole_matrix(ref):
    _, chips, rows, units = ref.shape
    return ref[...].reshape(chips * rows, units)


def first_step():
    return (pl.program_id(0) == 0) & (pl.program_id(1) == 0)


def last_step():
    return (pl.program_id(0) == pl.num_programs(0) - 1) & (
        pl.program_id(1) == pl.num_programs(1) - 1
    )


def feed_kernel(
    size,
    x,
    w_up,
    w_gate,
    w_down,
    s_u,
    s_v,
    cotangent,
    up_out,
    gate_out,
    units_out,
    branch,
    spread,
    acc,
    send,
    receive,
    local,
):
    exchange = Exchange(
        size,
        cotangent,
        spread,
        row_part(spread.shape[0]),
        column_part(cotangent.shape[1]),
        send,
        receive,
        local,
    )

    @pl.when(first_step())
    def _():
        greet_all(size)
        exchange.start()

    part = pl.program_id(1)
    up = dot(x[...], whole_matrix(w_up))
    gate = dot(x[...], whole_matrix(w_gate))
    up_out[0] = up.astype(BF16)
    gate_out[0] = gate.astype(BF16)
    scaled = gate * s_v[0]
    units = (up * s_u[0] * (scaled / (1.0 + jnp.exp(-scaled)))).astype(BF16)
    units_out[0] = units
    term = dot(units, whole_matrix(w_down), NT)

    @pl.when(part == 0)
    def _():
        acc[...] = term

    @pl.when(part > 0)
    def _():
        acc[...] += term

    @pl.when(part == pl.num_programs(1) - 1)
    def _():
        branch[...] = acc[...].astype(BF16)

    @pl.when(last_step())
    def _():
        exchange.wait()


def packed_specs(packed, width):
    _, chips, _, units = packed.shape
    return [
        pl.BlockSpec((1, chips, width // chips, units), lambda t, m, w=w: (m, 0, w, 0))
        for w in range(3)
    ]


def feed(x, packed, s_u, s_v, cotangent, collective):
    tokens, width = x.shape
    parts, _, _, units = packed.shape
    size = parts
    block = min(512, tokens)
    rows = pl.BlockSpec((block, width), lambda t, m: (t, 0))
    vector = pl.BlockSpec((1, 1, units), lambda t, m: (m, 0, 0))
    piece = pl.BlockSpec((1, block, units), lambda t, m: (m, t, 0))
    hidden = jax.ShapeDtypeStruct((parts, tokens, units), BF16)
    slots, part = cotangent.shape
    return pl.pallas_call(
        functools.partial(feed_kernel, size),
        grid=(tokens // block, parts),
        in_specs=[rows, *packed_specs(packed, width), vector, vector, ANY],
        out_specs=[piece, piece, piece, rows, ANY],
        out_shape=[
            hidden,
            hidden,
            hidden,
            jax.ShapeDtypeStruct((tokens, width), BF16),
            jax.ShapeDtypeStruct((slots // size, size * part), BF16),
        ],
        scratch_shapes=[pltpu.VMEM((block, width), F32), *exchange_semaphores(size)],
        compiler_params=remote_params(collective),
        cost_estimate=pl.CostEstimate(
            flops=6 * tokens * width * parts * units, bytes_accessed=60 << 20, transcendentals=0
        ),
        name="feed",
    )(x, packed, packed, packed, s_u, s_v, cotangent)


def feed_back_kernel(
    size,
    dbranch,
    w_up,
    w_gate,
    w_down,
    s_u,
    s_v,
    up_in,
    gate_in,
    result,
    dup_out,
    dgate_out,
    dx,
    grad_u,
    grad_v,
    spread,
    acc,
    sum_u,
    sum_v,
    send,
    receive,
    local,
):
    exchange = Exchange(
        size,
        result,
        spread,
        column_part(spread.shape[1]),
        row_part(result.shape[0]),
        send,
        receive,
        local,
    )

    @pl.when(first_step())
    def _():
        greet_all(size)
        exchange.start()

    block = pl.program_id(0)
    part = pl.program_id(1)
    dunits = dot(dbranch[...], whole_matrix(w_down))
    up = up_in[0].astype(F32)
    gate = gate_in[0].astype(F32)
    scaled = gate * s_v[0]
    sigmoid = 1.0 / (1.0 + jnp.exp(-scaled))
    silu = scaled * sigmoid
    slope = sigmoid * (1.0 + scaled - silu)
    through_up = dunits * silu
    through_gate = dunits * up * s_u[0] * slope
    dup = (through_up * s_u[0]).astype(BF16)
    dgate = (through_gate * s_v[0]).astype(BF16)
    dup_out[0] = dup
    dgate_out[0] = dgate
    term = dot(dup, whole_matrix(w_up), NT) + dot(dgate, whole_matrix(w_gate), NT)
    part_u = jnp.sum(through_up * up, axis=0, keepdims=True)
    part_v = jnp.sum(through_gate * gate, axis=0, keepdims=True)

    @pl.when(block == 0)
    def _():
        sum_u[part] = part_u
        sum_v[part] = part_v

    @pl.when(block > 0)
    def _():
        sum_u[part] += part_u
        sum_v[part] += part_v

    @pl.when(part == 0)
    def _():
        acc[...] = term

    @pl.when(part > 0)
    def _():
        acc[...] += term

    @pl.when(part == pl.num_programs(1) - 1)
    def _():
        dx[...] = acc[...].astype(BF16)

    @pl.when(last_step())
    def _():
        grad_u[...] = sum_u[...]
        grad_v[...] = sum_v[...]
        exchange.wait()


def feed_back(dbranch, packed, s_u, s_v, up, gate, result, collective):
    tokens, width = dbranch.shape
    parts, _, _, units = packed.shape
    size = parts
    block = min(512, tokens)
    rows = pl.BlockSpec((block, width), lambda t, m: (t, 0))
    vector = pl.BlockSpec((1, 1, units), lambda t, m: (m, 0, 0))
    piece = pl.BlockSpec((1, block, units), lambda t, m: (m, t, 0))
    vectors = pl.BlockSpec((parts, 1, units), lambda t, m: (0, 0, 0))
    hidden = jax.ShapeDtypeStruct((parts, tokens, units), BF16)
    sums = jax.ShapeDtypeStruct((parts, 1, units), F32)
    mine = result.shape[0]
    return pl.pallas_call(
        functools.partial(feed_back_kernel, size),
        grid=(tokens // block, parts),
        in_specs=[rows, *packed_specs(packed, width), vector, vector, piece, piece, ANY],
        out_specs=[piece, piece, rows, vectors, vectors, ANY],
        out_shape=[
            hidden,
            hidden,
            jax.ShapeDtypeStruct((tokens, width), BF16),
            sums,
            sums,
            jax.ShapeDtypeStruct((size * mine, width // size), BF16),
        ],
        scratch_shapes=[
            pltpu.VMEM((block, width), F32),
            pltpu.VMEM((parts, 1, units), F32),
            pltpu.VMEM((parts, 1, units), F32),
            *exchange_semaphores(size),
        ],
        compiler_params=remote_params(collective),
        cost_estimate=pl.CostEstimate(
            flops=6 * tokens * width * parts * units, bytes_accessed=70 << 20, transcendentals=0
        ),
        name="feed_back",
    )(dbranch, packed, packed, packed, s_u, s_v, up, gate, result)


def feed_grads_kernel(
    size,
    x,
    dbranch,
    dup,
    dgate,
    units,
    dmerged,
    grads,
    dattended,
    x_turned,
    d_turned,
    send,
    receive,
    local,
):
    exchange = Exchange(
        size,
        dmerged,
        dattended,
        column_part(dattended.shape[1]),
        row_part(dmerged.shape[0]),
        send,
        receive,
        local,
    )

    @pl.when(first_step())
    def _():
        greet_all(size)
        exchange.start()
        x_turned[...] = x[...].T
        d_turned[...] = dbranch[...].T

    _, chips, rows, _ = grads.shape
    for which, left, right in (
        (0, x_turned, dup),
        (1, x_turned, dgate),
        (2, d_turned, units),
    ):

        @pl.when(pl.program_id(0) == which)
        def _():
            total = dot(left[...], right[0])
            grads[0] = total.astype(BF16).reshape(chips, rows, total.shape[1])

    @pl.when(last_step())
    def _():
        exchange.wait()


def feed_grads(x, dbranch, dup, dgate, units_in, dmerged, chips, collective):
    tokens, width = x.shape
    parts, _, units = dup.shape
    size = parts
    rows = width // chips
    mine = dmerged.shape[0]
    whole = pl.BlockSpec((tokens, width), lambda w, m: (0, 0))

    def piece(which):
        def at(w, m):
            return (jnp.where(w == which, m, jnp.where(w < which, 0, parts - 1)), 0, 0)

        return pl.BlockSpec((1, tokens, units), at)

    return pl.pallas_call(
        functools.partial(feed_grads_kernel, size),
        grid=(3, parts),
        in_specs=[whole, whole, piece(0), piece(1), piece(2), ANY],
        out_specs=[pl.BlockSpec((1, chips, rows, units), lambda w, m: (m, 0, w, 0)), ANY],
        out_shape=[
            jax.ShapeDtypeStruct((parts, chips, 3 * rows, units), BF16),
            jax.ShapeDtypeStruct((size * mine, width // size), BF16),
        ],
        scratch_shapes=[
            pltpu.VMEM((width, tokens), BF16),
            pltpu.VMEM((width, tokens), BF16),
            *exchange_semaphores(size),
        ],
        compiler_params=remote_params(collective),
        cost_estimate=pl.CostEstimate(
            flops=6 * tokens * width * parts * units, bytes_accessed=40 << 20, transcendentals=0
        ),
        name="feed_grads",
    )(x, dbranch, dup, dgate, units_in, dmerged)


def rope_tables(positions, head_size):
    half_size = head_size // 2
    freq_index = jnp.arange(half_size, dtype=F32)
    inverse = jnp.exp(freq_index * (-2.0 * math.log(ROPE_BASE) / head_size))
    angles = positions.astype(F32)[..., None] * inverse
    return (jnp.cos(angles), jnp.sin(angles))


def document_starts(doc_ids):
    slot_index = jnp.arange(doc_ids.shape[-1], dtype=jnp.int32)
    earlier = jnp.concatenate([doc_ids[..., :1] - 1, doc_ids[..., :-1]], axis=-1)
    starts = jnp.where(doc_ids != earlier, slot_index, jnp.zeros_like(slot_index))
    return lax.cummax(starts, axis=starts.ndim - 1)


def row_scale(value):
    return lax.rsqrt(jnp.sum(value * value, axis=-1, keepdims=True) + EPSILON)


def residual_forward(resid, branch, alpha):
    branch_scale = row_scale(branch)
    unit = branch * branch_scale
    mixed = resid + alpha * (unit - resid)
    mixed_scale = row_scale(mixed)
    return (mixed * mixed_scale, (unit, branch_scale, mixed_scale))


def residual_backward(grad_out, result, resid, alpha, kept):
    unit, branch_scale, mixed_scale = kept
    grad_mixed = mixed_scale * (
        grad_out - result * jnp.sum(grad_out * result, axis=-1, keepdims=True)
    )
    grad_alpha = jnp.sum(grad_mixed * (unit - resid), axis=0)
    grad_resid = grad_mixed * (1.0 - alpha)
    grad_unit = grad_mixed * alpha
    grad_branch = branch_scale * (
        grad_unit - unit * jnp.sum(grad_unit * unit, axis=-1, keepdims=True)
    )
    return (grad_resid, grad_branch, grad_alpha)


def other_core(value):
    return lax.ppermute(value, "core", [(0, 1), (1, 0)])


def make_on_device(chips, size):
    def on_device(
        hidden,
        wq,
        wk,
        wv,
        wo,
        w_up,
        w_gate,
        w_down,
        s_qk,
        s_u,
        s_v,
        alpha_a,
        alpha_m,
        doc_ids,
        valid,
        cotangent,
    ):
        _, slots, part = hidden.shape
        width = part * size
        heads = s_qk.shape[0] // DK
        rows = wq.shape[0]
        units = w_up.shape[1] // 2
        mine = slots // size
        block = min(512, slots)
        me = lax.axis_index("mp")
        core = lax.axis_index("core")

        place = paired_place(heads)
        in_pairs = (
            lambda w: w.reshape(w.shape[0], heads, 2, HALF)
            .transpose(0, 2, 1, 3)
            .reshape(w.shape[0], heads * DK)
        )
        low_qkv = jnp.concatenate([in_pairs(wq), in_pairs(wk), wv], axis=1).astype(BF16)
        stacked = jnp.stack([w_up, w_gate, w_down.T]).astype(BF16).reshape(3, rows, 2, units)
        keep = lax.dynamic_index_in_dim(stacked, core, 2, keepdims=False)
        give = lax.dynamic_index_in_dim(stacked, 1 - core, 2, keepdims=False)
        low_wo = wo.astype(BF16).T.reshape(rows // 2, 2 * part)
        given = jnp.concatenate([give.reshape(3 * rows, units), low_wo])
        got = other_core(given)

        def in_order(own, other):
            return jnp.where(core == 0, jnp.stack([own, other], 1), jnp.stack([other, own], 1))

        pair = in_order(keep, got[: 3 * rows].reshape(3, rows, units))
        pair_wo = in_order(low_wo[None], got[3 * rows :][None])
        packed = jnp.concatenate([pair.reshape(6 * rows, units), pair_wo.reshape(rows, units)])
        vectors = jnp.concatenate([s_u, s_v * math.sqrt(width), alpha_a, alpha_m])
        wide, full_qkv, packed, vectors = gather_all(
            hidden[0].astype(BF16), low_qkv, packed, vectors[None], size, chips, 0
        )
        full_qkv = full_qkv.reshape(size, part, 3 * part)
        full_wo = packed[:, :, 6 * rows :].reshape(size, width, part)
        vectors = vectors[:, 0]
        s_up = lax.dynamic_slice_in_dim(vectors[:, : 2 * units], core * units, units, 1)
        s_gate = lax.dynamic_slice_in_dim(
            vectors[:, 2 * units : 4 * units], core * units, units, 1
        )
        s_up = s_up[:, None, :]
        s_gate = s_gate[:, None, :]
        alpha_attn = vectors[:, 4 * units : 4 * units + part].reshape(width)
        alpha_mlp = vectors[:, 4 * units + part :].reshape(width)

        docs = doc_ids[0]
        starts = document_starts(docs)
        slot = jnp.arange(slots, dtype=jnp.int32)
        cosine, sine = rope_tables(slot - starts, DK)
        cosine = jnp.tile(cosine, (1, heads))
        sine = jnp.tile(sine, (1, heads))
        low = starts[::block] // block
        key_docs = jnp.where(valid[0] == 1, docs, -1)
        to_pair = placing_matrix(place, heads)
        to_plain = placing_matrix(np.arange(heads * DK), heads)
        place_pair = jnp.asarray(to_pair, BF16)
        place_plain = jnp.asarray(to_plain, BF16)
        collect_pair = jnp.asarray(to_pair.T.reshape(heads, EXT, heads * DK), BF16)
        collect_plain = jnp.asarray(to_plain.T.reshape(heads, EXT, heads * DK), BF16)
        sums = jnp.asarray(head_sum_matrix(heads))
        gain = in_pairs(s_qk[None, :])

        q, k, v, rq, rk = project(
            wide, full_qkv, cosine, sine, gain, place_pair, place_plain, sums
        )
        attended, qback = attend(
            low,
            q,
            k,
            v,
            docs[:, None],
            key_docs.reshape(slots // block, 1, block),
            collect_plain,
        )
        merged = spread_tokens(attended, size, 1)
        resid = lax.dynamic_slice_in_dim(wide, me * mine, mine, 1)
        resid = resid.transpose(1, 0, 2).reshape(mine, width).astype(F32)
        merged_parts = merged.reshape(mine, size, part)
        branch_attn = jnp.einsum("tmh,mdh->td", merged_parts, full_wo, preferred_element_type=F32)
        middle, kept_attn = residual_forward(resid, branch_attn, alpha_attn)

        middle_low = middle.astype(BF16)
        x = jnp.concatenate([middle_low, other_core(middle_low)])
        up, gate, hidden_units, down_term, spread_cot = feed(
            x, packed, s_up, s_gate, cotangent[0].astype(BF16), 2
        )
        branch_mlp = down_term[:mine].astype(F32) + other_core(down_term[mine:]).astype(F32)
        result, kept_mlp = residual_forward(middle, branch_mlp, alpha_mlp)

        grad_middle, grad_branch_mlp, grad_alpha_mlp = residual_backward(
            spread_cot.astype(F32), result, middle, alpha_mlp, kept_mlp
        )
        grad_branch_mlp = grad_branch_mlp.astype(BF16)
        dbranch = jnp.concatenate([grad_branch_mlp, other_core(grad_branch_mlp)])
        dup, dgate, dx, grad_u, grad_v, out_low = feed_back(
            dbranch, packed, s_up, s_gate, up, gate, result.astype(BF16), 3
        )
        out_hidden = out_low.astype(F32)
        grad_middle = (
            grad_middle + dx[:mine].astype(F32) + other_core(dx[mine:]).astype(F32)
        )

        grad_resid, grad_branch_attn, grad_alpha_attn = residual_backward(
            grad_middle, middle, resid, alpha_attn, kept_attn
        )
        grad_branch_attn = grad_branch_attn.astype(BF16)
        grad_merged = jnp.einsum(
            "td,mdh->tmh", grad_branch_attn, full_wo, preferred_element_type=F32
        ).astype(BF16)
        grads, dattended = feed_grads(
            x, dbranch, dup, dgate, hidden_units, grad_merged.reshape(mine, width), chips, 4
        )
        grad_wo = jnp.einsum(
            "td,tmh->mdh", grad_branch_attn, merged_parts, preferred_element_type=F32
        ).astype(BF16)
        dq, dk, dv, term, grad_gain = attend_back(
            low,
            qback,
            dattended,
            attended,
            k,
            v,
            docs.reshape(slots // block, 1, block),
            key_docs[:, None],
            cosine,
            sine,
            rq,
            rk,
            gain,
            full_qkv,
            place_plain,
            collect_plain,
            collect_pair,
            sums,
        )
        own = lax.dynamic_slice_in_dim(term, me * mine, mine, 1).astype(F32)
        own = own + grad_resid.reshape(mine, size, part).transpose(1, 0, 2)
        term = lax.dynamic_update_slice_in_dim(term, own.astype(BF16), me * mine, 1)
        grad_qkv = jnp.concatenate(
            [
                jnp.einsum("mtd,tf->mdf", wide, d, preferred_element_type=F32)
                .astype(BF16)
                .reshape(width, part)
                for d in (dq, dk, dv)
            ],
            axis=1,
        )
        out_pairs = (
            lambda w: w.reshape(w.shape[0], 2, heads, HALF)
            .transpose(0, 2, 1, 3)
            .reshape(w.shape[0], heads * DK)
        )

        zero = jnp.zeros((size, 2, units), F32)
        placed_u = lax.dynamic_update_slice(zero, grad_u, (0, core, 0))
        placed_v = lax.dynamic_update_slice(zero, grad_v * math.sqrt(width), (0, core, 0))
        placed_qk = lax.dynamic_update_slice(
            jnp.zeros((size, part), F32), out_pairs(grad_gain), (me, 0)
        )
        placed = jnp.concatenate(
            [
                placed_u.reshape(size, 2 * units),
                placed_v.reshape(size, 2 * units),
                placed_qk,
                grad_alpha_attn.reshape(size, part),
                grad_alpha_mlp.reshape(size, part),
            ],
            axis=1,
        )
        grad_hidden, owned, owned_output, owned_qkv, summed = sum_all(
            term,
            grads,
            grad_wo.reshape(size, chips, 2, rows, part),
            grad_qkv.reshape(chips, 2, rows, 3 * part),
            placed[:, None],
            chips,
            5,
        )
        owned_upward, owned_gating, owned_downward = owned[0], owned[1], owned[2].T
        owned_output = owned_output.T
        owned_query = out_pairs(owned_qkv[:, :part])
        owned_keys = out_pairs(owned_qkv[:, part : 2 * part])
        owned_values = owned_qkv[:, 2 * part :]
        bounds = [2 * units, 4 * units, 4 * units + part, 4 * units + 2 * part]
        summed_up, summed_gate, summed_qk, summed_attn, summed_mlp = jnp.split(
            summed[0], bounds
        )
        return (
            out_hidden[None],
            grad_hidden[None],
            owned_query,
            owned_keys,
            owned_values,
            owned_output,
            owned_upward,
            owned_gating,
            owned_downward,
            summed_qk,
            summed_up,
            summed_gate,
            summed_attn,
            summed_mlp,
        )

    return on_device


def solution(mesh):
    rows, size = mesh.shape["dp"], mesh.shape["mp"]
    paired = Mesh(mesh.devices.reshape(rows // 2, 2, size), ("chip", "core", "mp"))
    return jax.shard_map(
        make_on_device(rows // 2, size),
        mesh=paired,
        in_specs=(
            P(DP, None, "mp"),
            P(DP, "mp"),
            P(DP, "mp"),
            P(DP, "mp"),
            P("mp", DP),
            P(DP, "mp"),
            P(DP, "mp"),
            P("mp", DP),
            P("mp"),
            P("mp"),
            P("mp"),
            P("mp"),
            P("mp"),
            P(DP, None),
            P(DP, None),
            P(DP, None, "mp"),
        ),
        out_specs=(
            P(DP, None, "mp"),
            P(DP, None, "mp"),
            P(DP, "mp"),
            P(DP, "mp"),
            P(DP, "mp"),
            P("mp", DP),
            P(DP, "mp"),
            P(DP, "mp"),
            P("mp", DP),
            P("mp"),
            P("mp"),
            P("mp"),
            P("mp"),
            P("mp"),
        ),
        check_vma=False,
    )
```

```python
import functools
import math

import jax
import jax.numpy as jnp
import numpy as np
from jax import lax
from jax.experimental import pallas as pl
from jax.experimental.pallas import tpu as pltpu
from jax.sharding import Mesh
from jax.sharding import PartitionSpec as P

DK = 64
HALF = DK // 2
EXT = 128
EPSILON = 1e-06
ROPE_BASE = 10000.0
VMEM_LIMIT = 60 * 1024 * 1024
F32 = jnp.float32
BF16 = jnp.bfloat16
DP = ("chip", "core")


def dot(left, right, dims=((1,), (0,)), precision=None):
    return lax.dot_general(
        left, right, (dims, ((), ())), precision=precision, preferred_element_type=F32
    )


NT = ((1,), (1,))
TN = ((0,), (0,))


def grid_params(dims):
    return pltpu.CompilerParams(
        dimension_semantics=("arbitrary",) * dims, vmem_limit_bytes=VMEM_LIMIT
    )


ANY = pl.BlockSpec(memory_space=pl.ANY)


def remote_params(collective, **more):
    return pltpu.CompilerParams(
        collective_id=collective,
        has_side_effects=True,
        vmem_limit_bytes=VMEM_LIMIT,
        **more,
    )


def to_device(source, target, send, receive, where):
    return pltpu.make_async_remote_copy(
        src_ref=source,
        dst_ref=target,
        send_sem=send,
        recv_sem=receive,
        device_id=where,
        device_id_type=pl.DeviceIdType.MESH,
    )


def to_member(source, target, send, receive, member):
    return to_device(source, target, send, receive, {"mp": member})


def flip(index, mask):
    bit = 1
    while bit <= mask:
        if mask & bit:
            index = index + bit - 2 * bit * lax.rem(lax.div(index, bit), 2)
        bit *= 2
    return index


def bits_below(count):
    return [1 << k for k in range(count.bit_length() - 1)]


def greet(where):
    pl.semaphore_signal(
        pltpu.get_barrier_semaphore(),
        inc=1,
        device_id=where,
        device_id_type=pl.DeviceIdType.MESH,
    )


def greet_all(size):
    me = lax.axis_index("mp")
    for k in range(1, size):
        greet({"mp": flip(me, k)})
    pl.semaphore_wait(pltpu.get_barrier_semaphore(), size - 1)


def greet_around(size, chips):
    me, chip, core = (lax.axis_index(name) for name in ("mp", "chip", "core"))
    for k in range(1, size):
        greet({"mp": flip(me, k)})
    for bit in bits_below(chips):
        greet({"chip": flip(chip, bit)})
    greet({"core": 1 - core})
    pl.semaphore_wait(pltpu.get_barrier_semaphore(), size + len(bits_below(chips)))


class Exchange:
    def __init__(self, size, source, target, piece, place, send, receive, local):
        me = lax.axis_index("mp")
        self.local = pltpu.make_async_copy(piece(source, me), place(target, me), local)
        self.remote = [
            to_member(
                piece(source, flip(me, k)),
                place(target, me),
                send.at[k],
                receive.at[k],
                flip(me, k),
            )
            for k in range(1, size)
        ]

    def start(self):
        for copy in self.remote:
            copy.start()
        self.local.start()

    def wait(self):
        self.local.wait()
        for copy in self.remote:
            copy.wait()


def exchange_semaphores(size):
    return [
        pltpu.SemaphoreType.DMA((size,)),
        pltpu.SemaphoreType.DMA((size,)),
        pltpu.SemaphoreType.DMA,
    ]


def row_part(rows):
    return lambda ref, j: ref.at[pl.ds(pl.multiple_of(j * rows, rows), rows), :]


def column_part(columns):
    return lambda ref, j: ref.at[:, pl.ds(pl.multiple_of(j * columns, columns), columns)]


class Gather:
    def __init__(self, block, index, bits, where, send, receive):
        self.block, self.index, self.bits, self.where = block, index, bits, where
        self.send, self.receive = send, receive

    def copies(self, stage, incoming):
        span = [0]
        for bit in self.bits[:stage]:
            span += [held | bit for held in span]
        bit = self.bits[stage]
        for order, held in enumerate(span):
            ref = self.block(flip(self.index, held | bit if incoming else held))
            slot = (1 << stage) - 1 + order
            yield to_device(
                ref,
                ref,
                self.send(slot),
                self.receive(slot),
                self.where(flip(self.index, bit)),
            )

    def start(self, stage):
        if stage < len(self.bits):
            for copy in self.copies(stage, False):
                copy.start()

    def arrive(self, stage):
        if stage < len(self.bits):
            for copy in self.copies(stage, True):
                copy.wait_recv()

    def close(self):
        for stage in range(len(self.bits)):
            for copy in self.copies(stage, False):
                copy.wait_send()


def gather_all_kernel(
    size,
    chips,
    chunks,
    split,
    hidden,
    qkv,
    packed,
    vectors,
    wide,
    full_qkv,
    full,
    full_vectors,
    local,
    hidden_up,
    hidden_down,
    hidden_got,
    packed_up,
    packed_down,
    packed_got,
    plane_sent,
    plane_got,
    qkv_sent,
    qkv_got,
    vector_sent,
    vector_got,
):
    me, chip, core = (lax.axis_index(name) for name in ("mp", "chip", "core"))
    tokens = hidden.shape[0]
    rows = tokens // chunks
    height = packed.shape[0]
    owner = chip * 2 + core
    bits = bits_below(chips)
    stages = len(bits)
    greet_around(size, chips)

    own = [
        pltpu.make_async_copy(qkv, full_qkv.at[owner], local.at[0]),
        pltpu.make_async_copy(packed, full.at[me, chip], local.at[1]),
        pltpu.make_async_copy(vectors, full_vectors.at[me], local.at[2]),
        pltpu.make_async_copy(hidden, wide.at[me], local.at[3]),
    ]
    for copy in own:
        copy.start()

    def hidden_hop(origin, chunk, ref, member, send):
        at = pl.ds(chunk * rows, rows)
        return to_member(
            ref.at[at, :],
            wide.at[origin, at, :],
            send.at[origin, chunk],
            hidden_got.at[origin, chunk],
            member,
        )

    def packed_hop(origin, ref, member, send):
        return to_member(
            ref, full.at[origin, chip], send.at[origin], packed_got.at[origin], member
        )

    vector_copies = [
        to_member(
            vectors, full_vectors.at[me], vector_sent.at[k], vector_got.at[k], flip(me, k)
        )
        for k in range(1, size)
    ]

    def plane(origin, slot):
        return [
            Gather(
                lambda i, at=at: full.at[origin, i, at, :],
                chip,
                order,
                lambda i: {"chip": i},
                lambda k, half=half: plane_sent.at[slot, half, k],
                lambda k, half=half: plane_got.at[slot, half, k],
            )
            for half, (at, order) in enumerate(
                (
                    (pl.ds(0, split), bits),
                    (pl.ds(split, height - split), bits[::-1]),
                )
            )
        ]

    gather_qkv = Gather(
        lambda i: full_qkv.at[i],
        owner,
        [2 * bit for bit in bits] + [1],
        lambda i: {"chip": lax.div(i, 2), "core": lax.rem(i, 2)},
        lambda k: qkv_sent.at[k],
        lambda k: qkv_got.at[k],
    )

    sources = {0: [(me >= 0, me, 0, None)]}
    for distance in range(1, size):
        sources[distance] = [
            (me >= distance, me - distance, 2 * distance - 1, True),
            (me + distance < size, me + distance, 2 * distance, False),
        ]

    own[0].wait()
    own[1].wait()

    def pass_on(origin, upward):
        block = full.at[origin, chip]
        if upward is not False:

            @pl.when(me < size - 1)
            def _():
                packed_hop(origin, block, me + 1, packed_up).start()

        if not upward:

            @pl.when(me > 0)
            def _():
                packed_hop(origin, block, me - 1, packed_down).start()

    def advance(distance, stage):
        for exists, origin, slot, _ in sources[distance]:

            @pl.when(exists)
            def _():
                for half in plane(origin, slot):
                    half.arrive(stage)
                    half.start(stage + 1)

    pass_on(me, None)
    gather_qkv.start(0)
    for half in plane(me, 0):
        half.start(0)
    for copy in vector_copies:
        copy.start()
    for stage in range(stages):
        gather_qkv.arrive(stage)
        gather_qkv.start(stage + 1)
    advance(0, 0)
    for distance in range(1, size):
        for exists, origin, slot, upward in sources[distance]:

            @pl.when(exists)
            def _():
                packed_hop(origin, full.at[origin, chip], me, packed_up).wait_recv()
                pass_on(origin, upward)
                for half in plane(origin, slot):
                    half.start(0)

        @pl.when(jnp.maximum(me, size - 1 - me) == distance)
        def _():
            for chunk in range(chunks):

                @pl.when(me < size - 1)
                def _():
                    hidden_hop(me, chunk, hidden, me + 1, hidden_up).start()

                @pl.when(me > 0)
                def _():
                    hidden_hop(me, chunk, hidden, me - 1, hidden_down).start()

        if distance > 1:
            advance(distance - 1, 0)
    advance(size - 1, 0)
    for distance in range(1, size):
        for chunk in range(chunks):
            for exists, origin, _, upward in sources[distance]:

                @pl.when(exists)
                def _():
                    block = wide.at[origin]
                    hidden_hop(origin, chunk, block, me, hidden_up).wait_recv()
                    if upward:

                        @pl.when(me < size - 1)
                        def _():
                            hidden_hop(origin, chunk, block, me + 1, hidden_up).start()
                    else:

                        @pl.when(me > 0)
                        def _():
                            hidden_hop(origin, chunk, block, me - 1, hidden_down).start()

    for stage in range(1, stages):
        for distance in range(size):
            advance(distance, stage)
    gather_qkv.arrive(stages)

    own[2].wait()
    own[3].wait()
    for copy in vector_copies:
        copy.wait()
    gather_qkv.close()
    for distance in range(size):
        for exists, origin, slot, upward in sources[distance]:

            @pl.when(exists)
            def _():
                for half in plane(origin, slot):
                    half.close()
                block = full.at[origin, chip]
                if upward is not False:

                    @pl.when(me < size - 1)
                    def _():
                        packed_hop(origin, block, me, packed_up).wait_send()
                        for chunk in range(chunks):
                            hidden_hop(origin, chunk, wide.at[origin], me, hidden_up).wait_send()

                if not upward:

                    @pl.when(me > 0)
                    def _():
                        packed_hop(origin, block, me, packed_down).wait_send()
                        for chunk in range(chunks):
                            hidden_hop(
                                origin, chunk, wide.at[origin], me, hidden_down
                            ).wait_send()


def gather_all(hidden, qkv, packed, vectors, size, chips, collective):
    chunks = 6
    height = packed.shape[0]
    dma = pltpu.SemaphoreType.DMA
    line = dma((size, chunks))
    plane = dma((2 * size - 1, 2, max(chips - 1, 1)))
    return pl.pallas_call(
        functools.partial(gather_all_kernel, size, chips, chunks, height // 32 * 16),
        in_specs=[ANY] * 4,
        out_specs=[ANY] * 4,
        out_shape=[
            jax.ShapeDtypeStruct((size, *hidden.shape), BF16),
            jax.ShapeDtypeStruct((2 * chips, *qkv.shape), BF16),
            jax.ShapeDtypeStruct((size, chips, *packed.shape), BF16),
            jax.ShapeDtypeStruct((size, *vectors.shape), F32),
        ],
        scratch_shapes=[
            dma((4,)),
            line,
            line,
            line,
            dma((size,)),
            dma((size,)),
            dma((size,)),
            plane,
            plane,
            dma((2 * chips - 1,)),
            dma((2 * chips - 1,)),
            dma((size,)),
            dma((size,)),
        ],
        compiler_params=remote_params(collective),
        name="gather_all",
    )(hidden, qkv, packed, vectors)


class LineSum:
    def __init__(self, size, chunks, term, up, down, sems):
        self.size, self.chunks = size, chunks
        self.term, self.up, self.down = term, up, down
        self.sent_up, self.sent_down, self.got_up, self.got_down = sems
        self.me = lax.axis_index("mp")
        self.rows = up.shape[1] // chunks

    def at(self, chunk):
        return pl.ds(chunk * self.rows, self.rows)

    def hop(self, upward, goal, chunk, member):
        slots = self.up if upward else self.down
        send = self.sent_up if upward else self.sent_down
        receive = self.got_up if upward else self.got_down
        ref = slots.at[goal, self.at(chunk), :]
        return to_member(ref, ref, send.at[goal, chunk], receive.at[goal, chunk], member)

    def step(self, order, chunk):
        me, last, at = self.me, self.size - 1, self.at(chunk)
        for upward, goal, ahead, first, member in (
            (True, last - order, me < last - order, me == 0, me + 1),
            (False, order, me > order, me == last, me - 1),
        ):
            slots = self.up if upward else self.down

            @pl.when(ahead & first)
            def _():
                slots[goal, at, :] = self.term(goal, at)

            @pl.when(ahead & jnp.logical_not(first))
            def _():
                self.hop(upward, goal, chunk, me).wait_recv()
                slots[goal, at, :] = (
                    slots[goal, at, :].astype(F32) + self.term(goal, at).astype(F32)
                ).astype(BF16)

            @pl.when(ahead)
            def _():
                self.hop(upward, goal, chunk, member).start()

    def result(self, chunk, out, out_at):
        me, at = self.me, self.at(chunk)
        out[out_at, :] = self.term(me, at).astype(F32)

        @pl.when(me > 0)
        def _():
            self.hop(True, me, chunk, me).wait_recv()
            out[out_at, :] += self.up[me, at, :].astype(F32)

        @pl.when(me < self.size - 1)
        def _():
            self.hop(False, me, chunk, me).wait_recv()
            out[out_at, :] += self.down[me, at, :].astype(F32)

    def close(self):
        for order in range(self.size - 1):
            for chunk in range(self.chunks):

                @pl.when(self.me < self.size - 1 - order)
                def _():
                    self.hop(True, self.size - 1 - order, chunk, self.me).wait_send()

                @pl.when(self.me > order)
                def _():
                    self.hop(False, order, chunk, self.me).wait_send()


class ChipSum:
    def __init__(self, layers, bits, source, acc, got, load, send, receive):
        self.layers, self.bits = layers, bits
        self.acc, self.got, self.chip = acc, got, lax.axis_index("chip")
        self.half = 1 << (len(bits) - 1)
        self.load = [
            pltpu.make_async_copy(
                source(layer, flip(self.chip, self.combo(slot))),
                acc.at[layer, slot],
                load.at[layer, slot],
            )
            for layer in range(layers)
            for slot in range(self.half)
        ]
        self.source, self.sent, self.received = source, send, receive

    def combo(self, slot):
        count = len(self.bits)
        return sum(self.bits[count - 1 - j] for j in range(count - 1) if slot >> j & 1)

    def copies(self, stage):
        count = self.half >> stage
        offset = 2 * self.half - 2 * count
        where = {"chip": flip(self.chip, self.bits[stage])}
        for layer in range(self.layers):
            for slot in range(count):
                if stage == 0:
                    other = flip(self.chip, self.bits[0] | self.combo(slot))
                    ref = self.source(layer, other)
                else:
                    ref = self.acc.at[layer, count + slot]
                at = offset + slot
                yield layer, slot, at, to_device(
                    ref,
                    self.got.at[layer, at],
                    self.sent.at[layer, at],
                    self.received.at[layer, at],
                    where,
                )

    def start(self, stage):
        if stage == 0:
            for copy in self.load:
                copy.start()
        for _, _, _, copy in self.copies(stage):
            copy.start()

    def add(self, stage):
        if stage == 0:
            for copy in self.load:
                copy.wait()
        for layer, slot, at, copy in self.copies(stage):
            copy.wait_recv()
            self.acc[layer, slot] = (
                self.acc[layer, slot].astype(F32) + self.got[layer, at].astype(F32)
            ).astype(BF16)

    def close(self):
        for stage in range(len(self.bits)):
            for _, _, _, copy in self.copies(stage):
                copy.wait_send()


def sum_all_kernel(
    size,
    chips,
    chunks,
    split,
    term,
    grads,
    grad_wo,
    grad_qkv,
    vectors,
    out,
    owned,
    owned_wo,
    owned_qkv,
    owned_vectors,
    term_up,
    term_down,
    acc_a,
    got_a,
    up_a,
    down_a,
    acc_b,
    got_b,
    up_b,
    down_b,
    pair_wo,
    other_wo,
    acc_wo,
    got_wo,
    up_wo,
    down_wo,
    pair_qkv,
    other_qkv,
    acc_qkv,
    got_qkv,
    whole,
    vector_sum,
    vector_got,
    vector_line,
    local,
    core_sent,
    core_got,
    vector_sent,
    vector_received,
    term_sems,
    line_sems,
    load_sems,
    chip_sent,
    chip_got,
):
    me, chip, core = (lax.axis_index(name) for name in ("mp", "chip", "core"))
    bits = bits_below(chips)
    stages = len(bits)
    greet_around(size, chips)
    other_core_is = {"core": 1 - core}

    def sems(ref, which):
        return [ref.at[which, k] for k in range(4)]

    line = LineSum(
        size, chunks, lambda goal, at: term[goal, at, :], term_up, term_down, sems(term_sems, 0)
    )
    sum_a = ChipSum(
        size,
        bits,
        lambda m, c: grads.at[m, c, pl.ds(0, split), :],
        acc_a,
        got_a,
        load_sems.at[0],
        chip_sent.at[0],
        chip_got.at[0],
    )
    sum_b = ChipSum(
        size,
        bits[::-1],
        lambda m, c: grads.at[m, c, pl.ds(split, grads.shape[2] - split), :],
        acc_b,
        got_b,
        load_sems.at[1],
        chip_sent.at[1],
        chip_got.at[1],
    )
    sum_wo = ChipSum(
        size,
        bits[::-1],
        lambda m, c: pair_wo.at[m, c],
        acc_wo,
        got_wo,
        load_sems.at[2],
        chip_sent.at[2],
        chip_got.at[2],
    )
    sum_qkv = ChipSum(
        1,
        bits,
        lambda m, c: pair_qkv.at[c],
        acc_qkv,
        got_qkv,
        load_sems.at[3],
        chip_sent.at[3],
        chip_got.at[3],
    )
    lines = [
        LineSum(
            size,
            1,
            lambda goal, at, acc=acc: acc[goal, 0, at, :],
            up,
            down,
            sems(line_sems, which),
        )
        for which, (acc, up, down) in enumerate(
            ((acc_a, up_a, down_a), (acc_b, up_b, down_b), (acc_wo, up_wo, down_wo))
        )
    ]

    own = [
        pltpu.make_async_copy(grad_wo.at[:, :, core], pair_wo, local.at[0]),
        pltpu.make_async_copy(grad_qkv.at[:, core], pair_qkv, local.at[1]),
    ]
    given = [
        to_device(
            grad_wo.at[:, :, 1 - core], other_wo, core_sent.at[0], core_got.at[0], other_core_is
        ),
        to_device(
            grad_qkv.at[:, 1 - core], other_qkv, core_sent.at[1], core_got.at[1], other_core_is
        ),
    ]
    vector_copies = [
        to_member(
            vectors.at[flip(me, k)],
            vector_line.at[k],
            vector_sent.at[k],
            vector_received.at[k],
            flip(me, k),
        )
        for k in range(1, size)
    ]
    for copy in own + given:
        copy.start()
    sum_a.start(0)
    sum_b.start(0)
    for copy in vector_copies:
        copy.start()

    owner = chip * 2 + core
    vector_bits = [1] + [2 * bit for bit in bits]

    def vector_copy(stage):
        partner = flip(owner, vector_bits[stage])
        return to_device(
            vector_sum.at[stage],
            vector_got.at[stage],
            vector_sent.at[size + stage],
            vector_received.at[size + stage],
            {"chip": lax.div(partner, 2), "core": lax.rem(partner, 2)},
        )

    def vector_step(stage):
        if stage == 0:
            total = vectors[me]
            for k, copy in enumerate(vector_copies):
                copy.wait_recv()
                total = total + vector_line[k + 1]
            vector_sum[0] = total
        else:
            vector_copy(stage - 1).wait_recv()
            vector_sum[stage] = vector_sum[stage - 1] + vector_got[stage - 1]
        if stage < len(vector_bits):
            vector_copy(stage).start()

    for chunk in range(chunks):
        line.step(0, chunk)
    for copy in own:
        copy.wait()
    for copy in given:
        copy.wait_recv()
    pair_wo[...] = (pair_wo[...].astype(F32) + other_wo[...].astype(F32)).astype(BF16)
    pair_qkv[...] = (pair_qkv[...].astype(F32) + other_qkv[...].astype(F32)).astype(BF16)
    sum_wo.start(0)
    sum_qkv.start(0)
    vector_step(0)
    vector_step(1)
    for order in range(1, size - 1):
        for chunk in range(chunks):
            line.step(order, chunk)
        if order - 1 < stages:
            for part in (sum_a, sum_b, sum_wo, sum_qkv):
                part.add(order - 1)
                if order < stages:
                    part.start(order)
    for stage in range(size - 2, stages):
        for part in (sum_a, sum_b, sum_wo, sum_qkv):
            part.add(stage)
            if stage + 1 < stages:
                part.start(stage + 1)
    lines[0].step(0, 0)
    lines[1].step(0, 0)
    lines[2].step(0, 0)
    for stage in range(2, len(vector_bits) + 1):
        vector_step(stage)
    for chunk in range(chunks):
        line.result(chunk, out, line.at(chunk))
    for order in range(1, size - 1):
        for part in lines:
            part.step(order, 0)
    owned_vectors[...] = vector_sum[len(vector_bits)]
    owned_qkv[...] = acc_qkv[0, 0].astype(F32)
    lines[0].result(0, whole, pl.ds(0, split))
    lines[1].result(0, whole, pl.ds(split, whole.shape[0] - split))
    lines[2].result(0, owned_wo, slice(None))

    matrices, rows, columns = owned.shape
    columns = columns // 2
    place = pl.ds(pl.multiple_of(core * columns, columns), columns)
    swaps = []
    for matrix in range(matrices):
        mine = pl.ds(pl.multiple_of((2 * matrix + core) * rows, rows), rows)
        theirs = pl.ds(pl.multiple_of((2 * matrix + 1 - core) * rows, rows), rows)
        swaps.append(
            to_device(
                whole.at[theirs, :],
                owned.at[matrix, :, place],
                core_sent.at[2 + matrix],
                core_got.at[2 + matrix],
                other_core_is,
            )
        )
        swaps[-1].start()
        copy = pltpu.make_async_copy(
            whole.at[mine, :], owned.at[matrix, :, place], local.at[2 + matrix]
        )
        copy.start()
        swaps.append(copy)
    for copy in swaps:
        copy.wait()

    for copy in given + vector_copies:
        copy.wait_send()
    for stage in range(len(vector_bits)):
        vector_copy(stage).wait_send()
    for part in (sum_a, sum_b, sum_wo, sum_qkv):
        part.close()
    line.close()
    for part in lines:
        part.close()


def sum_all(term, grads, grad_wo, grad_qkv, vectors, chips, collective):
    size, tokens, part = term.shape
    height, units = grads.shape[2:]
    rows = height // 6
    chunks = 6
    split = height // 32 * 16
    half, blocks = max(chips // 2, 1), max(chips - 1, 1)
    stages = chips.bit_length()
    dma = pltpu.SemaphoreType.DMA
    vmem = pl.BlockSpec(memory_space=pltpu.VMEM)
    wo_block, qkv_block = grad_wo.shape[3:], grad_qkv.shape[2:]
    long = vectors.shape[1:]

    def sums(layers, block):
        return [
            pltpu.VMEM((layers, half, *block), BF16),
            pltpu.VMEM((layers, blocks, *block), BF16),
        ]

    def line(block):
        return [pltpu.VMEM((size, *block), BF16)] * 2

    return pl.pallas_call(
        functools.partial(sum_all_kernel, size, chips, chunks, split),
        in_specs=[vmem, ANY, ANY, ANY, vmem],
        out_specs=[vmem] * 5,
        out_shape=[
            jax.ShapeDtypeStruct((tokens, part), F32),
            jax.ShapeDtypeStruct((3, rows, 2 * units), F32),
            jax.ShapeDtypeStruct(wo_block, F32),
            jax.ShapeDtypeStruct(qkv_block, F32),
            jax.ShapeDtypeStruct(long, F32),
        ],
        scratch_shapes=[
            *line((tokens, part)),
            *sums(size, (split, units)),
            *line((split, units)),
            *sums(size, (height - split, units)),
            *line((height - split, units)),
            pltpu.VMEM((size, chips, *wo_block), BF16),
            pltpu.VMEM((size, chips, *wo_block), BF16),
            *sums(size, wo_block),
            *line(wo_block),
            pltpu.VMEM((chips, *qkv_block), BF16),
            pltpu.VMEM((chips, *qkv_block), BF16),
            *sums(1, qkv_block),
            pltpu.VMEM((height, units), F32),
            pltpu.VMEM((stages + 1, *long), F32),
            pltpu.VMEM((stages + 1, *long), F32),
            pltpu.VMEM((size, *long), F32),
            dma((5,)),
            dma((5,)),
            dma((5,)),
            dma((size + stages,)),
            dma((size + stages,)),
            dma((1, 4, size, chunks)),
            dma((3, 4, size, 1)),
            dma((4, size, half)),
            dma((4, size, blocks)),
            dma((4, size, blocks)),
        ],
        compiler_params=remote_params(collective),
        name="sum_all",
    )(term, grads, grad_wo, grad_qkv, vectors)


def paired_place(heads):
    head, feature = np.divmod(np.arange(heads * DK), DK)
    return (feature // HALF) * (heads * HALF) + head * HALF + feature % HALF


def placing_matrix(place, heads):
    head, feature = np.divmod(np.arange(heads * DK), DK)
    matrix = np.zeros((heads * DK, heads * EXT), np.float32)
    matrix[place, head * EXT + feature] = 1
    return matrix


def head_sum_matrix(heads):
    lane = np.arange(heads * HALF) // HALF
    return (lane[:, None] == lane[None, :]).astype(np.float32)


def project_kernel(
    wide, weight, cosine, sine, gain, place_pair, place_plain, sums, q, k, v, rq, rk
):
    parts = wide.shape[0]
    heads = q.shape[0]
    pair = heads * HALF
    width = heads * DK
    raw = dot(wide[0], weight[0])
    for part in range(1, parts):
        raw += dot(wide[part], weight[part])
    rows = raw.shape[0]
    lane = lax.broadcasted_iota(jnp.int32, (rows, EXT), 1)
    cos = cosine[...]
    sin = sine[...]
    gain_first = gain[:, :pair]
    gain_second = gain[:, pair:]
    for offset, out, scale_out, factor in ((0, q, rq, math.sqrt(DK)), (width, k, rk, 1.0)):
        first = raw[:, offset : offset + pair]
        second = raw[:, offset + pair : offset + width]
        turned_first = first * cos - second * sin
        turned_second = second * cos + first * sin
        total = dot(
            turned_first * turned_first + turned_second * turned_second,
            sums[...],
            precision=lax.Precision.HIGHEST,
        )
        scale = lax.rsqrt(total + EPSILON)
        scale_out[...] = scale
        both = jnp.concatenate(
            [turned_first * scale * gain_first, turned_second * scale * gain_second], axis=1
        ).astype(BF16)
        padded = dot(both, place_pair[...]) * factor
        for head in range(heads):
            piece = padded[:, head * EXT : (head + 1) * EXT]
            if factor == 1.0:
                piece = jnp.where(lane < DK, piece, 1.0)
            out[head] = piece.astype(BF16)
    padded = dot(raw[:, 2 * width :].astype(BF16), place_plain[...])
    for head in range(heads):
        piece = padded[:, head * EXT : (head + 1) * EXT]
        v[head] = jnp.where(lane < DK, piece, 1.0).astype(BF16)


def project(wide, weight, cosine, sine, gain, place_pair, place_plain, sums):
    parts, tokens, part = wide.shape
    width = gain.shape[1]
    heads = width // DK
    block = min(512, tokens)
    padded = jax.ShapeDtypeStruct((heads, tokens, EXT), BF16)
    scale = jax.ShapeDtypeStruct((tokens, heads * HALF), F32)

    def whole(array):
        return pl.BlockSpec(array.shape, lambda i: (0,) * array.ndim)

    rows = pl.BlockSpec((block, heads * HALF), lambda i: (i, 0))
    headed = pl.BlockSpec((heads, block, EXT), lambda i: (0, i, 0))
    return pl.pallas_call(
        project_kernel,
        grid=(tokens // block,),
        in_specs=[
            pl.BlockSpec((parts, block, part), lambda i: (0, i, 0)),
            whole(weight),
            rows,
            rows,
            whole(gain),
            whole(place_pair),
            whole(place_plain),
            whole(sums),
        ],
        out_specs=[headed, headed, headed, rows, rows],
        out_shape=[padded, padded, padded, scale, scale],
        compiler_params=grid_params(1),
        cost_estimate=pl.CostEstimate(
            flops=2 * tokens * parts * part * width * 3,
            bytes_accessed=20 << 20,
            transcendentals=0,
        ),
        name="project",
    )(wide, weight, cosine, sine, gain, place_pair, place_plain, sums)


def split_three(value):
    high = value.astype(BF16).astype(F32)
    rest = value - high
    middle = rest.astype(BF16).astype(F32)
    return high, middle, rest - middle


def attend_kernel(low, q, k, v, qdoc, kdoc, collect, attended, qback, acc):
    heads, rows, _ = q.shape
    block = kdoc.shape[2]
    index = pl.program_id(0)
    acc[...] = jnp.zeros_like(acc)

    def step(j, diagonal):
        slots = pl.ds(pl.multiple_of(j * block, block), block)
        mask = qdoc[...] == kdoc[j]
        if diagonal:
            row = lax.broadcasted_iota(jnp.int32, (rows, block), 0)
            column = lax.broadcasted_iota(jnp.int32, (rows, block), 1)
            mask = (mask & (column < row)) | (column == row)
        for head in range(heads):
            scores = dot(q[head], k[head, slots, :], NT)
            weight = jnp.where(mask, jnp.exp(scores), 0.0).astype(BF16)
            acc[head] += dot(weight, v[head, slots, :])

    def earlier(j, carry):
        step(j, False)
        return carry

    lax.fori_loop(low[index], index, earlier, 0)
    step(index, True)

    lane = lax.broadcasted_iota(jnp.int32, (rows, EXT), 1)
    merged = jnp.zeros((rows, heads * DK), F32)
    for head in range(heads):
        both = acc[head]
        total = pltpu.roll(both, DK, 1)
        output = jnp.where(lane < DK, both / total, 0.0).astype(BF16)
        merged += dot(output, collect[head])
        high, middle, rest = split_three(-jnp.log(both))
        qback[head] = jnp.where(
            lane < DK,
            q[head].astype(F32),
            jnp.where(
                lane == DK,
                high,
                jnp.where(lane == DK + 1, middle, jnp.where(lane == DK + 2, rest, 0.0)),
            ),
        ).astype(BF16)
    attended[...] = merged.astype(BF16)


def attend(low, q, k, v, qdoc, kdoc, collect):
    heads, tokens, _ = q.shape
    block = kdoc.shape[2]
    width = heads * DK

    def whole(array):
        return pl.BlockSpec(array.shape, lambda i, low: (0,) * array.ndim)

    headed = pl.BlockSpec((heads, block, EXT), lambda i, low: (0, i, 0))
    return pl.pallas_call(
        attend_kernel,
        grid_spec=pltpu.PrefetchScalarGridSpec(
            num_scalar_prefetch=1,
            grid=(tokens // block,),
            in_specs=[
                headed,
                whole(k),
                whole(v),
                pl.BlockSpec((block, 1), lambda i, low: (i, 0)),
                whole(kdoc),
                whole(collect),
            ],
            out_specs=[pl.BlockSpec((block, width), lambda i, low: (i, 0)), headed],
            scratch_shapes=[pltpu.VMEM((heads, block, EXT), F32)],
        ),
        out_shape=[
            jax.ShapeDtypeStruct((tokens, width), BF16),
            jax.ShapeDtypeStruct((heads, tokens, EXT), BF16),
        ],
        compiler_params=grid_params(1),
        cost_estimate=pl.CostEstimate(
            flops=40_000_000_000, bytes_accessed=16 << 20, transcendentals=0
        ),
        name="attend",
    )(low, q, k, v, qdoc, kdoc, collect)


def gather_heads(padded, matrix, heads):
    total = None
    for head in range(heads):
        value = padded[head]
        high = value.astype(BF16)
        rest = (value - high.astype(F32)).astype(BF16)
        term = dot(high, matrix[head]) + dot(rest, matrix[head])
        total = term if total is None else total + term
    return total


def unrope(grad, unit, gain, scale, cos, sin, sums):
    pair = cos.shape[1]
    grad_gain = jnp.sum(grad * unit, axis=0, keepdims=True)
    dy = grad * gain
    prod = dy * unit
    total = dot(prod[:, :pair] + prod[:, pair:], sums, precision=lax.Precision.HIGHEST)
    first = scale * (dy[:, :pair] - unit[:, :pair] * total)
    second = scale * (dy[:, pair:] - unit[:, pair:] * total)
    raw = jnp.concatenate([first * cos + second * sin, second * cos - first * sin], axis=1)
    return raw.astype(BF16), grad_gain


def attend_back_kernel(
    low,
    qback,
    dout,
    attended,
    k,
    v,
    qdoc,
    kdoc,
    cosine,
    sine,
    rq,
    rk,
    gain,
    weight,
    place_plain,
    collect_plain,
    collect_pair,
    sums,
    wide,
    grad_resid,
    term_out,
    grad_qkv,
    gain_out,
    dk,
    dv,
    dq,
    dox,
    dq_low,
    total_qkv,
):
    heads, rows, _ = qback.shape
    steps = pl.num_programs(0) // 2
    step_at = pl.program_id(0)
    width = heads * DK
    scale = math.sqrt(DK)

    @pl.when(step_at == 0)
    def _():
        dk[...] = jnp.zeros_like(dk)
        dv[...] = jnp.zeros_like(dv)
        gain_out[...] = jnp.zeros_like(gain_out)

    @pl.when(step_at < steps)
    def _():
        index = step_at
        lane = lax.broadcasted_iota(jnp.int32, (rows, EXT), 1)
        spread_grad = dot(dout[...], place_plain[...])
        spread_out = dot(attended[...], place_plain[...])
        for head in range(heads):
            piece = spread_grad[:, head * EXT : (head + 1) * EXT]
            other = spread_out[:, head * EXT : (head + 1) * EXT]
            delta = jnp.sum(piece * other, axis=1, keepdims=True)
            high, middle, rest = split_three(-delta)
            dox[head] = jnp.where(
                lane < DK,
                piece,
                jnp.where(
                    lane == DK,
                    high,
                    jnp.where(lane == DK + 1, middle, jnp.where(lane == DK + 2, rest, 0.0)),
                ),
            ).astype(BF16)
        dq[...] = jnp.zeros_like(dq)

        def step(j, diagonal):
            slots = pl.ds(pl.multiple_of(j * rows, rows), rows)
            mask = kdoc[slots, :] == qdoc[0]
            if diagonal:
                key = lax.broadcasted_iota(jnp.int32, (rows, rows), 0)
                query = lax.broadcasted_iota(jnp.int32, (rows, rows), 1)
                mask = (mask & (key < query)) | (key == query)
            for head in range(heads):
                keys = k[head, slots, :]
                scores = dot(keys, qback[head], NT)
                probs = jnp.where(mask, jnp.exp(scores), 0.0)
                dv[head, slots, :] += dot(probs.astype(BF16), dox[head])
                dprobs = dot(v[head, slots, :], dox[head], NT)
                dscores = (probs * dprobs).astype(BF16)
                dk[head, slots, :] += dot(dscores, qback[head])
                dq[head] += dot(dscores, keys, TN)

        def earlier(j, carry):
            step(j, False)
            return carry

        lax.fori_loop(low[index], index, earlier, 0)
        step(index, True)

        grad = gather_heads(dq, collect_pair, heads) * scale
        query = dot(qback[0], collect_pair[0])
        for head in range(1, heads):
            query += dot(qback[head], collect_pair[head])
        unit = query * (1.0 / scale) / gain[...]
        raw, grad_gain = unrope(
            grad, unit, gain[...], rq[...], cosine[...], sine[...], sums[...]
        )
        gain_out[...] += grad_gain
        dq_low[pl.ds(pl.multiple_of(index * rows, rows), rows), :] = raw

    @pl.when(step_at >= steps)
    def _():
        index = step_at - steps
        slots = pl.ds(pl.multiple_of(index * rows, rows), rows)
        grad = gather_heads([dk[head, slots, :] for head in range(heads)], collect_pair, heads)
        keys = dot(k[0, slots, :], collect_pair[0])
        for head in range(1, heads):
            keys += dot(k[head, slots, :], collect_pair[head])
        raw, grad_gain = unrope(
            grad, keys / gain[...], gain[...], rk[...], cosine[...], sine[...], sums[...]
        )
        gain_out[...] += grad_gain
        dvalues = gather_heads(
            [dv[head, slots, :] for head in range(heads)], collect_plain, heads
        ).astype(BF16)
        together = jnp.concatenate([dq_low[slots, :], raw, dvalues], axis=1)
        parts, part = weight.shape[:2]
        for member in range(parts):
            term_out[member] = dot(together, weight[member], NT).astype(BF16)
            product = dot(wide[member], together, TN)

            @pl.when(index == 0)
            def _():
                total_qkv[member] = product

            @pl.when(index > 0)
            def _():
                total_qkv[member] += product

        strip = STRIP
        first = low[steps] * (grad_resid.shape[0] // strip)
        for half in range(rows // strip):
            number = index * (rows // strip) + half - first

            @pl.when((number >= 0) & (number < grad_resid.shape[0] // strip))
            def _():
                at = pl.ds(half * strip, strip)
                own = pl.ds(pl.multiple_of(number * strip, strip), strip)
                for member in range(parts):
                    term_out[member, at, :] = (
                        term_out[member, at, :].astype(F32)
                        + grad_resid[own, member * part : (member + 1) * part].astype(F32)
                    ).astype(BF16)

        @pl.when(index == steps - 1)
        def _():
            grad_qkv[...] = total_qkv[...].astype(BF16)


def attend_back(
    low,
    qback,
    dout,
    attended,
    k,
    v,
    qdoc,
    kdoc,
    cosine,
    sine,
    rq,
    rk,
    gain,
    weight,
    place_plain,
    collect_plain,
    collect_pair,
    sums,
    wide,
    grad_resid,
):
    heads, tokens, _ = k.shape
    block = qdoc.shape[2]
    width = heads * DK
    steps = tokens // block
    parts, part = weight.shape[:2]

    def whole(array):
        return pl.BlockSpec(array.shape, lambda i, low: (0,) * array.ndim)

    def now(i):
        return jnp.minimum(i, steps - 1)

    def after(i):
        return jnp.maximum(i - steps, 0)

    def both(i):
        return lax.rem(i, steps)

    def rows(columns, at):
        return pl.BlockSpec((block, columns), lambda i, low: (at(i), 0))

    return pl.pallas_call(
        attend_back_kernel,
        grid_spec=pltpu.PrefetchScalarGridSpec(
            num_scalar_prefetch=1,
            grid=(2 * steps,),
            in_specs=[
                pl.BlockSpec((heads, block, EXT), lambda i, low: (0, now(i), 0)),
                rows(width, now),
                rows(width, now),
                whole(k),
                whole(v),
                pl.BlockSpec((1, 1, block), lambda i, low: (now(i), 0, 0)),
                whole(kdoc),
                rows(width // 2, both),
                rows(width // 2, both),
                rows(width // 2, now),
                rows(width // 2, after),
                whole(gain),
                whole(weight),
                whole(place_plain),
                whole(collect_plain),
                whole(collect_pair),
                whole(sums),
                pl.BlockSpec((parts, block, part), lambda i, low: (0, after(i), 0)),
                whole(grad_resid),
            ],
            out_specs=[
                pl.BlockSpec((parts, block, part), lambda i, low: (0, after(i), 0)),
                pl.BlockSpec((parts, part, 3 * width), lambda i, low: (0, 0, 0)),
                pl.BlockSpec((1, width), lambda i, low: (0, 0)),
            ],
            scratch_shapes=[
                pltpu.VMEM((heads, tokens, EXT), F32),
                pltpu.VMEM((heads, tokens, EXT), F32),
                pltpu.VMEM((heads, block, EXT), F32),
                pltpu.VMEM((heads, block, EXT), BF16),
                pltpu.VMEM((tokens, width), BF16),
                pltpu.VMEM((parts, part, 3 * width), F32),
            ],
        ),
        out_shape=[
            jax.ShapeDtypeStruct((parts, tokens, part), BF16),
            jax.ShapeDtypeStruct((parts, part, 3 * width), BF16),
            jax.ShapeDtypeStruct((1, width), F32),
        ],
        compiler_params=grid_params(1),
        cost_estimate=pl.CostEstimate(
            flops=80_000_000_000, bytes_accessed=30 << 20, transcendentals=0
        ),
        name="attend_back",
    )(
        low,
        qback,
        dout,
        attended,
        k,
        v,
        qdoc,
        kdoc,
        cosine,
        sine,
        rq,
        rk,
        gain,
        weight,
        place_plain,
        collect_plain,
        collect_pair,
        sums,
        wide,
        grad_resid,
    )


def row_scale(value):
    return lax.rsqrt(jnp.sum(value * value, axis=-1, keepdims=True) + EPSILON)


def residual_backward(grad_out, result, resid, unit, alpha, branch_scale, mixed_scale):
    grad_mixed = mixed_scale * (
        grad_out - result * jnp.sum(grad_out * result, axis=-1, keepdims=True)
    )
    grad_alpha = jnp.sum(grad_mixed * (unit - resid), axis=0, keepdims=True)
    grad_unit = grad_mixed * alpha
    grad_branch = branch_scale * (
        grad_unit - unit * jnp.sum(grad_unit * unit, axis=-1, keepdims=True)
    )
    return grad_mixed * (1.0 - alpha), grad_branch, grad_alpha


STRIP = 256


def strips(rows):
    strip = min(STRIP, rows)
    return [pl.ds(start, strip) for start in range(0, rows, strip)]


def core_semaphores(count):
    return [pltpu.SemaphoreType.DMA((count,)), pltpu.SemaphoreType.DMA((count,))]


def greet_pair_and_line(size):
    me, core = lax.axis_index("mp"), lax.axis_index("core")
    for k in range(1, size):
        greet({"mp": flip(me, k)})
    greet({"core": 1 - core})
    pl.semaphore_wait(pltpu.get_barrier_semaphore(), size)


def output_matrix(packed_wo, whole):
    size, chips, rows, both = packed_wo.shape
    part = both // 2
    for chip in range(chips):
        for core in range(2):
            start = (2 * chip + core) * rows
            whole[:, start : start + rows, :] = packed_wo[
                :, chip, :, core * part : (core + 1) * part
            ]


def mix_kernel(
    size,
    attended,
    packed,
    wide,
    alpha,
    cotangent,
    x,
    middle_out,
    unit_out,
    branch_scale_out,
    mixed_scale_out,
    merged,
    full_wo,
    resid_out,
    cotangent_low,
    packed_wo,
    middle_low,
    resid,
    send,
    receive,
    local,
    own_sems,
    core_sent,
    core_got,
):
    me, core = lax.axis_index("mp"), lax.axis_index("core")
    mine, width = middle_out.shape
    part = width // size
    rows = packed_wo.shape[2]
    greet_pair_and_line(size)
    exchange = Exchange(
        size, attended, merged, row_part(mine), column_part(part), send, receive, local
    )
    exchange.start()
    own = [
        pltpu.make_async_copy(
            packed.at[:, :, pl.ds(packed.shape[2] - rows, rows), :], packed_wo, own_sems.at[0]
        )
    ]
    for member in range(size):
        own.append(
            pltpu.make_async_copy(
                wide.at[member, pl.ds(pl.multiple_of(me * mine, mine), mine), :],
                resid.at[:, pl.ds(member * part, part)],
                own_sems.at[1 + member],
            )
        )
    for copy in own:
        copy.start()
    for at in strips(cotangent.shape[0]):
        cotangent_low[at, :] = cotangent[at, :].astype(BF16)
    for copy in own:
        copy.wait()
    output_matrix(packed_wo, full_wo)
    resid_out[...] = resid[...]
    exchange.wait()

    swaps = []
    for order, at in enumerate(strips(mine)):
        branch = dot(merged[at, :part], full_wo[0], NT)
        for member in range(1, size):
            branch += dot(
                merged[at, member * part : (member + 1) * part], full_wo[member], NT
            )
        old = resid[at, :].astype(F32)
        branch_scale = row_scale(branch)
        unit = branch * branch_scale
        mixed = old + alpha[...] * (unit - old)
        mixed_scale = row_scale(mixed)
        middle = mixed * mixed_scale
        middle_out[at, :] = middle
        unit_out[at, :] = unit.astype(BF16)
        branch_scale_out[at, :] = branch_scale
        mixed_scale_out[at, :] = mixed_scale
        middle_low[at, :] = middle.astype(BF16)
        there = pl.ds(mine + at.start, at.size)
        swap = to_device(
            middle_low.at[at, :],
            x.at[there, :],
            core_sent.at[order],
            core_got.at[order],
            {"core": 1 - core},
        )
        swap.start()
        swaps.append(swap)
    keep = pltpu.make_async_copy(middle_low, x.at[pl.ds(0, mine), :], own_sems.at[0])
    keep.start()
    keep.wait()
    for swap in swaps:
        swap.wait()


def mix(attended, packed, rows, wide, alpha, cotangent, collective):
    size, slots, part = wide.shape
    chips = packed.shape[1]
    mine, width = slots // size, size * part
    vmem = pl.BlockSpec(memory_space=pltpu.VMEM)
    count = len(strips(mine))
    scale = jax.ShapeDtypeStruct((mine, 1), F32)
    return pl.pallas_call(
        functools.partial(mix_kernel, size),
        in_specs=[ANY, ANY, ANY, vmem, vmem],
        out_specs=[ANY, *[vmem] * 8],
        out_shape=[
            jax.ShapeDtypeStruct((2 * mine, width), BF16),
            jax.ShapeDtypeStruct((mine, width), F32),
            jax.ShapeDtypeStruct((mine, width), BF16),
            scale,
            scale,
            jax.ShapeDtypeStruct((mine, width), BF16),
            jax.ShapeDtypeStruct((size, width, part), BF16),
            jax.ShapeDtypeStruct((mine, width), BF16),
            jax.ShapeDtypeStruct((slots, part), BF16),
        ],
        scratch_shapes=[
            pltpu.VMEM((size, chips, rows, 2 * part), BF16),
            pltpu.VMEM((mine, width), BF16),
            pltpu.VMEM((mine, width), BF16),
            *exchange_semaphores(size),
            pltpu.SemaphoreType.DMA((1 + size,)),
            *core_semaphores(count),
        ],
        compiler_params=remote_params(collective),
        name="mix",
    )(attended, packed, wide, alpha, cotangent)


def whole_matrix(ref):
    _, chips, rows, units = ref.shape
    return ref[...].reshape(chips * rows, units)


def first_step():
    return (pl.program_id(0) == 0) & (pl.program_id(1) == 0)


def last_step():
    return (pl.program_id(0) == pl.num_programs(0) - 1) & (
        pl.program_id(1) == pl.num_programs(1) - 1
    )


def swap_cores(source, target, sems):
    return to_device(
        source, target, sems[0], sems[1], {"core": 1 - lax.axis_index("core")}
    )


def feed_kernel(
    size,
    x,
    w_up,
    w_gate,
    w_down,
    s_u,
    s_v,
    cotangent,
    middle,
    alpha,
    up_out,
    gate_out,
    units_out,
    result_out,
    grad_middle,
    dbranch,
    grad_alpha,
    acc,
    given,
    got,
    spread,
    low,
    send,
    receive,
    local,
    core_sent,
    core_got,
    keep_sems,
):
    exchange = Exchange(
        size,
        cotangent,
        spread,
        row_part(spread.shape[0]),
        column_part(cotangent.shape[1]),
        send,
        receive,
        local,
    )
    branch_swap = swap_cores(given, got, (core_sent.at[0], core_got.at[0]))

    @pl.when(first_step())
    def _():
        greet_pair_and_line(size)
        exchange.start()

    block, part = pl.program_id(0), pl.program_id(1)
    up = dot(x[...], whole_matrix(w_up))
    gate = dot(x[...], whole_matrix(w_gate))
    up_out[0] = up.astype(BF16)
    gate_out[0] = gate.astype(BF16)
    scaled = gate * s_v[0]
    units = (up * s_u[0] * (scaled / (1.0 + jnp.exp(-scaled)))).astype(BF16)
    units_out[0] = units
    term = dot(units, whole_matrix(w_down), NT)

    @pl.when(part == 0)
    def _():
        acc[...] = term

    @pl.when(part > 0)
    def _():
        acc[...] += term

    last = part == pl.num_programs(1) - 1

    @pl.when(last & (block == 0))
    def _():
        given[...] = acc[...].astype(BF16)
        branch_swap.start()

    @pl.when(last & (block == 1))
    def _():
        mine = acc.shape[0]
        branch_swap.wait()
        exchange.wait()
        swaps = []
        for order, at in enumerate(strips(mine)):
            branch = acc[at, :] + got[at, :].astype(F32)
            branch_scale = row_scale(branch)
            unit = branch * branch_scale
            old = middle[at, :]
            mixed = old + alpha[...] * (unit - old)
            mixed_scale = row_scale(mixed)
            result = mixed * mixed_scale
            result_out[at, :] = result.astype(BF16)
            grad_old, grad_branch, part_alpha = residual_backward(
                spread[at, :].astype(F32),
                result,
                old,
                unit,
                alpha[...],
                branch_scale,
                mixed_scale,
            )
            grad_middle[at, :] = grad_old
            if order == 0:
                grad_alpha[...] = part_alpha
            else:
                grad_alpha[...] += part_alpha
            low[at, :] = grad_branch.astype(BF16)
            there = pl.ds(mine + at.start, at.size)
            swaps.append(
                swap_cores(
                    low.at[at, :],
                    dbranch.at[there, :],
                    (core_sent.at[1 + order], core_got.at[1 + order]),
                )
            )
            swaps.append(
                pltpu.make_async_copy(low.at[at, :], dbranch.at[at, :], keep_sems.at[order])
            )
            swaps[-2].start()
            swaps[-1].start()
        for swap in swaps:
            swap.wait()


def packed_specs(packed, width):
    _, chips, _, units = packed.shape
    return [
        pl.BlockSpec((1, chips, width // chips, units), lambda t, m, w=w: (m, 0, w, 0))
        for w in range(3)
    ]


def feed(x, packed, s_u, s_v, cotangent, middle, alpha, collective):
    tokens, width = x.shape
    parts, _, _, units = packed.shape
    size = parts
    block = tokens // 2
    rows = pl.BlockSpec((block, width), lambda t, m: (1 - t, 0))
    vector = pl.BlockSpec((1, 1, units), lambda t, m: (m, 0, 0))
    piece = pl.BlockSpec((1, block, units), lambda t, m: (m, 1 - t, 0))
    vmem = pl.BlockSpec(memory_space=pltpu.VMEM)
    hidden = jax.ShapeDtypeStruct((parts, tokens, units), BF16)
    count = len(strips(block))
    low = pltpu.VMEM((block, width), BF16)
    return pl.pallas_call(
        functools.partial(feed_kernel, size),
        grid=(2, parts),
        in_specs=[rows, *packed_specs(packed, width), vector, vector, ANY, vmem, vmem],
        out_specs=[piece, piece, piece, vmem, vmem, ANY, vmem],
        out_shape=[
            hidden,
            hidden,
            hidden,
            jax.ShapeDtypeStruct((block, width), BF16),
            jax.ShapeDtypeStruct((block, width), F32),
            jax.ShapeDtypeStruct((tokens, width), BF16),
            jax.ShapeDtypeStruct((1, width), F32),
        ],
        scratch_shapes=[
            pltpu.VMEM((block, width), F32),
            low,
            low,
            low,
            low,
            *exchange_semaphores(size),
            *core_semaphores(1 + count),
            pltpu.SemaphoreType.DMA((count,)),
        ],
        compiler_params=remote_params(collective),
        cost_estimate=pl.CostEstimate(
            flops=6 * tokens * width * parts * units, bytes_accessed=60 << 20, transcendentals=0
        ),
        name="feed",
    )(x, packed, packed, packed, s_u, s_v, cotangent, middle, alpha)


def feed_back_kernel(
    size,
    dbranch,
    w_up,
    w_gate,
    w_down,
    s_u,
    s_v,
    up_in,
    gate_in,
    result,
    grad_middle,
    middle,
    resid,
    unit,
    branch_scale,
    mixed_scale,
    alpha,
    full_wo,
    dup_out,
    dgate_out,
    grad_u,
    grad_v,
    spread,
    grad_resid,
    dbranch_attn,
    dmerged,
    grad_alpha,
    acc,
    given,
    got,
    sum_u,
    sum_v,
    send,
    receive,
    local,
    core_sent,
    core_got,
):
    exchange = Exchange(
        size,
        result,
        spread,
        column_part(spread.shape[1]),
        row_part(result.shape[0]),
        send,
        receive,
        local,
    )
    dx_swap = swap_cores(given, got, (core_sent.at[0], core_got.at[0]))

    @pl.when(first_step())
    def _():
        greet_pair_and_line(size)
        exchange.start()

    block, part = pl.program_id(0), pl.program_id(1)
    dunits = dot(dbranch[...], whole_matrix(w_down))
    up = up_in[0].astype(F32)
    gate = gate_in[0].astype(F32)
    scaled = gate * s_v[0]
    sigmoid = 1.0 / (1.0 + jnp.exp(-scaled))
    silu = scaled * sigmoid
    slope = sigmoid * (1.0 + scaled - silu)
    through_up = dunits * silu
    through_gate = dunits * up * s_u[0] * slope
    dup = (through_up * s_u[0]).astype(BF16)
    dgate = (through_gate * s_v[0]).astype(BF16)
    dup_out[0] = dup
    dgate_out[0] = dgate
    term = dot(dup, whole_matrix(w_up), NT) + dot(dgate, whole_matrix(w_gate), NT)
    part_u = jnp.sum(through_up * up, axis=0, keepdims=True)
    part_v = jnp.sum(through_gate * gate, axis=0, keepdims=True)

    @pl.when(block == 0)
    def _():
        sum_u[part] = part_u
        sum_v[part] = part_v

    @pl.when(block > 0)
    def _():
        sum_u[part] += part_u
        sum_v[part] += part_v

    @pl.when(part == 0)
    def _():
        acc[...] = term

    @pl.when(part > 0)
    def _():
        acc[...] += term

    last = part == pl.num_programs(1) - 1

    @pl.when(last & (block == 0))
    def _():
        given[...] = acc[...].astype(BF16)
        dx_swap.start()

    @pl.when(last & (block == 1))
    def _():
        grad_u[...] = sum_u[...]
        grad_v[...] = sum_v[...]
        dx_swap.wait()
        for order, at in enumerate(strips(acc.shape[0])):
            grad_old, grad_branch, part_alpha = residual_backward(
                grad_middle[at, :] + acc[at, :] + got[at, :].astype(F32),
                middle[at, :],
                resid[at, :].astype(F32),
                unit[at, :].astype(F32),
                alpha[...],
                branch_scale[at, :],
                mixed_scale[at, :],
            )
            grad_resid[at, :] = grad_old.astype(BF16)
            if order == 0:
                grad_alpha[...] = part_alpha
            else:
                grad_alpha[...] += part_alpha
            low = grad_branch.astype(BF16)
            dbranch_attn[at, :] = low
            columns = full_wo.shape[2]
            for member in range(size):
                dmerged[at, member * columns : (member + 1) * columns] = dot(
                    low, full_wo[member]
                ).astype(BF16)
        exchange.wait()


def feed_back(
    dbranch,
    packed,
    s_u,
    s_v,
    up,
    gate,
    result,
    grad_middle,
    middle,
    resid,
    unit,
    branch_scale,
    mixed_scale,
    alpha,
    full_wo,
    collective,
):
    tokens, width = dbranch.shape
    parts, _, _, units = packed.shape
    size = parts
    block = tokens // 2
    rows = pl.BlockSpec((block, width), lambda t, m: (1 - t, 0))
    vector = pl.BlockSpec((1, 1, units), lambda t, m: (m, 0, 0))
    piece = pl.BlockSpec((1, block, units), lambda t, m: (m, 1 - t, 0))
    vmem = pl.BlockSpec(memory_space=pltpu.VMEM)
    hidden = jax.ShapeDtypeStruct((parts, tokens, units), BF16)
    sums = jax.ShapeDtypeStruct((parts, 1, units), F32)
    state = jax.ShapeDtypeStruct((block, width), BF16)
    return pl.pallas_call(
        functools.partial(feed_back_kernel, size),
        grid=(2, parts),
        in_specs=[
            rows,
            *packed_specs(packed, width),
            vector,
            vector,
            piece,
            piece,
            ANY,
            *[vmem] * 8,
        ],
        out_specs=[piece, piece, vmem, vmem, ANY, vmem, vmem, vmem, vmem],
        out_shape=[
            hidden,
            hidden,
            sums,
            sums,
            jax.ShapeDtypeStruct((size * block, width // size), BF16),
            state,
            state,
            state,
            jax.ShapeDtypeStruct((1, width), F32),
        ],
        scratch_shapes=[
            pltpu.VMEM((block, width), F32),
            pltpu.VMEM((block, width), BF16),
            pltpu.VMEM((block, width), BF16),
            pltpu.VMEM((parts, 1, units), F32),
            pltpu.VMEM((parts, 1, units), F32),
            *exchange_semaphores(size),
            *core_semaphores(1),
        ],
        compiler_params=remote_params(collective),
        cost_estimate=pl.CostEstimate(
            flops=6 * tokens * width * parts * units, bytes_accessed=70 << 20, transcendentals=0
        ),
        name="feed_back",
    )(
        dbranch,
        packed,
        packed,
        packed,
        s_u,
        s_v,
        up,
        gate,
        result,
        grad_middle,
        middle,
        resid,
        unit,
        branch_scale,
        mixed_scale,
        alpha,
        full_wo,
    )


def feed_grads_kernel(
    size,
    x,
    dbranch,
    dup,
    dgate,
    units,
    dbranch_attn,
    merged,
    dmerged,
    grads,
    grad_wo,
    dattended,
    x_turned,
    d_turned,
    attn_turned,
    send,
    receive,
    local,
):
    exchange = Exchange(
        size,
        dmerged,
        dattended,
        column_part(dattended.shape[1]),
        row_part(dmerged.shape[0]),
        send,
        receive,
        local,
    )

    @pl.when(first_step())
    def _():
        greet_all(size)
        exchange.start()
        x_turned[...] = x[...].T
        d_turned[...] = dbranch[...].T
        attn_turned[...] = dbranch_attn[...].T

    _, chips, rows, _ = grads.shape
    for which, left, right in (
        (0, x_turned, dup),
        (1, x_turned, dgate),
        (2, d_turned, units),
    ):

        @pl.when(pl.program_id(0) == which)
        def _():
            total = dot(left[...], right[0])
            grads[0] = total.astype(BF16).reshape(chips, rows, total.shape[1])

    @pl.when(pl.program_id(0) == 3)
    def _():
        total = dot(attn_turned[...], merged[...])
        grad_wo[...] = total.astype(BF16).reshape(grad_wo.shape)

    @pl.when(last_step())
    def _():
        exchange.wait()


def feed_grads(
    x, dbranch, dup, dgate, units_in, dbranch_attn, merged, dmerged, chips, collective
):
    tokens, width = x.shape
    parts, _, units = dup.shape
    size = parts
    rows = width // chips
    mine = dmerged.shape[0]
    part = width // size

    def whole(array):
        return pl.BlockSpec(array.shape, lambda w, m: (0, 0))

    def turn(w, m, which):
        return jnp.where(w == which, m, jnp.where(w < which, 0, parts - 1))

    def piece(which):
        return pl.BlockSpec((1, tokens, units), lambda w, m: (turn(w, m, which), 0, 0))

    return pl.pallas_call(
        functools.partial(feed_grads_kernel, size),
        grid=(4, parts),
        in_specs=[
            whole(x),
            whole(dbranch),
            piece(0),
            piece(1),
            piece(2),
            whole(dbranch_attn),
            pl.BlockSpec((mine, part), lambda w, m: (0, turn(w, m, 3))),
            ANY,
        ],
        out_specs=[
            pl.BlockSpec(
                (1, chips, rows, units),
                lambda w, m: (jnp.where(w < 3, m, parts - 1), 0, jnp.minimum(w, 2), 0),
            ),
            pl.BlockSpec(
                (1, chips, 2, rows // 2, part), lambda w, m: (turn(w, m, 3), 0, 0, 0, 0)
            ),
            ANY,
        ],
        out_shape=[
            jax.ShapeDtypeStruct((parts, chips, 3 * rows, units), BF16),
            jax.ShapeDtypeStruct((parts, chips, 2, rows // 2, part), BF16),
            jax.ShapeDtypeStruct((size * mine, part), BF16),
        ],
        scratch_shapes=[
            pltpu.VMEM((width, tokens), BF16),
            pltpu.VMEM((width, tokens), BF16),
            pltpu.VMEM((width, mine), BF16),
            *exchange_semaphores(size),
        ],
        compiler_params=remote_params(collective),
        cost_estimate=pl.CostEstimate(
            flops=6 * tokens * width * parts * units, bytes_accessed=40 << 20, transcendentals=0
        ),
        name="feed_grads",
    )(x, dbranch, dup, dgate, units_in, dbranch_attn, merged, dmerged)


def rope_tables(positions, head_size):
    half_size = head_size // 2
    freq_index = jnp.arange(half_size, dtype=F32)
    inverse = jnp.exp(freq_index * (-2.0 * math.log(ROPE_BASE) / head_size))
    angles = positions.astype(F32)[..., None] * inverse
    return (jnp.cos(angles), jnp.sin(angles))


def document_starts(doc_ids):
    slot_index = jnp.arange(doc_ids.shape[-1], dtype=jnp.int32)
    earlier = jnp.concatenate([doc_ids[..., :1] - 1, doc_ids[..., :-1]], axis=-1)
    starts = jnp.where(doc_ids != earlier, slot_index, jnp.zeros_like(slot_index))
    return lax.cummax(starts, axis=starts.ndim - 1)


def other_core(value):
    return lax.ppermute(value, "core", [(0, 1), (1, 0)])


def make_on_device(chips, size):
    def on_device(
        hidden,
        wq,
        wk,
        wv,
        wo,
        w_up,
        w_gate,
        w_down,
        s_qk,
        s_u,
        s_v,
        alpha_a,
        alpha_m,
        doc_ids,
        valid,
        cotangent,
    ):
        _, slots, part = hidden.shape
        width = part * size
        heads = s_qk.shape[0] // DK
        rows = wq.shape[0]
        units = w_up.shape[1] // 2
        mine = slots // size
        block = min(512, slots)
        me = lax.axis_index("mp")
        core = lax.axis_index("core")

        place = paired_place(heads)
        in_pairs = (
            lambda w: w.reshape(w.shape[0], heads, 2, HALF)
            .transpose(0, 2, 1, 3)
            .reshape(w.shape[0], heads * DK)
        )
        low_qkv = jnp.concatenate([in_pairs(wq), in_pairs(wk), wv], axis=1).astype(BF16)
        stacked = jnp.stack([w_up, w_gate, w_down.T]).astype(BF16).reshape(3, rows, 2, units)
        keep = lax.dynamic_index_in_dim(stacked, core, 2, keepdims=False)
        give = lax.dynamic_index_in_dim(stacked, 1 - core, 2, keepdims=False)
        low_wo = wo.astype(BF16).T
        wide_wo = jnp.concatenate([low_wo, low_wo], axis=1)
        given = jnp.concatenate([give.reshape(3 * rows, units), wide_wo])
        got = other_core(given)

        def in_order(own, other):
            return jnp.where(core == 0, jnp.stack([own, other], 1), jnp.stack([other, own], 1))

        pair = in_order(keep, got[: 3 * rows].reshape(3, rows, units))
        lane = jnp.arange(2 * part) // part
        pair_wo = jnp.where(lane == core, wide_wo, got[3 * rows :])
        packed = jnp.concatenate([pair.reshape(6 * rows, units), pair_wo])
        vectors = jnp.concatenate([s_u, s_v * math.sqrt(width), alpha_a, alpha_m])
        wide, full_qkv, packed, vectors = gather_all(
            hidden[0].astype(BF16), low_qkv, packed, vectors[None], size, chips, 0
        )
        full_qkv = full_qkv.reshape(size, part, 3 * part)
        vectors = vectors[:, 0]
        s_up = lax.dynamic_slice_in_dim(vectors[:, : 2 * units], core * units, units, 1)
        s_gate = lax.dynamic_slice_in_dim(
            vectors[:, 2 * units : 4 * units], core * units, units, 1
        )
        s_up = s_up[:, None, :]
        s_gate = s_gate[:, None, :]
        alpha_attn = vectors[:, 4 * units : 4 * units + part].reshape(1, width)
        alpha_mlp = vectors[:, 4 * units + part :].reshape(1, width)

        docs = doc_ids[0]
        starts = document_starts(docs)
        slot = jnp.arange(slots, dtype=jnp.int32)
        cosine, sine = rope_tables(slot - starts, DK)
        cosine = jnp.tile(cosine, (1, heads))
        sine = jnp.tile(sine, (1, heads))
        low = jnp.concatenate([starts[::block] // block, me[None]])
        key_docs = jnp.where(valid[0] == 1, docs, -1)
        to_pair = placing_matrix(place, heads)
        to_plain = placing_matrix(np.arange(heads * DK), heads)
        place_pair = jnp.asarray(to_pair, BF16)
        place_plain = jnp.asarray(to_plain, BF16)
        collect_pair = jnp.asarray(to_pair.T.reshape(heads, EXT, heads * DK), BF16)
        collect_plain = jnp.asarray(to_plain.T.reshape(heads, EXT, heads * DK), BF16)
        sums = jnp.asarray(head_sum_matrix(heads))
        gain = in_pairs(s_qk[None, :])

        q, k, v, rq, rk = project(
            wide, full_qkv, cosine, sine, gain, place_pair, place_plain, sums
        )
        attended, qback = attend(
            low,
            q,
            k,
            v,
            docs[:, None],
            key_docs.reshape(slots // block, 1, block),
            collect_plain,
        )
        (
            x,
            middle,
            unit,
            branch_scale,
            mixed_scale,
            merged,
            full_wo,
            resid,
            cotangent_low,
        ) = mix(attended, packed, rows, wide, alpha_attn, cotangent[0], 1)

        up, gate, hidden_units, result, grad_middle, dbranch, grad_alpha_mlp = feed(
            x, packed, s_up, s_gate, cotangent_low, middle, alpha_mlp, 2
        )
        (
            dup,
            dgate,
            grad_u,
            grad_v,
            out_low,
            grad_resid,
            dbranch_attn,
            dmerged,
            grad_alpha_attn,
        ) = feed_back(
            dbranch,
            packed,
            s_up,
            s_gate,
            up,
            gate,
            result,
            grad_middle,
            middle,
            resid,
            unit,
            branch_scale,
            mixed_scale,
            alpha_attn,
            full_wo,
            3,
        )
        out_hidden = out_low.astype(F32)
        grads, grad_wo, dattended = feed_grads(
            x, dbranch, dup, dgate, hidden_units, dbranch_attn, merged, dmerged, chips, 4
        )

        term, grad_qkv, grad_gain = attend_back(
            low,
            qback,
            dattended,
            attended,
            k,
            v,
            docs.reshape(slots // block, 1, block),
            key_docs[:, None],
            cosine,
            sine,
            rq,
            rk,
            gain,
            full_qkv,
            place_plain,
            collect_plain,
            collect_pair,
            sums,
            wide,
            grad_resid,
        )
        out_pairs = (
            lambda w: w.reshape(w.shape[0], 2, heads, HALF)
            .transpose(0, 2, 1, 3)
            .reshape(w.shape[0], heads * DK)
        )

        zero = jnp.zeros((size, 2, units), F32)
        placed_u = lax.dynamic_update_slice(zero, grad_u, (0, core, 0))
        placed_v = lax.dynamic_update_slice(zero, grad_v * math.sqrt(width), (0, core, 0))
        placed_qk = lax.dynamic_update_slice(
            jnp.zeros((size, part), F32), out_pairs(grad_gain), (me, 0)
        )
        placed = jnp.concatenate(
            [
                placed_u.reshape(size, 2 * units),
                placed_v.reshape(size, 2 * units),
                placed_qk,
                grad_alpha_attn.reshape(size, part),
                grad_alpha_mlp.reshape(size, part),
            ],
            axis=1,
        )
        grad_hidden, owned, owned_output, owned_qkv, summed = sum_all(
            term,
            grads,
            grad_wo,
            grad_qkv.reshape(chips, 2, rows, 3 * part),
            placed[:, None],
            chips,
            5,
        )
        owned_upward, owned_gating, owned_downward = owned[0], owned[1], owned[2].T
        owned_output = owned_output.T
        owned_query = out_pairs(owned_qkv[:, :part])
        owned_keys = out_pairs(owned_qkv[:, part : 2 * part])
        owned_values = owned_qkv[:, 2 * part :]
        bounds = [2 * units, 4 * units, 4 * units + part, 4 * units + 2 * part]
        summed_up, summed_gate, summed_qk, summed_attn, summed_mlp = jnp.split(
            summed[0], bounds
        )
        return (
            out_hidden[None],
            grad_hidden[None],
            owned_query,
            owned_keys,
            owned_values,
            owned_output,
            owned_upward,
            owned_gating,
            owned_downward,
            summed_qk,
            summed_up,
            summed_gate,
            summed_attn,
            summed_mlp,
        )

    return on_device


def solution(mesh):
    rows, size = mesh.shape["dp"], mesh.shape["mp"]
    paired = Mesh(mesh.devices.reshape(rows // 2, 2, size), ("chip", "core", "mp"))
    return jax.shard_map(
        make_on_device(rows // 2, size),
        mesh=paired,
        in_specs=(
            P(DP, None, "mp"),
            P(DP, "mp"),
            P(DP, "mp"),
            P(DP, "mp"),
            P("mp", DP),
            P(DP, "mp"),
            P(DP, "mp"),
            P("mp", DP),
            P("mp"),
            P("mp"),
            P("mp"),
            P("mp"),
            P("mp"),
            P(DP, None),
            P(DP, None),
            P(DP, None, "mp"),
        ),
        out_specs=(
            P(DP, None, "mp"),
            P(DP, None, "mp"),
            P(DP, "mp"),
            P(DP, "mp"),
            P(DP, "mp"),
            P("mp", DP),
            P(DP, "mp"),
            P(DP, "mp"),
            P("mp", DP),
            P("mp"),
            P("mp"),
            P("mp"),
            P("mp"),
            P("mp"),
        ),
        check_vma=False,
    )
```

```python
import functools
import math

import jax
import jax.numpy as jnp
import numpy as np
from jax import lax
from jax.experimental import pallas as pl
from jax.experimental.pallas import tpu as pltpu
from jax.sharding import Mesh
from jax.sharding import PartitionSpec as P

DK = 64
HALF = DK // 2
EXT = 128
EPSILON = 1e-06
ROPE_BASE = 10000.0
VMEM_LIMIT = 60 * 1024 * 1024
F32 = jnp.float32
BF16 = jnp.bfloat16
DP = ("chip", "core")


def dot(left, right, dims=((1,), (0,)), precision=None):
    return lax.dot_general(
        left, right, (dims, ((), ())), precision=precision, preferred_element_type=F32
    )


NT = ((1,), (1,))
TN = ((0,), (0,))


def grid_params(dims):
    return pltpu.CompilerParams(
        dimension_semantics=("arbitrary",) * dims, vmem_limit_bytes=VMEM_LIMIT
    )


ANY = pl.BlockSpec(memory_space=pl.ANY)


def remote_params(collective, **more):
    return pltpu.CompilerParams(
        collective_id=collective,
        has_side_effects=True,
        vmem_limit_bytes=VMEM_LIMIT,
        **more,
    )


def to_device(source, target, send, receive, where):
    return pltpu.make_async_remote_copy(
        src_ref=source,
        dst_ref=target,
        send_sem=send,
        recv_sem=receive,
        device_id=where,
        device_id_type=pl.DeviceIdType.MESH,
    )


def to_member(source, target, send, receive, member):
    return to_device(source, target, send, receive, {"mp": member})


def flip(index, mask):
    bit = 1
    while bit <= mask:
        if mask & bit:
            index = index + bit - 2 * bit * lax.rem(lax.div(index, bit), 2)
        bit *= 2
    return index


def bits_below(count):
    return [1 << k for k in range(count.bit_length() - 1)]


def greet(where):
    pl.semaphore_signal(
        pltpu.get_barrier_semaphore(),
        inc=1,
        device_id=where,
        device_id_type=pl.DeviceIdType.MESH,
    )


def greet_all(size):
    me = lax.axis_index("mp")
    for k in range(1, size):
        greet({"mp": flip(me, k)})
    pl.semaphore_wait(pltpu.get_barrier_semaphore(), size - 1)


def greet_around(size, chips):
    me, chip, core = (lax.axis_index(name) for name in ("mp", "chip", "core"))
    for k in range(1, size):
        greet({"mp": flip(me, k)})
    for bit in bits_below(chips):
        greet({"chip": flip(chip, bit)})
    greet({"core": 1 - core})
    pl.semaphore_wait(pltpu.get_barrier_semaphore(), size + len(bits_below(chips)))


class Exchange:
    def __init__(self, size, source, target, piece, place, send, receive, local):
        me = lax.axis_index("mp")
        self.local = pltpu.make_async_copy(piece(source, me), place(target, me), local)
        self.remote = [
            to_member(
                piece(source, flip(me, k)),
                place(target, me),
                send.at[k],
                receive.at[k],
                flip(me, k),
            )
            for k in range(1, size)
        ]

    def start(self):
        for copy in self.remote:
            copy.start()
        self.local.start()

    def wait(self):
        self.local.wait()
        for copy in self.remote:
            copy.wait()


def exchange_semaphores(size):
    return [
        pltpu.SemaphoreType.DMA((size,)),
        pltpu.SemaphoreType.DMA((size,)),
        pltpu.SemaphoreType.DMA,
    ]


def row_part(rows):
    return lambda ref, j: ref.at[pl.ds(pl.multiple_of(j * rows, rows), rows), :]


def column_part(columns):
    return lambda ref, j: ref.at[:, pl.ds(pl.multiple_of(j * columns, columns), columns)]


class Gather:
    def __init__(self, block, index, bits, where, send, receive):
        self.block, self.index, self.bits, self.where = block, index, bits, where
        self.send, self.receive = send, receive

    def copies(self, stage, incoming):
        span = [0]
        for bit in self.bits[:stage]:
            span += [held | bit for held in span]
        bit = self.bits[stage]
        for order, held in enumerate(span):
            ref = self.block(flip(self.index, held | bit if incoming else held))
            slot = (1 << stage) - 1 + order
            yield to_device(
                ref,
                ref,
                self.send(slot),
                self.receive(slot),
                self.where(flip(self.index, bit)),
            )

    def start(self, stage):
        if stage < len(self.bits):
            for copy in self.copies(stage, False):
                copy.start()

    def arrive(self, stage):
        if stage < len(self.bits):
            for copy in self.copies(stage, True):
                copy.wait_recv()

    def close(self):
        for stage in range(len(self.bits)):
            for copy in self.copies(stage, False):
                copy.wait_send()


def gather_all_kernel(
    size,
    chips,
    chunks,
    split,
    hidden,
    qkv,
    packed,
    vectors,
    wide,
    full_qkv,
    full,
    full_vectors,
    local,
    hidden_up,
    hidden_down,
    hidden_got,
    packed_up,
    packed_down,
    packed_got,
    plane_sent,
    plane_got,
    qkv_sent,
    qkv_got,
    vector_sent,
    vector_got,
):
    me, chip, core = (lax.axis_index(name) for name in ("mp", "chip", "core"))
    tokens = hidden.shape[0]
    rows = tokens // chunks
    height = packed.shape[0]
    owner = chip * 2 + core
    bits = bits_below(chips)
    stages = len(bits)
    greet_around(size, chips)

    own = [
        pltpu.make_async_copy(qkv, full_qkv.at[owner], local.at[0]),
        pltpu.make_async_copy(packed, full.at[me, chip], local.at[1]),
        pltpu.make_async_copy(vectors, full_vectors.at[me], local.at[2]),
        pltpu.make_async_copy(hidden, wide.at[me], local.at[3]),
    ]
    for copy in own:
        copy.start()

    def hidden_hop(origin, chunk, ref, member, send):
        at = pl.ds(chunk * rows, rows)
        return to_member(
            ref.at[at, :],
            wide.at[origin, at, :],
            send.at[origin, chunk],
            hidden_got.at[origin, chunk],
            member,
        )

    def packed_hop(origin, ref, member, send):
        return to_member(
            ref, full.at[origin, chip], send.at[origin], packed_got.at[origin], member
        )

    vector_copies = [
        to_member(
            vectors, full_vectors.at[me], vector_sent.at[k], vector_got.at[k], flip(me, k)
        )
        for k in range(1, size)
    ]

    def plane(origin, slot):
        return [
            Gather(
                lambda i, at=at: full.at[origin, i, at, :],
                chip,
                order,
                lambda i: {"chip": i},
                lambda k, half=half: plane_sent.at[slot, half, k],
                lambda k, half=half: plane_got.at[slot, half, k],
            )
            for half, (at, order) in enumerate(
                (
                    (pl.ds(0, split), bits),
                    (pl.ds(split, height - split), bits[::-1]),
                )
            )
        ]

    gather_qkv = Gather(
        lambda i: full_qkv.at[i],
        owner,
        [2 * bit for bit in bits] + [1],
        lambda i: {"chip": lax.div(i, 2), "core": lax.rem(i, 2)},
        lambda k: qkv_sent.at[k],
        lambda k: qkv_got.at[k],
    )

    sources = {0: [(me >= 0, me, 0, None)]}
    for distance in range(1, size):
        sources[distance] = [
            (me >= distance, me - distance, 2 * distance - 1, True),
            (me + distance < size, me + distance, 2 * distance, False),
        ]

    own[0].wait()
    own[1].wait()

    def pass_on(origin, upward):
        block = full.at[origin, chip]
        if upward is not False:

            @pl.when(me < size - 1)
            def _():
                packed_hop(origin, block, me + 1, packed_up).start()

        if not upward:

            @pl.when(me > 0)
            def _():
                packed_hop(origin, block, me - 1, packed_down).start()

    def advance(distance, stage):
        for exists, origin, slot, _ in sources[distance]:

            @pl.when(exists)
            def _():
                for half in plane(origin, slot):
                    half.arrive(stage)
                    half.start(stage + 1)

    pass_on(me, None)
    gather_qkv.start(0)
    for half in plane(me, 0):
        half.start(0)
    for copy in vector_copies:
        copy.start()
    for stage in range(stages):
        gather_qkv.arrive(stage)
        gather_qkv.start(stage + 1)
    advance(0, 0)
    for distance in range(1, size):
        for exists, origin, slot, upward in sources[distance]:

            @pl.when(exists)
            def _():
                packed_hop(origin, full.at[origin, chip], me, packed_up).wait_recv()
                pass_on(origin, upward)
                for half in plane(origin, slot):
                    half.start(0)

        @pl.when(jnp.maximum(me, size - 1 - me) == distance)
        def _():
            for chunk in range(chunks):

                @pl.when(me < size - 1)
                def _():
                    hidden_hop(me, chunk, hidden, me + 1, hidden_up).start()

                @pl.when(me > 0)
                def _():
                    hidden_hop(me, chunk, hidden, me - 1, hidden_down).start()

        if distance > 1:
            advance(distance - 1, 0)
    advance(size - 1, 0)
    for distance in range(1, size):
        for chunk in range(chunks):
            for exists, origin, _, upward in sources[distance]:

                @pl.when(exists)
                def _():
                    block = wide.at[origin]
                    hidden_hop(origin, chunk, block, me, hidden_up).wait_recv()
                    if upward:

                        @pl.when(me < size - 1)
                        def _():
                            hidden_hop(origin, chunk, block, me + 1, hidden_up).start()
                    else:

                        @pl.when(me > 0)
                        def _():
                            hidden_hop(origin, chunk, block, me - 1, hidden_down).start()

    for stage in range(1, stages):
        for distance in range(size):
            advance(distance, stage)
    gather_qkv.arrive(stages)

    own[2].wait()
    own[3].wait()
    for copy in vector_copies:
        copy.wait()
    gather_qkv.close()
    for distance in range(size):
        for exists, origin, slot, upward in sources[distance]:

            @pl.when(exists)
            def _():
                for half in plane(origin, slot):
                    half.close()
                block = full.at[origin, chip]
                if upward is not False:

                    @pl.when(me < size - 1)
                    def _():
                        packed_hop(origin, block, me, packed_up).wait_send()
                        for chunk in range(chunks):
                            hidden_hop(origin, chunk, wide.at[origin], me, hidden_up).wait_send()

                if not upward:

                    @pl.when(me > 0)
                    def _():
                        packed_hop(origin, block, me, packed_down).wait_send()
                        for chunk in range(chunks):
                            hidden_hop(
                                origin, chunk, wide.at[origin], me, hidden_down
                            ).wait_send()


def gather_all(hidden, qkv, packed, vectors, size, chips, collective):
    chunks = 6
    height = packed.shape[0]
    dma = pltpu.SemaphoreType.DMA
    line = dma((size, chunks))
    plane = dma((2 * size - 1, 2, max(chips - 1, 1)))
    return pl.pallas_call(
        functools.partial(gather_all_kernel, size, chips, chunks, height // 32 * 16),
        in_specs=[pl.BlockSpec(memory_space=pltpu.VMEM)] * 4,
        out_specs=[ANY] * 4,
        out_shape=[
            jax.ShapeDtypeStruct((size, *hidden.shape), BF16),
            jax.ShapeDtypeStruct((2 * chips, *qkv.shape), BF16),
            jax.ShapeDtypeStruct((size, chips, *packed.shape), BF16),
            jax.ShapeDtypeStruct((size, *vectors.shape), F32),
        ],
        scratch_shapes=[
            dma((4,)),
            line,
            line,
            line,
            dma((size,)),
            dma((size,)),
            dma((size,)),
            plane,
            plane,
            dma((2 * chips - 1,)),
            dma((2 * chips - 1,)),
            dma((size,)),
            dma((size,)),
        ],
        compiler_params=remote_params(collective),
        name="gather_all",
    )(hidden, qkv, packed, vectors)


class LineSum:
    def __init__(self, size, chunks, term, up, down, sems):
        self.size, self.chunks = size, chunks
        self.term, self.up, self.down = term, up, down
        self.sent_up, self.sent_down, self.got_up, self.got_down = sems
        self.me = lax.axis_index("mp")
        self.rows = up.shape[1] // chunks

    def at(self, chunk):
        return pl.ds(chunk * self.rows, self.rows)

    def hop(self, upward, goal, chunk, member):
        slots = self.up if upward else self.down
        send = self.sent_up if upward else self.sent_down
        receive = self.got_up if upward else self.got_down
        ref = slots.at[goal, self.at(chunk), :]
        return to_member(ref, ref, send.at[goal, chunk], receive.at[goal, chunk], member)

    def step(self, order, chunk):
        me, last, at = self.me, self.size - 1, self.at(chunk)
        for upward, goal, ahead, first, member in (
            (True, last - order, me < last - order, me == 0, me + 1),
            (False, order, me > order, me == last, me - 1),
        ):
            slots = self.up if upward else self.down

            @pl.when(ahead & first)
            def _():
                slots[goal, at, :] = self.term(goal, at)

            @pl.when(ahead & jnp.logical_not(first))
            def _():
                self.hop(upward, goal, chunk, me).wait_recv()
                slots[goal, at, :] = (
                    slots[goal, at, :].astype(F32) + self.term(goal, at).astype(F32)
                ).astype(BF16)

            @pl.when(ahead)
            def _():
                self.hop(upward, goal, chunk, member).start()

    def result(self, chunk, out, out_at):
        me, at = self.me, self.at(chunk)
        out[out_at, :] = self.term(me, at).astype(F32)

        @pl.when(me > 0)
        def _():
            self.hop(True, me, chunk, me).wait_recv()
            out[out_at, :] += self.up[me, at, :].astype(F32)

        @pl.when(me < self.size - 1)
        def _():
            self.hop(False, me, chunk, me).wait_recv()
            out[out_at, :] += self.down[me, at, :].astype(F32)

    def close(self):
        for order in range(self.size - 1):
            for chunk in range(self.chunks):

                @pl.when(self.me < self.size - 1 - order)
                def _():
                    self.hop(True, self.size - 1 - order, chunk, self.me).wait_send()

                @pl.when(self.me > order)
                def _():
                    self.hop(False, order, chunk, self.me).wait_send()


class ChipSum:
    def __init__(self, layers, bits, source, acc, got, load, send, receive):
        self.layers, self.bits = layers, bits
        self.acc, self.got, self.chip = acc, got, lax.axis_index("chip")
        self.half = 1 << (len(bits) - 1)
        self.load = [
            pltpu.make_async_copy(
                source(layer, flip(self.chip, self.combo(slot))),
                acc.at[layer, slot],
                load.at[layer, slot],
            )
            for layer in range(layers)
            for slot in range(self.half)
        ]
        self.source, self.sent, self.received = source, send, receive

    def combo(self, slot):
        count = len(self.bits)
        return sum(self.bits[count - 1 - j] for j in range(count - 1) if slot >> j & 1)

    def copies(self, stage):
        count = self.half >> stage
        offset = 2 * self.half - 2 * count
        where = {"chip": flip(self.chip, self.bits[stage])}
        for layer in range(self.layers):
            for slot in range(count):
                if stage == 0:
                    other = flip(self.chip, self.bits[0] | self.combo(slot))
                    ref = self.source(layer, other)
                else:
                    ref = self.acc.at[layer, count + slot]
                at = offset + slot
                yield layer, slot, at, to_device(
                    ref,
                    self.got.at[layer, at],
                    self.sent.at[layer, at],
                    self.received.at[layer, at],
                    where,
                )

    def start(self, stage):
        if stage == 0:
            for copy in self.load:
                copy.start()
        for _, _, _, copy in self.copies(stage):
            copy.start()

    def add(self, stage):
        if stage == 0:
            for copy in self.load:
                copy.wait()
        for layer, slot, at, copy in self.copies(stage):
            copy.wait_recv()
            self.acc[layer, slot] = (
                self.acc[layer, slot].astype(F32) + self.got[layer, at].astype(F32)
            ).astype(BF16)

    def close(self):
        for stage in range(len(self.bits)):
            for _, _, _, copy in self.copies(stage):
                copy.wait_send()


def sum_all_kernel(
    size,
    chips,
    chunks,
    split,
    term,
    grads,
    grad_wo,
    grad_qkv,
    vectors,
    out,
    owned,
    owned_wo,
    owned_qkv,
    owned_vectors,
    term_up,
    term_down,
    acc_a,
    got_a,
    up_a,
    down_a,
    acc_b,
    got_b,
    up_b,
    down_b,
    pair_wo,
    other_wo,
    acc_wo,
    got_wo,
    up_wo,
    down_wo,
    pair_qkv,
    other_qkv,
    acc_qkv,
    got_qkv,
    whole,
    vector_sum,
    vector_got,
    vector_line,
    local,
    core_sent,
    core_got,
    vector_sent,
    vector_received,
    term_sems,
    line_sems,
    load_sems,
    chip_sent,
    chip_got,
):
    me, chip, core = (lax.axis_index(name) for name in ("mp", "chip", "core"))
    bits = bits_below(chips)
    stages = len(bits)
    greet_around(size, chips)
    other_core_is = {"core": 1 - core}

    def sems(ref, which):
        return [ref.at[which, k] for k in range(4)]

    line = LineSum(
        size, chunks, lambda goal, at: term[goal, at, :], term_up, term_down, sems(term_sems, 0)
    )
    sum_a = ChipSum(
        size,
        bits,
        lambda m, c: grads.at[m, c, pl.ds(0, split), :],
        acc_a,
        got_a,
        load_sems.at[0],
        chip_sent.at[0],
        chip_got.at[0],
    )
    sum_b = ChipSum(
        size,
        bits[::-1],
        lambda m, c: grads.at[m, c, pl.ds(split, grads.shape[2] - split), :],
        acc_b,
        got_b,
        load_sems.at[1],
        chip_sent.at[1],
        chip_got.at[1],
    )
    sum_wo = ChipSum(
        size,
        bits[::-1],
        lambda m, c: pair_wo.at[m, c],
        acc_wo,
        got_wo,
        load_sems.at[2],
        chip_sent.at[2],
        chip_got.at[2],
    )
    sum_qkv = ChipSum(
        1,
        bits,
        lambda m, c: pair_qkv.at[c],
        acc_qkv,
        got_qkv,
        load_sems.at[3],
        chip_sent.at[3],
        chip_got.at[3],
    )
    lines = [
        LineSum(
            size,
            1,
            lambda goal, at, acc=acc: acc[goal, 0, at, :],
            up,
            down,
            sems(line_sems, which),
        )
        for which, (acc, up, down) in enumerate(
            ((acc_a, up_a, down_a), (acc_b, up_b, down_b), (acc_wo, up_wo, down_wo))
        )
    ]

    own = [
        pltpu.make_async_copy(grad_wo.at[:, :, core], pair_wo, local.at[0]),
        pltpu.make_async_copy(grad_qkv.at[:, core], pair_qkv, local.at[1]),
    ]
    given = [
        to_device(
            grad_wo.at[:, :, 1 - core], other_wo, core_sent.at[0], core_got.at[0], other_core_is
        ),
        to_device(
            grad_qkv.at[:, 1 - core], other_qkv, core_sent.at[1], core_got.at[1], other_core_is
        ),
    ]
    vector_copies = [
        to_member(
            vectors.at[flip(me, k)],
            vector_line.at[k],
            vector_sent.at[k],
            vector_received.at[k],
            flip(me, k),
        )
        for k in range(1, size)
    ]
    for copy in own + given:
        copy.start()
    sum_a.start(0)
    sum_b.start(0)
    for copy in vector_copies:
        copy.start()

    owner = chip * 2 + core
    vector_bits = [1] + [2 * bit for bit in bits]

    def vector_copy(stage):
        partner = flip(owner, vector_bits[stage])
        return to_device(
            vector_sum.at[stage],
            vector_got.at[stage],
            vector_sent.at[size + stage],
            vector_received.at[size + stage],
            {"chip": lax.div(partner, 2), "core": lax.rem(partner, 2)},
        )

    def vector_step(stage):
        if stage == 0:
            total = vectors[me]
            for k, copy in enumerate(vector_copies):
                copy.wait_recv()
                total = total + vector_line[k + 1]
            vector_sum[0] = total
        else:
            vector_copy(stage - 1).wait_recv()
            vector_sum[stage] = vector_sum[stage - 1] + vector_got[stage - 1]
        if stage < len(vector_bits):
            vector_copy(stage).start()

    for chunk in range(chunks):
        line.step(0, chunk)
    for copy in own:
        copy.wait()
    for copy in given:
        copy.wait_recv()
    pair_wo[...] = (pair_wo[...].astype(F32) + other_wo[...].astype(F32)).astype(BF16)
    pair_qkv[...] = (pair_qkv[...].astype(F32) + other_qkv[...].astype(F32)).astype(BF16)
    sum_wo.start(0)
    sum_qkv.start(0)
    vector_step(0)
    vector_step(1)
    for order in range(1, size - 1):
        for chunk in range(chunks):
            line.step(order, chunk)
        if order - 1 < stages:
            for part in (sum_a, sum_b, sum_wo, sum_qkv):
                part.add(order - 1)
                if order < stages:
                    part.start(order)
    for stage in range(size - 2, stages):
        for part in (sum_a, sum_b, sum_wo, sum_qkv):
            part.add(stage)
            if stage + 1 < stages:
                part.start(stage + 1)
    lines[0].step(0, 0)
    lines[1].step(0, 0)
    lines[2].step(0, 0)
    for stage in range(2, len(vector_bits) + 1):
        vector_step(stage)
    for chunk in range(chunks):
        line.result(chunk, out, line.at(chunk))
    for order in range(1, size - 1):
        for part in lines:
            part.step(order, 0)
    owned_vectors[...] = vector_sum[len(vector_bits)]
    owned_qkv[...] = acc_qkv[0, 0].astype(F32)
    lines[0].result(0, whole, pl.ds(0, split))
    lines[1].result(0, whole, pl.ds(split, whole.shape[0] - split))
    lines[2].result(0, owned_wo, slice(None))

    matrices, rows, columns = owned.shape
    columns = columns // 2
    place = pl.ds(pl.multiple_of(core * columns, columns), columns)
    swaps = []
    for matrix in range(matrices):
        mine = pl.ds(pl.multiple_of((2 * matrix + core) * rows, rows), rows)
        theirs = pl.ds(pl.multiple_of((2 * matrix + 1 - core) * rows, rows), rows)
        swaps.append(
            to_device(
                whole.at[theirs, :],
                owned.at[matrix, :, place],
                core_sent.at[2 + matrix],
                core_got.at[2 + matrix],
                other_core_is,
            )
        )
        swaps[-1].start()
        copy = pltpu.make_async_copy(
            whole.at[mine, :], owned.at[matrix, :, place], local.at[2 + matrix]
        )
        copy.start()
        swaps.append(copy)
    for copy in swaps:
        copy.wait()

    for copy in given + vector_copies:
        copy.wait_send()
    for stage in range(len(vector_bits)):
        vector_copy(stage).wait_send()
    for part in (sum_a, sum_b, sum_wo, sum_qkv):
        part.close()
    line.close()
    for part in lines:
        part.close()


def sum_all(term, grads, grad_wo, grad_qkv, vectors, chips, collective):
    size, tokens, part = term.shape
    height, units = grads.shape[2:]
    rows = height // 6
    chunks = 6
    split = height // 32 * 16
    half, blocks = max(chips // 2, 1), max(chips - 1, 1)
    stages = chips.bit_length()
    dma = pltpu.SemaphoreType.DMA
    vmem = pl.BlockSpec(memory_space=pltpu.VMEM)
    wo_block, qkv_block = grad_wo.shape[3:], grad_qkv.shape[2:]
    long = vectors.shape[1:]

    def sums(layers, block):
        return [
            pltpu.VMEM((layers, half, *block), BF16),
            pltpu.VMEM((layers, blocks, *block), BF16),
        ]

    def line(block):
        return [pltpu.VMEM((size, *block), BF16)] * 2

    return pl.pallas_call(
        functools.partial(sum_all_kernel, size, chips, chunks, split),
        in_specs=[vmem, ANY, ANY, ANY, vmem],
        out_specs=[vmem] * 5,
        out_shape=[
            jax.ShapeDtypeStruct((tokens, part), F32),
            jax.ShapeDtypeStruct((3, rows, 2 * units), F32),
            jax.ShapeDtypeStruct(wo_block, F32),
            jax.ShapeDtypeStruct(qkv_block, F32),
            jax.ShapeDtypeStruct(long, F32),
        ],
        scratch_shapes=[
            *line((tokens, part)),
            *sums(size, (split, units)),
            *line((split, units)),
            *sums(size, (height - split, units)),
            *line((height - split, units)),
            pltpu.VMEM((size, chips, *wo_block), BF16),
            pltpu.VMEM((size, chips, *wo_block), BF16),
            *sums(size, wo_block),
            *line(wo_block),
            pltpu.VMEM((chips, *qkv_block), BF16),
            pltpu.VMEM((chips, *qkv_block), BF16),
            *sums(1, qkv_block),
            pltpu.VMEM((height, units), F32),
            pltpu.VMEM((stages + 1, *long), F32),
            pltpu.VMEM((stages + 1, *long), F32),
            pltpu.VMEM((size, *long), F32),
            dma((5,)),
            dma((5,)),
            dma((5,)),
            dma((size + stages,)),
            dma((size + stages,)),
            dma((1, 4, size, chunks)),
            dma((3, 4, size, 1)),
            dma((4, size, half)),
            dma((4, size, blocks)),
            dma((4, size, blocks)),
        ],
        compiler_params=remote_params(collective),
        name="sum_all",
    )(term, grads, grad_wo, grad_qkv, vectors)


def paired_place(heads):
    head, feature = np.divmod(np.arange(heads * DK), DK)
    return (feature // HALF) * (heads * HALF) + head * HALF + feature % HALF


def placing_matrix(place, heads):
    head, feature = np.divmod(np.arange(heads * DK), DK)
    matrix = np.zeros((heads * DK, heads * EXT), np.float32)
    matrix[place, head * EXT + feature] = 1
    return matrix


def delta_matrix(heads):
    lane = np.arange(heads * EXT)
    head = np.arange(heads * DK) // DK
    return ((head[:, None] == lane[None, :] // EXT) & (lane % EXT >= DK) & (lane % EXT < DK + 3)).astype(
        np.float32
    )


def head_sum_matrix(heads):
    lane = np.arange(heads * HALF) // HALF
    return (lane[:, None] == lane[None, :]).astype(np.float32)


def split_dot(value, matrix):
    high = value.astype(BF16)
    rest = (value - high.astype(F32)).astype(BF16)
    return dot(high, matrix) + dot(rest, matrix)


def project_kernel(
    wide, weight, cosine, sine, gain, place_pair, place_plain, sums, q, k, v, q_pair, k_pair, rq, rk
):
    parts = wide.shape[0]
    heads = q.shape[0]
    pair = heads * HALF
    width = heads * DK
    raw = dot(wide[0], weight[0])
    for part in range(1, parts):
        raw += dot(wide[part], weight[part])
    rows = raw.shape[0]
    lane = lax.broadcasted_iota(jnp.int32, (rows, EXT), 1)
    cos = cosine[...]
    sin = sine[...]
    gain_first = gain[:, :pair]
    gain_second = gain[:, pair:]
    for offset, out, pair_out, scale_out, factor in (
        (0, q, q_pair, rq, math.sqrt(DK)),
        (width, k, k_pair, rk, 1.0),
    ):
        first = raw[:, offset : offset + pair]
        second = raw[:, offset + pair : offset + width]
        turned_first = first * cos - second * sin
        turned_second = second * cos + first * sin
        total = split_dot(
            turned_first * turned_first + turned_second * turned_second, sums[...]
        )
        scale = lax.rsqrt(total + EPSILON)
        scale_out[...] = scale
        both = jnp.concatenate(
            [turned_first * scale * gain_first, turned_second * scale * gain_second], axis=1
        ).astype(BF16)
        pair_out[...] = both
        padded = dot(both, place_pair[...]) * factor
        for head in range(heads):
            piece = padded[:, head * EXT : (head + 1) * EXT]
            if factor == 1.0:
                piece = jnp.where(lane < DK, piece, 1.0)
            out[head] = piece.astype(BF16)
    padded = dot(raw[:, 2 * width :].astype(BF16), place_plain[...])
    for head in range(heads):
        piece = padded[:, head * EXT : (head + 1) * EXT]
        v[head] = jnp.where(lane < DK, piece, 1.0).astype(BF16)


def project(wide, weight, cosine, sine, gain, place_pair, place_plain, sums):
    parts, tokens, part = wide.shape
    width = gain.shape[1]
    heads = width // DK
    block = min(512, tokens)
    padded = jax.ShapeDtypeStruct((heads, tokens, EXT), BF16)
    scale = jax.ShapeDtypeStruct((tokens, heads * HALF), F32)

    def whole(array):
        return pl.BlockSpec(array.shape, lambda i: (0,) * array.ndim)

    rows = pl.BlockSpec((block, heads * HALF), lambda i: (i, 0))
    headed = pl.BlockSpec((heads, block, EXT), lambda i: (0, i, 0))
    paired = pl.BlockSpec((block, width), lambda i: (i, 0))
    both = jax.ShapeDtypeStruct((tokens, width), BF16)
    return pl.pallas_call(
        project_kernel,
        grid=(tokens // block,),
        in_specs=[
            pl.BlockSpec((parts, block, part), lambda i: (0, i, 0)),
            whole(weight),
            rows,
            rows,
            whole(gain),
            whole(place_pair),
            whole(place_plain),
            whole(sums),
        ],
        out_specs=[headed, headed, headed, paired, paired, rows, rows],
        out_shape=[padded, padded, padded, both, both, scale, scale],
        compiler_params=grid_params(1),
        cost_estimate=pl.CostEstimate(
            flops=2 * tokens * parts * part * width * 3,
            bytes_accessed=20 << 20,
            transcendentals=0,
        ),
        name="project",
    )(wide, weight, cosine, sine, gain, place_pair, place_plain, sums)


def split_three(value):
    high = value.astype(BF16).astype(F32)
    rest = value - high
    middle = rest.astype(BF16).astype(F32)
    return high, middle, rest - middle


def attend_kernel(low, q, k, v, qdoc, kdoc, collect, attended, qback, acc):
    heads, rows, _ = q.shape
    block = kdoc.shape[2]
    index = pl.program_id(0)
    acc[...] = jnp.zeros_like(acc)

    def step(j, diagonal):
        slots = pl.ds(pl.multiple_of(j * block, block), block)
        mask = qdoc[...] == kdoc[j]
        if diagonal:
            row = lax.broadcasted_iota(jnp.int32, (rows, block), 0)
            column = lax.broadcasted_iota(jnp.int32, (rows, block), 1)
            mask = (mask & (column < row)) | (column == row)
        for head in range(heads):
            scores = dot(q[head], k[head, slots, :], NT)
            weight = jnp.where(mask, jnp.exp(scores), 0.0).astype(BF16)
            acc[head] += dot(weight, v[head, slots, :])

    def earlier(j, carry):
        step(j, False)
        return carry

    lax.fori_loop(low[index], index, earlier, 0)
    step(index, True)

    lane = lax.broadcasted_iota(jnp.int32, (rows, EXT), 1)
    merged = jnp.zeros((rows, heads * DK), F32)
    for head in range(heads):
        both = acc[head]
        total = pltpu.roll(both, DK, 1)
        output = jnp.where(lane < DK, both / total, 0.0).astype(BF16)
        merged += dot(output, collect[head])
        high, middle, rest = split_three(-jnp.log(both))
        qback[head] = jnp.where(
            lane < DK,
            q[head].astype(F32),
            jnp.where(
                lane == DK,
                high,
                jnp.where(lane == DK + 1, middle, jnp.where(lane == DK + 2, rest, 0.0)),
            ),
        ).astype(BF16)
    attended[...] = merged.astype(BF16)


def attend(low, q, k, v, qdoc, kdoc, collect):
    heads, tokens, _ = q.shape
    block = kdoc.shape[2]
    width = heads * DK

    def whole(array):
        return pl.BlockSpec(array.shape, lambda i, low: (0,) * array.ndim)

    headed = pl.BlockSpec((heads, block, EXT), lambda i, low: (0, i, 0))
    return pl.pallas_call(
        attend_kernel,
        grid_spec=pltpu.PrefetchScalarGridSpec(
            num_scalar_prefetch=1,
            grid=(tokens // block,),
            in_specs=[
                headed,
                whole(k),
                whole(v),
                pl.BlockSpec((block, 1), lambda i, low: (i, 0)),
                whole(kdoc),
                whole(collect),
            ],
            out_specs=[pl.BlockSpec((block, width), lambda i, low: (i, 0)), headed],
            scratch_shapes=[pltpu.VMEM((heads, block, EXT), F32)],
        ),
        out_shape=[
            jax.ShapeDtypeStruct((tokens, width), BF16),
            jax.ShapeDtypeStruct((heads, tokens, EXT), BF16),
        ],
        compiler_params=grid_params(1),
        cost_estimate=pl.CostEstimate(
            flops=40_000_000_000, bytes_accessed=16 << 20, transcendentals=0
        ),
        name="attend",
    )(low, q, k, v, qdoc, kdoc, collect)


def unrope(grad, unit, gain, scale, cos, sin, sums):
    pair = cos.shape[1]
    grad_gain = jnp.sum(grad * unit, axis=0, keepdims=True)
    dy = grad * gain
    prod = dy * unit
    total = split_dot(prod[:, :pair] + prod[:, pair:], sums)
    first = scale * (dy[:, :pair] - unit[:, :pair] * total)
    second = scale * (dy[:, pair:] - unit[:, pair:] * total)
    raw = jnp.concatenate([first * cos + second * sin, second * cos - first * sin], axis=1)
    return raw.astype(BF16), grad_gain


def head_lanes(shape, head, paired):
    lane = lax.broadcasted_iota(jnp.int32, shape, 1)
    if paired:
        return lax.div(lax.rem(lane, shape[1] // 2), HALF) == head
    return lax.div(lane, DK) == head


def attend_back_kernel(
    low,
    qback,
    q_pair,
    dout,
    attended,
    k,
    k_pair,
    v,
    qdoc,
    kdoc,
    cosine,
    sine,
    rq,
    rk,
    gain,
    weight,
    place_plain,
    place_delta,
    sums,
    wide,
    grad_resid,
    term_out,
    grad_qkv,
    gain_out,
    dk,
    dv,
    dq,
    dox,
    q_heads,
    d_heads,
    k_heads,
    probs_all,
    scores_all,
    dq_low,
    total_qkv,
):
    heads, rows, _ = qback.shape
    steps = pl.num_programs(0) // 2
    step_at = pl.program_id(0)
    width = heads * DK
    scale = math.sqrt(DK)

    @pl.when(step_at == 0)
    def _():
        dk[...] = jnp.zeros_like(dk)
        dv[...] = jnp.zeros_like(dv)
        gain_out[...] = jnp.zeros_like(gain_out)
        keys = k_pair[...]
        for head in range(heads):
            k_heads[head] = jnp.where(head_lanes(keys.shape, head, True), keys, 0)

    @pl.when(step_at < steps)
    def _():
        index = step_at
        lane = lax.broadcasted_iota(jnp.int32, (rows, EXT), 1)
        grads = dout[...]
        queries = q_pair[...]
        spread = dot(grads, place_plain[...])
        delta = split_dot(grads.astype(F32) * attended[...].astype(F32), place_delta[...])
        for head in range(heads):
            at = slice(head * EXT, (head + 1) * EXT)
            high, middle, rest = split_three(-delta[:, at])
            dox[head] = jnp.where(
                lane < DK,
                spread[:, at],
                jnp.where(lane == DK, high, jnp.where(lane == DK + 1, middle, rest)),
            ).astype(BF16)
            stack = slice(head * rows, (head + 1) * rows)
            q_heads[stack, :] = jnp.where(head_lanes(queries.shape, head, True), queries, 0)
            d_heads[stack, :] = jnp.where(head_lanes(grads.shape, head, False), grads, 0)
        dq[...] = jnp.zeros_like(dq)

        def step(j, diagonal):
            slots = pl.ds(pl.multiple_of(j * rows, rows), rows)
            mask = kdoc[slots, :] == qdoc[0]
            if diagonal:
                key = lax.broadcasted_iota(jnp.int32, (rows, rows), 0)
                query = lax.broadcasted_iota(jnp.int32, (rows, rows), 1)
                mask = (mask & (key < query)) | (key == query)
            total = dq[...]
            for head in range(heads):
                scores = dot(k[head, slots, :], qback[head], NT)
                probs = jnp.where(mask, jnp.exp(scores), 0.0)
                dprobs = dot(v[head, slots, :], dox[head], NT)
                dscores = (probs * dprobs).astype(BF16)
                stack = slice(head * rows, (head + 1) * rows)
                probs_all[:, stack] = probs.astype(BF16)
                scores_all[:, stack] = dscores
                total += dot(dscores, k_heads[head, slots, :], TN)
            dq[...] = total
            dv[slots, :] += dot(probs_all[...], d_heads[...])
            dk[slots, :] += dot(scores_all[...], q_heads[...])

        def earlier(j, carry):
            step(j, False)
            return carry

        lax.fori_loop(low[index], index, earlier, 0)
        step(index, True)

        raw, grad_gain = unrope(
            dq[...] * scale,
            queries.astype(F32) / gain[...],
            gain[...],
            rq[...],
            cosine[...],
            sine[...],
            sums[...],
        )
        gain_out[...] += grad_gain
        dq_low[pl.ds(pl.multiple_of(index * rows, rows), rows), :] = raw

    @pl.when(step_at >= steps)
    def _():
        index = step_at - steps
        slots = pl.ds(pl.multiple_of(index * rows, rows), rows)
        raw, grad_gain = unrope(
            dk[slots, :] * scale,
            k_pair[slots, :].astype(F32) / gain[...],
            gain[...],
            rk[...],
            cosine[...],
            sine[...],
            sums[...],
        )
        gain_out[...] += grad_gain
        together = jnp.concatenate([dq_low[slots, :], raw, dv[slots, :].astype(BF16)], axis=1)
        parts, part = weight.shape[:2]
        for member in range(parts):
            term_out[member] = dot(together, weight[member], NT).astype(BF16)
            product = dot(wide[member], together, TN)

            @pl.when(index == 0)
            def _():
                total_qkv[member] = product

            @pl.when(index > 0)
            def _():
                total_qkv[member] += product

        strip = STRIP
        first = low[steps] * (grad_resid.shape[0] // strip)
        for half in range(rows // strip):
            number = index * (rows // strip) + half - first

            @pl.when((number >= 0) & (number < grad_resid.shape[0] // strip))
            def _():
                at = pl.ds(half * strip, strip)
                own = pl.ds(pl.multiple_of(number * strip, strip), strip)
                for member in range(parts):
                    term_out[member, at, :] = (
                        term_out[member, at, :].astype(F32)
                        + grad_resid[own, member * part : (member + 1) * part].astype(F32)
                    ).astype(BF16)

        @pl.when(index == steps - 1)
        def _():
            grad_qkv[...] = total_qkv[...].astype(BF16)


def attend_back(
    low,
    qback,
    q_pair,
    dout,
    attended,
    k,
    k_pair,
    v,
    qdoc,
    kdoc,
    cosine,
    sine,
    rq,
    rk,
    gain,
    weight,
    place_plain,
    place_delta,
    sums,
    wide,
    grad_resid,
):
    heads, tokens, _ = k.shape
    block = qdoc.shape[2]
    width = heads * DK
    steps = tokens // block
    parts, part = weight.shape[:2]

    def whole(array):
        return pl.BlockSpec(array.shape, lambda i, low: (0,) * array.ndim)

    def now(i):
        return jnp.minimum(i, steps - 1)

    def after(i):
        return jnp.maximum(i - steps, 0)

    def both(i):
        return lax.rem(i, steps)

    def rows(columns, at):
        return pl.BlockSpec((block, columns), lambda i, low: (at(i), 0))

    return pl.pallas_call(
        attend_back_kernel,
        grid_spec=pltpu.PrefetchScalarGridSpec(
            num_scalar_prefetch=1,
            grid=(2 * steps,),
            in_specs=[
                pl.BlockSpec((heads, block, EXT), lambda i, low: (0, now(i), 0)),
                rows(width, now),
                rows(width, now),
                rows(width, now),
                whole(k),
                whole(k_pair),
                whole(v),
                pl.BlockSpec((1, 1, block), lambda i, low: (now(i), 0, 0)),
                whole(kdoc),
                rows(width // 2, both),
                rows(width // 2, both),
                rows(width // 2, now),
                rows(width // 2, after),
                whole(gain),
                whole(weight),
                whole(place_plain),
                whole(place_delta),
                whole(sums),
                pl.BlockSpec((parts, block, part), lambda i, low: (0, after(i), 0)),
                whole(grad_resid),
            ],
            out_specs=[
                pl.BlockSpec((parts, block, part), lambda i, low: (0, after(i), 0)),
                pl.BlockSpec((parts, part, 3 * width), lambda i, low: (0, 0, 0)),
                pl.BlockSpec((1, width), lambda i, low: (0, 0)),
            ],
            scratch_shapes=[
                pltpu.VMEM((tokens, width), F32),
                pltpu.VMEM((tokens, width), F32),
                pltpu.VMEM((block, width), F32),
                pltpu.VMEM((heads, block, EXT), BF16),
                pltpu.VMEM((heads * block, width), BF16),
                pltpu.VMEM((heads * block, width), BF16),
                pltpu.VMEM((heads, tokens, width), BF16),
                pltpu.VMEM((block, heads * block), BF16),
                pltpu.VMEM((block, heads * block), BF16),
                pltpu.VMEM((tokens, width), BF16),
                pltpu.VMEM((parts, part, 3 * width), F32),
            ],
        ),
        out_shape=[
            jax.ShapeDtypeStruct((parts, tokens, part), BF16),
            jax.ShapeDtypeStruct((parts, part, 3 * width), BF16),
            jax.ShapeDtypeStruct((1, width), F32),
        ],
        compiler_params=grid_params(1),
        cost_estimate=pl.CostEstimate(
            flops=80_000_000_000, bytes_accessed=30 << 20, transcendentals=0
        ),
        name="attend_back",
    )(
        low,
        qback,
        q_pair,
        dout,
        attended,
        k,
        k_pair,
        v,
        qdoc,
        kdoc,
        cosine,
        sine,
        rq,
        rk,
        gain,
        weight,
        place_plain,
        place_delta,
        sums,
        wide,
        grad_resid,
    )


def row_scale(value):
    return lax.rsqrt(jnp.sum(value * value, axis=-1, keepdims=True) + EPSILON)


def residual_backward(grad_out, result, resid, unit, alpha, branch_scale, mixed_scale):
    grad_mixed = mixed_scale * (
        grad_out - result * jnp.sum(grad_out * result, axis=-1, keepdims=True)
    )
    grad_alpha = jnp.sum(grad_mixed * (unit - resid), axis=0, keepdims=True)
    grad_unit = grad_mixed * alpha
    grad_branch = branch_scale * (
        grad_unit - unit * jnp.sum(grad_unit * unit, axis=-1, keepdims=True)
    )
    return grad_mixed * (1.0 - alpha), grad_branch, grad_alpha


STRIP = 256


def strips(rows):
    strip = min(STRIP, rows)
    return [pl.ds(start, strip) for start in range(0, rows, strip)]


def core_semaphores(count):
    return [pltpu.SemaphoreType.DMA((count,)), pltpu.SemaphoreType.DMA((count,))]


def greet_pair_and_line(size):
    me, core = lax.axis_index("mp"), lax.axis_index("core")
    for k in range(1, size):
        greet({"mp": flip(me, k)})
    greet({"core": 1 - core})
    pl.semaphore_wait(pltpu.get_barrier_semaphore(), size)


def output_matrix(packed_wo, whole):
    size, chips, rows, both = packed_wo.shape
    part = both // 2
    for chip in range(chips):
        for core in range(2):
            start = (2 * chip + core) * rows
            whole[:, start : start + rows, :] = packed_wo[
                :, chip, :, core * part : (core + 1) * part
            ]


def mix_kernel(
    size,
    attended,
    packed,
    wide,
    alpha,
    cotangent,
    x,
    middle_out,
    unit_out,
    branch_scale_out,
    mixed_scale_out,
    merged,
    full_wo,
    resid_out,
    cotangent_low,
    packed_wo,
    middle_low,
    resid,
    send,
    receive,
    local,
    own_sems,
    core_sent,
    core_got,
):
    me, core = lax.axis_index("mp"), lax.axis_index("core")
    mine, width = middle_out.shape
    part = width // size
    rows = packed_wo.shape[2]
    greet_pair_and_line(size)
    exchange = Exchange(
        size, attended, merged, row_part(mine), column_part(part), send, receive, local
    )
    exchange.start()
    own = [
        pltpu.make_async_copy(
            packed.at[:, :, pl.ds(packed.shape[2] - rows, rows), :], packed_wo, own_sems.at[0]
        )
    ]
    for member in range(size):
        own.append(
            pltpu.make_async_copy(
                wide.at[member, pl.ds(pl.multiple_of(me * mine, mine), mine), :],
                resid.at[:, pl.ds(member * part, part)],
                own_sems.at[1 + member],
            )
        )
    for copy in own:
        copy.start()
    for at in strips(cotangent.shape[0]):
        cotangent_low[at, :] = cotangent[at, :].astype(BF16)
    for copy in own:
        copy.wait()
    output_matrix(packed_wo, full_wo)
    resid_out[...] = resid[...]
    exchange.wait()

    swaps = []
    for order, at in enumerate(strips(mine)):
        branch = dot(merged[at, :part], full_wo[0], NT)
        for member in range(1, size):
            branch += dot(
                merged[at, member * part : (member + 1) * part], full_wo[member], NT
            )
        old = resid[at, :].astype(F32)
        branch_scale = row_scale(branch)
        unit = branch * branch_scale
        mixed = old + alpha[...] * (unit - old)
        mixed_scale = row_scale(mixed)
        middle = mixed * mixed_scale
        middle_out[at, :] = middle
        unit_out[at, :] = unit.astype(BF16)
        branch_scale_out[at, :] = branch_scale
        mixed_scale_out[at, :] = mixed_scale
        middle_low[at, :] = middle.astype(BF16)
        there = pl.ds(mine + at.start, at.size)
        swap = to_device(
            middle_low.at[at, :],
            x.at[there, :],
            core_sent.at[order],
            core_got.at[order],
            {"core": 1 - core},
        )
        swap.start()
        swaps.append(swap)
    keep = pltpu.make_async_copy(middle_low, x.at[pl.ds(0, mine), :], own_sems.at[0])
    keep.start()
    keep.wait()
    for swap in swaps:
        swap.wait()


def mix(attended, packed, rows, wide, alpha, cotangent, collective):
    size, slots, part = wide.shape
    chips = packed.shape[1]
    mine, width = slots // size, size * part
    vmem = pl.BlockSpec(memory_space=pltpu.VMEM)
    count = len(strips(mine))
    scale = jax.ShapeDtypeStruct((mine, 1), F32)
    return pl.pallas_call(
        functools.partial(mix_kernel, size),
        in_specs=[ANY, ANY, ANY, vmem, vmem],
        out_specs=[ANY, *[vmem] * 8],
        out_shape=[
            jax.ShapeDtypeStruct((2 * mine, width), BF16),
            jax.ShapeDtypeStruct((mine, width), F32),
            jax.ShapeDtypeStruct((mine, width), BF16),
            scale,
            scale,
            jax.ShapeDtypeStruct((mine, width), BF16),
            jax.ShapeDtypeStruct((size, width, part), BF16),
            jax.ShapeDtypeStruct((mine, width), BF16),
            jax.ShapeDtypeStruct((slots, part), BF16),
        ],
        scratch_shapes=[
            pltpu.VMEM((size, chips, rows, 2 * part), BF16),
            pltpu.VMEM((mine, width), BF16),
            pltpu.VMEM((mine, width), BF16),
            *exchange_semaphores(size),
            pltpu.SemaphoreType.DMA((1 + size,)),
            *core_semaphores(count),
        ],
        compiler_params=remote_params(collective),
        name="mix",
    )(attended, packed, wide, alpha, cotangent)


def whole_matrix(ref):
    _, chips, rows, units = ref.shape
    return ref[...].reshape(chips * rows, units)


def first_step():
    return (pl.program_id(0) == 0) & (pl.program_id(1) == 0)


def last_step():
    return (pl.program_id(0) == pl.num_programs(0) - 1) & (
        pl.program_id(1) == pl.num_programs(1) - 1
    )


def swap_cores(source, target, sems):
    return to_device(
        source, target, sems[0], sems[1], {"core": 1 - lax.axis_index("core")}
    )


def feed_kernel(
    size,
    x,
    w_up,
    w_gate,
    w_down,
    s_u,
    s_v,
    cotangent,
    middle,
    alpha,
    up_out,
    gate_out,
    units_out,
    result_out,
    grad_middle,
    dbranch,
    grad_alpha,
    acc,
    given,
    got,
    spread,
    low,
    send,
    receive,
    local,
    core_sent,
    core_got,
    keep_sems,
):
    exchange = Exchange(
        size,
        cotangent,
        spread,
        row_part(spread.shape[0]),
        column_part(cotangent.shape[1]),
        send,
        receive,
        local,
    )
    branch_swap = swap_cores(given, got, (core_sent.at[0], core_got.at[0]))

    @pl.when(first_step())
    def _():
        greet_pair_and_line(size)
        exchange.start()

    block, part = pl.program_id(0), pl.program_id(1)
    up = dot(x[...], whole_matrix(w_up))
    gate = dot(x[...], whole_matrix(w_gate))
    up_out[0] = up.astype(BF16)
    gate_out[0] = gate.astype(BF16)
    scaled = gate * s_v[0]
    units = (up * s_u[0] * (scaled / (1.0 + jnp.exp(-scaled)))).astype(BF16)
    units_out[0] = units
    term = dot(units, whole_matrix(w_down), NT)

    @pl.when(part == 0)
    def _():
        acc[...] = term

    @pl.when(part > 0)
    def _():
        acc[...] += term

    last = part == pl.num_programs(1) - 1

    @pl.when(last & (block == 0))
    def _():
        given[...] = acc[...].astype(BF16)
        branch_swap.start()

    @pl.when(last & (block == 1))
    def _():
        mine = acc.shape[0]
        branch_swap.wait()
        exchange.wait()
        swaps = []
        for order, at in enumerate(strips(mine)):
            branch = acc[at, :] + got[at, :].astype(F32)
            branch_scale = row_scale(branch)
            unit = branch * branch_scale
            old = middle[at, :]
            mixed = old + alpha[...] * (unit - old)
            mixed_scale = row_scale(mixed)
            result = mixed * mixed_scale
            result_out[at, :] = result.astype(BF16)
            grad_old, grad_branch, part_alpha = residual_backward(
                spread[at, :].astype(F32),
                result,
                old,
                unit,
                alpha[...],
                branch_scale,
                mixed_scale,
            )
            grad_middle[at, :] = grad_old
            if order == 0:
                grad_alpha[...] = part_alpha
            else:
                grad_alpha[...] += part_alpha
            low[at, :] = grad_branch.astype(BF16)
            there = pl.ds(mine + at.start, at.size)
            swaps.append(
                swap_cores(
                    low.at[at, :],
                    dbranch.at[there, :],
                    (core_sent.at[1 + order], core_got.at[1 + order]),
                )
            )
            swaps.append(
                pltpu.make_async_copy(low.at[at, :], dbranch.at[at, :], keep_sems.at[order])
            )
            swaps[-2].start()
            swaps[-1].start()
        for swap in swaps:
            swap.wait()


def packed_specs(packed, width):
    _, chips, _, units = packed.shape
    return [
        pl.BlockSpec((1, chips, width // chips, units), lambda t, m, w=w: (m, 0, w, 0))
        for w in range(3)
    ]


def feed(x, packed, s_u, s_v, cotangent, middle, alpha, collective):
    tokens, width = x.shape
    parts, _, _, units = packed.shape
    size = parts
    block = tokens // 2
    rows = pl.BlockSpec((block, width), lambda t, m: (1 - t, 0))
    vector = pl.BlockSpec((1, 1, units), lambda t, m: (m, 0, 0))
    piece = pl.BlockSpec((1, block, units), lambda t, m: (m, 1 - t, 0))
    vmem = pl.BlockSpec(memory_space=pltpu.VMEM)
    hidden = jax.ShapeDtypeStruct((parts, tokens, units), BF16)
    count = len(strips(block))
    low = pltpu.VMEM((block, width), BF16)
    return pl.pallas_call(
        functools.partial(feed_kernel, size),
        grid=(2, parts),
        in_specs=[rows, *packed_specs(packed, width), vector, vector, ANY, vmem, vmem],
        out_specs=[piece, piece, piece, vmem, vmem, ANY, vmem],
        out_shape=[
            hidden,
            hidden,
            hidden,
            jax.ShapeDtypeStruct((block, width), BF16),
            jax.ShapeDtypeStruct((block, width), F32),
            jax.ShapeDtypeStruct((tokens, width), BF16),
            jax.ShapeDtypeStruct((1, width), F32),
        ],
        scratch_shapes=[
            pltpu.VMEM((block, width), F32),
            low,
            low,
            low,
            low,
            *exchange_semaphores(size),
            *core_semaphores(1 + count),
            pltpu.SemaphoreType.DMA((count,)),
        ],
        compiler_params=remote_params(collective),
        cost_estimate=pl.CostEstimate(
            flops=6 * tokens * width * parts * units, bytes_accessed=60 << 20, transcendentals=0
        ),
        name="feed",
    )(x, packed, packed, packed, s_u, s_v, cotangent, middle, alpha)


def feed_back_kernel(
    size,
    dbranch,
    w_up,
    w_gate,
    w_down,
    s_u,
    s_v,
    up_in,
    gate_in,
    result,
    grad_middle,
    middle,
    resid,
    unit,
    branch_scale,
    mixed_scale,
    alpha,
    full_wo,
    dup_out,
    dgate_out,
    grad_u,
    grad_v,
    spread,
    grad_resid,
    dbranch_attn,
    dmerged,
    grad_alpha,
    acc,
    given,
    got,
    sum_u,
    sum_v,
    send,
    receive,
    local,
    core_sent,
    core_got,
):
    exchange = Exchange(
        size,
        result,
        spread,
        column_part(spread.shape[1]),
        row_part(result.shape[0]),
        send,
        receive,
        local,
    )
    dx_swap = swap_cores(given, got, (core_sent.at[0], core_got.at[0]))

    @pl.when(first_step())
    def _():
        greet_pair_and_line(size)
        exchange.start()

    block, part = pl.program_id(0), pl.program_id(1)
    dunits = dot(dbranch[...], whole_matrix(w_down))
    up = up_in[0].astype(F32)
    gate = gate_in[0].astype(F32)
    scaled = gate * s_v[0]
    sigmoid = 1.0 / (1.0 + jnp.exp(-scaled))
    silu = scaled * sigmoid
    slope = sigmoid * (1.0 + scaled - silu)
    through_up = dunits * silu
    through_gate = dunits * up * s_u[0] * slope
    dup = (through_up * s_u[0]).astype(BF16)
    dgate = (through_gate * s_v[0]).astype(BF16)
    dup_out[0] = dup
    dgate_out[0] = dgate
    term = dot(dup, whole_matrix(w_up), NT) + dot(dgate, whole_matrix(w_gate), NT)
    part_u = jnp.sum(through_up * up, axis=0, keepdims=True)
    part_v = jnp.sum(through_gate * gate, axis=0, keepdims=True)

    @pl.when(block == 0)
    def _():
        sum_u[part] = part_u
        sum_v[part] = part_v

    @pl.when(block > 0)
    def _():
        sum_u[part] += part_u
        sum_v[part] += part_v

    @pl.when(part == 0)
    def _():
        acc[...] = term

    @pl.when(part > 0)
    def _():
        acc[...] += term

    last = part == pl.num_programs(1) - 1

    @pl.when(last & (block == 0))
    def _():
        given[...] = acc[...].astype(BF16)
        dx_swap.start()

    @pl.when(last & (block == 1))
    def _():
        grad_u[...] = sum_u[...]
        grad_v[...] = sum_v[...]
        dx_swap.wait()
        for order, at in enumerate(strips(acc.shape[0])):
            grad_old, grad_branch, part_alpha = residual_backward(
                grad_middle[at, :] + acc[at, :] + got[at, :].astype(F32),
                middle[at, :],
                resid[at, :].astype(F32),
                unit[at, :].astype(F32),
                alpha[...],
                branch_scale[at, :],
                mixed_scale[at, :],
            )
            grad_resid[at, :] = grad_old.astype(BF16)
            if order == 0:
                grad_alpha[...] = part_alpha
            else:
                grad_alpha[...] += part_alpha
            low = grad_branch.astype(BF16)
            dbranch_attn[at, :] = low
            columns = full_wo.shape[2]
            for member in range(size):
                dmerged[at, member * columns : (member + 1) * columns] = dot(
                    low, full_wo[member]
                ).astype(BF16)
        exchange.wait()


def feed_back(
    dbranch,
    packed,
    s_u,
    s_v,
    up,
    gate,
    result,
    grad_middle,
    middle,
    resid,
    unit,
    branch_scale,
    mixed_scale,
    alpha,
    full_wo,
    collective,
):
    tokens, width = dbranch.shape
    parts, _, _, units = packed.shape
    size = parts
    block = tokens // 2
    rows = pl.BlockSpec((block, width), lambda t, m: (1 - t, 0))
    vector = pl.BlockSpec((1, 1, units), lambda t, m: (m, 0, 0))
    piece = pl.BlockSpec((1, block, units), lambda t, m: (m, 1 - t, 0))
    vmem = pl.BlockSpec(memory_space=pltpu.VMEM)
    hidden = jax.ShapeDtypeStruct((parts, tokens, units), BF16)
    sums = jax.ShapeDtypeStruct((parts, 1, units), F32)
    state = jax.ShapeDtypeStruct((block, width), BF16)
    return pl.pallas_call(
        functools.partial(feed_back_kernel, size),
        grid=(2, parts),
        in_specs=[
            rows,
            *packed_specs(packed, width),
            vector,
            vector,
            piece,
            piece,
            ANY,
            *[vmem] * 8,
        ],
        out_specs=[piece, piece, vmem, vmem, ANY, vmem, vmem, vmem, vmem],
        out_shape=[
            hidden,
            hidden,
            sums,
            sums,
            jax.ShapeDtypeStruct((size * block, width // size), BF16),
            state,
            state,
            state,
            jax.ShapeDtypeStruct((1, width), F32),
        ],
        scratch_shapes=[
            pltpu.VMEM((block, width), F32),
            pltpu.VMEM((block, width), BF16),
            pltpu.VMEM((block, width), BF16),
            pltpu.VMEM((parts, 1, units), F32),
            pltpu.VMEM((parts, 1, units), F32),
            *exchange_semaphores(size),
            *core_semaphores(1),
        ],
        compiler_params=remote_params(collective),
        cost_estimate=pl.CostEstimate(
            flops=6 * tokens * width * parts * units, bytes_accessed=70 << 20, transcendentals=0
        ),
        name="feed_back",
    )(
        dbranch,
        packed,
        packed,
        packed,
        s_u,
        s_v,
        up,
        gate,
        result,
        grad_middle,
        middle,
        resid,
        unit,
        branch_scale,
        mixed_scale,
        alpha,
        full_wo,
    )


def feed_grads_kernel(
    size,
    x,
    dbranch,
    dup,
    dgate,
    units,
    dbranch_attn,
    merged,
    dmerged,
    grads,
    grad_wo,
    dattended,
    x_turned,
    d_turned,
    attn_turned,
    send,
    receive,
    local,
):
    exchange = Exchange(
        size,
        dmerged,
        dattended,
        column_part(dattended.shape[1]),
        row_part(dmerged.shape[0]),
        send,
        receive,
        local,
    )

    @pl.when(first_step())
    def _():
        greet_all(size)
        exchange.start()
        x_turned[...] = x[...].T
        d_turned[...] = dbranch[...].T
        attn_turned[...] = dbranch_attn[...].T

    _, chips, rows, _ = grads.shape
    for which, left, right in (
        (0, x_turned, dup),
        (1, x_turned, dgate),
        (2, d_turned, units),
    ):

        @pl.when(pl.program_id(0) == which)
        def _():
            total = dot(left[...], right[0])
            grads[0] = total.astype(BF16).reshape(chips, rows, total.shape[1])

    @pl.when(pl.program_id(0) == 3)
    def _():
        total = dot(attn_turned[...], merged[...])
        grad_wo[...] = total.astype(BF16).reshape(grad_wo.shape)

    @pl.when(last_step())
    def _():
        exchange.wait()


def feed_grads(
    x, dbranch, dup, dgate, units_in, dbranch_attn, merged, dmerged, chips, collective
):
    tokens, width = x.shape
    parts, _, units = dup.shape
    size = parts
    rows = width // chips
    mine = dmerged.shape[0]
    part = width // size

    def whole(array):
        return pl.BlockSpec(array.shape, lambda w, m: (0, 0))

    def turn(w, m, which):
        return jnp.where(w == which, m, jnp.where(w < which, 0, parts - 1))

    def piece(which):
        return pl.BlockSpec((1, tokens, units), lambda w, m: (turn(w, m, which), 0, 0))

    return pl.pallas_call(
        functools.partial(feed_grads_kernel, size),
        grid=(4, parts),
        in_specs=[
            whole(x),
            whole(dbranch),
            piece(0),
            piece(1),
            piece(2),
            whole(dbranch_attn),
            pl.BlockSpec((mine, part), lambda w, m: (0, turn(w, m, 3))),
            ANY,
        ],
        out_specs=[
            pl.BlockSpec(
                (1, chips, rows, units),
                lambda w, m: (jnp.where(w < 3, m, parts - 1), 0, jnp.minimum(w, 2), 0),
            ),
            pl.BlockSpec(
                (1, chips, 2, rows // 2, part), lambda w, m: (turn(w, m, 3), 0, 0, 0, 0)
            ),
            ANY,
        ],
        out_shape=[
            jax.ShapeDtypeStruct((parts, chips, 3 * rows, units), BF16),
            jax.ShapeDtypeStruct((parts, chips, 2, rows // 2, part), BF16),
            jax.ShapeDtypeStruct((size * mine, part), BF16),
        ],
        scratch_shapes=[
            pltpu.VMEM((width, tokens), BF16),
            pltpu.VMEM((width, tokens), BF16),
            pltpu.VMEM((width, mine), BF16),
            *exchange_semaphores(size),
        ],
        compiler_params=remote_params(collective),
        cost_estimate=pl.CostEstimate(
            flops=6 * tokens * width * parts * units, bytes_accessed=40 << 20, transcendentals=0
        ),
        name="feed_grads",
    )(x, dbranch, dup, dgate, units_in, dbranch_attn, merged, dmerged)


def rope_tables(positions, head_size):
    half_size = head_size // 2
    freq_index = jnp.arange(half_size, dtype=F32)
    inverse = jnp.exp(freq_index * (-2.0 * math.log(ROPE_BASE) / head_size))
    angles = positions.astype(F32)[..., None] * inverse
    return (jnp.cos(angles), jnp.sin(angles))


def document_starts(doc_ids):
    slot_index = jnp.arange(doc_ids.shape[-1], dtype=jnp.int32)
    earlier = jnp.concatenate([doc_ids[..., :1] - 1, doc_ids[..., :-1]], axis=-1)
    starts = jnp.where(doc_ids != earlier, slot_index, jnp.zeros_like(slot_index))
    return lax.cummax(starts, axis=starts.ndim - 1)


def other_core(value):
    return lax.ppermute(value, "core", [(0, 1), (1, 0)])


def make_on_device(chips, size):
    def on_device(
        hidden,
        wq,
        wk,
        wv,
        wo,
        w_up,
        w_gate,
        w_down,
        s_qk,
        s_u,
        s_v,
        alpha_a,
        alpha_m,
        doc_ids,
        valid,
        cotangent,
    ):
        _, slots, part = hidden.shape
        width = part * size
        heads = s_qk.shape[0] // DK
        rows = wq.shape[0]
        units = w_up.shape[1] // 2
        mine = slots // size
        block = min(512, slots)
        me = lax.axis_index("mp")
        core = lax.axis_index("core")

        place = paired_place(heads)
        in_pairs = (
            lambda w: w.reshape(w.shape[0], heads, 2, HALF)
            .transpose(0, 2, 1, 3)
            .reshape(w.shape[0], heads * DK)
        )
        low_qkv = jnp.concatenate([in_pairs(wq), in_pairs(wk), wv], axis=1).astype(BF16)
        stacked = jnp.stack([w_up, w_gate, w_down.T]).astype(BF16).reshape(3, rows, 2, units)
        keep = lax.dynamic_index_in_dim(stacked, core, 2, keepdims=False)
        give = lax.dynamic_index_in_dim(stacked, 1 - core, 2, keepdims=False)
        low_wo = wo.astype(BF16).T
        wide_wo = jnp.concatenate([low_wo, low_wo], axis=1)
        given = jnp.concatenate([give.reshape(3 * rows, units), wide_wo])
        got = other_core(given)

        def in_order(own, other):
            return jnp.where(core == 0, jnp.stack([own, other], 1), jnp.stack([other, own], 1))

        pair = in_order(keep, got[: 3 * rows].reshape(3, rows, units))
        lane = jnp.arange(2 * part) // part
        pair_wo = jnp.where(lane == core, wide_wo, got[3 * rows :])
        packed = jnp.concatenate([pair.reshape(6 * rows, units), pair_wo])
        vectors = jnp.concatenate([s_u, s_v * math.sqrt(width), alpha_a, alpha_m])
        wide, full_qkv, packed, vectors = gather_all(
            hidden[0].astype(BF16), low_qkv, packed, vectors[None], size, chips, 0
        )
        full_qkv = full_qkv.reshape(size, part, 3 * part)
        vectors = vectors[:, 0]
        s_up = lax.dynamic_slice_in_dim(vectors[:, : 2 * units], core * units, units, 1)
        s_gate = lax.dynamic_slice_in_dim(
            vectors[:, 2 * units : 4 * units], core * units, units, 1
        )
        s_up = s_up[:, None, :]
        s_gate = s_gate[:, None, :]
        alpha_attn = vectors[:, 4 * units : 4 * units + part].reshape(1, width)
        alpha_mlp = vectors[:, 4 * units + part :].reshape(1, width)

        docs = doc_ids[0]
        starts = document_starts(docs)
        slot = jnp.arange(slots, dtype=jnp.int32)
        cosine, sine = rope_tables(slot - starts, DK)
        cosine = jnp.tile(cosine, (1, heads))
        sine = jnp.tile(sine, (1, heads))
        low = jnp.concatenate([starts[::block] // block, me[None]])
        key_docs = jnp.where(valid[0] == 1, docs, -1)
        to_pair = placing_matrix(place, heads)
        to_plain = placing_matrix(np.arange(heads * DK), heads)
        place_pair = jnp.asarray(to_pair, BF16)
        place_plain = jnp.asarray(to_plain, BF16)
        place_delta = jnp.asarray(delta_matrix(heads), BF16)
        collect_plain = jnp.asarray(to_plain.T.reshape(heads, EXT, heads * DK), BF16)
        sums = jnp.asarray(head_sum_matrix(heads), BF16)
        gain = in_pairs(s_qk[None, :])

        q, k, v, q_pair, k_pair, rq, rk = project(
            wide, full_qkv, cosine, sine, gain, place_pair, place_plain, sums
        )
        attended, qback = attend(
            low,
            q,
            k,
            v,
            docs[:, None],
            key_docs.reshape(slots // block, 1, block),
            collect_plain,
        )
        (
            x,
            middle,
            unit,
            branch_scale,
            mixed_scale,
            merged,
            full_wo,
            resid,
            cotangent_low,
        ) = mix(attended, packed, rows, wide, alpha_attn, cotangent[0], 1)

        up, gate, hidden_units, result, grad_middle, dbranch, grad_alpha_mlp = feed(
            x, packed, s_up, s_gate, cotangent_low, middle, alpha_mlp, 2
        )
        (
            dup,
            dgate,
            grad_u,
            grad_v,
            out_low,
            grad_resid,
            dbranch_attn,
            dmerged,
            grad_alpha_attn,
        ) = feed_back(
            dbranch,
            packed,
            s_up,
            s_gate,
            up,
            gate,
            result,
            grad_middle,
            middle,
            resid,
            unit,
            branch_scale,
            mixed_scale,
            alpha_attn,
            full_wo,
            3,
        )
        out_hidden = out_low.astype(F32)
        grads, grad_wo, dattended = feed_grads(
            x, dbranch, dup, dgate, hidden_units, dbranch_attn, merged, dmerged, chips, 4
        )

        term, grad_qkv, grad_gain = attend_back(
            low,
            qback,
            q_pair,
            dattended,
            attended,
            k,
            k_pair,
            v,
            docs.reshape(slots // block, 1, block),
            key_docs[:, None],
            cosine,
            sine,
            rq,
            rk,
            gain,
            full_qkv,
            place_plain,
            place_delta,
            sums,
            wide,
            grad_resid,
        )
        out_pairs = (
            lambda w: w.reshape(w.shape[0], 2, heads, HALF)
            .transpose(0, 2, 1, 3)
            .reshape(w.shape[0], heads * DK)
        )

        zero = jnp.zeros((size, 2, units), F32)
        placed_u = lax.dynamic_update_slice(zero, grad_u, (0, core, 0))
        placed_v = lax.dynamic_update_slice(zero, grad_v * math.sqrt(width), (0, core, 0))
        placed_qk = lax.dynamic_update_slice(
            jnp.zeros((size, part), F32), out_pairs(grad_gain), (me, 0)
        )
        placed = jnp.concatenate(
            [
                placed_u.reshape(size, 2 * units),
                placed_v.reshape(size, 2 * units),
                placed_qk,
                grad_alpha_attn.reshape(size, part),
                grad_alpha_mlp.reshape(size, part),
            ],
            axis=1,
        )
        grad_hidden, owned, owned_output, owned_qkv, summed = sum_all(
            term,
            grads,
            grad_wo,
            grad_qkv.reshape(chips, 2, rows, 3 * part),
            placed[:, None],
            chips,
            5,
        )
        owned_upward, owned_gating, owned_downward = owned[0], owned[1], owned[2].T
        owned_output = owned_output.T
        owned_query = out_pairs(owned_qkv[:, :part])
        owned_keys = out_pairs(owned_qkv[:, part : 2 * part])
        owned_values = owned_qkv[:, 2 * part :]
        bounds = [2 * units, 4 * units, 4 * units + part, 4 * units + 2 * part]
        summed_up, summed_gate, summed_qk, summed_attn, summed_mlp = jnp.split(
            summed[0], bounds
        )
        return (
            out_hidden[None],
            grad_hidden[None],
            owned_query,
            owned_keys,
            owned_values,
            owned_output,
            owned_upward,
            owned_gating,
            owned_downward,
            summed_qk,
            summed_up,
            summed_gate,
            summed_attn,
            summed_mlp,
        )

    return on_device


def solution(mesh):
    rows, size = mesh.shape["dp"], mesh.shape["mp"]
    paired = Mesh(mesh.devices.reshape(rows // 2, 2, size), ("chip", "core", "mp"))
    return jax.shard_map(
        make_on_device(rows // 2, size),
        mesh=paired,
        in_specs=(
            P(DP, None, "mp"),
            P(DP, "mp"),
            P(DP, "mp"),
            P(DP, "mp"),
            P("mp", DP),
            P(DP, "mp"),
            P(DP, "mp"),
            P("mp", DP),
            P("mp"),
            P("mp"),
            P("mp"),
            P("mp"),
            P("mp"),
            P(DP, None),
            P(DP, None),
            P(DP, None, "mp"),
        ),
        out_specs=(
            P(DP, None, "mp"),
            P(DP, None, "mp"),
            P(DP, "mp"),
            P(DP, "mp"),
            P(DP, "mp"),
            P("mp", DP),
            P(DP, "mp"),
            P(DP, "mp"),
            P("mp", DP),
            P("mp"),
            P("mp"),
            P("mp"),
            P("mp"),
            P("mp"),
        ),
        check_vma=False,
    )
```

```python
import functools
import math

import jax
import jax.numpy as jnp
import numpy as np
from jax import lax
from jax.experimental import pallas as pl
from jax.experimental.pallas import tpu as pltpu
from jax.sharding import Mesh
from jax.sharding import PartitionSpec as P

DK = 64
HALF = DK // 2
EXT = 128
EPSILON = 1e-06
ROPE_BASE = 10000.0
VMEM_LIMIT = 60 * 1024 * 1024
F32 = jnp.float32
BF16 = jnp.bfloat16
DP = ("chip", "core")


def dot(left, right, dims=((1,), (0,)), precision=None):
    return lax.dot_general(
        left, right, (dims, ((), ())), precision=precision, preferred_element_type=F32
    )


NT = ((1,), (1,))
TN = ((0,), (0,))


def grid_params(dims):
    return pltpu.CompilerParams(
        dimension_semantics=("arbitrary",) * dims, vmem_limit_bytes=VMEM_LIMIT
    )


ANY = pl.BlockSpec(memory_space=pl.ANY)


def remote_params(collective, **more):
    return pltpu.CompilerParams(
        collective_id=collective,
        has_side_effects=True,
        vmem_limit_bytes=VMEM_LIMIT,
        **more,
    )


def to_device(source, target, send, receive, where):
    return pltpu.make_async_remote_copy(
        src_ref=source,
        dst_ref=target,
        send_sem=send,
        recv_sem=receive,
        device_id=where,
        device_id_type=pl.DeviceIdType.MESH,
    )


def to_member(source, target, send, receive, member):
    return to_device(source, target, send, receive, {"mp": member})


def flip(index, mask):
    bit = 1
    while bit <= mask:
        if mask & bit:
            index = index + bit - 2 * bit * lax.rem(lax.div(index, bit), 2)
        bit *= 2
    return index


def bits_below(count):
    return [1 << k for k in range(count.bit_length() - 1)]


def greet(where):
    pl.semaphore_signal(
        pltpu.get_barrier_semaphore(),
        inc=1,
        device_id=where,
        device_id_type=pl.DeviceIdType.MESH,
    )


def greet_all(size):
    me = lax.axis_index("mp")
    for k in range(1, size):
        greet({"mp": flip(me, k)})
    pl.semaphore_wait(pltpu.get_barrier_semaphore(), size - 1)


def greet_around(size, chips):
    me, chip, core = (lax.axis_index(name) for name in ("mp", "chip", "core"))
    for k in range(1, size):
        greet({"mp": flip(me, k)})
    for bit in bits_below(chips):
        greet({"chip": flip(chip, bit)})
    greet({"core": 1 - core})
    pl.semaphore_wait(pltpu.get_barrier_semaphore(), size + len(bits_below(chips)))


class Exchange:
    def __init__(self, size, source, target, piece, place, send, receive, local):
        me = lax.axis_index("mp")
        self.local = pltpu.make_async_copy(piece(source, me), place(target, me), local)
        self.remote = [
            to_member(
                piece(source, flip(me, k)),
                place(target, me),
                send.at[k],
                receive.at[k],
                flip(me, k),
            )
            for k in range(1, size)
        ]

    def start(self):
        for copy in self.remote:
            copy.start()
        self.local.start()

    def wait(self):
        self.local.wait()
        for copy in self.remote:
            copy.wait()


def exchange_semaphores(size):
    return [
        pltpu.SemaphoreType.DMA((size,)),
        pltpu.SemaphoreType.DMA((size,)),
        pltpu.SemaphoreType.DMA,
    ]


def row_part(rows):
    return lambda ref, j: ref.at[pl.ds(pl.multiple_of(j * rows, rows), rows), :]


def column_part(columns):
    return lambda ref, j: ref.at[:, pl.ds(pl.multiple_of(j * columns, columns), columns)]


class Gather:
    def __init__(self, block, index, bits, where, send, receive):
        self.block, self.index, self.bits, self.where = block, index, bits, where
        self.send, self.receive = send, receive

    def copies(self, stage, incoming):
        span = [0]
        for bit in self.bits[:stage]:
            span += [held | bit for held in span]
        bit = self.bits[stage]
        for order, held in enumerate(span):
            ref = self.block(flip(self.index, held | bit if incoming else held))
            slot = (1 << stage) - 1 + order
            yield to_device(
                ref,
                ref,
                self.send(slot),
                self.receive(slot),
                self.where(flip(self.index, bit)),
            )

    def start(self, stage):
        if stage < len(self.bits):
            for copy in self.copies(stage, False):
                copy.start()

    def arrive(self, stage):
        if stage < len(self.bits):
            for copy in self.copies(stage, True):
                copy.wait_recv()

    def close(self):
        for stage in range(len(self.bits)):
            for copy in self.copies(stage, False):
                copy.wait_send()


def front_kernel(
    size,
    chips,
    chunks,
    split,
    hidden,
    wq,
    wk,
    wv,
    wo,
    w_up,
    w_gate,
    w_down,
    vectors,
    positions,
    frequency,
    gain,
    in_pairs,
    place_pair,
    place_plain,
    sums,
    wide_out,
    qkv_out,
    full,
    full_vectors,
    q_out,
    k_out,
    v_out,
    q_pair_out,
    k_pair_out,
    rq_out,
    rk_out,
    cosine_out,
    sine_out,
    wide,
    full_qkv,
    packed,
    matrices,
    wo_turned,
    q,
    k,
    v,
    q_pair,
    k_pair,
    rq,
    rk,
    cosine,
    sine,
    local,
    out_sems,
    core_sent,
    core_got,
    hidden_up,
    hidden_down,
    hidden_got,
    packed_up,
    packed_down,
    packed_got,
    plane_sent,
    plane_got,
    qkv_sent,
    qkv_got,
    vector_sent,
    vector_got,
):
    me, chip, core = (lax.axis_index(name) for name in ("mp", "chip", "core"))
    tokens, part = hidden.shape
    rows = tokens // chunks
    height, units = packed.shape
    lines = height // 7
    owner = chip * 2 + core
    bits = bits_below(chips)
    stages = len(bits)
    greet_around(size, chips)

    matrices[0] = w_up[...].astype(BF16)
    matrices[1] = w_gate[...].astype(BF16)
    matrices[2] = w_down[...].T.astype(BF16)
    wo_turned[...] = wo[...].T.astype(BF16)

    def half_of(which):
        return pl.ds(pl.multiple_of(which * units, units), units)

    def place_of(matrix):
        return pl.ds(pl.multiple_of((2 * matrix + core) * lines, lines), lines)

    wo_place = (
        pl.ds(6 * lines, lines),
        pl.ds(pl.multiple_of(core * part, part), part),
    )
    given = [
        to_device(
            matrices.at[matrix, :, half_of(1 - core)],
            packed.at[place_of(matrix), :],
            core_sent.at[matrix],
            core_got.at[matrix],
            {"core": 1 - core},
        )
        for matrix in range(3)
    ]
    given.append(
        to_device(
            wo_turned, packed.at[wo_place], core_sent.at[3], core_got.at[3], {"core": 1 - core}
        )
    )
    for copy in given:
        copy.start()
    for matrix in range(3):
        packed[place_of(matrix), :] = matrices[matrix, :, half_of(core)]
    packed[wo_place] = wo_turned[...]
    full_qkv[owner] = jnp.concatenate(
        [
            dot(wq[...].astype(BF16), in_pairs[...]).astype(BF16),
            dot(wk[...].astype(BF16), in_pairs[...]).astype(BF16),
            wv[...].astype(BF16),
        ],
        axis=1,
    )

    def hidden_hop(origin, chunk, member, send):
        at = pl.ds(pl.multiple_of(chunk * rows, rows), rows)
        ref = wide.at[origin, at, :]
        return to_member(ref, ref, send.at[origin, chunk], hidden_got.at[origin, chunk], member)

    def packed_hop(origin, ref, member, send):
        return to_member(
            ref, full.at[origin, chip], send.at[origin], packed_got.at[origin], member
        )

    vector_copies = [
        to_member(
            vectors, full_vectors.at[me], vector_sent.at[k], vector_got.at[k], flip(me, k)
        )
        for k in range(1, size)
    ]

    def plane(origin, slot):
        return [
            Gather(
                lambda i, at=at: full.at[origin, i, at, :],
                chip,
                order,
                lambda i: {"chip": i},
                lambda k, half=half: plane_sent.at[slot, half, k],
                lambda k, half=half: plane_got.at[slot, half, k],
            )
            for half, (at, order) in enumerate(
                (
                    (pl.ds(0, split), bits),
                    (pl.ds(split, height - split), bits[::-1]),
                )
            )
        ]

    gather_qkv = Gather(
        lambda i: full_qkv.at[i],
        owner,
        [2 * bit for bit in bits] + [1],
        lambda i: {"chip": lax.div(i, 2), "core": lax.rem(i, 2)},
        lambda k: qkv_sent.at[k],
        lambda k: qkv_got.at[k],
    )

    sources = {0: [(me >= 0, me, 0, None)]}
    for distance in range(1, size):
        sources[distance] = [
            (me >= distance, me - distance, 2 * distance - 1, True),
            (me + distance < size, me + distance, 2 * distance, False),
        ]

    def pass_on(origin, ref, upward):
        if upward is not False:

            @pl.when(me < size - 1)
            def _():
                packed_hop(origin, ref, me + 1, packed_up).start()

        if not upward:

            @pl.when(me > 0)
            def _():
                packed_hop(origin, ref, me - 1, packed_down).start()

    def advance(distance, stage):
        for exists, origin, slot, _ in sources[distance]:

            @pl.when(exists)
            def _():
                for half in plane(origin, slot):
                    half.arrive(stage)
                    half.start(stage + 1)

    for copy in given:
        copy.wait_recv()
    pass_on(me, packed, None)
    own = [
        pltpu.make_async_copy(packed, full.at[me, chip], local.at[0]),
        pltpu.make_async_copy(vectors, full_vectors.at[me], local.at[1]),
    ]
    for copy in own:
        copy.start()
    gather_qkv.start(0)
    for copy in vector_copies:
        copy.start()
    for chunk in range(chunks):
        at = pl.ds(chunk * rows, rows)
        wide[me, at, :] = hidden[at, :].astype(BF16)
    own[0].wait()
    for half in plane(me, 0):
        half.start(0)
    for chunk in range(chunks):
        at = pl.ds(chunk * rows, rows)
        angles = positions[at, :] * frequency[...]
        cosine[at, :] = jnp.cos(angles)
        sine[at, :] = jnp.sin(angles)
    for stage in range(stages):
        gather_qkv.arrive(stage)
        gather_qkv.start(stage + 1)
    advance(0, 0)
    for distance in range(1, size):
        for exists, origin, slot, upward in sources[distance]:

            @pl.when(exists)
            def _():
                block = full.at[origin, chip]
                packed_hop(origin, block, me, packed_up).wait_recv()
                pass_on(origin, block, upward)
                for half in plane(origin, slot):
                    half.start(0)

        @pl.when(jnp.maximum(me, size - 1 - me) == distance)
        def _():
            for chunk in range(chunks):

                @pl.when(me < size - 1)
                def _():
                    hidden_hop(me, chunk, me + 1, hidden_up).start()

                @pl.when(me > 0)
                def _():
                    hidden_hop(me, chunk, me - 1, hidden_down).start()

        if distance > 1:
            advance(distance - 1, 0)
    gather_qkv.arrive(stages)
    qkv_copy = pltpu.make_async_copy(full_qkv, qkv_out, local.at[2])
    qkv_copy.start()
    advance(size - 1, 0)

    def come(distance, chunk):
        for exists, origin, _, upward in sources[distance]:

            @pl.when(exists)
            def _():
                hidden_hop(origin, chunk, me, hidden_up).wait_recv()
                if upward:

                    @pl.when(me < size - 1)
                    def _():
                        hidden_hop(origin, chunk, me + 1, hidden_up).start()
                else:

                    @pl.when(me > 0)
                    def _():
                        hidden_hop(origin, chunk, me - 1, hidden_down).start()

    for distance in range(1, size - 1):
        for chunk in range(chunks):
            come(distance, chunk)

    results = (
        (q, q_out),
        (k, k_out),
        (v, v_out),
        (q_pair, q_pair_out),
        (k_pair, k_pair_out),
        (rq, rq_out),
        (rk, rk_out),
        (cosine, cosine_out),
        (sine, sine_out),
        (wide, wide_out),
    )

    def write_out(chunk):
        at = pl.ds(pl.multiple_of(chunk * rows, rows), rows)
        for order, (here, there) in enumerate(results):
            lead = (slice(None),) * (len(here.shape) - 2)
            yield pltpu.make_async_copy(
                here.at[(*lead, at)], there.at[(*lead, at)], out_sems.at[order, chunk]
            )

    each = part // lines

    def finish(chunk, carry):
        come(size - 1, chunk)
        at = pl.ds(pl.multiple_of(chunk * rows, rows), rows)
        project_block(
            [wide[member, at, :] for member in range(size)],
            [
                full_qkv[member * each : (member + 1) * each].reshape(part, 3 * part)
                for member in range(size)
            ],
            cosine[at, :],
            sine[at, :],
            gain[...],
            place_pair[...],
            place_plain[...],
            sums[...],
            at,
            [here for here, _ in results[:7]],
        )
        for copy in write_out(chunk):
            copy.start()
        return carry

    lax.fori_loop(0, chunks, finish, 0)
    for stage in range(1, stages):
        for distance in range(size):
            advance(distance, stage)

    own[1].wait()
    qkv_copy.wait()
    for copy in vector_copies:
        copy.wait()
    for copy in given:
        copy.wait_send()
    for chunk in range(chunks):
        for copy in write_out(chunk):
            copy.wait()
    gather_qkv.close()
    for distance in range(size):
        for exists, origin, slot, upward in sources[distance]:

            @pl.when(exists)
            def _():
                for half in plane(origin, slot):
                    half.close()
                block = packed if distance == 0 else full.at[origin, chip]
                if upward is not False:

                    @pl.when(me < size - 1)
                    def _():
                        packed_hop(origin, block, me, packed_up).wait_send()
                        for chunk in range(chunks):
                            hidden_hop(origin, chunk, me, hidden_up).wait_send()

                if not upward:

                    @pl.when(me > 0)
                    def _():
                        packed_hop(origin, block, me, packed_down).wait_send()
                        for chunk in range(chunks):
                            hidden_hop(origin, chunk, me, hidden_down).wait_send()


def front(
    hidden,
    weights,
    vectors,
    positions,
    frequency,
    gain,
    in_pairs,
    place_pair,
    place_plain,
    sums,
    size,
    chips,
    collective,
):
    chunks = 6
    tokens, part = hidden.shape
    lines, both = weights[4].shape
    units = both // 2
    heads = part // DK
    height = 7 * lines
    dma = pltpu.SemaphoreType.DMA
    line = dma((size, chunks))
    plane = dma((2 * size - 1, 2, max(chips - 1, 1)))
    vmem = pl.BlockSpec(memory_space=pltpu.VMEM)
    padded = ((heads, tokens, EXT), BF16)
    paired = ((tokens, part), BF16)
    scale = ((tokens, heads * HALF), F32)
    wide = ((size, tokens, part), BF16)
    qkv = ((2 * chips, lines, 3 * part), BF16)
    results = [padded, padded, padded, paired, paired, scale, scale, scale, scale]
    return pl.pallas_call(
        functools.partial(front_kernel, size, chips, chunks, height // 32 * 16),
        in_specs=[vmem] * 16,
        out_specs=[ANY] * 13,
        out_shape=[
            jax.ShapeDtypeStruct(*each)
            for each in [
                wide,
                qkv,
                ((size, chips, height, units), BF16),
                ((size, *vectors.shape), F32),
                *results,
            ]
        ],
        scratch_shapes=[
            pltpu.VMEM(*wide),
            pltpu.VMEM(*qkv),
            pltpu.VMEM((height, units), BF16),
            pltpu.VMEM((3, lines, both), BF16),
            pltpu.VMEM((lines, part), BF16),
            *[pltpu.VMEM(*each) for each in results],
            dma((3,)),
            dma((10, chunks)),
            dma((4,)),
            dma((4,)),
            line,
            line,
            line,
            dma((size,)),
            dma((size,)),
            dma((size,)),
            plane,
            plane,
            dma((2 * chips - 1,)),
            dma((2 * chips - 1,)),
            dma((size,)),
            dma((size,)),
        ],
        compiler_params=remote_params(collective),
        name="front",
    )(
        hidden,
        *weights,
        vectors,
        positions,
        frequency,
        gain,
        in_pairs,
        place_pair,
        place_plain,
        sums,
    )


class LineSum:
    def __init__(self, size, chunks, term, up, down, sems):
        self.size, self.chunks = size, chunks
        self.term, self.up, self.down = term, up, down
        self.sent_up, self.sent_down, self.got_up, self.got_down = sems
        self.me = lax.axis_index("mp")
        self.rows = up.shape[1] // chunks

    def at(self, chunk):
        return pl.ds(chunk * self.rows, self.rows)

    def hop(self, upward, goal, chunk, member):
        slots = self.up if upward else self.down
        send = self.sent_up if upward else self.sent_down
        receive = self.got_up if upward else self.got_down
        ref = slots.at[goal, self.at(chunk), :]
        return to_member(ref, ref, send.at[goal, chunk], receive.at[goal, chunk], member)

    def step(self, order, chunk):
        me, last, at = self.me, self.size - 1, self.at(chunk)
        for upward, goal, ahead, first, member in (
            (True, last - order, me < last - order, me == 0, me + 1),
            (False, order, me > order, me == last, me - 1),
        ):
            slots = self.up if upward else self.down

            @pl.when(ahead & first)
            def _():
                slots[goal, at, :] = self.term(goal, at)

            @pl.when(ahead & jnp.logical_not(first))
            def _():
                self.hop(upward, goal, chunk, me).wait_recv()
                slots[goal, at, :] = (
                    slots[goal, at, :].astype(F32) + self.term(goal, at).astype(F32)
                ).astype(BF16)

            @pl.when(ahead)
            def _():
                self.hop(upward, goal, chunk, member).start()

    def result(self, chunk, out, out_at):
        me, at = self.me, self.at(chunk)
        out[out_at, :] = self.term(me, at).astype(F32)

        @pl.when(me > 0)
        def _():
            self.hop(True, me, chunk, me).wait_recv()
            out[out_at, :] += self.up[me, at, :].astype(F32)

        @pl.when(me < self.size - 1)
        def _():
            self.hop(False, me, chunk, me).wait_recv()
            out[out_at, :] += self.down[me, at, :].astype(F32)

    def close(self):
        for order in range(self.size - 1):
            for chunk in range(self.chunks):

                @pl.when(self.me < self.size - 1 - order)
                def _():
                    self.hop(True, self.size - 1 - order, chunk, self.me).wait_send()

                @pl.when(self.me > order)
                def _():
                    self.hop(False, order, chunk, self.me).wait_send()


class ChipSum:
    def __init__(self, layers, bits, source, acc, got, load, send, receive):
        self.layers, self.bits = layers, bits
        self.acc, self.got, self.chip = acc, got, lax.axis_index("chip")
        self.half = 1 << (len(bits) - 1)
        self.load = [
            pltpu.make_async_copy(
                source(layer, flip(self.chip, self.combo(slot))),
                acc.at[layer, slot],
                load.at[layer, slot],
            )
            for layer in range(layers)
            for slot in range(self.half)
        ]
        self.source, self.sent, self.received = source, send, receive

    def combo(self, slot):
        count = len(self.bits)
        return sum(self.bits[count - 1 - j] for j in range(count - 1) if slot >> j & 1)

    def copies(self, stage):
        count = self.half >> stage
        offset = 2 * self.half - 2 * count
        where = {"chip": flip(self.chip, self.bits[stage])}
        for layer in range(self.layers):
            for slot in range(count):
                if stage == 0:
                    other = flip(self.chip, self.bits[0] | self.combo(slot))
                    ref = self.source(layer, other)
                else:
                    ref = self.acc.at[layer, count + slot]
                at = offset + slot
                yield layer, slot, at, to_device(
                    ref,
                    self.got.at[layer, at],
                    self.sent.at[layer, at],
                    self.received.at[layer, at],
                    where,
                )

    def start(self, stage):
        if stage == 0:
            for copy in self.load:
                copy.start()
        for _, _, _, copy in self.copies(stage):
            copy.start()

    def add(self, stage):
        if stage == 0:
            for copy in self.load:
                copy.wait()
        for layer, slot, at, copy in self.copies(stage):
            copy.wait_recv()
            self.acc[layer, slot] = (
                self.acc[layer, slot].astype(F32) + self.got[layer, at].astype(F32)
            ).astype(BF16)

    def close(self):
        for stage in range(len(self.bits)):
            for _, _, _, copy in self.copies(stage):
                copy.wait_send()


def sum_all_kernel(
    size,
    chips,
    chunks,
    split,
    term,
    grads,
    grad_wo,
    grad_qkv,
    vectors,
    out,
    owned,
    owned_wo,
    owned_qkv,
    owned_vectors,
    term_up,
    term_down,
    acc_a,
    got_a,
    up_a,
    down_a,
    acc_b,
    got_b,
    up_b,
    down_b,
    pair_wo,
    other_wo,
    acc_wo,
    got_wo,
    up_wo,
    down_wo,
    pair_qkv,
    other_qkv,
    acc_qkv,
    got_qkv,
    whole,
    vector_sum,
    vector_got,
    vector_line,
    local,
    core_sent,
    core_got,
    vector_sent,
    vector_received,
    term_sems,
    line_sems,
    load_sems,
    chip_sent,
    chip_got,
):
    me, chip, core = (lax.axis_index(name) for name in ("mp", "chip", "core"))
    bits = bits_below(chips)
    stages = len(bits)
    greet_around(size, chips)
    other_core_is = {"core": 1 - core}

    def sems(ref, which):
        return [ref.at[which, k] for k in range(4)]

    line = LineSum(
        size, chunks, lambda goal, at: term[goal, at, :], term_up, term_down, sems(term_sems, 0)
    )
    sum_a = ChipSum(
        size,
        bits,
        lambda m, c: grads.at[m, c, pl.ds(0, split), :],
        acc_a,
        got_a,
        load_sems.at[0],
        chip_sent.at[0],
        chip_got.at[0],
    )
    sum_b = ChipSum(
        size,
        bits[::-1],
        lambda m, c: grads.at[m, c, pl.ds(split, grads.shape[2] - split), :],
        acc_b,
        got_b,
        load_sems.at[1],
        chip_sent.at[1],
        chip_got.at[1],
    )
    sum_wo = ChipSum(
        size,
        bits[::-1],
        lambda m, c: pair_wo.at[m, c],
        acc_wo,
        got_wo,
        load_sems.at[2],
        chip_sent.at[2],
        chip_got.at[2],
    )
    sum_qkv = ChipSum(
        1,
        bits,
        lambda m, c: pair_qkv.at[c],
        acc_qkv,
        got_qkv,
        load_sems.at[3],
        chip_sent.at[3],
        chip_got.at[3],
    )
    lines = [
        LineSum(
            size,
            1,
            lambda goal, at, acc=acc: acc[goal, 0, at, :],
            up,
            down,
            sems(line_sems, which),
        )
        for which, (acc, up, down) in enumerate(
            ((acc_a, up_a, down_a), (acc_b, up_b, down_b), (acc_wo, up_wo, down_wo))
        )
    ]

    own = [
        pltpu.make_async_copy(grad_wo.at[:, :, core], pair_wo, local.at[0]),
        pltpu.make_async_copy(grad_qkv.at[:, core], pair_qkv, local.at[1]),
    ]
    given = [
        to_device(
            grad_wo.at[:, :, 1 - core], other_wo, core_sent.at[0], core_got.at[0], other_core_is
        ),
        to_device(
            grad_qkv.at[:, 1 - core], other_qkv, core_sent.at[1], core_got.at[1], other_core_is
        ),
    ]
    vector_copies = [
        to_member(
            vectors.at[flip(me, k)],
            vector_line.at[k],
            vector_sent.at[k],
            vector_received.at[k],
            flip(me, k),
        )
        for k in range(1, size)
    ]
    for copy in own + given:
        copy.start()
    sum_a.start(0)
    sum_b.start(0)
    for copy in vector_copies:
        copy.start()

    owner = chip * 2 + core
    vector_bits = [1] + [2 * bit for bit in bits]

    def vector_copy(stage):
        partner = flip(owner, vector_bits[stage])
        return to_device(
            vector_sum.at[stage],
            vector_got.at[stage],
            vector_sent.at[size + stage],
            vector_received.at[size + stage],
            {"chip": lax.div(partner, 2), "core": lax.rem(partner, 2)},
        )

    def vector_step(stage):
        if stage == 0:
            total = vectors[me]
            for k, copy in enumerate(vector_copies):
                copy.wait_recv()
                total = total + vector_line[k + 1]
            vector_sum[0] = total
        else:
            vector_copy(stage - 1).wait_recv()
            vector_sum[stage] = vector_sum[stage - 1] + vector_got[stage - 1]
        if stage < len(vector_bits):
            vector_copy(stage).start()

    for chunk in range(chunks):
        line.step(0, chunk)
    for copy in own:
        copy.wait()
    for copy in given:
        copy.wait_recv()
    pair_wo[...] = (pair_wo[...].astype(F32) + other_wo[...].astype(F32)).astype(BF16)
    pair_qkv[...] = (pair_qkv[...].astype(F32) + other_qkv[...].astype(F32)).astype(BF16)
    sum_wo.start(0)
    sum_qkv.start(0)
    vector_step(0)
    vector_step(1)
    for order in range(1, size - 1):
        for chunk in range(chunks):
            line.step(order, chunk)
        if order - 1 < stages:
            for part in (sum_a, sum_b, sum_wo, sum_qkv):
                part.add(order - 1)
                if order < stages:
                    part.start(order)
    for stage in range(size - 2, stages):
        for part in (sum_a, sum_b, sum_wo, sum_qkv):
            part.add(stage)
            if stage + 1 < stages:
                part.start(stage + 1)
    lines[0].step(0, 0)
    lines[1].step(0, 0)
    lines[2].step(0, 0)
    for stage in range(2, len(vector_bits) + 1):
        vector_step(stage)
    for chunk in range(chunks):
        line.result(chunk, out, line.at(chunk))
    for order in range(1, size - 1):
        for part in lines:
            part.step(order, 0)
    owned_vectors[...] = vector_sum[len(vector_bits)]
    owned_qkv[...] = acc_qkv[0, 0].astype(F32)
    lines[0].result(0, whole, pl.ds(0, split))
    lines[1].result(0, whole, pl.ds(split, whole.shape[0] - split))
    lines[2].result(0, owned_wo, slice(None))

    matrices, rows, columns = owned.shape
    columns = columns // 2
    place = pl.ds(pl.multiple_of(core * columns, columns), columns)
    swaps = []
    for matrix in range(matrices):
        mine = pl.ds(pl.multiple_of((2 * matrix + core) * rows, rows), rows)
        theirs = pl.ds(pl.multiple_of((2 * matrix + 1 - core) * rows, rows), rows)
        swaps.append(
            to_device(
                whole.at[theirs, :],
                owned.at[matrix, :, place],
                core_sent.at[2 + matrix],
                core_got.at[2 + matrix],
                other_core_is,
            )
        )
        swaps[-1].start()
        copy = pltpu.make_async_copy(
            whole.at[mine, :], owned.at[matrix, :, place], local.at[2 + matrix]
        )
        copy.start()
        swaps.append(copy)
    for copy in swaps:
        copy.wait()

    for copy in given + vector_copies:
        copy.wait_send()
    for stage in range(len(vector_bits)):
        vector_copy(stage).wait_send()
    for part in (sum_a, sum_b, sum_wo, sum_qkv):
        part.close()
    line.close()
    for part in lines:
        part.close()


def sum_all(term, grads, grad_wo, grad_qkv, vectors, chips, collective):
    size, tokens, part = term.shape
    height, units = grads.shape[2:]
    rows = height // 6
    chunks = 6
    split = height // 32 * 16
    half, blocks = max(chips // 2, 1), max(chips - 1, 1)
    stages = chips.bit_length()
    dma = pltpu.SemaphoreType.DMA
    vmem = pl.BlockSpec(memory_space=pltpu.VMEM)
    wo_block, qkv_block = grad_wo.shape[3:], grad_qkv.shape[2:]
    long = vectors.shape[1:]

    def sums(layers, block):
        return [
            pltpu.VMEM((layers, half, *block), BF16),
            pltpu.VMEM((layers, blocks, *block), BF16),
        ]

    def line(block):
        return [pltpu.VMEM((size, *block), BF16)] * 2

    return pl.pallas_call(
        functools.partial(sum_all_kernel, size, chips, chunks, split),
        in_specs=[vmem, ANY, ANY, ANY, vmem],
        out_specs=[vmem] * 5,
        out_shape=[
            jax.ShapeDtypeStruct((tokens, part), F32),
            jax.ShapeDtypeStruct((3, rows, 2 * units), F32),
            jax.ShapeDtypeStruct(wo_block, F32),
            jax.ShapeDtypeStruct(qkv_block, F32),
            jax.ShapeDtypeStruct(long, F32),
        ],
        scratch_shapes=[
            *line((tokens, part)),
            *sums(size, (split, units)),
            *line((split, units)),
            *sums(size, (height - split, units)),
            *line((height - split, units)),
            pltpu.VMEM((size, chips, *wo_block), BF16),
            pltpu.VMEM((size, chips, *wo_block), BF16),
            *sums(size, wo_block),
            *line(wo_block),
            pltpu.VMEM((chips, *qkv_block), BF16),
            pltpu.VMEM((chips, *qkv_block), BF16),
            *sums(1, qkv_block),
            pltpu.VMEM((height, units), F32),
            pltpu.VMEM((stages + 1, *long), F32),
            pltpu.VMEM((stages + 1, *long), F32),
            pltpu.VMEM((size, *long), F32),
            dma((5,)),
            dma((5,)),
            dma((5,)),
            dma((size + stages,)),
            dma((size + stages,)),
            dma((1, 4, size, chunks)),
            dma((3, 4, size, 1)),
            dma((4, size, half)),
            dma((4, size, blocks)),
            dma((4, size, blocks)),
        ],
        compiler_params=remote_params(collective),
        name="sum_all",
    )(term, grads, grad_wo, grad_qkv, vectors)


def paired_place(heads):
    head, feature = np.divmod(np.arange(heads * DK), DK)
    return (feature // HALF) * (heads * HALF) + head * HALF + feature % HALF


def placing_matrix(place, heads):
    head, feature = np.divmod(np.arange(heads * DK), DK)
    matrix = np.zeros((heads * DK, heads * EXT), np.float32)
    matrix[place, head * EXT + feature] = 1
    return matrix


def delta_matrix(heads):
    lane = np.arange(heads * EXT)
    head = np.arange(heads * DK) // DK
    return ((head[:, None] == lane[None, :] // EXT) & (lane % EXT >= DK) & (lane % EXT < DK + 3)).astype(
        np.float32
    )


def head_sum_matrix(heads):
    lane = np.arange(heads * HALF) // HALF
    return (lane[:, None] == lane[None, :]).astype(np.float32)


def split_dot(value, matrix):
    high = value.astype(BF16)
    rest = (value - high.astype(F32)).astype(BF16)
    return dot(high, matrix) + dot(rest, matrix)


def project_block(wide, weight, cos, sin, gain, place_pair, place_plain, sums, at, outs):
    q, k, v, q_pair, k_pair, rq, rk = outs
    heads = q.shape[0]
    pair, width = heads * HALF, heads * DK
    raw = dot(wide[0], weight[0])
    for part in range(1, len(wide)):
        raw += dot(wide[part], weight[part])
    lane = lax.broadcasted_iota(jnp.int32, (raw.shape[0], EXT), 1)
    for offset, out, pair_out, scale_out, factor in (
        (0, q, q_pair, rq, math.sqrt(DK)),
        (width, k, k_pair, rk, 1.0),
    ):
        first = raw[:, offset : offset + pair]
        second = raw[:, offset + pair : offset + width]
        turned_first = first * cos - second * sin
        turned_second = second * cos + first * sin
        total = split_dot(turned_first * turned_first + turned_second * turned_second, sums)
        scale = lax.rsqrt(total + EPSILON)
        scale_out[at, :] = scale
        both = jnp.concatenate(
            [
                turned_first * scale * gain[:, :pair],
                turned_second * scale * gain[:, pair:],
            ],
            axis=1,
        ).astype(BF16)
        pair_out[at, :] = both
        padded = dot(both, place_pair) * factor
        for head in range(heads):
            piece = padded[:, head * EXT : (head + 1) * EXT]
            if factor == 1.0:
                piece = jnp.where(lane < DK, piece, 1.0)
            out[head, at, :] = piece.astype(BF16)
    padded = dot(raw[:, 2 * width :].astype(BF16), place_plain)
    for head in range(heads):
        piece = padded[:, head * EXT : (head + 1) * EXT]
        v[head, at, :] = jnp.where(lane < DK, piece, 1.0).astype(BF16)


def split_three(value):
    high = value.astype(BF16).astype(F32)
    rest = value - high
    middle = rest.astype(BF16).astype(F32)
    return high, middle, rest - middle


def attend_kernel(low, q, k, v, qdoc, kdoc, collect, attended, qback, acc):
    heads, rows, _ = q.shape
    block = kdoc.shape[2]
    index = pl.program_id(0)
    acc[...] = jnp.zeros_like(acc)

    def step(j, diagonal):
        slots = pl.ds(pl.multiple_of(j * block, block), block)
        mask = qdoc[...] == kdoc[j]
        if diagonal:
            row = lax.broadcasted_iota(jnp.int32, (rows, block), 0)
            column = lax.broadcasted_iota(jnp.int32, (rows, block), 1)
            mask = (mask & (column < row)) | (column == row)
        for head in range(heads):
            scores = dot(q[head], k[head, slots, :], NT)
            weight = jnp.where(mask, jnp.exp(scores), 0.0).astype(BF16)
            acc[head] += dot(weight, v[head, slots, :])

    def earlier(j, carry):
        step(j, False)
        return carry

    lax.fori_loop(low[index], index, earlier, 0)
    step(index, True)

    lane = lax.broadcasted_iota(jnp.int32, (rows, EXT), 1)
    merged = jnp.zeros((rows, heads * DK), F32)
    for head in range(heads):
        both = acc[head]
        total = pltpu.roll(both, DK, 1)
        output = jnp.where(lane < DK, both / total, 0.0).astype(BF16)
        merged += dot(output, collect[head])
        high, middle, rest = split_three(-jnp.log(both))
        qback[head] = jnp.where(
            lane < DK,
            q[head].astype(F32),
            jnp.where(
                lane == DK,
                high,
                jnp.where(lane == DK + 1, middle, jnp.where(lane == DK + 2, rest, 0.0)),
            ),
        ).astype(BF16)
    attended[...] = merged.astype(BF16)


def attend(low, q, k, v, qdoc, kdoc, collect):
    heads, tokens, _ = q.shape
    block = kdoc.shape[2]
    width = heads * DK

    def whole(array):
        return pl.BlockSpec(array.shape, lambda i, low: (0,) * array.ndim)

    headed = pl.BlockSpec((heads, block, EXT), lambda i, low: (0, i, 0))
    return pl.pallas_call(
        attend_kernel,
        grid_spec=pltpu.PrefetchScalarGridSpec(
            num_scalar_prefetch=1,
            grid=(tokens // block,),
            in_specs=[
                headed,
                whole(k),
                whole(v),
                pl.BlockSpec((block, 1), lambda i, low: (i, 0)),
                whole(kdoc),
                whole(collect),
            ],
            out_specs=[pl.BlockSpec((block, width), lambda i, low: (i, 0)), headed],
            scratch_shapes=[pltpu.VMEM((heads, block, EXT), F32)],
        ),
        out_shape=[
            jax.ShapeDtypeStruct((tokens, width), BF16),
            jax.ShapeDtypeStruct((heads, tokens, EXT), BF16),
        ],
        compiler_params=grid_params(1),
        cost_estimate=pl.CostEstimate(
            flops=40_000_000_000, bytes_accessed=16 << 20, transcendentals=0
        ),
        name="attend",
    )(low, q, k, v, qdoc, kdoc, collect)


def unrope(grad, unit, gain, scale, cos, sin, sums):
    pair = cos.shape[1]
    grad_gain = jnp.sum(grad * unit, axis=0, keepdims=True)
    dy = grad * gain
    prod = dy * unit
    total = split_dot(prod[:, :pair] + prod[:, pair:], sums)
    first = scale * (dy[:, :pair] - unit[:, :pair] * total)
    second = scale * (dy[:, pair:] - unit[:, pair:] * total)
    raw = jnp.concatenate([first * cos + second * sin, second * cos - first * sin], axis=1)
    return raw.astype(BF16), grad_gain


def head_lanes(shape, head, paired):
    lane = lax.broadcasted_iota(jnp.int32, shape, 1)
    if paired:
        return lax.div(lax.rem(lane, shape[1] // 2), HALF) == head
    return lax.div(lane, DK) == head


def attend_back_kernel(
    low,
    qback,
    q_pair,
    dout,
    attended,
    k,
    k_pair,
    v,
    qdoc,
    kdoc,
    cosine,
    sine,
    rq,
    rk,
    gain,
    weight,
    place_plain,
    place_delta,
    sums,
    wide,
    grad_resid,
    term_out,
    grad_qkv,
    gain_out,
    dk,
    dv,
    dq,
    dox,
    q_heads,
    d_heads,
    k_heads,
    probs_all,
    scores_all,
    dq_low,
    total_qkv,
):
    heads, rows, _ = qback.shape
    steps = pl.num_programs(0) // 2
    step_at = pl.program_id(0)
    width = heads * DK
    scale = math.sqrt(DK)

    @pl.when(step_at == 0)
    def _():
        dk[...] = jnp.zeros_like(dk)
        dv[...] = jnp.zeros_like(dv)
        gain_out[...] = jnp.zeros_like(gain_out)
        keys = k_pair[...]
        for head in range(heads):
            k_heads[head] = jnp.where(head_lanes(keys.shape, head, True), keys, 0)

    @pl.when(step_at < steps)
    def _():
        index = step_at
        lane = lax.broadcasted_iota(jnp.int32, (rows, EXT), 1)
        grads = dout[...]
        queries = q_pair[...]
        spread = dot(grads, place_plain[...])
        delta = split_dot(grads.astype(F32) * attended[...].astype(F32), place_delta[...])
        for head in range(heads):
            at = slice(head * EXT, (head + 1) * EXT)
            high, middle, rest = split_three(-delta[:, at])
            dox[head] = jnp.where(
                lane < DK,
                spread[:, at],
                jnp.where(lane == DK, high, jnp.where(lane == DK + 1, middle, rest)),
            ).astype(BF16)
            stack = slice(head * rows, (head + 1) * rows)
            q_heads[stack, :] = jnp.where(head_lanes(queries.shape, head, True), queries, 0)
            d_heads[stack, :] = jnp.where(head_lanes(grads.shape, head, False), grads, 0)
        dq[...] = jnp.zeros_like(dq)

        def step(j, diagonal):
            slots = pl.ds(pl.multiple_of(j * rows, rows), rows)
            mask = kdoc[slots, :] == qdoc[0]
            if diagonal:
                key = lax.broadcasted_iota(jnp.int32, (rows, rows), 0)
                query = lax.broadcasted_iota(jnp.int32, (rows, rows), 1)
                mask = (mask & (key < query)) | (key == query)
            total = dq[...]
            for head in range(heads):
                scores = dot(k[head, slots, :], qback[head], NT)
                probs = jnp.where(mask, jnp.exp(scores), 0.0)
                dprobs = dot(v[head, slots, :], dox[head], NT)
                dscores = (probs * dprobs).astype(BF16)
                stack = slice(head * rows, (head + 1) * rows)
                probs_all[:, stack] = probs.astype(BF16)
                scores_all[:, stack] = dscores
                total += dot(dscores, k_heads[head, slots, :], TN)
            dq[...] = total
            dv[slots, :] += dot(probs_all[...], d_heads[...])
            dk[slots, :] += dot(scores_all[...], q_heads[...])

        def earlier(j, carry):
            step(j, False)
            return carry

        lax.fori_loop(low[index], index, earlier, 0)
        step(index, True)

        raw, grad_gain = unrope(
            dq[...] * scale,
            queries.astype(F32) / gain[...],
            gain[...],
            rq[...],
            cosine[...],
            sine[...],
            sums[...],
        )
        gain_out[...] += grad_gain
        dq_low[pl.ds(pl.multiple_of(index * rows, rows), rows), :] = raw

    @pl.when(step_at >= steps)
    def _():
        index = step_at - steps
        slots = pl.ds(pl.multiple_of(index * rows, rows), rows)
        raw, grad_gain = unrope(
            dk[slots, :] * scale,
            k_pair[slots, :].astype(F32) / gain[...],
            gain[...],
            rk[...],
            cosine[...],
            sine[...],
            sums[...],
        )
        gain_out[...] += grad_gain
        together = jnp.concatenate([dq_low[slots, :], raw, dv[slots, :].astype(BF16)], axis=1)
        parts, part = weight.shape[:2]
        for member in range(parts):
            term_out[member] = dot(together, weight[member], NT).astype(BF16)
            product = dot(wide[member], together, TN)

            @pl.when(index == 0)
            def _():
                total_qkv[member] = product

            @pl.when(index > 0)
            def _():
                total_qkv[member] += product

        strip = STRIP
        first = low[steps] * (grad_resid.shape[0] // strip)
        for half in range(rows // strip):
            number = index * (rows // strip) + half - first

            @pl.when((number >= 0) & (number < grad_resid.shape[0] // strip))
            def _():
                at = pl.ds(half * strip, strip)
                own = pl.ds(pl.multiple_of(number * strip, strip), strip)
                for member in range(parts):
                    term_out[member, at, :] = (
                        term_out[member, at, :].astype(F32)
                        + grad_resid[own, member * part : (member + 1) * part].astype(F32)
                    ).astype(BF16)

        @pl.when(index == steps - 1)
        def _():
            grad_qkv[...] = total_qkv[...].astype(BF16)


def attend_back(
    low,
    qback,
    q_pair,
    dout,
    attended,
    k,
    k_pair,
    v,
    qdoc,
    kdoc,
    cosine,
    sine,
    rq,
    rk,
    gain,
    weight,
    place_plain,
    place_delta,
    sums,
    wide,
    grad_resid,
):
    heads, tokens, _ = k.shape
    block = qdoc.shape[2]
    width = heads * DK
    steps = tokens // block
    parts, part = weight.shape[:2]

    def whole(array):
        return pl.BlockSpec(array.shape, lambda i, low: (0,) * array.ndim)

    def now(i):
        return jnp.minimum(i, steps - 1)

    def after(i):
        return jnp.maximum(i - steps, 0)

    def both(i):
        return lax.rem(i, steps)

    def rows(columns, at):
        return pl.BlockSpec((block, columns), lambda i, low: (at(i), 0))

    return pl.pallas_call(
        attend_back_kernel,
        grid_spec=pltpu.PrefetchScalarGridSpec(
            num_scalar_prefetch=1,
            grid=(2 * steps,),
            in_specs=[
                pl.BlockSpec((heads, block, EXT), lambda i, low: (0, now(i), 0)),
                rows(width, now),
                rows(width, now),
                rows(width, now),
                whole(k),
                whole(k_pair),
                whole(v),
                pl.BlockSpec((1, 1, block), lambda i, low: (now(i), 0, 0)),
                whole(kdoc),
                rows(width // 2, both),
                rows(width // 2, both),
                rows(width // 2, now),
                rows(width // 2, after),
                whole(gain),
                whole(weight),
                whole(place_plain),
                whole(place_delta),
                whole(sums),
                pl.BlockSpec((parts, block, part), lambda i, low: (0, after(i), 0)),
                whole(grad_resid),
            ],
            out_specs=[
                pl.BlockSpec((parts, block, part), lambda i, low: (0, after(i), 0)),
                pl.BlockSpec((parts, part, 3 * width), lambda i, low: (0, 0, 0)),
                pl.BlockSpec((1, width), lambda i, low: (0, 0)),
            ],
            scratch_shapes=[
                pltpu.VMEM((tokens, width), F32),
                pltpu.VMEM((tokens, width), F32),
                pltpu.VMEM((block, width), F32),
                pltpu.VMEM((heads, block, EXT), BF16),
                pltpu.VMEM((heads * block, width), BF16),
                pltpu.VMEM((heads * block, width), BF16),
                pltpu.VMEM((heads, tokens, width), BF16),
                pltpu.VMEM((block, heads * block), BF16),
                pltpu.VMEM((block, heads * block), BF16),
                pltpu.VMEM((tokens, width), BF16),
                pltpu.VMEM((parts, part, 3 * width), F32),
            ],
        ),
        out_shape=[
            jax.ShapeDtypeStruct((parts, tokens, part), BF16),
            jax.ShapeDtypeStruct((parts, part, 3 * width), BF16),
            jax.ShapeDtypeStruct((1, width), F32),
        ],
        compiler_params=grid_params(1),
        cost_estimate=pl.CostEstimate(
            flops=80_000_000_000, bytes_accessed=30 << 20, transcendentals=0
        ),
        name="attend_back",
    )(
        low,
        qback,
        q_pair,
        dout,
        attended,
        k,
        k_pair,
        v,
        qdoc,
        kdoc,
        cosine,
        sine,
        rq,
        rk,
        gain,
        weight,
        place_plain,
        place_delta,
        sums,
        wide,
        grad_resid,
    )


def row_scale(value):
    return lax.rsqrt(jnp.sum(value * value, axis=-1, keepdims=True) + EPSILON)


def residual_backward(grad_out, result, resid, unit, alpha, branch_scale, mixed_scale):
    grad_mixed = mixed_scale * (
        grad_out - result * jnp.sum(grad_out * result, axis=-1, keepdims=True)
    )
    grad_alpha = jnp.sum(grad_mixed * (unit - resid), axis=0, keepdims=True)
    grad_unit = grad_mixed * alpha
    grad_branch = branch_scale * (
        grad_unit - unit * jnp.sum(grad_unit * unit, axis=-1, keepdims=True)
    )
    return grad_mixed * (1.0 - alpha), grad_branch, grad_alpha


STRIP = 256


def strips(rows):
    strip = min(STRIP, rows)
    return [pl.ds(start, strip) for start in range(0, rows, strip)]


def core_semaphores(count):
    return [pltpu.SemaphoreType.DMA((count,)), pltpu.SemaphoreType.DMA((count,))]


def greet_pair_and_line(size):
    me, core = lax.axis_index("mp"), lax.axis_index("core")
    for k in range(1, size):
        greet({"mp": flip(me, k)})
    greet({"core": 1 - core})
    pl.semaphore_wait(pltpu.get_barrier_semaphore(), size)


def output_matrix(packed_wo, whole):
    size, chips, rows, both = packed_wo.shape
    part = both // 2
    for chip in range(chips):
        for core in range(2):
            start = (2 * chip + core) * rows
            whole[:, start : start + rows, :] = packed_wo[
                :, chip, :, core * part : (core + 1) * part
            ]


def mix_kernel(
    size,
    attended,
    packed,
    wide,
    alpha,
    cotangent,
    x,
    middle_out,
    unit_out,
    branch_scale_out,
    mixed_scale_out,
    merged,
    full_wo,
    resid_out,
    cotangent_low,
    packed_wo,
    middle_low,
    resid,
    send,
    receive,
    local,
    own_sems,
    core_sent,
    core_got,
):
    me, core = lax.axis_index("mp"), lax.axis_index("core")
    mine, width = middle_out.shape
    part = width // size
    rows = packed_wo.shape[2]
    greet_pair_and_line(size)
    exchange = Exchange(
        size, attended, merged, row_part(mine), column_part(part), send, receive, local
    )
    exchange.start()
    own = [
        pltpu.make_async_copy(
            packed.at[:, :, pl.ds(packed.shape[2] - rows, rows), :], packed_wo, own_sems.at[0]
        )
    ]
    for member in range(size):
        own.append(
            pltpu.make_async_copy(
                wide.at[member, pl.ds(pl.multiple_of(me * mine, mine), mine), :],
                resid.at[:, pl.ds(member * part, part)],
                own_sems.at[1 + member],
            )
        )
    for copy in own:
        copy.start()
    for at in strips(cotangent.shape[0]):
        cotangent_low[at, :] = cotangent[at, :].astype(BF16)
    for copy in own:
        copy.wait()
    output_matrix(packed_wo, full_wo)
    resid_out[...] = resid[...]
    exchange.wait()

    swaps = []
    for order, at in enumerate(strips(mine)):
        branch = dot(merged[at, :part], full_wo[0], NT)
        for member in range(1, size):
            branch += dot(
                merged[at, member * part : (member + 1) * part], full_wo[member], NT
            )
        old = resid[at, :].astype(F32)
        branch_scale = row_scale(branch)
        unit = branch * branch_scale
        mixed = old + alpha[...] * (unit - old)
        mixed_scale = row_scale(mixed)
        middle = mixed * mixed_scale
        middle_out[at, :] = middle
        unit_out[at, :] = unit.astype(BF16)
        branch_scale_out[at, :] = branch_scale
        mixed_scale_out[at, :] = mixed_scale
        middle_low[at, :] = middle.astype(BF16)
        there = pl.ds(mine + at.start, at.size)
        swap = to_device(
            middle_low.at[at, :],
            x.at[there, :],
            core_sent.at[order],
            core_got.at[order],
            {"core": 1 - core},
        )
        swap.start()
        swaps.append(swap)
    keep = pltpu.make_async_copy(middle_low, x.at[pl.ds(0, mine), :], own_sems.at[0])
    keep.start()
    keep.wait()
    for swap in swaps:
        swap.wait()


def mix(attended, packed, rows, wide, alpha, cotangent, collective):
    size, slots, part = wide.shape
    chips = packed.shape[1]
    mine, width = slots // size, size * part
    vmem = pl.BlockSpec(memory_space=pltpu.VMEM)
    count = len(strips(mine))
    scale = jax.ShapeDtypeStruct((mine, 1), F32)
    return pl.pallas_call(
        functools.partial(mix_kernel, size),
        in_specs=[ANY, ANY, ANY, vmem, vmem],
        out_specs=[ANY, *[vmem] * 8],
        out_shape=[
            jax.ShapeDtypeStruct((2 * mine, width), BF16),
            jax.ShapeDtypeStruct((mine, width), F32),
            jax.ShapeDtypeStruct((mine, width), BF16),
            scale,
            scale,
            jax.ShapeDtypeStruct((mine, width), BF16),
            jax.ShapeDtypeStruct((size, width, part), BF16),
            jax.ShapeDtypeStruct((mine, width), BF16),
            jax.ShapeDtypeStruct((slots, part), BF16),
        ],
        scratch_shapes=[
            pltpu.VMEM((size, chips, rows, 2 * part), BF16),
            pltpu.VMEM((mine, width), BF16),
            pltpu.VMEM((mine, width), BF16),
            *exchange_semaphores(size),
            pltpu.SemaphoreType.DMA((1 + size,)),
            *core_semaphores(count),
        ],
        compiler_params=remote_params(collective),
        name="mix",
    )(attended, packed, wide, alpha, cotangent)


def whole_matrix(ref):
    _, chips, rows, units = ref.shape
    return ref[...].reshape(chips * rows, units)


def first_step():
    return (pl.program_id(0) == 0) & (pl.program_id(1) == 0)


def last_step():
    return (pl.program_id(0) == pl.num_programs(0) - 1) & (
        pl.program_id(1) == pl.num_programs(1) - 1
    )


def swap_cores(source, target, sems):
    return to_device(
        source, target, sems[0], sems[1], {"core": 1 - lax.axis_index("core")}
    )


def feed_kernel(
    size,
    x,
    w_up,
    w_gate,
    w_down,
    s_u,
    s_v,
    cotangent,
    middle,
    alpha,
    up_out,
    gate_out,
    units_out,
    result_out,
    grad_middle,
    dbranch,
    grad_alpha,
    acc,
    given,
    got,
    spread,
    low,
    send,
    receive,
    local,
    core_sent,
    core_got,
    keep_sems,
):
    exchange = Exchange(
        size,
        cotangent,
        spread,
        row_part(spread.shape[0]),
        column_part(cotangent.shape[1]),
        send,
        receive,
        local,
    )
    branch_swap = swap_cores(given, got, (core_sent.at[0], core_got.at[0]))

    @pl.when(first_step())
    def _():
        greet_pair_and_line(size)
        exchange.start()

    block, part = pl.program_id(0), pl.program_id(1)
    up = dot(x[...], whole_matrix(w_up))
    gate = dot(x[...], whole_matrix(w_gate))
    up_out[0] = up.astype(BF16)
    gate_out[0] = gate.astype(BF16)
    scaled = gate * s_v[0]
    units = (up * s_u[0] * (scaled / (1.0 + jnp.exp(-scaled)))).astype(BF16)
    units_out[0] = units
    term = dot(units, whole_matrix(w_down), NT)

    @pl.when(part == 0)
    def _():
        acc[...] = term

    @pl.when(part > 0)
    def _():
        acc[...] += term

    last = part == pl.num_programs(1) - 1

    @pl.when(last & (block == 0))
    def _():
        given[...] = acc[...].astype(BF16)
        branch_swap.start()

    @pl.when(last & (block == 1))
    def _():
        mine = acc.shape[0]
        branch_swap.wait()
        exchange.wait()
        swaps = []
        for order, at in enumerate(strips(mine)):
            branch = acc[at, :] + got[at, :].astype(F32)
            branch_scale = row_scale(branch)
            unit = branch * branch_scale
            old = middle[at, :]
            mixed = old + alpha[...] * (unit - old)
            mixed_scale = row_scale(mixed)
            result = mixed * mixed_scale
            result_out[at, :] = result.astype(BF16)
            grad_old, grad_branch, part_alpha = residual_backward(
                spread[at, :].astype(F32),
                result,
                old,
                unit,
                alpha[...],
                branch_scale,
                mixed_scale,
            )
            grad_middle[at, :] = grad_old
            if order == 0:
                grad_alpha[...] = part_alpha
            else:
                grad_alpha[...] += part_alpha
            low[at, :] = grad_branch.astype(BF16)
            there = pl.ds(mine + at.start, at.size)
            swaps.append(
                swap_cores(
                    low.at[at, :],
                    dbranch.at[there, :],
                    (core_sent.at[1 + order], core_got.at[1 + order]),
                )
            )
            swaps.append(
                pltpu.make_async_copy(low.at[at, :], dbranch.at[at, :], keep_sems.at[order])
            )
            swaps[-2].start()
            swaps[-1].start()
        for swap in swaps:
            swap.wait()


def packed_specs(packed, width):
    _, chips, _, units = packed.shape
    return [
        pl.BlockSpec((1, chips, width // chips, units), lambda t, m, w=w: (m, 0, w, 0))
        for w in range(3)
    ]


def feed(x, packed, s_u, s_v, cotangent, middle, alpha, collective):
    tokens, width = x.shape
    parts, _, _, units = packed.shape
    size = parts
    block = tokens // 2
    rows = pl.BlockSpec((block, width), lambda t, m: (1 - t, 0))
    vector = pl.BlockSpec((1, 1, units), lambda t, m: (m, 0, 0))
    piece = pl.BlockSpec((1, block, units), lambda t, m: (m, 1 - t, 0))
    vmem = pl.BlockSpec(memory_space=pltpu.VMEM)
    hidden = jax.ShapeDtypeStruct((parts, tokens, units), BF16)
    count = len(strips(block))
    low = pltpu.VMEM((block, width), BF16)
    return pl.pallas_call(
        functools.partial(feed_kernel, size),
        grid=(2, parts),
        in_specs=[rows, *packed_specs(packed, width), vector, vector, ANY, vmem, vmem],
        out_specs=[piece, piece, piece, vmem, vmem, ANY, vmem],
        out_shape=[
            hidden,
            hidden,
            hidden,
            jax.ShapeDtypeStruct((block, width), BF16),
            jax.ShapeDtypeStruct((block, width), F32),
            jax.ShapeDtypeStruct((tokens, width), BF16),
            jax.ShapeDtypeStruct((1, width), F32),
        ],
        scratch_shapes=[
            pltpu.VMEM((block, width), F32),
            low,
            low,
            low,
            low,
            *exchange_semaphores(size),
            *core_semaphores(1 + count),
            pltpu.SemaphoreType.DMA((count,)),
        ],
        compiler_params=remote_params(collective),
        cost_estimate=pl.CostEstimate(
            flops=6 * tokens * width * parts * units, bytes_accessed=60 << 20, transcendentals=0
        ),
        name="feed",
    )(x, packed, packed, packed, s_u, s_v, cotangent, middle, alpha)


def feed_back_kernel(
    size,
    dbranch,
    w_up,
    w_gate,
    w_down,
    s_u,
    s_v,
    up_in,
    gate_in,
    result,
    grad_middle,
    middle,
    resid,
    unit,
    branch_scale,
    mixed_scale,
    alpha,
    full_wo,
    dup_out,
    dgate_out,
    grad_u,
    grad_v,
    spread,
    grad_resid,
    dbranch_attn,
    dmerged,
    grad_alpha,
    acc,
    given,
    got,
    sum_u,
    sum_v,
    send,
    receive,
    local,
    core_sent,
    core_got,
):
    exchange = Exchange(
        size,
        result,
        spread,
        column_part(spread.shape[1]),
        row_part(result.shape[0]),
        send,
        receive,
        local,
    )
    dx_swap = swap_cores(given, got, (core_sent.at[0], core_got.at[0]))

    @pl.when(first_step())
    def _():
        greet_pair_and_line(size)
        exchange.start()

    block, part = pl.program_id(0), pl.program_id(1)
    dunits = dot(dbranch[...], whole_matrix(w_down))
    up = up_in[0].astype(F32)
    gate = gate_in[0].astype(F32)
    scaled = gate * s_v[0]
    sigmoid = 1.0 / (1.0 + jnp.exp(-scaled))
    silu = scaled * sigmoid
    slope = sigmoid * (1.0 + scaled - silu)
    through_up = dunits * silu
    through_gate = dunits * up * s_u[0] * slope
    dup = (through_up * s_u[0]).astype(BF16)
    dgate = (through_gate * s_v[0]).astype(BF16)
    dup_out[0] = dup
    dgate_out[0] = dgate
    term = dot(dup, whole_matrix(w_up), NT) + dot(dgate, whole_matrix(w_gate), NT)
    part_u = jnp.sum(through_up * up, axis=0, keepdims=True)
    part_v = jnp.sum(through_gate * gate, axis=0, keepdims=True)

    @pl.when(block == 0)
    def _():
        sum_u[part] = part_u
        sum_v[part] = part_v

    @pl.when(block > 0)
    def _():
        sum_u[part] += part_u
        sum_v[part] += part_v

    @pl.when(part == 0)
    def _():
        acc[...] = term

    @pl.when(part > 0)
    def _():
        acc[...] += term

    last = part == pl.num_programs(1) - 1

    @pl.when(last & (block == 0))
    def _():
        given[...] = acc[...].astype(BF16)
        dx_swap.start()

    @pl.when(last & (block == 1))
    def _():
        grad_u[...] = sum_u[...]
        grad_v[...] = sum_v[...]
        dx_swap.wait()
        for order, at in enumerate(strips(acc.shape[0])):
            grad_old, grad_branch, part_alpha = residual_backward(
                grad_middle[at, :] + acc[at, :] + got[at, :].astype(F32),
                middle[at, :],
                resid[at, :].astype(F32),
                unit[at, :].astype(F32),
                alpha[...],
                branch_scale[at, :],
                mixed_scale[at, :],
            )
            grad_resid[at, :] = grad_old.astype(BF16)
            if order == 0:
                grad_alpha[...] = part_alpha
            else:
                grad_alpha[...] += part_alpha
            low = grad_branch.astype(BF16)
            dbranch_attn[at, :] = low
            columns = full_wo.shape[2]
            for member in range(size):
                dmerged[at, member * columns : (member + 1) * columns] = dot(
                    low, full_wo[member]
                ).astype(BF16)
        exchange.wait()


def feed_back(
    dbranch,
    packed,
    s_u,
    s_v,
    up,
    gate,
    result,
    grad_middle,
    middle,
    resid,
    unit,
    branch_scale,
    mixed_scale,
    alpha,
    full_wo,
    collective,
):
    tokens, width = dbranch.shape
    parts, _, _, units = packed.shape
    size = parts
    block = tokens // 2
    rows = pl.BlockSpec((block, width), lambda t, m: (1 - t, 0))
    vector = pl.BlockSpec((1, 1, units), lambda t, m: (m, 0, 0))
    piece = pl.BlockSpec((1, block, units), lambda t, m: (m, 1 - t, 0))
    vmem = pl.BlockSpec(memory_space=pltpu.VMEM)
    hidden = jax.ShapeDtypeStruct((parts, tokens, units), BF16)
    sums = jax.ShapeDtypeStruct((parts, 1, units), F32)
    state = jax.ShapeDtypeStruct((block, width), BF16)
    return pl.pallas_call(
        functools.partial(feed_back_kernel, size),
        grid=(2, parts),
        in_specs=[
            rows,
            *packed_specs(packed, width),
            vector,
            vector,
            piece,
            piece,
            ANY,
            *[vmem] * 8,
        ],
        out_specs=[piece, piece, vmem, vmem, ANY, vmem, vmem, vmem, vmem],
        out_shape=[
            hidden,
            hidden,
            sums,
            sums,
            jax.ShapeDtypeStruct((size * block, width // size), BF16),
            state,
            state,
            state,
            jax.ShapeDtypeStruct((1, width), F32),
        ],
        scratch_shapes=[
            pltpu.VMEM((block, width), F32),
            pltpu.VMEM((block, width), BF16),
            pltpu.VMEM((block, width), BF16),
            pltpu.VMEM((parts, 1, units), F32),
            pltpu.VMEM((parts, 1, units), F32),
            *exchange_semaphores(size),
            *core_semaphores(1),
        ],
        compiler_params=remote_params(collective),
        cost_estimate=pl.CostEstimate(
            flops=6 * tokens * width * parts * units, bytes_accessed=70 << 20, transcendentals=0
        ),
        name="feed_back",
    )(
        dbranch,
        packed,
        packed,
        packed,
        s_u,
        s_v,
        up,
        gate,
        result,
        grad_middle,
        middle,
        resid,
        unit,
        branch_scale,
        mixed_scale,
        alpha,
        full_wo,
    )


def feed_grads_kernel(
    size,
    x,
    dbranch,
    dup,
    dgate,
    units,
    dbranch_attn,
    merged,
    dmerged,
    grads,
    grad_wo,
    dattended,
    x_turned,
    d_turned,
    attn_turned,
    send,
    receive,
    local,
):
    exchange = Exchange(
        size,
        dmerged,
        dattended,
        column_part(dattended.shape[1]),
        row_part(dmerged.shape[0]),
        send,
        receive,
        local,
    )

    @pl.when(first_step())
    def _():
        greet_all(size)
        exchange.start()
        x_turned[...] = x[...].T
        d_turned[...] = dbranch[...].T
        attn_turned[...] = dbranch_attn[...].T

    _, chips, rows, _ = grads.shape
    for which, left, right in (
        (0, x_turned, dup),
        (1, x_turned, dgate),
        (2, d_turned, units),
    ):

        @pl.when(pl.program_id(0) == which)
        def _():
            total = dot(left[...], right[0])
            grads[0] = total.astype(BF16).reshape(chips, rows, total.shape[1])

    @pl.when(pl.program_id(0) == 3)
    def _():
        total = dot(attn_turned[...], merged[...])
        grad_wo[...] = total.astype(BF16).reshape(grad_wo.shape)

    @pl.when(last_step())
    def _():
        exchange.wait()


def feed_grads(
    x, dbranch, dup, dgate, units_in, dbranch_attn, merged, dmerged, chips, collective
):
    tokens, width = x.shape
    parts, _, units = dup.shape
    size = parts
    rows = width // chips
    mine = dmerged.shape[0]
    part = width // size

    def whole(array):
        return pl.BlockSpec(array.shape, lambda w, m: (0, 0))

    def turn(w, m, which):
        return jnp.where(w == which, m, jnp.where(w < which, 0, parts - 1))

    def piece(which):
        return pl.BlockSpec((1, tokens, units), lambda w, m: (turn(w, m, which), 0, 0))

    return pl.pallas_call(
        functools.partial(feed_grads_kernel, size),
        grid=(4, parts),
        in_specs=[
            whole(x),
            whole(dbranch),
            piece(0),
            piece(1),
            piece(2),
            whole(dbranch_attn),
            pl.BlockSpec((mine, part), lambda w, m: (0, turn(w, m, 3))),
            ANY,
        ],
        out_specs=[
            pl.BlockSpec(
                (1, chips, rows, units),
                lambda w, m: (jnp.where(w < 3, m, parts - 1), 0, jnp.minimum(w, 2), 0),
            ),
            pl.BlockSpec(
                (1, chips, 2, rows // 2, part), lambda w, m: (turn(w, m, 3), 0, 0, 0, 0)
            ),
            ANY,
        ],
        out_shape=[
            jax.ShapeDtypeStruct((parts, chips, 3 * rows, units), BF16),
            jax.ShapeDtypeStruct((parts, chips, 2, rows // 2, part), BF16),
            jax.ShapeDtypeStruct((size * mine, part), BF16),
        ],
        scratch_shapes=[
            pltpu.VMEM((width, tokens), BF16),
            pltpu.VMEM((width, tokens), BF16),
            pltpu.VMEM((width, mine), BF16),
            *exchange_semaphores(size),
        ],
        compiler_params=remote_params(collective),
        cost_estimate=pl.CostEstimate(
            flops=6 * tokens * width * parts * units, bytes_accessed=40 << 20, transcendentals=0
        ),
        name="feed_grads",
    )(x, dbranch, dup, dgate, units_in, dbranch_attn, merged, dmerged)


def document_starts(doc_ids):
    slot_index = jnp.arange(doc_ids.shape[-1], dtype=jnp.int32)
    earlier = jnp.concatenate([doc_ids[..., :1] - 1, doc_ids[..., :-1]], axis=-1)
    starts = jnp.where(doc_ids != earlier, slot_index, jnp.zeros_like(slot_index))
    return lax.cummax(starts, axis=starts.ndim - 1)


def make_on_device(chips, size):
    def on_device(
        hidden,
        wq,
        wk,
        wv,
        wo,
        w_up,
        w_gate,
        w_down,
        s_qk,
        s_u,
        s_v,
        alpha_a,
        alpha_m,
        doc_ids,
        valid,
        cotangent,
    ):
        _, slots, part = hidden.shape
        width = part * size
        heads = s_qk.shape[0] // DK
        rows = wq.shape[0]
        units = w_up.shape[1] // 2
        mine = slots // size
        block = min(512, slots)
        me = lax.axis_index("mp")
        core = lax.axis_index("core")

        place = paired_place(heads)
        to_pair = placing_matrix(place, heads)
        to_plain = placing_matrix(np.arange(heads * DK), heads)
        turn = np.zeros((part, part), np.float32)
        turn[np.arange(part), place] = 1
        place_pair = jnp.asarray(to_pair, BF16)
        place_plain = jnp.asarray(to_plain, BF16)
        place_delta = jnp.asarray(delta_matrix(heads), BF16)
        collect_plain = jnp.asarray(to_plain.T.reshape(heads, EXT, heads * DK), BF16)
        sums = jnp.asarray(head_sum_matrix(heads), BF16)
        gain = s_qk.reshape(heads, 2, HALF).transpose(1, 0, 2).reshape(1, part)
        docs = doc_ids[0]
        starts = document_starts(docs)
        slot = jnp.arange(slots, dtype=jnp.int32)
        low = jnp.concatenate([starts[::block] // block, me[None]])
        key_docs = jnp.where(valid[0] == 1, docs, -1)
        inverse = jnp.exp(
            jnp.arange(HALF, dtype=F32) * (-2.0 * math.log(ROPE_BASE) / DK)
        )

        vectors = jnp.concatenate([s_u, s_v * math.sqrt(width), alpha_a, alpha_m])
        (
            wide,
            full_qkv,
            packed,
            vectors,
            q,
            k,
            v,
            q_pair,
            k_pair,
            rq,
            rk,
            cosine,
            sine,
        ) = front(
            hidden[0],
            (wq, wk, wv, wo, w_up, w_gate, w_down),
            vectors[None],
            (slot - starts).astype(F32)[:, None],
            jnp.tile(inverse, heads)[None],
            gain,
            jnp.asarray(turn, BF16),
            place_pair,
            place_plain,
            sums,
            size,
            chips,
            0,
        )
        full_qkv = full_qkv.reshape(size, part, 3 * part)
        vectors = vectors[:, 0]
        s_up = lax.dynamic_slice_in_dim(vectors[:, : 2 * units], core * units, units, 1)
        s_gate = lax.dynamic_slice_in_dim(
            vectors[:, 2 * units : 4 * units], core * units, units, 1
        )
        s_up = s_up[:, None, :]
        s_gate = s_gate[:, None, :]
        alpha_attn = vectors[:, 4 * units : 4 * units + part].reshape(1, width)
        alpha_mlp = vectors[:, 4 * units + part :].reshape(1, width)

        attended, qback = attend(
            low,
            q,
            k,
            v,
            docs[:, None],
            key_docs.reshape(slots // block, 1, block),
            collect_plain,
        )
        (
            x,
            middle,
            unit,
            branch_scale,
            mixed_scale,
            merged,
            full_wo,
            resid,
            cotangent_low,
        ) = mix(attended, packed, rows, wide, alpha_attn, cotangent[0], 1)

        up, gate, hidden_units, result, grad_middle, dbranch, grad_alpha_mlp = feed(
            x, packed, s_up, s_gate, cotangent_low, middle, alpha_mlp, 2
        )
        (
            dup,
            dgate,
            grad_u,
            grad_v,
            out_low,
            grad_resid,
            dbranch_attn,
            dmerged,
            grad_alpha_attn,
        ) = feed_back(
            dbranch,
            packed,
            s_up,
            s_gate,
            up,
            gate,
            result,
            grad_middle,
            middle,
            resid,
            unit,
            branch_scale,
            mixed_scale,
            alpha_attn,
            full_wo,
            3,
        )
        out_hidden = out_low.astype(F32)
        grads, grad_wo, dattended = feed_grads(
            x, dbranch, dup, dgate, hidden_units, dbranch_attn, merged, dmerged, chips, 4
        )

        term, grad_qkv, grad_gain = attend_back(
            low,
            qback,
            q_pair,
            dattended,
            attended,
            k,
            k_pair,
            v,
            docs.reshape(slots // block, 1, block),
            key_docs[:, None],
            cosine,
            sine,
            rq,
            rk,
            gain,
            full_qkv,
            place_plain,
            place_delta,
            sums,
            wide,
            grad_resid,
        )
        out_pairs = (
            lambda w: w.reshape(w.shape[0], 2, heads, HALF)
            .transpose(0, 2, 1, 3)
            .reshape(w.shape[0], heads * DK)
        )

        zero = jnp.zeros((size, 2, units), F32)
        placed_u = lax.dynamic_update_slice(zero, grad_u, (0, core, 0))
        placed_v = lax.dynamic_update_slice(zero, grad_v * math.sqrt(width), (0, core, 0))
        placed_qk = lax.dynamic_update_slice(
            jnp.zeros((size, part), F32), out_pairs(grad_gain), (me, 0)
        )
        placed = jnp.concatenate(
            [
                placed_u.reshape(size, 2 * units),
                placed_v.reshape(size, 2 * units),
                placed_qk,
                grad_alpha_attn.reshape(size, part),
                grad_alpha_mlp.reshape(size, part),
            ],
            axis=1,
        )
        grad_hidden, owned, owned_output, owned_qkv, summed = sum_all(
            term,
            grads,
            grad_wo,
            grad_qkv.reshape(chips, 2, rows, 3 * part),
            placed[:, None],
            chips,
            5,
        )
        owned_upward, owned_gating, owned_downward = owned[0], owned[1], owned[2].T
        owned_output = owned_output.T
        owned_query = out_pairs(owned_qkv[:, :part])
        owned_keys = out_pairs(owned_qkv[:, part : 2 * part])
        owned_values = owned_qkv[:, 2 * part :]
        bounds = [2 * units, 4 * units, 4 * units + part, 4 * units + 2 * part]
        summed_up, summed_gate, summed_qk, summed_attn, summed_mlp = jnp.split(
            summed[0], bounds
        )
        return (
            out_hidden[None],
            grad_hidden[None],
            owned_query,
            owned_keys,
            owned_values,
            owned_output,
            owned_upward,
            owned_gating,
            owned_downward,
            summed_qk,
            summed_up,
            summed_gate,
            summed_attn,
            summed_mlp,
        )

    return on_device


def solution(mesh):
    rows, size = mesh.shape["dp"], mesh.shape["mp"]
    paired = Mesh(mesh.devices.reshape(rows // 2, 2, size), ("chip", "core", "mp"))
    return jax.shard_map(
        make_on_device(rows // 2, size),
        mesh=paired,
        in_specs=(
            P(DP, None, "mp"),
            P(DP, "mp"),
            P(DP, "mp"),
            P(DP, "mp"),
            P("mp", DP),
            P(DP, "mp"),
            P(DP, "mp"),
            P("mp", DP),
            P("mp"),
            P("mp"),
            P("mp"),
            P("mp"),
            P("mp"),
            P(DP, None),
            P(DP, None),
            P(DP, None, "mp"),
        ),
        out_specs=(
            P(DP, None, "mp"),
            P(DP, None, "mp"),
            P(DP, "mp"),
            P(DP, "mp"),
            P(DP, "mp"),
            P("mp", DP),
            P(DP, "mp"),
            P(DP, "mp"),
            P("mp", DP),
            P("mp"),
            P("mp"),
            P("mp"),
            P("mp"),
            P("mp"),
        ),
        check_vma=False,
    )
```

```python
import functools
import math

import jax
import jax.numpy as jnp
import numpy as np
from jax import lax
from jax.experimental import pallas as pl
from jax.experimental.pallas import tpu as pltpu
from jax.sharding import Mesh
from jax.sharding import PartitionSpec as P

DK = 64
HALF = DK // 2
EXT = 128
EPSILON = 1e-06
ROPE_BASE = 10000.0
VMEM_LIMIT = 60 * 1024 * 1024
F32 = jnp.float32
BF16 = jnp.bfloat16
DP = ("chip", "core")


def dot(left, right, dims=((1,), (0,)), precision=None):
    return lax.dot_general(
        left, right, (dims, ((), ())), precision=precision, preferred_element_type=F32
    )


NT = ((1,), (1,))
TN = ((0,), (0,))


def grid_params(dims):
    return pltpu.CompilerParams(
        dimension_semantics=("arbitrary",) * dims, vmem_limit_bytes=VMEM_LIMIT
    )


ANY = pl.BlockSpec(memory_space=pl.ANY)


def remote_params(collective, **more):
    return pltpu.CompilerParams(
        collective_id=collective,
        has_side_effects=True,
        vmem_limit_bytes=VMEM_LIMIT,
        **more,
    )


def to_device(source, target, send, receive, where):
    return pltpu.make_async_remote_copy(
        src_ref=source,
        dst_ref=target,
        send_sem=send,
        recv_sem=receive,
        device_id=where,
        device_id_type=pl.DeviceIdType.MESH,
    )


def to_member(source, target, send, receive, member):
    return to_device(source, target, send, receive, {"mp": member})


def flip(index, mask):
    bit = 1
    while bit <= mask:
        if mask & bit:
            index = index + bit - 2 * bit * lax.rem(lax.div(index, bit), 2)
        bit *= 2
    return index


def bits_below(count):
    return [1 << k for k in range(count.bit_length() - 1)]


def greet(where):
    pl.semaphore_signal(
        pltpu.get_barrier_semaphore(),
        inc=1,
        device_id=where,
        device_id_type=pl.DeviceIdType.MESH,
    )


def greet_all(size):
    me = lax.axis_index("mp")
    for k in range(1, size):
        greet({"mp": flip(me, k)})
    pl.semaphore_wait(pltpu.get_barrier_semaphore(), size - 1)


def greet_around(size, chips):
    me, chip, core = (lax.axis_index(name) for name in ("mp", "chip", "core"))
    for k in range(1, size):
        greet({"mp": flip(me, k)})
    for bit in bits_below(chips):
        greet({"chip": flip(chip, bit)})
    greet({"core": 1 - core})
    pl.semaphore_wait(pltpu.get_barrier_semaphore(), size + len(bits_below(chips)))


class Exchange:
    def __init__(self, size, source, target, piece, place, send, receive, local):
        me = lax.axis_index("mp")
        self.local = pltpu.make_async_copy(piece(source, me), place(target, me), local)
        self.remote = [
            to_member(
                piece(source, flip(me, k)),
                place(target, me),
                send.at[k],
                receive.at[k],
                flip(me, k),
            )
            for k in range(1, size)
        ]

    def start(self):
        for copy in self.remote:
            copy.start()
        self.local.start()

    def wait(self):
        self.local.wait()
        for copy in self.remote:
            copy.wait()


def exchange_semaphores(size):
    return [
        pltpu.SemaphoreType.DMA((size,)),
        pltpu.SemaphoreType.DMA((size,)),
        pltpu.SemaphoreType.DMA,
    ]


def row_part(rows):
    return lambda ref, j: ref.at[pl.ds(pl.multiple_of(j * rows, rows), rows), :]


def column_part(columns):
    return lambda ref, j: ref.at[:, pl.ds(pl.multiple_of(j * columns, columns), columns)]


class Gather:
    def __init__(self, block, index, bits, where, send, receive):
        self.block, self.index, self.bits, self.where = block, index, bits, where
        self.send, self.receive = send, receive

    def copies(self, stage, incoming):
        span = [0]
        for bit in self.bits[:stage]:
            span += [held | bit for held in span]
        bit = self.bits[stage]
        for order, held in enumerate(span):
            ref = self.block(flip(self.index, held | bit if incoming else held))
            slot = (1 << stage) - 1 + order
            yield to_device(
                ref,
                ref,
                self.send(slot),
                self.receive(slot),
                self.where(flip(self.index, bit)),
            )

    def start(self, stage):
        if stage < len(self.bits):
            for copy in self.copies(stage, False):
                copy.start()

    def arrive(self, stage):
        if stage < len(self.bits):
            for copy in self.copies(stage, True):
                copy.wait_recv()

    def close(self):
        for stage in range(len(self.bits)):
            for copy in self.copies(stage, False):
                copy.wait_send()


EARLY = 2


def front_kernel(
    size,
    chips,
    chunks,
    split,
    hidden,
    wq,
    wk,
    wv,
    wo,
    w_up,
    w_gate,
    w_down,
    vectors,
    columns,
    frequency,
    gain,
    in_pairs,
    place_pair,
    place_plain,
    sums,
    wide_out,
    qkv_out,
    full,
    full_vectors,
    q_out,
    k_out,
    v_out,
    q_pair_out,
    k_pair_out,
    rq_out,
    rk_out,
    cosine_out,
    sine_out,
    wide,
    full_qkv,
    packed,
    matrices,
    wo_turned,
    q,
    k,
    v,
    q_pair,
    k_pair,
    rq,
    rk,
    cosine,
    sine,
    local,
    out_sems,
    core_sent,
    core_got,
    hidden_up,
    hidden_down,
    hidden_got,
    packed_up,
    packed_down,
    packed_got,
    plane_sent,
    plane_got,
    qkv_sent,
    qkv_got,
    vector_sent,
    vector_got,
):
    me, chip, core = (lax.axis_index(name) for name in ("mp", "chip", "core"))
    tokens, part = hidden.shape
    rows = tokens // chunks
    height, units = packed.shape
    lines = height // 7
    owner = chip * 2 + core
    bits = bits_below(chips)
    stages = len(bits)
    greet_around(size, chips)

    def hidden_hop(origin, chunk, member, send):
        at = pl.ds(pl.multiple_of(chunk * rows, rows), rows)
        ref = wide.at[origin, at, :]
        return to_member(ref, ref, send.at[origin, chunk], hidden_got.at[origin, chunk], member)

    def send_hidden(chunk):
        @pl.when(me < size - 1)
        def _():
            hidden_hop(me, chunk, me + 1, hidden_up).start()

        @pl.when(me > 0)
        def _():
            hidden_hop(me, chunk, me - 1, hidden_down).start()

    for chunk in range(EARLY):
        at = pl.ds(chunk * rows, rows)
        wide[me, at, :] = hidden[at, :].astype(BF16)
        send_hidden(chunk)

    matrices[0] = w_up[...].astype(BF16)
    matrices[1] = w_gate[...].astype(BF16)
    matrices[2] = w_down[...].T.astype(BF16)
    wo_turned[...] = wo[...].T.astype(BF16)

    def half_of(which):
        return pl.ds(pl.multiple_of(which * units, units), units)

    def place_of(matrix):
        return pl.ds(pl.multiple_of((2 * matrix + core) * lines, lines), lines)

    wo_place = (
        pl.ds(6 * lines, lines),
        pl.ds(pl.multiple_of(core * part, part), part),
    )
    given = [
        to_device(
            matrices.at[matrix, :, half_of(1 - core)],
            packed.at[place_of(matrix), :],
            core_sent.at[matrix],
            core_got.at[matrix],
            {"core": 1 - core},
        )
        for matrix in range(3)
    ]
    given.append(
        to_device(
            wo_turned, packed.at[wo_place], core_sent.at[3], core_got.at[3], {"core": 1 - core}
        )
    )
    for copy in given:
        copy.start()
    for matrix in range(3):
        packed[place_of(matrix), :] = matrices[matrix, :, half_of(core)]
    packed[wo_place] = wo_turned[...]
    full_qkv[owner] = jnp.concatenate(
        [
            dot(wq[...].astype(BF16), in_pairs[...]).astype(BF16),
            dot(wk[...].astype(BF16), in_pairs[...]).astype(BF16),
            wv[...].astype(BF16),
        ],
        axis=1,
    )

    def packed_hop(origin, ref, member, send):
        return to_member(
            ref, full.at[origin, chip], send.at[origin], packed_got.at[origin], member
        )

    vector_copies = [
        to_member(
            vectors, full_vectors.at[me], vector_sent.at[k], vector_got.at[k], flip(me, k)
        )
        for k in range(1, size)
    ]

    def plane(origin, slot):
        return [
            Gather(
                lambda i, at=at: full.at[origin, i, at, :],
                chip,
                order,
                lambda i: {"chip": i},
                lambda k, half=half: plane_sent.at[slot, half, k],
                lambda k, half=half: plane_got.at[slot, half, k],
            )
            for half, (at, order) in enumerate(
                (
                    (pl.ds(0, split), bits),
                    (pl.ds(split, height - split), bits[::-1]),
                )
            )
        ]

    gather_qkv = Gather(
        lambda i: full_qkv.at[i],
        owner,
        [2 * bit for bit in bits] + [1],
        lambda i: {"chip": lax.div(i, 2), "core": lax.rem(i, 2)},
        lambda k: qkv_sent.at[k],
        lambda k: qkv_got.at[k],
    )

    sources = {0: [(me >= 0, me, 0, None)]}
    for distance in range(1, size):
        sources[distance] = [
            (me >= distance, me - distance, 2 * distance - 1, True),
            (me + distance < size, me + distance, 2 * distance, False),
        ]

    def pass_on(origin, ref, upward):
        if upward is not False:

            @pl.when(me < size - 1)
            def _():
                packed_hop(origin, ref, me + 1, packed_up).start()

        if not upward:

            @pl.when(me > 0)
            def _():
                packed_hop(origin, ref, me - 1, packed_down).start()

    def advance(distance, stage):
        for exists, origin, slot, _ in sources[distance]:

            @pl.when(exists)
            def _():
                for half in plane(origin, slot):
                    half.arrive(stage)
                    half.start(stage + 1)

    for copy in given:
        copy.wait_recv()
    pass_on(me, packed, None)
    own = [
        pltpu.make_async_copy(packed, full.at[me, chip], local.at[0]),
        pltpu.make_async_copy(vectors, full_vectors.at[me], local.at[1]),
    ]
    for copy in own:
        copy.start()
    gather_qkv.start(0)
    for copy in vector_copies:
        copy.start()
    for chunk in range(EARLY, chunks):
        at = pl.ds(chunk * rows, rows)
        wide[me, at, :] = hidden[at, :].astype(BF16)
    own[0].wait()
    for half in plane(me, 0):
        half.start(0)
    for chunk in range(chunks):
        at = pl.ds(chunk * rows, rows)
        angles = columns[at, 0:1] * frequency[...]
        cosine[at, :] = jnp.cos(angles)
        sine[at, :] = jnp.sin(angles)
    for stage in range(stages):
        gather_qkv.arrive(stage)
        gather_qkv.start(stage + 1)
    advance(0, 0)
    for distance in range(1, size):
        for exists, origin, slot, upward in sources[distance]:

            @pl.when(exists)
            def _():
                block = full.at[origin, chip]
                packed_hop(origin, block, me, packed_up).wait_recv()
                pass_on(origin, block, upward)
                for half in plane(origin, slot):
                    half.start(0)

        @pl.when(jnp.maximum(me, size - 1 - me) == distance)
        def _():
            for chunk in range(EARLY, chunks):
                send_hidden(chunk)

        if distance > 1:
            advance(distance - 1, 0)
    gather_qkv.arrive(stages)
    qkv_copy = pltpu.make_async_copy(full_qkv, qkv_out, local.at[2])
    qkv_copy.start()
    advance(size - 1, 0)

    def come(distance, chunk):
        for exists, origin, _, upward in sources[distance]:

            @pl.when(exists)
            def _():
                hidden_hop(origin, chunk, me, hidden_up).wait_recv()
                if upward:

                    @pl.when(me < size - 1)
                    def _():
                        hidden_hop(origin, chunk, me + 1, hidden_up).start()
                else:

                    @pl.when(me > 0)
                    def _():
                        hidden_hop(origin, chunk, me - 1, hidden_down).start()

    for distance in range(1, size - 1):
        for chunk in range(chunks):
            come(distance, chunk)

    results = (
        (q, q_out),
        (k, k_out),
        (v, v_out),
        (q_pair, q_pair_out),
        (k_pair, k_pair_out),
        (rq, rq_out),
        (rk, rk_out),
        (cosine, cosine_out),
        (sine, sine_out),
        (wide, wide_out),
    )

    def write_out(chunk):
        at = pl.ds(pl.multiple_of(chunk * rows, rows), rows)
        for order, (here, there) in enumerate(results):
            lead = (slice(None),) * (len(here.shape) - 2)
            yield pltpu.make_async_copy(
                here.at[(*lead, at)], there.at[(*lead, at)], out_sems.at[order, chunk]
            )

    each = part // lines

    def finish(chunk, carry):
        come(size - 1, chunk)
        at = pl.ds(pl.multiple_of(chunk * rows, rows), rows)
        project_block(
            [wide[member, at, :] for member in range(size)],
            [
                full_qkv[member * each : (member + 1) * each].reshape(part, 3 * part)
                for member in range(size)
            ],
            cosine[at, :],
            sine[at, :],
            gain[...],
            place_pair[...],
            place_plain[...],
            sums[...],
            at,
            [here for here, _ in results[:7]],
        )
        for copy in write_out(chunk):
            copy.start()
        return carry

    lax.fori_loop(0, chunks, finish, 0)
    for stage in range(1, stages):
        for distance in range(size):
            advance(distance, stage)

    own[1].wait()
    qkv_copy.wait()
    for copy in vector_copies:
        copy.wait()
    for copy in given:
        copy.wait_send()
    for chunk in range(chunks):
        for copy in write_out(chunk):
            copy.wait()
    gather_qkv.close()
    for distance in range(size):
        for exists, origin, slot, upward in sources[distance]:

            @pl.when(exists)
            def _():
                for half in plane(origin, slot):
                    half.close()
                block = packed if distance == 0 else full.at[origin, chip]
                if upward is not False:

                    @pl.when(me < size - 1)
                    def _():
                        packed_hop(origin, block, me, packed_up).wait_send()
                        for chunk in range(chunks):
                            hidden_hop(origin, chunk, me, hidden_up).wait_send()

                if not upward:

                    @pl.when(me > 0)
                    def _():
                        packed_hop(origin, block, me, packed_down).wait_send()
                        for chunk in range(chunks):
                            hidden_hop(origin, chunk, me, hidden_down).wait_send()


def front(
    hidden,
    weights,
    vectors,
    positions,
    frequency,
    gain,
    in_pairs,
    place_pair,
    place_plain,
    sums,
    size,
    chips,
    collective,
):
    chunks = 6
    tokens, part = hidden.shape
    lines, both = weights[4].shape
    units = both // 2
    heads = part // DK
    height = 7 * lines
    dma = pltpu.SemaphoreType.DMA
    line = dma((size, chunks))
    plane = dma((2 * size - 1, 2, max(chips - 1, 1)))
    vmem = pl.BlockSpec(memory_space=pltpu.VMEM)
    padded = ((heads, tokens, EXT), BF16)
    paired = ((tokens, part), BF16)
    scale = ((tokens, heads * HALF), F32)
    wide = ((size, tokens, part), BF16)
    qkv = ((2 * chips, lines, 3 * part), BF16)
    results = [padded, padded, padded, paired, paired, scale, scale, scale, scale]
    return pl.pallas_call(
        functools.partial(front_kernel, size, chips, chunks, height // 32 * 16),
        in_specs=[vmem] * 16,
        out_specs=[ANY] * 13,
        out_shape=[
            jax.ShapeDtypeStruct(*each)
            for each in [
                wide,
                qkv,
                ((size, chips, height, units), BF16),
                ((size, *vectors.shape), F32),
                *results,
            ]
        ],
        scratch_shapes=[
            pltpu.VMEM(*wide),
            pltpu.VMEM(*qkv),
            pltpu.VMEM((height, units), BF16),
            pltpu.VMEM((3, lines, both), BF16),
            pltpu.VMEM((lines, part), BF16),
            *[pltpu.VMEM(*each) for each in results],
            dma((3,)),
            dma((10, chunks)),
            dma((4,)),
            dma((4,)),
            line,
            line,
            line,
            dma((size,)),
            dma((size,)),
            dma((size,)),
            plane,
            plane,
            dma((2 * chips - 1,)),
            dma((2 * chips - 1,)),
            dma((size,)),
            dma((size,)),
        ],
        compiler_params=remote_params(collective),
        name="front",
    )(
        hidden,
        *weights,
        vectors,
        positions,
        frequency,
        gain,
        in_pairs,
        place_pair,
        place_plain,
        sums,
    )


class LineSum:
    def __init__(self, size, chunks, term, up, down, sems):
        self.size, self.chunks = size, chunks
        self.term, self.up, self.down = term, up, down
        self.sent_up, self.sent_down, self.got_up, self.got_down = sems
        self.me = lax.axis_index("mp")
        self.rows = up.shape[1] // chunks

    def at(self, chunk):
        return pl.ds(chunk * self.rows, self.rows)

    def hop(self, upward, goal, chunk, member):
        slots = self.up if upward else self.down
        send = self.sent_up if upward else self.sent_down
        receive = self.got_up if upward else self.got_down
        ref = slots.at[goal, self.at(chunk), :]
        return to_member(ref, ref, send.at[goal, chunk], receive.at[goal, chunk], member)

    def step(self, order, chunk):
        me, last, at = self.me, self.size - 1, self.at(chunk)
        for upward, goal, ahead, first, member in (
            (True, last - order, me < last - order, me == 0, me + 1),
            (False, order, me > order, me == last, me - 1),
        ):
            slots = self.up if upward else self.down

            @pl.when(ahead & first)
            def _():
                slots[goal, at, :] = self.term(goal, at)

            @pl.when(ahead & jnp.logical_not(first))
            def _():
                self.hop(upward, goal, chunk, me).wait_recv()
                slots[goal, at, :] = (
                    slots[goal, at, :].astype(F32) + self.term(goal, at).astype(F32)
                ).astype(BF16)

            if order > 0:
                older = goal + 1 if upward else goal - 1
                sent = (me < older) if upward else (me > older)

                @pl.when(sent)
                def _():
                    self.hop(upward, older, chunk, member).wait_send()

            @pl.when(ahead)
            def _():
                self.hop(upward, goal, chunk, member).start()

    def result(self, chunk, out, out_at):
        me, at = self.me, self.at(chunk)
        out[out_at, :] = self.term(me, at).astype(F32)

        @pl.when(me > 0)
        def _():
            self.hop(True, me, chunk, me).wait_recv()
            out[out_at, :] += self.up[me, at, :].astype(F32)

        @pl.when(me < self.size - 1)
        def _():
            self.hop(False, me, chunk, me).wait_recv()
            out[out_at, :] += self.down[me, at, :].astype(F32)

    def close(self):
        order = self.size - 2
        for chunk in range(self.chunks):

            @pl.when(self.me < self.size - 1 - order)
            def _():
                self.hop(True, self.size - 1 - order, chunk, self.me).wait_send()

            @pl.when(self.me > order)
            def _():
                self.hop(False, order, chunk, self.me).wait_send()


MIDDLE, LATE = 4, 5


class ChipSum:
    def __init__(self, layers, bits, source, acc, got, load, send, receive):
        self.layers, self.bits = layers, bits
        self.acc, self.got, self.chip = acc, got, lax.axis_index("chip")
        self.half = 1 << (len(bits) - 1)
        self.load = [
            pltpu.make_async_copy(
                source(layer, flip(self.chip, self.combo(slot))),
                acc.at[layer, slot],
                load.at[layer, slot],
            )
            for layer in layers
            for slot in range(self.half)
        ]
        self.source, self.sent, self.received = source, send, receive

    def combo(self, slot):
        count = len(self.bits)
        return sum(self.bits[count - 1 - j] for j in range(count - 1) if slot >> j & 1)

    def copies(self, stage):
        count = self.half >> stage
        offset = 2 * self.half - 2 * count
        where = {"chip": flip(self.chip, self.bits[stage])}
        for layer in self.layers:
            for slot in range(count):
                if stage == 0:
                    other = flip(self.chip, self.bits[0] | self.combo(slot))
                    ref = self.source(layer, other)
                else:
                    ref = self.acc.at[layer, count + slot]
                at = offset + slot
                yield layer, slot, at, to_device(
                    ref,
                    self.got.at[layer, at],
                    self.sent.at[layer, at],
                    self.received.at[layer, at],
                    where,
                )

    def start(self, stage):
        if stage == 0:
            for copy in self.load:
                copy.start()
        for _, _, _, copy in self.copies(stage):
            copy.start()

    def add(self, stage):
        if stage == 0:
            for copy in self.load:
                copy.wait()
        for layer, slot, at, copy in self.copies(stage):
            copy.wait_recv()
            self.acc[layer, slot] = (
                self.acc[layer, slot].astype(F32) + self.got[layer, at].astype(F32)
            ).astype(BF16)

    def close(self):
        for stage in range(len(self.bits)):
            for _, _, _, copy in self.copies(stage):
                copy.wait_send()


def sum_all_kernel(
    size,
    chips,
    chunks,
    split,
    term,
    grads,
    grad_wo,
    grad_qkv,
    vectors,
    out_pairs,
    out,
    owned_up,
    owned_gate,
    owned_down,
    owned_wo,
    owned_q,
    owned_k,
    owned_v,
    owned_vectors,
    term_up,
    term_down,
    acc_a,
    got_a,
    up_a,
    down_a,
    acc_b,
    got_b,
    up_b,
    down_b,
    pair_wo,
    other_wo,
    acc_wo,
    got_wo,
    up_wo,
    down_wo,
    pair_qkv,
    other_qkv,
    acc_qkv,
    got_qkv,
    whole,
    owned,
    turned_wo,
    vector_sum,
    vector_got,
    vector_line,
    local,
    core_sent,
    core_got,
    vector_sent,
    vector_received,
    term_sems,
    line_sems,
    load_sems,
    chip_sent,
    chip_got,
):
    me, chip, core = (lax.axis_index(name) for name in ("mp", "chip", "core"))
    bits = bits_below(chips)
    stages = len(bits)
    greet_around(size, chips)
    other_core_is = {"core": 1 - core}

    def sems(ref, which):
        return [ref.at[which, k] for k in range(4)]

    line = LineSum(
        size, chunks, lambda goal, at: term[goal, at, :], term_up, term_down, sems(term_sems, 0)
    )
    ends = sorted({0, size - 1})
    inner = [layer for layer in range(size) if layer not in ends]

    def plane_sums(layers):
        return [
            ChipSum(
                layers,
                bits,
                lambda m, c: grads.at[m, c, pl.ds(0, split), :],
                acc_a,
                got_a,
                load_sems.at[0],
                chip_sent.at[0],
                chip_got.at[0],
            ),
            ChipSum(
                layers,
                bits[::-1],
                lambda m, c: grads.at[m, c, pl.ds(split, grads.shape[2] - split), :],
                acc_b,
                got_b,
                load_sems.at[1],
                chip_sent.at[1],
                chip_got.at[1],
            ),
        ]

    sums_ends, sums_inner = plane_sums(ends), plane_sums(inner)
    sum_wo = ChipSum(
        range(size),
        bits[::-1],
        lambda m, c: pair_wo.at[m, c],
        acc_wo,
        got_wo,
        load_sems.at[2],
        chip_sent.at[2],
        chip_got.at[2],
    )
    sum_qkv = ChipSum(
        range(1),
        bits,
        lambda m, c: pair_qkv.at[c],
        acc_qkv,
        got_qkv,
        load_sems.at[3],
        chip_sent.at[3],
        chip_got.at[3],
    )
    lines = [
        LineSum(
            size,
            1,
            lambda goal, at, acc=acc: acc[goal, 0, at, :],
            up,
            down,
            sems(line_sems, which),
        )
        for which, (acc, up, down) in enumerate(
            ((acc_a, up_a, down_a), (acc_b, up_b, down_b), (acc_wo, up_wo, down_wo))
        )
    ]

    own = [
        pltpu.make_async_copy(grad_wo.at[:, :, core], pair_wo, local.at[0]),
        pltpu.make_async_copy(grad_qkv.at[:, core], pair_qkv, local.at[1]),
    ]
    given = [
        to_device(
            grad_wo.at[:, :, 1 - core], other_wo, core_sent.at[0], core_got.at[0], other_core_is
        ),
        to_device(
            grad_qkv.at[:, 1 - core], other_qkv, core_sent.at[1], core_got.at[1], other_core_is
        ),
    ]
    vector_copies = [
        to_member(
            vectors.at[flip(me, k)],
            vector_line.at[k],
            vector_sent.at[k],
            vector_received.at[k],
            flip(me, k),
        )
        for k in range(1, size)
    ]
    for copy in own + given:
        copy.start()
    for part in sums_ends:
        part.start(0)
    for copy in vector_copies:
        copy.start()

    owner = chip * 2 + core
    vector_bits = [1] + [2 * bit for bit in bits]

    def vector_copy(stage):
        partner = flip(owner, vector_bits[stage])
        return to_device(
            vector_sum.at[stage],
            vector_got.at[stage],
            vector_sent.at[size + stage],
            vector_received.at[size + stage],
            {"chip": lax.div(partner, 2), "core": lax.rem(partner, 2)},
        )

    def vector_step(stage):
        if stage == 0:
            total = vectors[me]
            for k, copy in enumerate(vector_copies):
                copy.wait_recv()
                total = total + vector_line[k + 1]
            vector_sum[0] = total
        else:
            vector_copy(stage - 1).wait_recv()
            vector_sum[stage] = vector_sum[stage - 1] + vector_got[stage - 1]
        if stage < len(vector_bits):
            vector_copy(stage).start()

    def add(group, stage):
        for part in group:
            part.add(stage)
            if stage + 1 < stages:
                part.start(stage + 1)

    small = [sum_wo, sum_qkv]
    rest = [*sums_inner, *small]
    vector_at = 0
    for order in range(size - 1):
        for chunk in range(chunks):
            line.step(order, chunk)
            if order == 0 and chunk >= 1 and vector_at <= len(vector_bits):
                vector_step(vector_at)
                vector_at += 1
            if order == 1 and chunk == MIDDLE:
                for stage in range(1, stages):
                    add(sums_ends, stage)
                for part in rest:
                    part.start(0)
            if order == 2 and chunk == LATE:
                add(rest, 0)
        if order == 0:
            for copy in own:
                copy.wait()
            for copy in given:
                copy.wait_recv()
            pair_wo[...] = (pair_wo[...].astype(F32) + other_wo[...].astype(F32)).astype(BF16)
            pair_qkv[...] = (pair_qkv[...].astype(F32) + other_qkv[...].astype(F32)).astype(
                BF16
            )
            add(sums_ends, 0)
        if order == 1:
            lines[0].step(0, 0)
            lines[1].step(0, 0)
    for stage in range(1, stages):
        add(rest, stage)
    for order in range(size - 1):
        if order > 0:
            lines[0].step(order, 0)
            lines[1].step(order, 0)
        lines[2].step(order, 0)
    for stage in range(vector_at, len(vector_bits) + 1):
        vector_step(stage)
    for chunk in range(chunks):
        line.result(chunk, out, line.at(chunk))
    owned_vectors[...] = vector_sum[len(vector_bits)]
    part = owned_v.shape[1]
    total_qkv = acc_qkv[0, 0]
    owned_q[...] = dot(total_qkv[:, :part], out_pairs[...])
    owned_k[...] = dot(total_qkv[:, part : 2 * part], out_pairs[...])
    owned_v[...] = total_qkv[:, 2 * part :].astype(F32)
    lines[0].result(0, whole, pl.ds(0, split))
    lines[1].result(0, whole, pl.ds(split, whole.shape[0] - split))
    lines[2].result(0, turned_wo, slice(None))

    matrices, rows, columns = owned.shape
    columns = columns // 2
    place = pl.ds(pl.multiple_of(core * columns, columns), columns)
    swaps = []
    for matrix in range(matrices):
        mine = pl.ds(pl.multiple_of((2 * matrix + core) * rows, rows), rows)
        theirs = pl.ds(pl.multiple_of((2 * matrix + 1 - core) * rows, rows), rows)
        swaps.append(
            to_device(
                whole.at[theirs, :],
                owned.at[matrix, :, place],
                core_sent.at[2 + matrix],
                core_got.at[2 + matrix],
                other_core_is,
            )
        )
        swaps[-1].start()
        copy = pltpu.make_async_copy(
            whole.at[mine, :], owned.at[matrix, :, place], local.at[2 + matrix]
        )
        copy.start()
        swaps.append(copy)
    owned_wo[...] = turned_wo[...].T
    for copy in swaps:
        copy.wait()
    owned_up[...] = owned[0]
    owned_gate[...] = owned[1]
    owned_down[...] = owned[2].T

    for copy in given + vector_copies:
        copy.wait_send()
    for stage in range(len(vector_bits)):
        vector_copy(stage).wait_send()
    for part in [*sums_ends, *rest]:
        part.close()
    line.close()
    for part in lines:
        part.close()


def sum_all(term, grads, grad_wo, grad_qkv, vectors, out_pairs, chips, collective):
    size, tokens, part = term.shape
    height, units = grads.shape[2:]
    rows = height // 6
    chunks = 6
    split = height // 32 * 16
    half, blocks = max(chips // 2, 1), max(chips - 1, 1)
    stages = chips.bit_length()
    dma = pltpu.SemaphoreType.DMA
    vmem = pl.BlockSpec(memory_space=pltpu.VMEM)
    wo_block, qkv_block = grad_wo.shape[3:], grad_qkv.shape[2:]
    long = vectors.shape[1:]

    def sums(layers, block):
        return [
            pltpu.VMEM((layers, half, *block), BF16),
            pltpu.VMEM((layers, blocks, *block), BF16),
        ]

    def line(block):
        return [pltpu.VMEM((size, *block), BF16)] * 2

    return pl.pallas_call(
        functools.partial(sum_all_kernel, size, chips, chunks, split),
        in_specs=[vmem, ANY, ANY, ANY, vmem, vmem],
        out_specs=[vmem] * 9,
        out_shape=[
            jax.ShapeDtypeStruct((tokens, part), F32),
            jax.ShapeDtypeStruct((rows, 2 * units), F32),
            jax.ShapeDtypeStruct((rows, 2 * units), F32),
            jax.ShapeDtypeStruct((2 * units, rows), F32),
            jax.ShapeDtypeStruct(wo_block[::-1], F32),
            *[jax.ShapeDtypeStruct((qkv_block[0], part), F32)] * 3,
            jax.ShapeDtypeStruct(long, F32),
        ],
        scratch_shapes=[
            *line((tokens, part)),
            *sums(size, (split, units)),
            *line((split, units)),
            *sums(size, (height - split, units)),
            *line((height - split, units)),
            pltpu.VMEM((size, chips, *wo_block), BF16),
            pltpu.VMEM((size, chips, *wo_block), BF16),
            *sums(size, wo_block),
            *line(wo_block),
            pltpu.VMEM((chips, *qkv_block), BF16),
            pltpu.VMEM((chips, *qkv_block), BF16),
            *sums(1, qkv_block),
            pltpu.VMEM((height, units), F32),
            pltpu.VMEM((3, rows, 2 * units), F32),
            pltpu.VMEM(wo_block, F32),
            pltpu.VMEM((stages + 1, *long), F32),
            pltpu.VMEM((stages + 1, *long), F32),
            pltpu.VMEM((size, *long), F32),
            dma((5,)),
            dma((5,)),
            dma((5,)),
            dma((size + stages,)),
            dma((size + stages,)),
            dma((1, 4, size, chunks)),
            dma((3, 4, size, 1)),
            dma((4, size, half)),
            dma((4, size, blocks)),
            dma((4, size, blocks)),
        ],
        compiler_params=remote_params(collective),
        name="sum_all",
    )(term, grads, grad_wo, grad_qkv, vectors, out_pairs)


def paired_place(heads):
    head, feature = np.divmod(np.arange(heads * DK), DK)
    return (feature // HALF) * (heads * HALF) + head * HALF + feature % HALF


def placing_matrix(place, heads):
    head, feature = np.divmod(np.arange(heads * DK), DK)
    matrix = np.zeros((heads * DK, heads * EXT), np.float32)
    matrix[place, head * EXT + feature] = 1
    return matrix


def delta_matrix(heads):
    lane = np.arange(heads * EXT)
    head = np.arange(heads * DK) // DK
    return ((head[:, None] == lane[None, :] // EXT) & (lane % EXT >= DK) & (lane % EXT < DK + 3)).astype(
        np.float32
    )


def head_sum_matrix(heads):
    lane = np.arange(heads * HALF) // HALF
    return (lane[:, None] == lane[None, :]).astype(np.float32)


def split_dot(value, matrix):
    high = value.astype(BF16)
    rest = (value - high.astype(F32)).astype(BF16)
    return dot(high, matrix) + dot(rest, matrix)


def project_block(wide, weight, cos, sin, gain, place_pair, place_plain, sums, at, outs):
    q, k, v, q_pair, k_pair, rq, rk = outs
    heads = q.shape[0]
    pair, width = heads * HALF, heads * DK
    raw = dot(wide[0], weight[0])
    for part in range(1, len(wide)):
        raw += dot(wide[part], weight[part])
    lane = lax.broadcasted_iota(jnp.int32, (raw.shape[0], EXT), 1)
    for offset, out, pair_out, scale_out, factor in (
        (0, q, q_pair, rq, math.sqrt(DK)),
        (width, k, k_pair, rk, 1.0),
    ):
        first = raw[:, offset : offset + pair]
        second = raw[:, offset + pair : offset + width]
        turned_first = first * cos - second * sin
        turned_second = second * cos + first * sin
        total = split_dot(turned_first * turned_first + turned_second * turned_second, sums)
        scale = lax.rsqrt(total + EPSILON)
        scale_out[at, :] = scale
        both = jnp.concatenate(
            [
                turned_first * scale * gain[:, :pair],
                turned_second * scale * gain[:, pair:],
            ],
            axis=1,
        ).astype(BF16)
        pair_out[at, :] = both
        padded = dot(both, place_pair) * factor
        for head in range(heads):
            piece = padded[:, head * EXT : (head + 1) * EXT]
            if factor == 1.0:
                piece = jnp.where(lane < DK, piece, 1.0)
            out[head, at, :] = piece.astype(BF16)
    padded = dot(raw[:, 2 * width :].astype(BF16), place_plain)
    for head in range(heads):
        piece = padded[:, head * EXT : (head + 1) * EXT]
        v[head, at, :] = jnp.where(lane < DK, piece, 1.0).astype(BF16)


def split_three(value):
    high = value.astype(BF16).astype(F32)
    rest = value - high
    middle = rest.astype(BF16).astype(F32)
    return high, middle, rest - middle


def attend_kernel(low, q, k, v, columns, kdoc, collect, attended, qback, acc):
    heads, rows, _ = q.shape
    block = kdoc.shape[2]
    index = pl.program_id(0)
    acc[...] = jnp.zeros_like(acc)

    def earlier(j, carry):
        slots = pl.ds(pl.multiple_of(j * block, block), block)
        mask = columns[:, 1:2] == kdoc[j]
        for head in range(heads):
            scores = dot(q[head], k[head, slots, :], NT)
            weight = jnp.where(mask, jnp.exp(scores), 0.0).astype(BF16)
            acc[head] += dot(weight, v[head, slots, :])
        return carry

    lax.fori_loop(low[index], index, earlier, 0)

    strip = max(rows // 2, min(rows, 128))
    for start in range(0, rows, strip):
        at = slice(start, start + strip)
        end = start + strip
        slots = pl.ds(pl.multiple_of(index * block, block), end)
        row = start + lax.broadcasted_iota(jnp.int32, (strip, end), 0)
        column = lax.broadcasted_iota(jnp.int32, (strip, end), 1)
        mask = columns[at, 1:2] == kdoc[index][:, :end]
        mask = (mask & (column < row)) | (column == row)
        for head in range(heads):
            scores = dot(q[head, at, :], k[head, slots, :], NT)
            weight = jnp.where(mask, jnp.exp(scores), 0.0).astype(BF16)
            acc[head, at, :] += dot(weight, v[head, slots, :])

    lane = lax.broadcasted_iota(jnp.int32, (rows, EXT), 1)
    merged = jnp.zeros((rows, heads * DK), F32)
    for head in range(heads):
        both = acc[head]
        total = pltpu.roll(both, DK, 1)
        output = jnp.where(lane < DK, both / total, 0.0).astype(BF16)
        merged += dot(output, collect[head])
        high, middle, rest = split_three(-jnp.log(both))
        qback[head] = jnp.where(
            lane < DK,
            q[head].astype(F32),
            jnp.where(
                lane == DK,
                high,
                jnp.where(lane == DK + 1, middle, jnp.where(lane == DK + 2, rest, 0.0)),
            ),
        ).astype(BF16)
    attended[...] = merged.astype(BF16)


def attend(low, q, k, v, columns, kdoc, collect):
    heads, tokens, _ = q.shape
    block = kdoc.shape[2]
    width = heads * DK

    def whole(array):
        return pl.BlockSpec(array.shape, lambda i, low: (0,) * array.ndim)

    headed = pl.BlockSpec((heads, block, EXT), lambda i, low: (0, i, 0))
    return pl.pallas_call(
        attend_kernel,
        grid_spec=pltpu.PrefetchScalarGridSpec(
            num_scalar_prefetch=1,
            grid=(tokens // block,),
            in_specs=[
                headed,
                whole(k),
                whole(v),
                pl.BlockSpec((block, columns.shape[1]), lambda i, low: (i, 0)),
                whole(kdoc),
                whole(collect),
            ],
            out_specs=[pl.BlockSpec((block, width), lambda i, low: (i, 0)), headed],
            scratch_shapes=[pltpu.VMEM((heads, block, EXT), F32)],
        ),
        out_shape=[
            jax.ShapeDtypeStruct((tokens, width), BF16),
            jax.ShapeDtypeStruct((heads, tokens, EXT), BF16),
        ],
        compiler_params=grid_params(1),
        cost_estimate=pl.CostEstimate(
            flops=40_000_000_000, bytes_accessed=16 << 20, transcendentals=0
        ),
        name="attend",
    )(low, q, k, v, columns, kdoc, collect)


def unrope(grad, unit, gain, scale, cos, sin, sums):
    pair = cos.shape[1]
    grad_gain = jnp.sum(grad * unit, axis=0, keepdims=True)
    dy = grad * gain
    prod = dy * unit
    total = split_dot(prod[:, :pair] + prod[:, pair:], sums)
    first = scale * (dy[:, :pair] - unit[:, :pair] * total)
    second = scale * (dy[:, pair:] - unit[:, pair:] * total)
    raw = jnp.concatenate([first * cos + second * sin, second * cos - first * sin], axis=1)
    return raw.astype(BF16), grad_gain


def head_lanes(shape, head, paired):
    lane = lax.broadcasted_iota(jnp.int32, shape, 1)
    if paired:
        return lax.div(lax.rem(lane, shape[1] // 2), HALF) == head
    return lax.div(lane, DK) == head


def attend_back_kernel(
    low,
    qback,
    q_pair,
    dout,
    attended,
    k,
    k_pair,
    v,
    qdoc,
    columns,
    cosine,
    sine,
    rq,
    rk,
    gain,
    weight,
    place_plain,
    place_delta,
    sums,
    wide,
    grad_resid,
    term_out,
    grad_qkv,
    gain_out,
    dk,
    dv,
    dq,
    dox,
    q_heads,
    d_heads,
    k_heads,
    probs_all,
    scores_all,
    dq_low,
    total_qkv,
):
    heads, rows, _ = qback.shape
    steps = pl.num_programs(0) // 2
    step_at = pl.program_id(0)
    width = heads * DK
    scale = math.sqrt(DK)

    @pl.when(step_at == 0)
    def _():
        dk[...] = jnp.zeros_like(dk)
        dv[...] = jnp.zeros_like(dv)
        gain_out[...] = jnp.zeros_like(gain_out)
        keys = k_pair[...]
        for head in range(heads):
            k_heads[head] = jnp.where(head_lanes(keys.shape, head, True), keys, 0)

    @pl.when(step_at < steps)
    def _():
        index = step_at
        lane = lax.broadcasted_iota(jnp.int32, (rows, EXT), 1)
        grads = dout[...]
        queries = q_pair[...]
        spread = dot(grads, place_plain[...])
        delta = split_dot(grads.astype(F32) * attended[...].astype(F32), place_delta[...])
        for head in range(heads):
            at = slice(head * EXT, (head + 1) * EXT)
            high, middle, rest = split_three(-delta[:, at])
            dox[head] = jnp.where(
                lane < DK,
                spread[:, at],
                jnp.where(lane == DK, high, jnp.where(lane == DK + 1, middle, rest)),
            ).astype(BF16)
            stack = slice(head * rows, (head + 1) * rows)
            q_heads[stack, :] = jnp.where(head_lanes(queries.shape, head, True), queries, 0)
            d_heads[stack, :] = jnp.where(head_lanes(grads.shape, head, False), grads, 0)
        dq[...] = jnp.zeros_like(dq)

        def earlier(j, carry):
            slots = pl.ds(pl.multiple_of(j * rows, rows), rows)
            mask = columns[slots, 2:3] == qdoc[0]
            total = dq[...]
            for head in range(heads):
                scores = dot(k[head, slots, :], qback[head], NT)
                probs = jnp.where(mask, jnp.exp(scores), 0.0)
                dprobs = dot(v[head, slots, :], dox[head], NT)
                dscores = (probs * dprobs).astype(BF16)
                stack = slice(head * rows, (head + 1) * rows)
                probs_all[:, stack] = probs.astype(BF16)
                scores_all[:, stack] = dscores
                total += dot(dscores, k_heads[head, slots, :], TN)
            dq[...] = total
            dv[slots, :] += dot(probs_all[...], d_heads[...])
            dk[slots, :] += dot(scores_all[...], q_heads[...])
            return carry

        lax.fori_loop(low[index], index, earlier, 0)

        strip = max(rows // 2, min(rows, 128))
        for start in range(0, rows, strip):
            after_start = slice(start, rows)
            count = rows - start
            slots = pl.ds(pl.multiple_of(index * rows + start, strip), strip)
            key = start + lax.broadcasted_iota(jnp.int32, (strip, count), 0)
            query = start + lax.broadcasted_iota(jnp.int32, (strip, count), 1)
            mask = columns[slots, 2:3] == qdoc[0][:, after_start]
            mask = (mask & (key < query)) | (key == query)
            values, keys, queries_grad = None, None, None
            for head in range(heads):
                scores = dot(k[head, slots, :], qback[head, after_start, :], NT)
                probs = jnp.where(mask, jnp.exp(scores), 0.0)
                dprobs = dot(v[head, slots, :], dox[head, after_start, :], NT)
                dscores = (probs * dprobs).astype(BF16)
                stack = slice(head * rows + start, (head + 1) * rows)
                terms = (
                    dot(probs.astype(BF16), d_heads[stack, :]),
                    dot(dscores, q_heads[stack, :]),
                    dot(dscores, k_heads[head, slots, :], TN),
                )
                if head == 0:
                    values, keys, queries_grad = terms
                else:
                    values, keys, queries_grad = (
                        values + terms[0],
                        keys + terms[1],
                        queries_grad + terms[2],
                    )
            dv[slots, :] += values
            dk[slots, :] += keys
            dq[after_start, :] += queries_grad

        raw, grad_gain = unrope(
            dq[...] * scale,
            queries.astype(F32) * (1.0 / gain[...]),
            gain[...],
            rq[...],
            cosine[...],
            sine[...],
            sums[...],
        )
        gain_out[...] += grad_gain
        dq_low[pl.ds(pl.multiple_of(index * rows, rows), rows), :] = raw

    @pl.when(step_at >= steps)
    def _():
        index = step_at - steps
        slots = pl.ds(pl.multiple_of(index * rows, rows), rows)
        raw, grad_gain = unrope(
            dk[slots, :] * scale,
            k_pair[slots, :].astype(F32) * (1.0 / gain[...]),
            gain[...],
            rk[...],
            cosine[...],
            sine[...],
            sums[...],
        )
        gain_out[...] += grad_gain
        together = jnp.concatenate([dq_low[slots, :], raw, dv[slots, :].astype(BF16)], axis=1)
        parts, part = weight.shape[:2]
        for member in range(parts):
            term_out[member] = dot(together, weight[member], NT).astype(BF16)
            product = dot(wide[member], together, TN)

            @pl.when(index == 0)
            def _():
                total_qkv[member] = product

            @pl.when(index > 0)
            def _():
                total_qkv[member] += product

        strip = STRIP
        first = low[steps] * (grad_resid.shape[0] // strip)
        for half in range(rows // strip):
            number = index * (rows // strip) + half - first

            @pl.when((number >= 0) & (number < grad_resid.shape[0] // strip))
            def _():
                at = pl.ds(half * strip, strip)
                own = pl.ds(pl.multiple_of(number * strip, strip), strip)
                for member in range(parts):
                    term_out[member, at, :] = (
                        term_out[member, at, :].astype(F32)
                        + grad_resid[own, member * part : (member + 1) * part].astype(F32)
                    ).astype(BF16)

        @pl.when(index == steps - 1)
        def _():
            grad_qkv[...] = total_qkv[...].astype(BF16)


def attend_back(
    low,
    qback,
    q_pair,
    dout,
    attended,
    k,
    k_pair,
    v,
    qdoc,
    columns,
    cosine,
    sine,
    rq,
    rk,
    gain,
    weight,
    place_plain,
    place_delta,
    sums,
    wide,
    grad_resid,
):
    heads, tokens, _ = k.shape
    block = qdoc.shape[2]
    width = heads * DK
    steps = tokens // block
    parts, part = weight.shape[:2]

    def whole(array):
        return pl.BlockSpec(array.shape, lambda i, low: (0,) * array.ndim)

    def now(i):
        return jnp.minimum(i, steps - 1)

    def after(i):
        return jnp.maximum(i - steps, 0)

    def both(i):
        return lax.rem(i, steps)

    def rows(columns, at):
        return pl.BlockSpec((block, columns), lambda i, low: (at(i), 0))

    return pl.pallas_call(
        attend_back_kernel,
        grid_spec=pltpu.PrefetchScalarGridSpec(
            num_scalar_prefetch=1,
            grid=(2 * steps,),
            in_specs=[
                pl.BlockSpec((heads, block, EXT), lambda i, low: (0, now(i), 0)),
                rows(width, now),
                rows(width, now),
                rows(width, now),
                whole(k),
                whole(k_pair),
                whole(v),
                pl.BlockSpec((1, 1, block), lambda i, low: (now(i), 0, 0)),
                whole(columns),
                rows(width // 2, both),
                rows(width // 2, both),
                rows(width // 2, now),
                rows(width // 2, after),
                whole(gain),
                whole(weight),
                whole(place_plain),
                whole(place_delta),
                whole(sums),
                pl.BlockSpec((parts, block, part), lambda i, low: (0, after(i), 0)),
                whole(grad_resid),
            ],
            out_specs=[
                pl.BlockSpec((parts, block, part), lambda i, low: (0, after(i), 0)),
                pl.BlockSpec((parts, part, 3 * width), lambda i, low: (0, 0, 0)),
                pl.BlockSpec((1, width), lambda i, low: (0, 0)),
            ],
            scratch_shapes=[
                pltpu.VMEM((tokens, width), F32),
                pltpu.VMEM((tokens, width), F32),
                pltpu.VMEM((block, width), F32),
                pltpu.VMEM((heads, block, EXT), BF16),
                pltpu.VMEM((heads * block, width), BF16),
                pltpu.VMEM((heads * block, width), BF16),
                pltpu.VMEM((heads, tokens, width), BF16),
                pltpu.VMEM((block, heads * block), BF16),
                pltpu.VMEM((block, heads * block), BF16),
                pltpu.VMEM((tokens, width), BF16),
                pltpu.VMEM((parts, part, 3 * width), F32),
            ],
        ),
        out_shape=[
            jax.ShapeDtypeStruct((parts, tokens, part), BF16),
            jax.ShapeDtypeStruct((parts, part, 3 * width), BF16),
            jax.ShapeDtypeStruct((1, width), F32),
        ],
        compiler_params=grid_params(1),
        cost_estimate=pl.CostEstimate(
            flops=80_000_000_000, bytes_accessed=30 << 20, transcendentals=0
        ),
        name="attend_back",
    )(
        low,
        qback,
        q_pair,
        dout,
        attended,
        k,
        k_pair,
        v,
        qdoc,
        columns,
        cosine,
        sine,
        rq,
        rk,
        gain,
        weight,
        place_plain,
        place_delta,
        sums,
        wide,
        grad_resid,
    )


def row_scale(value):
    return lax.rsqrt(jnp.sum(value * value, axis=-1, keepdims=True) + EPSILON)


def residual_backward(grad_out, result, resid, unit, alpha, branch_scale, mixed_scale):
    grad_mixed = mixed_scale * (
        grad_out - result * jnp.sum(grad_out * result, axis=-1, keepdims=True)
    )
    grad_alpha = jnp.sum(grad_mixed * (unit - resid), axis=0, keepdims=True)
    grad_unit = grad_mixed * alpha
    grad_branch = branch_scale * (
        grad_unit - unit * jnp.sum(grad_unit * unit, axis=-1, keepdims=True)
    )
    return grad_mixed * (1.0 - alpha), grad_branch, grad_alpha


STRIP = 256


def strips(rows):
    strip = min(STRIP, rows)
    return [pl.ds(start, strip) for start in range(0, rows, strip)]


def core_semaphores(count):
    return [pltpu.SemaphoreType.DMA((count,)), pltpu.SemaphoreType.DMA((count,))]


def greet_pair_and_line(size):
    me, core = lax.axis_index("mp"), lax.axis_index("core")
    for k in range(1, size):
        greet({"mp": flip(me, k)})
    greet({"core": 1 - core})
    pl.semaphore_wait(pltpu.get_barrier_semaphore(), size)


def output_matrix(packed_wo, whole):
    size, chips, rows, both = packed_wo.shape
    part = both // 2
    for chip in range(chips):
        for core in range(2):
            start = (2 * chip + core) * rows
            whole[:, start : start + rows, :] = packed_wo[
                :, chip, :, core * part : (core + 1) * part
            ]


def mix_kernel(
    size,
    attended,
    packed,
    wide,
    alpha,
    cotangent,
    x,
    middle_out,
    unit_out,
    branch_scale_out,
    mixed_scale_out,
    merged,
    full_wo,
    resid_out,
    cotangent_low,
    packed_wo,
    middle_low,
    resid,
    send,
    receive,
    local,
    own_sems,
    core_sent,
    core_got,
):
    me, core = lax.axis_index("mp"), lax.axis_index("core")
    mine, width = middle_out.shape
    part = width // size
    rows = packed_wo.shape[2]
    greet_pair_and_line(size)
    every = strips(mine)

    def exchange(order):
        at = every[order]
        return Exchange(
            size,
            attended,
            merged,
            lambda ref, j: ref.at[
                pl.ds(pl.multiple_of(j * mine + at.start, at.size), at.size), :
            ],
            lambda ref, j: ref.at[at, pl.ds(pl.multiple_of(j * part, part), part)],
            send.at[order],
            receive.at[order],
            local.at[order],
        )

    exchange(0).start()
    own = [
        pltpu.make_async_copy(
            packed.at[:, :, pl.ds(packed.shape[2] - rows, rows), :], packed_wo, own_sems.at[0]
        )
    ]
    for member in range(size):
        own.append(
            pltpu.make_async_copy(
                wide.at[member, pl.ds(pl.multiple_of(me * mine, mine), mine), :],
                resid.at[:, pl.ds(member * part, part)],
                own_sems.at[1 + member],
            )
        )
    for copy in own:
        copy.start()
    for at in strips(cotangent.shape[0]):
        cotangent_low[at, :] = cotangent[at, :].astype(BF16)
    for copy in own:
        copy.wait()
    output_matrix(packed_wo, full_wo)
    resid_out[...] = resid[...]

    swaps = []
    for order, at in enumerate(every):
        exchange(order).wait()
        if order + 1 < len(every):
            exchange(order + 1).start()
        branch = dot(merged[at, :part], full_wo[0], NT)
        for member in range(1, size):
            branch += dot(
                merged[at, member * part : (member + 1) * part], full_wo[member], NT
            )
        old = resid[at, :].astype(F32)
        branch_scale = row_scale(branch)
        unit = branch * branch_scale
        mixed = old + alpha[...] * (unit - old)
        mixed_scale = row_scale(mixed)
        middle = mixed * mixed_scale
        middle_out[at, :] = middle
        unit_out[at, :] = unit.astype(BF16)
        branch_scale_out[at, :] = branch_scale
        mixed_scale_out[at, :] = mixed_scale
        middle_low[at, :] = middle.astype(BF16)
        there = pl.ds(mine + at.start, at.size)
        swap = to_device(
            middle_low.at[at, :],
            x.at[there, :],
            core_sent.at[order],
            core_got.at[order],
            {"core": 1 - core},
        )
        swap.start()
        swaps.append(swap)
    keep = pltpu.make_async_copy(middle_low, x.at[pl.ds(0, mine), :], own_sems.at[0])
    keep.start()
    keep.wait()
    for swap in swaps:
        swap.wait()


def mix(attended, packed, rows, wide, alpha, cotangent, collective):
    size, slots, part = wide.shape
    chips = packed.shape[1]
    mine, width = slots // size, size * part
    vmem = pl.BlockSpec(memory_space=pltpu.VMEM)
    count = len(strips(mine))
    scale = jax.ShapeDtypeStruct((mine, 1), F32)
    return pl.pallas_call(
        functools.partial(mix_kernel, size),
        in_specs=[ANY, ANY, ANY, vmem, vmem],
        out_specs=[ANY, *[vmem] * 8],
        out_shape=[
            jax.ShapeDtypeStruct((2 * mine, width), BF16),
            jax.ShapeDtypeStruct((mine, width), F32),
            jax.ShapeDtypeStruct((mine, width), BF16),
            scale,
            scale,
            jax.ShapeDtypeStruct((mine, width), BF16),
            jax.ShapeDtypeStruct((size, width, part), BF16),
            jax.ShapeDtypeStruct((mine, width), BF16),
            jax.ShapeDtypeStruct((slots, part), BF16),
        ],
        scratch_shapes=[
            pltpu.VMEM((size, chips, rows, 2 * part), BF16),
            pltpu.VMEM((mine, width), BF16),
            pltpu.VMEM((mine, width), BF16),
            pltpu.SemaphoreType.DMA((count, size)),
            pltpu.SemaphoreType.DMA((count, size)),
            pltpu.SemaphoreType.DMA((count,)),
            pltpu.SemaphoreType.DMA((1 + size,)),
            *core_semaphores(count),
        ],
        compiler_params=remote_params(collective),
        name="mix",
    )(attended, packed, wide, alpha, cotangent)


def whole_matrix(ref):
    _, chips, rows, units = ref.shape
    return ref[...].reshape(chips * rows, units)


def first_step():
    return (pl.program_id(0) == 0) & (pl.program_id(1) == 0)


def last_step():
    return (pl.program_id(0) == pl.num_programs(0) - 1) & (
        pl.program_id(1) == pl.num_programs(1) - 1
    )


def swap_cores(source, target, sems):
    return to_device(
        source, target, sems[0], sems[1], {"core": 1 - lax.axis_index("core")}
    )


def feed_kernel(
    size,
    x,
    w_up,
    w_gate,
    w_down,
    s_u,
    s_v,
    cotangent,
    middle,
    alpha,
    up_out,
    gate_out,
    units_out,
    result_out,
    grad_middle,
    dbranch,
    grad_alpha,
    acc,
    given,
    got,
    spread,
    low,
    send,
    receive,
    local,
    core_sent,
    core_got,
    keep_sems,
):
    exchange = Exchange(
        size,
        cotangent,
        spread,
        row_part(spread.shape[0]),
        column_part(cotangent.shape[1]),
        send,
        receive,
        local,
    )
    branch_swap = swap_cores(given, got, (core_sent.at[0], core_got.at[0]))

    @pl.when(first_step())
    def _():
        greet_pair_and_line(size)
        exchange.start()

    block, part = pl.program_id(0), pl.program_id(1)
    up = dot(x[...], whole_matrix(w_up))
    gate = dot(x[...], whole_matrix(w_gate))
    up_out[0] = up.astype(BF16)
    gate_out[0] = gate.astype(BF16)
    scaled = gate * s_v[0]
    units = (up * s_u[0] * (scaled / (1.0 + jnp.exp(-scaled)))).astype(BF16)
    units_out[0] = units
    term = dot(units, whole_matrix(w_down), NT)

    @pl.when(part == 0)
    def _():
        acc[...] = term

    @pl.when(part > 0)
    def _():
        acc[...] += term

    last = part == pl.num_programs(1) - 1

    @pl.when(last & (block == 0))
    def _():
        given[...] = acc[...].astype(BF16)
        branch_swap.start()

    @pl.when(last & (block == 1))
    def _():
        mine = acc.shape[0]
        branch_swap.wait()
        exchange.wait()
        swaps = []
        for order, at in enumerate(strips(mine)):
            branch = acc[at, :] + got[at, :].astype(F32)
            branch_scale = row_scale(branch)
            unit = branch * branch_scale
            old = middle[at, :]
            mixed = old + alpha[...] * (unit - old)
            mixed_scale = row_scale(mixed)
            result = mixed * mixed_scale
            result_out[at, :] = result.astype(BF16)
            grad_old, grad_branch, part_alpha = residual_backward(
                spread[at, :].astype(F32),
                result,
                old,
                unit,
                alpha[...],
                branch_scale,
                mixed_scale,
            )
            grad_middle[at, :] = grad_old
            if order == 0:
                grad_alpha[...] = part_alpha
            else:
                grad_alpha[...] += part_alpha
            low[at, :] = grad_branch.astype(BF16)
            there = pl.ds(mine + at.start, at.size)
            swaps.append(
                swap_cores(
                    low.at[at, :],
                    dbranch.at[there, :],
                    (core_sent.at[1 + order], core_got.at[1 + order]),
                )
            )
            swaps.append(
                pltpu.make_async_copy(low.at[at, :], dbranch.at[at, :], keep_sems.at[order])
            )
            swaps[-2].start()
            swaps[-1].start()
        for swap in swaps:
            swap.wait()


def packed_specs(packed, width):
    _, chips, _, units = packed.shape
    return [
        pl.BlockSpec((1, chips, width // chips, units), lambda t, m, w=w: (m, 0, w, 0))
        for w in range(3)
    ]


def feed(x, packed, s_u, s_v, cotangent, middle, alpha, collective):
    tokens, width = x.shape
    parts, _, _, units = packed.shape
    size = parts
    block = tokens // 2
    rows = pl.BlockSpec((block, width), lambda t, m: (1 - t, 0))
    vector = pl.BlockSpec((1, 1, units), lambda t, m: (m, 0, 0))
    piece = pl.BlockSpec((1, block, units), lambda t, m: (m, 1 - t, 0))
    vmem = pl.BlockSpec(memory_space=pltpu.VMEM)
    hidden = jax.ShapeDtypeStruct((parts, tokens, units), BF16)
    count = len(strips(block))
    low = pltpu.VMEM((block, width), BF16)
    return pl.pallas_call(
        functools.partial(feed_kernel, size),
        grid=(2, parts),
        in_specs=[rows, *packed_specs(packed, width), vector, vector, ANY, vmem, vmem],
        out_specs=[piece, piece, piece, vmem, vmem, ANY, vmem],
        out_shape=[
            hidden,
            hidden,
            hidden,
            jax.ShapeDtypeStruct((block, width), BF16),
            jax.ShapeDtypeStruct((block, width), F32),
            jax.ShapeDtypeStruct((tokens, width), BF16),
            jax.ShapeDtypeStruct((1, width), F32),
        ],
        scratch_shapes=[
            pltpu.VMEM((block, width), F32),
            low,
            low,
            low,
            low,
            *exchange_semaphores(size),
            *core_semaphores(1 + count),
            pltpu.SemaphoreType.DMA((count,)),
        ],
        compiler_params=remote_params(collective),
        cost_estimate=pl.CostEstimate(
            flops=6 * tokens * width * parts * units, bytes_accessed=60 << 20, transcendentals=0
        ),
        name="feed",
    )(x, packed, packed, packed, s_u, s_v, cotangent, middle, alpha)


def feed_back_kernel(
    size,
    dbranch,
    w_up,
    w_gate,
    w_down,
    s_u,
    s_v,
    up_in,
    gate_in,
    result,
    grad_middle_in,
    middle_in,
    resid_in,
    unit_in,
    branch_scale,
    mixed_scale,
    alpha,
    full_wo_in,
    dup_out,
    dgate_out,
    grad_u,
    grad_v,
    spread,
    grad_resid,
    dbranch_attn,
    dmerged,
    grad_alpha,
    acc,
    given,
    got,
    sum_u,
    sum_v,
    grad_middle,
    middle,
    resid,
    unit,
    full_wo,
    send,
    receive,
    local,
    core_sent,
    core_got,
    load_sems,
):
    loads = [
        pltpu.make_async_copy(there, here, load_sems.at[order])
        for order, (there, here) in enumerate(
            (
                (grad_middle_in, grad_middle),
                (middle_in, middle),
                (resid_in, resid),
                (unit_in, unit),
                (full_wo_in, full_wo),
            )
        )
    ]
    exchange = Exchange(
        size,
        result,
        spread,
        column_part(spread.shape[1]),
        row_part(result.shape[0]),
        send,
        receive,
        local,
    )
    dx_swap = swap_cores(given, got, (core_sent.at[0], core_got.at[0]))

    @pl.when(first_step())
    def _():
        for copy in loads:
            copy.start()
        greet_pair_and_line(size)
        exchange.start()

    block, part = pl.program_id(0), pl.program_id(1)
    dunits = dot(dbranch[...], whole_matrix(w_down))
    up = up_in[0].astype(F32)
    gate = gate_in[0].astype(F32)
    scaled = gate * s_v[0]
    sigmoid = 1.0 / (1.0 + jnp.exp(-scaled))
    silu = scaled * sigmoid
    slope = sigmoid * (1.0 + scaled - silu)
    through_up = dunits * silu
    through_gate = dunits * up * s_u[0] * slope
    dup = (through_up * s_u[0]).astype(BF16)
    dgate = (through_gate * s_v[0]).astype(BF16)
    dup_out[0] = dup
    dgate_out[0] = dgate
    term = dot(dup, whole_matrix(w_up), NT) + dot(dgate, whole_matrix(w_gate), NT)
    part_u = jnp.sum(through_up * up, axis=0, keepdims=True)
    part_v = jnp.sum(through_gate * gate, axis=0, keepdims=True)

    @pl.when(block == 0)
    def _():
        sum_u[part] = part_u
        sum_v[part] = part_v

    @pl.when(block > 0)
    def _():
        sum_u[part] += part_u
        sum_v[part] += part_v

    @pl.when(part == 0)
    def _():
        acc[...] = term

    @pl.when(part > 0)
    def _():
        acc[...] += term

    last = part == pl.num_programs(1) - 1

    @pl.when(last & (block == 0))
    def _():
        given[...] = acc[...].astype(BF16)
        dx_swap.start()

    @pl.when(last & (block == 1))
    def _():
        grad_u[...] = sum_u[...]
        grad_v[...] = sum_v[...]
        for copy in loads:
            copy.wait()
        dx_swap.wait()
        for order, at in enumerate(strips(acc.shape[0])):
            grad_old, grad_branch, part_alpha = residual_backward(
                grad_middle[at, :] + acc[at, :] + got[at, :].astype(F32),
                middle[at, :],
                resid[at, :].astype(F32),
                unit[at, :].astype(F32),
                alpha[...],
                branch_scale[at, :],
                mixed_scale[at, :],
            )
            grad_resid[at, :] = grad_old.astype(BF16)
            if order == 0:
                grad_alpha[...] = part_alpha
            else:
                grad_alpha[...] += part_alpha
            low = grad_branch.astype(BF16)
            dbranch_attn[at, :] = low
            columns = full_wo.shape[2]
            for member in range(size):
                dmerged[at, member * columns : (member + 1) * columns] = dot(
                    low, full_wo[member]
                ).astype(BF16)
        exchange.wait()


def feed_back(
    dbranch,
    packed,
    s_u,
    s_v,
    up,
    gate,
    result,
    grad_middle,
    middle,
    resid,
    unit,
    branch_scale,
    mixed_scale,
    alpha,
    full_wo,
    collective,
):
    tokens, width = dbranch.shape
    parts, _, _, units = packed.shape
    size = parts
    block = tokens // 2
    rows = pl.BlockSpec((block, width), lambda t, m: (1 - t, 0))
    vector = pl.BlockSpec((1, 1, units), lambda t, m: (m, 0, 0))
    piece = pl.BlockSpec((1, block, units), lambda t, m: (m, 1 - t, 0))
    vmem = pl.BlockSpec(memory_space=pltpu.VMEM)
    hidden = jax.ShapeDtypeStruct((parts, tokens, units), BF16)
    sums = jax.ShapeDtypeStruct((parts, 1, units), F32)
    state = jax.ShapeDtypeStruct((block, width), BF16)
    kept = (grad_middle, middle, resid, unit, full_wo)
    return pl.pallas_call(
        functools.partial(feed_back_kernel, size),
        grid=(2, parts),
        in_specs=[
            rows,
            *packed_specs(packed, width),
            vector,
            vector,
            piece,
            piece,
            ANY,
            *[ANY] * 4,
            *[vmem] * 3,
            ANY,
        ],
        out_specs=[piece, piece, vmem, vmem, ANY, vmem, vmem, vmem, vmem],
        out_shape=[
            hidden,
            hidden,
            sums,
            sums,
            jax.ShapeDtypeStruct((size * block, width // size), BF16),
            state,
            state,
            state,
            jax.ShapeDtypeStruct((1, width), F32),
        ],
        scratch_shapes=[
            pltpu.VMEM((block, width), F32),
            pltpu.VMEM((block, width), BF16),
            pltpu.VMEM((block, width), BF16),
            pltpu.VMEM((parts, 1, units), F32),
            pltpu.VMEM((parts, 1, units), F32),
            *[pltpu.VMEM(each.shape, each.dtype) for each in kept],
            *exchange_semaphores(size),
            *core_semaphores(1),
            pltpu.SemaphoreType.DMA((len(kept),)),
        ],
        compiler_params=remote_params(collective),
        cost_estimate=pl.CostEstimate(
            flops=6 * tokens * width * parts * units, bytes_accessed=70 << 20, transcendentals=0
        ),
        name="feed_back",
    )(
        dbranch,
        packed,
        packed,
        packed,
        s_u,
        s_v,
        up,
        gate,
        result,
        grad_middle,
        middle,
        resid,
        unit,
        branch_scale,
        mixed_scale,
        alpha,
        full_wo,
    )


def feed_grads_kernel(
    size,
    x,
    dbranch,
    dup,
    dgate,
    units,
    dbranch_attn,
    merged,
    dmerged,
    grads,
    grad_wo,
    dattended,
    x_turned,
    d_turned,
    attn_turned,
    send,
    receive,
    local,
):
    exchange = Exchange(
        size,
        dmerged,
        dattended,
        column_part(dattended.shape[1]),
        row_part(dmerged.shape[0]),
        send,
        receive,
        local,
    )

    @pl.when(first_step())
    def _():
        greet_all(size)
        exchange.start()
        x_turned[...] = x[...].T
        d_turned[...] = dbranch[...].T
        attn_turned[...] = dbranch_attn[...].T

    _, chips, rows, _ = grads.shape
    for which, left, right in (
        (0, x_turned, dup),
        (1, x_turned, dgate),
        (2, d_turned, units),
    ):

        @pl.when(pl.program_id(0) == which)
        def _():
            total = dot(left[...], right[0])
            grads[0] = total.astype(BF16).reshape(chips, rows, total.shape[1])

    @pl.when(pl.program_id(0) == 3)
    def _():
        total = dot(attn_turned[...], merged[...])
        grad_wo[...] = total.astype(BF16).reshape(grad_wo.shape)

    @pl.when(last_step())
    def _():
        exchange.wait()


def feed_grads(
    x, dbranch, dup, dgate, units_in, dbranch_attn, merged, dmerged, chips, collective
):
    tokens, width = x.shape
    parts, _, units = dup.shape
    size = parts
    rows = width // chips
    mine = dmerged.shape[0]
    part = width // size

    def whole(array):
        return pl.BlockSpec(array.shape, lambda w, m: (0, 0))

    def turn(w, m, which):
        return jnp.where(w == which, m, jnp.where(w < which, 0, parts - 1))

    def piece(which):
        return pl.BlockSpec((1, tokens, units), lambda w, m: (turn(w, m, which), 0, 0))

    return pl.pallas_call(
        functools.partial(feed_grads_kernel, size),
        grid=(4, parts),
        in_specs=[
            whole(x),
            whole(dbranch),
            piece(0),
            piece(1),
            piece(2),
            whole(dbranch_attn),
            pl.BlockSpec((mine, part), lambda w, m: (0, turn(w, m, 3))),
            ANY,
        ],
        out_specs=[
            pl.BlockSpec(
                (1, chips, rows, units),
                lambda w, m: (jnp.where(w < 3, m, parts - 1), 0, jnp.minimum(w, 2), 0),
            ),
            pl.BlockSpec(
                (1, chips, 2, rows // 2, part), lambda w, m: (turn(w, m, 3), 0, 0, 0, 0)
            ),
            ANY,
        ],
        out_shape=[
            jax.ShapeDtypeStruct((parts, chips, 3 * rows, units), BF16),
            jax.ShapeDtypeStruct((parts, chips, 2, rows // 2, part), BF16),
            jax.ShapeDtypeStruct((size * mine, part), BF16),
        ],
        scratch_shapes=[
            pltpu.VMEM((width, tokens), BF16),
            pltpu.VMEM((width, tokens), BF16),
            pltpu.VMEM((width, mine), BF16),
            *exchange_semaphores(size),
        ],
        compiler_params=remote_params(collective),
        cost_estimate=pl.CostEstimate(
            flops=6 * tokens * width * parts * units, bytes_accessed=40 << 20, transcendentals=0
        ),
        name="feed_grads",
    )(x, dbranch, dup, dgate, units_in, dbranch_attn, merged, dmerged)


def document_starts(doc_ids):
    slot_index = jnp.arange(doc_ids.shape[-1], dtype=jnp.int32)
    earlier = jnp.concatenate([doc_ids[..., :1] - 1, doc_ids[..., :-1]], axis=-1)
    starts = jnp.where(doc_ids != earlier, slot_index, jnp.zeros_like(slot_index))
    return lax.cummax(starts, axis=starts.ndim - 1)


def make_on_device(chips, size):
    def on_device(
        hidden,
        wq,
        wk,
        wv,
        wo,
        w_up,
        w_gate,
        w_down,
        s_qk,
        s_u,
        s_v,
        alpha_a,
        alpha_m,
        doc_ids,
        valid,
        cotangent,
    ):
        _, slots, part = hidden.shape
        width = part * size
        heads = s_qk.shape[0] // DK
        rows = wq.shape[0]
        units = w_up.shape[1] // 2
        mine = slots // size
        block = min(512, slots)
        me = lax.axis_index("mp")
        core = lax.axis_index("core")

        place = paired_place(heads)
        to_pair = placing_matrix(place, heads)
        to_plain = placing_matrix(np.arange(heads * DK), heads)
        turn = np.zeros((part, part), np.float32)
        turn[np.arange(part), place] = 1
        place_pair = jnp.asarray(to_pair, BF16)
        place_plain = jnp.asarray(to_plain, BF16)
        place_delta = jnp.asarray(delta_matrix(heads), BF16)
        collect_plain = jnp.asarray(to_plain.T.reshape(heads, EXT, heads * DK), BF16)
        sums = jnp.asarray(head_sum_matrix(heads), BF16)
        gain = s_qk.reshape(heads, 2, HALF).transpose(1, 0, 2).reshape(1, part)
        docs = doc_ids[0]
        starts = document_starts(docs)
        slot = jnp.arange(slots, dtype=jnp.int32)
        low = jnp.concatenate([starts[::block] // block, me[None]])
        key_docs = jnp.where(valid[0] == 1, docs, -1)
        columns = jnp.stack([slot - starts, docs, key_docs], axis=1).astype(F32)
        inverse = jnp.exp(
            jnp.arange(HALF, dtype=F32) * (-2.0 * math.log(ROPE_BASE) / DK)
        )

        vectors = jnp.concatenate([s_u, s_v * math.sqrt(width), alpha_a, alpha_m])
        (
            wide,
            full_qkv,
            packed,
            vectors,
            q,
            k,
            v,
            q_pair,
            k_pair,
            rq,
            rk,
            cosine,
            sine,
        ) = front(
            hidden[0],
            (wq, wk, wv, wo, w_up, w_gate, w_down),
            vectors[None],
            columns,
            jnp.tile(inverse, heads)[None],
            gain,
            jnp.asarray(turn, BF16),
            place_pair,
            place_plain,
            sums,
            size,
            chips,
            0,
        )
        full_qkv = full_qkv.reshape(size, part, 3 * part)
        vectors = vectors[:, 0]
        s_up = lax.dynamic_slice_in_dim(vectors[:, : 2 * units], core * units, units, 1)
        s_gate = lax.dynamic_slice_in_dim(
            vectors[:, 2 * units : 4 * units], core * units, units, 1
        )
        s_up = s_up[:, None, :]
        s_gate = s_gate[:, None, :]
        alpha_attn = vectors[:, 4 * units : 4 * units + part].reshape(1, width)
        alpha_mlp = vectors[:, 4 * units + part :].reshape(1, width)

        attended, qback = attend(
            low,
            q,
            k,
            v,
            columns,
            key_docs.astype(F32).reshape(slots // block, 1, block),
            collect_plain,
        )
        (
            x,
            middle,
            unit,
            branch_scale,
            mixed_scale,
            merged,
            full_wo,
            resid,
            cotangent_low,
        ) = mix(attended, packed, rows, wide, alpha_attn, cotangent[0], 1)

        up, gate, hidden_units, result, grad_middle, dbranch, grad_alpha_mlp = feed(
            x, packed, s_up, s_gate, cotangent_low, middle, alpha_mlp, 2
        )
        (
            dup,
            dgate,
            grad_u,
            grad_v,
            out_low,
            grad_resid,
            dbranch_attn,
            dmerged,
            grad_alpha_attn,
        ) = feed_back(
            dbranch,
            packed,
            s_up,
            s_gate,
            up,
            gate,
            result,
            grad_middle,
            middle,
            resid,
            unit,
            branch_scale,
            mixed_scale,
            alpha_attn,
            full_wo,
            3,
        )
        out_hidden = out_low.astype(F32)
        grads, grad_wo, dattended = feed_grads(
            x, dbranch, dup, dgate, hidden_units, dbranch_attn, merged, dmerged, chips, 4
        )

        term, grad_qkv, grad_gain = attend_back(
            low,
            qback,
            q_pair,
            dattended,
            attended,
            k,
            k_pair,
            v,
            docs.astype(F32).reshape(slots // block, 1, block),
            columns,
            cosine,
            sine,
            rq,
            rk,
            gain,
            full_qkv,
            place_plain,
            place_delta,
            sums,
            wide,
            grad_resid,
        )
        out_pairs = (
            lambda w: w.reshape(w.shape[0], 2, heads, HALF)
            .transpose(0, 2, 1, 3)
            .reshape(w.shape[0], heads * DK)
        )

        zero = jnp.zeros((size, 2, units), F32)
        placed_u = lax.dynamic_update_slice(zero, grad_u, (0, core, 0))
        placed_v = lax.dynamic_update_slice(zero, grad_v * math.sqrt(width), (0, core, 0))
        placed_qk = lax.dynamic_update_slice(
            jnp.zeros((size, part), F32), out_pairs(grad_gain), (me, 0)
        )
        placed = jnp.concatenate(
            [
                placed_u.reshape(size, 2 * units),
                placed_v.reshape(size, 2 * units),
                placed_qk,
                grad_alpha_attn.reshape(size, part),
                grad_alpha_mlp.reshape(size, part),
            ],
            axis=1,
        )
        (
            grad_hidden,
            owned_upward,
            owned_gating,
            owned_downward,
            owned_output,
            owned_query,
            owned_keys,
            owned_values,
            summed,
        ) = sum_all(
            term,
            grads,
            grad_wo,
            grad_qkv.reshape(chips, 2, rows, 3 * part),
            placed[:, None],
            jnp.asarray(turn.T, BF16),
            chips,
            5,
        )
        bounds = [2 * units, 4 * units, 4 * units + part, 4 * units + 2 * part]
        summed_up, summed_gate, summed_qk, summed_attn, summed_mlp = jnp.split(
            summed[0], bounds
        )
        return (
            out_hidden[None],
            grad_hidden[None],
            owned_query,
            owned_keys,
            owned_values,
            owned_output,
            owned_upward,
            owned_gating,
            owned_downward,
            summed_qk,
            summed_up,
            summed_gate,
            summed_attn,
            summed_mlp,
        )

    return on_device


def solution(mesh):
    rows, size = mesh.shape["dp"], mesh.shape["mp"]
    paired = Mesh(mesh.devices.reshape(rows // 2, 2, size), ("chip", "core", "mp"))
    return jax.shard_map(
        make_on_device(rows // 2, size),
        mesh=paired,
        in_specs=(
            P(DP, None, "mp"),
            P(DP, "mp"),
            P(DP, "mp"),
            P(DP, "mp"),
            P("mp", DP),
            P(DP, "mp"),
            P(DP, "mp"),
            P("mp", DP),
            P("mp"),
            P("mp"),
            P("mp"),
            P("mp"),
            P("mp"),
            P(DP, None),
            P(DP, None),
            P(DP, None, "mp"),
        ),
        out_specs=(
            P(DP, None, "mp"),
            P(DP, None, "mp"),
            P(DP, "mp"),
            P(DP, "mp"),
            P(DP, "mp"),
            P("mp", DP),
            P(DP, "mp"),
            P(DP, "mp"),
            P("mp", DP),
            P("mp"),
            P("mp"),
            P("mp"),
            P("mp"),
            P("mp"),
        ),
        check_vma=False,
    )
```

```python
import functools
import math

import jax
import jax.numpy as jnp
import numpy as np
from jax import lax
from jax.experimental import pallas as pl
from jax.experimental.pallas import tpu as pltpu
from jax.sharding import Mesh
from jax.sharding import PartitionSpec as P

DK = 64
HALF = DK // 2
EXT = 128
EPSILON = 1e-06
ROPE_BASE = 10000.0
VMEM_LIMIT = 60 * 1024 * 1024
F32 = jnp.float32
BF16 = jnp.bfloat16
DP = ("chip", "core")


def dot(left, right, dims=((1,), (0,)), precision=None):
    return lax.dot_general(
        left, right, (dims, ((), ())), precision=precision, preferred_element_type=F32
    )


NT = ((1,), (1,))
TN = ((0,), (0,))


def grid_params(dims):
    return pltpu.CompilerParams(
        dimension_semantics=("arbitrary",) * dims, vmem_limit_bytes=VMEM_LIMIT
    )


ANY = pl.BlockSpec(memory_space=pl.ANY)


def remote_params(collective, **more):
    return pltpu.CompilerParams(
        collective_id=collective,
        has_side_effects=True,
        vmem_limit_bytes=VMEM_LIMIT,
        **more,
    )


def to_device(source, target, send, receive, where):
    return pltpu.make_async_remote_copy(
        src_ref=source,
        dst_ref=target,
        send_sem=send,
        recv_sem=receive,
        device_id=where,
        device_id_type=pl.DeviceIdType.MESH,
    )


def to_member(source, target, send, receive, member):
    return to_device(source, target, send, receive, {"mp": member})


def flip(index, mask):
    bit = 1
    while bit <= mask:
        if mask & bit:
            index = index + bit - 2 * bit * lax.rem(lax.div(index, bit), 2)
        bit *= 2
    return index


def bits_below(count):
    return [1 << k for k in range(count.bit_length() - 1)]


def greet(where):
    pl.semaphore_signal(
        pltpu.get_barrier_semaphore(),
        inc=1,
        device_id=where,
        device_id_type=pl.DeviceIdType.MESH,
    )


def greet_all(size):
    me = lax.axis_index("mp")
    for k in range(1, size):
        greet({"mp": flip(me, k)})
    pl.semaphore_wait(pltpu.get_barrier_semaphore(), size - 1)


def greet_around(size, chips):
    me, chip, core = (lax.axis_index(name) for name in ("mp", "chip", "core"))
    for k in range(1, size):
        greet({"mp": flip(me, k)})
    for bit in bits_below(chips):
        greet({"chip": flip(chip, bit)})
    greet({"core": 1 - core})
    pl.semaphore_wait(pltpu.get_barrier_semaphore(), size + len(bits_below(chips)))


class Exchange:
    def __init__(self, size, source, target, piece, place, send, receive, local):
        me = lax.axis_index("mp")
        self.local = pltpu.make_async_copy(piece(source, me), place(target, me), local)
        self.remote = [
            to_member(
                piece(source, flip(me, k)),
                place(target, me),
                send.at[k],
                receive.at[k],
                flip(me, k),
            )
            for k in range(1, size)
        ]

    def start(self):
        for copy in self.remote:
            copy.start()
        self.local.start()

    def wait(self):
        self.local.wait()
        for copy in self.remote:
            copy.wait()


def exchange_semaphores(size):
    return [
        pltpu.SemaphoreType.DMA((size,)),
        pltpu.SemaphoreType.DMA((size,)),
        pltpu.SemaphoreType.DMA,
    ]


def row_part(rows):
    return lambda ref, j: ref.at[pl.ds(pl.multiple_of(j * rows, rows), rows), :]


def column_part(columns):
    return lambda ref, j: ref.at[:, pl.ds(pl.multiple_of(j * columns, columns), columns)]


class Gather:
    def __init__(self, block, index, bits, where, send, receive):
        self.block, self.index, self.bits, self.where = block, index, bits, where
        self.send, self.receive = send, receive

    def copies(self, stage, incoming):
        span = [0]
        for bit in self.bits[:stage]:
            span += [held | bit for held in span]
        bit = self.bits[stage]
        for order, held in enumerate(span):
            ref = self.block(flip(self.index, held | bit if incoming else held))
            slot = (1 << stage) - 1 + order
            yield to_device(
                ref,
                ref,
                self.send(slot),
                self.receive(slot),
                self.where(flip(self.index, bit)),
            )

    def start(self, stage):
        if stage < len(self.bits):
            for copy in self.copies(stage, False):
                copy.start()

    def arrive(self, stage):
        if stage < len(self.bits):
            for copy in self.copies(stage, True):
                copy.wait_recv()

    def close(self):
        for stage in range(len(self.bits)):
            for copy in self.copies(stage, False):
                copy.wait_send()


EARLY = 2


def front_kernel(
    size,
    chips,
    chunks,
    split,
    hidden_in,
    wq,
    wk,
    wv,
    wo,
    w_up,
    w_gate,
    w_down,
    vectors,
    columns,
    frequency,
    gain,
    in_pairs,
    place_pair,
    place_plain,
    sums,
    wide_out,
    qkv_out,
    full,
    full_vectors,
    q_out,
    k_out,
    v_out,
    q_pair_out,
    k_pair_out,
    rq_out,
    rk_out,
    cosine_out,
    sine_out,
    hidden,
    wide,
    full_qkv,
    packed,
    matrices,
    wo_turned,
    q,
    k,
    v,
    q_pair,
    k_pair,
    rq,
    rk,
    cosine,
    sine,
    local,
    out_sems,
    core_sent,
    core_got,
    hidden_up,
    hidden_down,
    hidden_got,
    packed_up,
    packed_down,
    packed_got,
    plane_sent,
    plane_got,
    qkv_sent,
    qkv_got,
    vector_sent,
    vector_got,
    load_sems,
):
    me, chip, core = (lax.axis_index(name) for name in ("mp", "chip", "core"))
    tokens, part = hidden_in.shape
    rows = tokens // chunks
    hidden_loads = [
        pltpu.make_async_copy(
            hidden_in.at[pl.ds(chunk * rows, rows), :],
            hidden.at[pl.ds(chunk * rows, rows), :],
            load_sems.at[chunk],
        )
        for chunk in range(chunks)
    ]
    for copy in hidden_loads:
        copy.start()
    height, units = packed.shape
    lines = height // 7
    owner = chip * 2 + core
    bits = bits_below(chips)
    stages = len(bits)
    greet_around(size, chips)

    def hidden_hop(origin, chunk, member, send):
        at = pl.ds(pl.multiple_of(chunk * rows, rows), rows)
        ref = wide.at[origin, at, :]
        return to_member(ref, ref, send.at[origin, chunk], hidden_got.at[origin, chunk], member)

    def send_hidden(chunk):
        @pl.when(me < size - 1)
        def _():
            hidden_hop(me, chunk, me + 1, hidden_up).start()

        @pl.when(me > 0)
        def _():
            hidden_hop(me, chunk, me - 1, hidden_down).start()

    for chunk in range(EARLY):
        at = pl.ds(chunk * rows, rows)
        hidden_loads[chunk].wait()
        wide[me, at, :] = hidden[at, :].astype(BF16)
        send_hidden(chunk)

    matrices[0] = w_up[...].astype(BF16)
    matrices[1] = w_gate[...].astype(BF16)
    matrices[2] = w_down[...].T.astype(BF16)
    wo_turned[...] = wo[...].T.astype(BF16)

    def half_of(which):
        return pl.ds(pl.multiple_of(which * units, units), units)

    def place_of(matrix):
        return pl.ds(pl.multiple_of((2 * matrix + core) * lines, lines), lines)

    wo_place = (
        pl.ds(6 * lines, lines),
        pl.ds(pl.multiple_of(core * part, part), part),
    )
    given = [
        to_device(
            matrices.at[matrix, :, half_of(1 - core)],
            packed.at[place_of(matrix), :],
            core_sent.at[matrix],
            core_got.at[matrix],
            {"core": 1 - core},
        )
        for matrix in range(3)
    ]
    given.append(
        to_device(
            wo_turned, packed.at[wo_place], core_sent.at[3], core_got.at[3], {"core": 1 - core}
        )
    )
    for copy in given:
        copy.start()
    for matrix in range(3):
        packed[place_of(matrix), :] = matrices[matrix, :, half_of(core)]
    packed[wo_place] = wo_turned[...]
    full_qkv[owner] = jnp.concatenate(
        [
            dot(wq[...].astype(BF16), in_pairs[...]).astype(BF16),
            dot(wk[...].astype(BF16), in_pairs[...]).astype(BF16),
            wv[...].astype(BF16),
        ],
        axis=1,
    )

    def packed_hop(origin, ref, member, send):
        return to_member(
            ref, full.at[origin, chip], send.at[origin], packed_got.at[origin], member
        )

    vector_copies = [
        to_member(
            vectors, full_vectors.at[me], vector_sent.at[k], vector_got.at[k], flip(me, k)
        )
        for k in range(1, size)
    ]

    def plane(origin, slot):
        return [
            Gather(
                lambda i, at=at: full.at[origin, i, at, :],
                chip,
                order,
                lambda i: {"chip": i},
                lambda k, half=half: plane_sent.at[slot, half, k],
                lambda k, half=half: plane_got.at[slot, half, k],
            )
            for half, (at, order) in enumerate(
                (
                    (pl.ds(0, split), bits),
                    (pl.ds(split, height - split), bits[::-1]),
                )
            )
        ]

    gather_qkv = Gather(
        lambda i: full_qkv.at[i],
        owner,
        [2 * bit for bit in bits] + [1],
        lambda i: {"chip": lax.div(i, 2), "core": lax.rem(i, 2)},
        lambda k: qkv_sent.at[k],
        lambda k: qkv_got.at[k],
    )

    sources = {0: [(me >= 0, me, 0, None)]}
    for distance in range(1, size):
        sources[distance] = [
            (me >= distance, me - distance, 2 * distance - 1, True),
            (me + distance < size, me + distance, 2 * distance, False),
        ]

    def pass_on(origin, ref, upward):
        if upward is not False:

            @pl.when(me < size - 1)
            def _():
                packed_hop(origin, ref, me + 1, packed_up).start()

        if not upward:

            @pl.when(me > 0)
            def _():
                packed_hop(origin, ref, me - 1, packed_down).start()

    def advance(distance, stage):
        for exists, origin, slot, _ in sources[distance]:

            @pl.when(exists)
            def _():
                for half in plane(origin, slot):
                    half.arrive(stage)
                    half.start(stage + 1)

    for copy in given:
        copy.wait_recv()
    pass_on(me, packed, None)
    own = [
        pltpu.make_async_copy(packed, full.at[me, chip], local.at[0]),
        pltpu.make_async_copy(vectors, full_vectors.at[me], local.at[1]),
    ]
    for copy in own:
        copy.start()
    gather_qkv.start(0)
    for copy in vector_copies:
        copy.start()
    for chunk in range(EARLY, chunks):
        at = pl.ds(chunk * rows, rows)
        hidden_loads[chunk].wait()
        wide[me, at, :] = hidden[at, :].astype(BF16)
    own[0].wait()
    for half in plane(me, 0):
        half.start(0)
    for chunk in range(chunks):
        at = pl.ds(chunk * rows, rows)
        angles = columns[at, 0:1] * frequency[...]
        cosine[at, :] = jnp.cos(angles)
        sine[at, :] = jnp.sin(angles)
    for stage in range(stages):
        gather_qkv.arrive(stage)
        gather_qkv.start(stage + 1)
    advance(0, 0)
    for distance in range(1, size):
        for exists, origin, slot, upward in sources[distance]:

            @pl.when(exists)
            def _():
                block = full.at[origin, chip]
                packed_hop(origin, block, me, packed_up).wait_recv()
                pass_on(origin, block, upward)
                for half in plane(origin, slot):
                    half.start(0)

        @pl.when(jnp.maximum(me, size - 1 - me) == distance)
        def _():
            for chunk in range(EARLY, chunks):
                send_hidden(chunk)

        if distance > 1:
            advance(distance - 1, 0)
    gather_qkv.arrive(stages)
    qkv_copy = pltpu.make_async_copy(full_qkv, qkv_out, local.at[2])
    qkv_copy.start()
    advance(size - 1, 0)

    def come(distance, chunk):
        for exists, origin, _, upward in sources[distance]:

            @pl.when(exists)
            def _():
                hidden_hop(origin, chunk, me, hidden_up).wait_recv()
                if upward:

                    @pl.when(me < size - 1)
                    def _():
                        hidden_hop(origin, chunk, me + 1, hidden_up).start()
                else:

                    @pl.when(me > 0)
                    def _():
                        hidden_hop(origin, chunk, me - 1, hidden_down).start()

    for distance in range(1, size - 1):
        for chunk in range(chunks):
            come(distance, chunk)

    results = (
        (q, q_out),
        (k, k_out),
        (v, v_out),
        (q_pair, q_pair_out),
        (k_pair, k_pair_out),
        (rq, rq_out),
        (rk, rk_out),
        (cosine, cosine_out),
        (sine, sine_out),
        (wide, wide_out),
    )

    def write_out(chunk):
        at = pl.ds(pl.multiple_of(chunk * rows, rows), rows)
        for order, (here, there) in enumerate(results):
            lead = (slice(None),) * (len(here.shape) - 2)
            yield pltpu.make_async_copy(
                here.at[(*lead, at)], there.at[(*lead, at)], out_sems.at[order, chunk]
            )

    each = part // lines

    def finish(chunk, carry):
        come(size - 1, chunk)
        at = pl.ds(pl.multiple_of(chunk * rows, rows), rows)
        project_block(
            [wide[member, at, :] for member in range(size)],
            [
                full_qkv[member * each : (member + 1) * each].reshape(part, 3 * part)
                for member in range(size)
            ],
            cosine[at, :],
            sine[at, :],
            gain[...],
            place_pair[...],
            place_plain[...],
            sums[...],
            at,
            [here for here, _ in results[:7]],
        )
        for copy in write_out(chunk):
            copy.start()
        return carry

    lax.fori_loop(0, chunks, finish, 0)
    for stage in range(1, stages):
        for distance in range(size):
            advance(distance, stage)

    own[1].wait()
    qkv_copy.wait()
    for copy in vector_copies:
        copy.wait()
    for copy in given:
        copy.wait_send()
    for chunk in range(chunks):
        for copy in write_out(chunk):
            copy.wait()
    gather_qkv.close()
    for distance in range(size):
        for exists, origin, slot, upward in sources[distance]:

            @pl.when(exists)
            def _():
                for half in plane(origin, slot):
                    half.close()
                block = packed if distance == 0 else full.at[origin, chip]
                if upward is not False:

                    @pl.when(me < size - 1)
                    def _():
                        packed_hop(origin, block, me, packed_up).wait_send()
                        for chunk in range(chunks):
                            hidden_hop(origin, chunk, me, hidden_up).wait_send()

                if not upward:

                    @pl.when(me > 0)
                    def _():
                        packed_hop(origin, block, me, packed_down).wait_send()
                        for chunk in range(chunks):
                            hidden_hop(origin, chunk, me, hidden_down).wait_send()


def front(
    hidden,
    weights,
    vectors,
    positions,
    frequency,
    gain,
    in_pairs,
    place_pair,
    place_plain,
    sums,
    size,
    chips,
    collective,
):
    chunks = 6
    tokens, part = hidden.shape
    lines, both = weights[4].shape
    units = both // 2
    heads = part // DK
    height = 7 * lines
    dma = pltpu.SemaphoreType.DMA
    line = dma((size, chunks))
    plane = dma((2 * size - 1, 2, max(chips - 1, 1)))
    vmem = pl.BlockSpec(memory_space=pltpu.VMEM)
    padded = ((heads, tokens, EXT), BF16)
    paired = ((tokens, part), BF16)
    scale = ((tokens, heads * HALF), F32)
    wide = ((size, tokens, part), BF16)
    qkv = ((2 * chips, lines, 3 * part), BF16)
    results = [padded, padded, padded, paired, paired, scale, scale, scale, scale]
    return pl.pallas_call(
        functools.partial(front_kernel, size, chips, chunks, height // 32 * 16),
        in_specs=[ANY, *[vmem] * 15],
        out_specs=[ANY] * 13,
        out_shape=[
            jax.ShapeDtypeStruct(*each)
            for each in [
                wide,
                qkv,
                ((size, chips, height, units), BF16),
                ((size, *vectors.shape), F32),
                *results,
            ]
        ],
        scratch_shapes=[
            pltpu.VMEM((tokens, part), F32),
            pltpu.VMEM(*wide),
            pltpu.VMEM(*qkv),
            pltpu.VMEM((height, units), BF16),
            pltpu.VMEM((3, lines, both), BF16),
            pltpu.VMEM((lines, part), BF16),
            *[pltpu.VMEM(*each) for each in results],
            dma((3,)),
            dma((10, chunks)),
            dma((4,)),
            dma((4,)),
            line,
            line,
            line,
            dma((size,)),
            dma((size,)),
            dma((size,)),
            plane,
            plane,
            dma((2 * chips - 1,)),
            dma((2 * chips - 1,)),
            dma((size,)),
            dma((size,)),
            dma((chunks,)),
        ],
        compiler_params=remote_params(collective),
        name="front",
    )(
        hidden,
        *weights,
        vectors,
        positions,
        frequency,
        gain,
        in_pairs,
        place_pair,
        place_plain,
        sums,
    )


class LineSum:
    def __init__(self, size, chunks, term, up, down, sems):
        self.size, self.chunks = size, chunks
        self.term, self.up, self.down = term, up, down
        self.sent_up, self.sent_down, self.got_up, self.got_down = sems
        self.me = lax.axis_index("mp")
        self.rows = up.shape[1] // chunks

    def at(self, chunk):
        return pl.ds(chunk * self.rows, self.rows)

    def hop(self, upward, goal, chunk, member):
        slots = self.up if upward else self.down
        send = self.sent_up if upward else self.sent_down
        receive = self.got_up if upward else self.got_down
        ref = slots.at[goal, self.at(chunk), :]
        return to_member(ref, ref, send.at[goal, chunk], receive.at[goal, chunk], member)

    def step(self, order, chunk):
        me, last, at = self.me, self.size - 1, self.at(chunk)
        for upward, goal, ahead, first, member in (
            (True, last - order, me < last - order, me == 0, me + 1),
            (False, order, me > order, me == last, me - 1),
        ):
            slots = self.up if upward else self.down

            @pl.when(ahead & first)
            def _():
                slots[goal, at, :] = self.term(goal, at)

            @pl.when(ahead & jnp.logical_not(first))
            def _():
                self.hop(upward, goal, chunk, me).wait_recv()
                slots[goal, at, :] = (
                    slots[goal, at, :].astype(F32) + self.term(goal, at).astype(F32)
                ).astype(BF16)

            if order > 0:
                older = goal + 1 if upward else goal - 1
                sent = (me < older) if upward else (me > older)

                @pl.when(sent)
                def _():
                    self.hop(upward, older, chunk, member).wait_send()

            @pl.when(ahead)
            def _():
                self.hop(upward, goal, chunk, member).start()

    def result(self, chunk, out, out_at):
        me, at = self.me, self.at(chunk)
        out[out_at, :] = self.term(me, at).astype(F32)

        @pl.when(me > 0)
        def _():
            self.hop(True, me, chunk, me).wait_recv()
            out[out_at, :] += self.up[me, at, :].astype(F32)

        @pl.when(me < self.size - 1)
        def _():
            self.hop(False, me, chunk, me).wait_recv()
            out[out_at, :] += self.down[me, at, :].astype(F32)

    def close(self):
        order = self.size - 2
        for chunk in range(self.chunks):

            @pl.when(self.me < self.size - 1 - order)
            def _():
                self.hop(True, self.size - 1 - order, chunk, self.me).wait_send()

            @pl.when(self.me > order)
            def _():
                self.hop(False, order, chunk, self.me).wait_send()


MIDDLE, LATE = 4, 5


class ChipSum:
    def __init__(self, layers, bits, source, acc, got, load, send, receive):
        self.layers, self.bits = layers, bits
        self.acc, self.got, self.chip = acc, got, lax.axis_index("chip")
        self.half = 1 << (len(bits) - 1)
        self.load = [
            pltpu.make_async_copy(
                source(layer, flip(self.chip, self.combo(slot))),
                acc.at[layer, slot],
                load.at[layer, slot],
            )
            for layer in layers
            for slot in range(self.half)
        ]
        self.source, self.sent, self.received = source, send, receive

    def combo(self, slot):
        count = len(self.bits)
        return sum(self.bits[count - 1 - j] for j in range(count - 1) if slot >> j & 1)

    def copies(self, stage):
        count = self.half >> stage
        offset = 2 * self.half - 2 * count
        where = {"chip": flip(self.chip, self.bits[stage])}
        for layer in self.layers:
            for slot in range(count):
                if stage == 0:
                    other = flip(self.chip, self.bits[0] | self.combo(slot))
                    ref = self.source(layer, other)
                else:
                    ref = self.acc.at[layer, count + slot]
                at = offset + slot
                yield layer, slot, at, to_device(
                    ref,
                    self.got.at[layer, at],
                    self.sent.at[layer, at],
                    self.received.at[layer, at],
                    where,
                )

    def start(self, stage):
        if stage == 0:
            for copy in self.load:
                copy.start()
        for _, _, _, copy in self.copies(stage):
            copy.start()

    def add(self, stage):
        if stage == 0:
            for copy in self.load:
                copy.wait()
        for layer, slot, at, copy in self.copies(stage):
            copy.wait_recv()
            self.acc[layer, slot] = (
                self.acc[layer, slot].astype(F32) + self.got[layer, at].astype(F32)
            ).astype(BF16)

    def close(self):
        for stage in range(len(self.bits)):
            for _, _, _, copy in self.copies(stage):
                copy.wait_send()


def sum_all_kernel(
    size,
    chips,
    chunks,
    split,
    term_in,
    grads,
    grad_wo,
    grad_qkv,
    grad_u,
    grad_v,
    grad_gain,
    grad_alpha_a,
    grad_alpha_m,
    out_pairs,
    out_there,
    owned_up,
    owned_gate,
    owned_down,
    owned_wo,
    owned_q,
    owned_k,
    owned_v,
    owned_vectors,
    term,
    out,
    vectors,
    term_up,
    term_down,
    acc_a,
    got_a,
    up_a,
    down_a,
    acc_b,
    got_b,
    up_b,
    down_b,
    pair_wo,
    other_wo,
    acc_wo,
    got_wo,
    up_wo,
    down_wo,
    pair_qkv,
    other_qkv,
    acc_qkv,
    got_qkv,
    whole,
    owned,
    turned_wo,
    vector_sum,
    vector_got,
    vector_line,
    local,
    core_sent,
    core_got,
    vector_sent,
    vector_received,
    term_sems,
    line_sems,
    load_sems,
    chip_sent,
    chip_got,
):
    me, chip, core = (lax.axis_index(name) for name in ("mp", "chip", "core"))
    bits = bits_below(chips)
    stages = len(bits)
    greet_around(size, chips)
    other_core_is = {"core": 1 - core}

    def sems(ref, which):
        return [ref.at[which, k] for k in range(4)]

    term_loads = [
        pltpu.make_async_copy(term_in.at[goal], term.at[goal], local.at[5 + goal])
        for goal in range(size)
    ]
    line = LineSum(
        size, chunks, lambda goal, at: term[goal, at, :], term_up, term_down, sems(term_sems, 0)
    )
    ends = sorted({0, size - 1})
    inner = [layer for layer in range(size) if layer not in ends]

    def plane_sums(layers):
        return [
            ChipSum(
                layers,
                bits,
                lambda m, c: grads.at[m, c, pl.ds(0, split), :],
                acc_a,
                got_a,
                load_sems.at[0],
                chip_sent.at[0],
                chip_got.at[0],
            ),
            ChipSum(
                layers,
                bits[::-1],
                lambda m, c: grads.at[m, c, pl.ds(split, grads.shape[2] - split), :],
                acc_b,
                got_b,
                load_sems.at[1],
                chip_sent.at[1],
                chip_got.at[1],
            ),
        ]

    sums_ends, sums_inner = plane_sums(ends), plane_sums(inner)
    sum_wo = ChipSum(
        range(size),
        bits[::-1],
        lambda m, c: pair_wo.at[m, c],
        acc_wo,
        got_wo,
        load_sems.at[2],
        chip_sent.at[2],
        chip_got.at[2],
    )
    sum_qkv = ChipSum(
        range(1),
        bits,
        lambda m, c: pair_qkv.at[c],
        acc_qkv,
        got_qkv,
        load_sems.at[3],
        chip_sent.at[3],
        chip_got.at[3],
    )
    lines = [
        LineSum(
            size,
            1,
            lambda goal, at, acc=acc: acc[goal, 0, at, :],
            up,
            down,
            sems(line_sems, which),
        )
        for which, (acc, up, down) in enumerate(
            ((acc_a, up_a, down_a), (acc_b, up_b, down_b), (acc_wo, up_wo, down_wo))
        )
    ]

    own = [
        pltpu.make_async_copy(grad_wo.at[:, :, core], pair_wo, local.at[0]),
        pltpu.make_async_copy(grad_qkv.at[:, core], pair_qkv, local.at[1]),
    ]
    given = [
        to_device(
            grad_wo.at[:, :, 1 - core], other_wo, core_sent.at[0], core_got.at[0], other_core_is
        ),
        to_device(
            grad_qkv.at[:, 1 - core], other_qkv, core_sent.at[1], core_got.at[1], other_core_is
        ),
    ]
    vector_copies = [
        to_member(
            vectors.at[flip(me, k)],
            vector_line.at[k],
            vector_sent.at[k],
            vector_received.at[k],
            flip(me, k),
        )
        for k in range(1, size)
    ]
    for copy in own + given:
        copy.start()
    for part in sums_ends:
        part.start(0)
    for copy in term_loads:
        copy.start()

    units = grad_u.shape[2]
    columns = out_pairs.shape[0]
    at_gain = 4 * units
    vectors[...] = jnp.zeros_like(vectors)
    for member in range(size):
        half = pl.multiple_of(core * units, units)
        vectors[member, :, pl.ds(half, units)] = grad_u[member]
        vectors[member, :, pl.ds(2 * units + half, units)] = grad_v[member] * math.sqrt(
            size * columns
        )
        these = slice(member * columns, (member + 1) * columns)
        vectors[member, :, at_gain + columns : at_gain + 2 * columns] = grad_alpha_a[:, these]
        vectors[member, :, at_gain + 2 * columns :] = grad_alpha_m[:, these]
    vectors[me, :, at_gain : at_gain + columns] = split_dot(grad_gain[...], out_pairs[...])
    for copy in vector_copies:
        copy.start()
    for copy in term_loads:
        copy.wait()

    owner = chip * 2 + core
    vector_bits = [1] + [2 * bit for bit in bits]

    def vector_copy(stage):
        partner = flip(owner, vector_bits[stage])
        return to_device(
            vector_sum.at[stage],
            vector_got.at[stage],
            vector_sent.at[size + stage],
            vector_received.at[size + stage],
            {"chip": lax.div(partner, 2), "core": lax.rem(partner, 2)},
        )

    def vector_step(stage):
        if stage == 0:
            total = vectors[me]
            for k, copy in enumerate(vector_copies):
                copy.wait_recv()
                total = total + vector_line[k + 1]
            vector_sum[0] = total
        else:
            vector_copy(stage - 1).wait_recv()
            vector_sum[stage] = vector_sum[stage - 1] + vector_got[stage - 1]
        if stage < len(vector_bits):
            vector_copy(stage).start()

    def add(group, stage):
        for part in group:
            part.add(stage)
            if stage + 1 < stages:
                part.start(stage + 1)

    small = [sum_wo, sum_qkv]
    rest = [*sums_inner, *small]
    vector_at = 0
    for order in range(size - 1):
        for chunk in range(chunks):
            line.step(order, chunk)
            if order == 0 and chunk >= 1 and vector_at <= len(vector_bits):
                vector_step(vector_at)
                vector_at += 1
            if order == 1 and chunk == MIDDLE:
                for stage in range(1, stages):
                    add(sums_ends, stage)
                for part in rest:
                    part.start(0)
            if order == 2 and chunk == LATE:
                add(rest, 0)
        if order == 0:
            for copy in own:
                copy.wait()
            for copy in given:
                copy.wait_recv()
            pair_wo[...] = (pair_wo[...].astype(F32) + other_wo[...].astype(F32)).astype(BF16)
            pair_qkv[...] = (pair_qkv[...].astype(F32) + other_qkv[...].astype(F32)).astype(
                BF16
            )
            add(sums_ends, 0)
        if order == 1:
            lines[0].step(0, 0)
            lines[1].step(0, 0)
    for stage in range(1, stages):
        add(rest, stage)
    for order in range(size - 1):
        if order > 0:
            lines[0].step(order, 0)
            lines[1].step(order, 0)
        lines[2].step(order, 0)
    for stage in range(vector_at, len(vector_bits) + 1):
        vector_step(stage)
    for chunk in range(chunks):
        line.result(chunk, out, line.at(chunk))
    out_copy = pltpu.make_async_copy(out, out_there, local.at[5 + size])
    out_copy.start()
    owned_vectors[...] = vector_sum[len(vector_bits)]
    part = owned_v.shape[1]
    total_qkv = acc_qkv[0, 0]
    owned_q[...] = dot(total_qkv[:, :part], out_pairs[...])
    owned_k[...] = dot(total_qkv[:, part : 2 * part], out_pairs[...])
    owned_v[...] = total_qkv[:, 2 * part :].astype(F32)
    lines[0].result(0, whole, pl.ds(0, split))
    lines[1].result(0, whole, pl.ds(split, whole.shape[0] - split))
    lines[2].result(0, turned_wo, slice(None))

    matrices, rows, columns = owned.shape
    columns = columns // 2
    place = pl.ds(pl.multiple_of(core * columns, columns), columns)
    swaps = []
    for matrix in range(matrices):
        mine = pl.ds(pl.multiple_of((2 * matrix + core) * rows, rows), rows)
        theirs = pl.ds(pl.multiple_of((2 * matrix + 1 - core) * rows, rows), rows)
        swaps.append(
            to_device(
                whole.at[theirs, :],
                owned.at[matrix, :, place],
                core_sent.at[2 + matrix],
                core_got.at[2 + matrix],
                other_core_is,
            )
        )
        swaps[-1].start()
        copy = pltpu.make_async_copy(
            whole.at[mine, :], owned.at[matrix, :, place], local.at[2 + matrix]
        )
        copy.start()
        swaps.append(copy)
    owned_wo[...] = turned_wo[...].T
    out_copy.wait()
    for copy in swaps:
        copy.wait()
    owned_up[...] = owned[0]
    owned_gate[...] = owned[1]
    owned_down[...] = owned[2].T

    for copy in given + vector_copies:
        copy.wait_send()
    for stage in range(len(vector_bits)):
        vector_copy(stage).wait_send()
    for part in [*sums_ends, *rest]:
        part.close()
    line.close()
    for part in lines:
        part.close()


def sum_all(term, grads, grad_wo, grad_qkv, shares, out_pairs, chips, collective):
    size, tokens, part = term.shape
    height, units = grads.shape[2:]
    rows = height // 6
    chunks = 6
    split = height // 32 * 16
    half, blocks = max(chips // 2, 1), max(chips - 1, 1)
    stages = chips.bit_length()
    dma = pltpu.SemaphoreType.DMA
    vmem = pl.BlockSpec(memory_space=pltpu.VMEM)
    wo_block, qkv_block = grad_wo.shape[3:], grad_qkv.shape[2:]
    long = (1, 4 * units + 3 * part)

    def sums(layers, block):
        return [
            pltpu.VMEM((layers, half, *block), BF16),
            pltpu.VMEM((layers, blocks, *block), BF16),
        ]

    def line(block):
        return [pltpu.VMEM((size, *block), BF16)] * 2

    return pl.pallas_call(
        functools.partial(sum_all_kernel, size, chips, chunks, split),
        in_specs=[ANY, ANY, ANY, ANY, *[vmem] * (len(shares) + 1)],
        out_specs=[ANY, *[vmem] * 8],
        out_shape=[
            jax.ShapeDtypeStruct((tokens, part), F32),
            jax.ShapeDtypeStruct((rows, 2 * units), F32),
            jax.ShapeDtypeStruct((rows, 2 * units), F32),
            jax.ShapeDtypeStruct((2 * units, rows), F32),
            jax.ShapeDtypeStruct(wo_block[::-1], F32),
            *[jax.ShapeDtypeStruct((qkv_block[0], part), F32)] * 3,
            jax.ShapeDtypeStruct(long, F32),
        ],
        scratch_shapes=[
            pltpu.VMEM((size, tokens, part), BF16),
            pltpu.VMEM((tokens, part), F32),
            pltpu.VMEM((size, *long), F32),
            *line((tokens, part)),
            *sums(size, (split, units)),
            *line((split, units)),
            *sums(size, (height - split, units)),
            *line((height - split, units)),
            pltpu.VMEM((size, chips, *wo_block), BF16),
            pltpu.VMEM((size, chips, *wo_block), BF16),
            *sums(size, wo_block),
            *line(wo_block),
            pltpu.VMEM((chips, *qkv_block), BF16),
            pltpu.VMEM((chips, *qkv_block), BF16),
            *sums(1, qkv_block),
            pltpu.VMEM((height, units), F32),
            pltpu.VMEM((3, rows, 2 * units), F32),
            pltpu.VMEM(wo_block, F32),
            pltpu.VMEM((stages + 1, *long), F32),
            pltpu.VMEM((stages + 1, *long), F32),
            pltpu.VMEM((size, *long), F32),
            dma((6 + size,)),
            dma((5,)),
            dma((5,)),
            dma((size + stages,)),
            dma((size + stages,)),
            dma((1, 4, size, chunks)),
            dma((3, 4, size, 1)),
            dma((4, size, half)),
            dma((4, size, blocks)),
            dma((4, size, blocks)),
        ],
        compiler_params=remote_params(collective),
        name="sum_all",
    )(term, grads, grad_wo, grad_qkv, *shares, out_pairs)


def paired_place(heads):
    head, feature = np.divmod(np.arange(heads * DK), DK)
    return (feature // HALF) * (heads * HALF) + head * HALF + feature % HALF


def placing_matrix(place, heads):
    head, feature = np.divmod(np.arange(heads * DK), DK)
    matrix = np.zeros((heads * DK, heads * EXT), np.float32)
    matrix[place, head * EXT + feature] = 1
    return matrix


def delta_matrix(heads):
    lane = np.arange(heads * EXT)
    head = np.arange(heads * DK) // DK
    return ((head[:, None] == lane[None, :] // EXT) & (lane % EXT >= DK) & (lane % EXT < DK + 3)).astype(
        np.float32
    )


def head_sum_matrix(heads):
    lane = np.arange(heads * HALF) // HALF
    return (lane[:, None] == lane[None, :]).astype(np.float32)


def split_dot(value, matrix):
    high = value.astype(BF16)
    rest = (value - high.astype(F32)).astype(BF16)
    return dot(high, matrix) + dot(rest, matrix)


def project_block(wide, weight, cos, sin, gain, place_pair, place_plain, sums, at, outs):
    q, k, v, q_pair, k_pair, rq, rk = outs
    heads = q.shape[0]
    pair, width = heads * HALF, heads * DK
    raw = dot(wide[0], weight[0])
    for part in range(1, len(wide)):
        raw += dot(wide[part], weight[part])
    lane = lax.broadcasted_iota(jnp.int32, (raw.shape[0], EXT), 1)
    for offset, out, pair_out, scale_out, factor in (
        (0, q, q_pair, rq, math.sqrt(DK)),
        (width, k, k_pair, rk, 1.0),
    ):
        first = raw[:, offset : offset + pair]
        second = raw[:, offset + pair : offset + width]
        turned_first = first * cos - second * sin
        turned_second = second * cos + first * sin
        total = split_dot(turned_first * turned_first + turned_second * turned_second, sums)
        scale = lax.rsqrt(total + EPSILON)
        scale_out[at, :] = scale
        both = jnp.concatenate(
            [
                turned_first * scale * gain[:, :pair],
                turned_second * scale * gain[:, pair:],
            ],
            axis=1,
        ).astype(BF16)
        pair_out[at, :] = both
        padded = dot(both, place_pair) * factor
        for head in range(heads):
            piece = padded[:, head * EXT : (head + 1) * EXT]
            if factor == 1.0:
                piece = jnp.where(lane < DK, piece, 1.0)
            out[head, at, :] = piece.astype(BF16)
    padded = dot(raw[:, 2 * width :].astype(BF16), place_plain)
    for head in range(heads):
        piece = padded[:, head * EXT : (head + 1) * EXT]
        v[head, at, :] = jnp.where(lane < DK, piece, 1.0).astype(BF16)


def split_three(value):
    high = value.astype(BF16).astype(F32)
    rest = value - high
    middle = rest.astype(BF16).astype(F32)
    return high, middle, rest - middle


def attend_kernel(low, q, k, v, columns, kdoc, collect, attended, qback, acc):
    heads, rows, _ = q.shape
    block = kdoc.shape[2]
    index = pl.program_id(0)
    acc[...] = jnp.zeros_like(acc)

    def earlier(j, carry):
        slots = pl.ds(pl.multiple_of(j * block, block), block)
        mask = columns[:, 1:2] == kdoc[j]
        for head in range(heads):
            scores = dot(q[head], k[head, slots, :], NT)
            weight = jnp.where(mask, jnp.exp(scores), 0.0).astype(BF16)
            acc[head] += dot(weight, v[head, slots, :])
        return carry

    lax.fori_loop(low[index], index, earlier, 0)

    strip = max(rows // 2, min(rows, 128))
    for start in range(0, rows, strip):
        at = slice(start, start + strip)
        end = start + strip
        slots = pl.ds(pl.multiple_of(index * block, block), end)
        row = start + lax.broadcasted_iota(jnp.int32, (strip, end), 0)
        column = lax.broadcasted_iota(jnp.int32, (strip, end), 1)
        mask = columns[at, 1:2] == kdoc[index][:, :end]
        mask = (mask & (column < row)) | (column == row)
        for head in range(heads):
            scores = dot(q[head, at, :], k[head, slots, :], NT)
            weight = jnp.where(mask, jnp.exp(scores), 0.0).astype(BF16)
            acc[head, at, :] += dot(weight, v[head, slots, :])

    lane = lax.broadcasted_iota(jnp.int32, (rows, EXT), 1)
    merged = jnp.zeros((rows, heads * DK), F32)
    for head in range(heads):
        both = acc[head]
        total = pltpu.roll(both, DK, 1)
        output = jnp.where(lane < DK, both / total, 0.0).astype(BF16)
        merged += dot(output, collect[head])
        high, middle, rest = split_three(-jnp.log(both))
        qback[head] = jnp.where(
            lane < DK,
            q[head].astype(F32),
            jnp.where(
                lane == DK,
                high,
                jnp.where(lane == DK + 1, middle, jnp.where(lane == DK + 2, rest, 0.0)),
            ),
        ).astype(BF16)
    attended[...] = merged.astype(BF16)


def attend(low, q, k, v, columns, kdoc, collect):
    heads, tokens, _ = q.shape
    block = kdoc.shape[2]
    width = heads * DK

    def whole(array):
        return pl.BlockSpec(array.shape, lambda i, low: (0,) * array.ndim)

    headed = pl.BlockSpec((heads, block, EXT), lambda i, low: (0, i, 0))
    return pl.pallas_call(
        attend_kernel,
        grid_spec=pltpu.PrefetchScalarGridSpec(
            num_scalar_prefetch=1,
            grid=(tokens // block,),
            in_specs=[
                headed,
                whole(k),
                whole(v),
                pl.BlockSpec((block, columns.shape[1]), lambda i, low: (i, 0)),
                whole(kdoc),
                whole(collect),
            ],
            out_specs=[pl.BlockSpec((block, width), lambda i, low: (i, 0)), headed],
            scratch_shapes=[pltpu.VMEM((heads, block, EXT), F32)],
        ),
        out_shape=[
            jax.ShapeDtypeStruct((tokens, width), BF16),
            jax.ShapeDtypeStruct((heads, tokens, EXT), BF16),
        ],
        compiler_params=grid_params(1),
        cost_estimate=pl.CostEstimate(
            flops=40_000_000_000, bytes_accessed=16 << 20, transcendentals=0
        ),
        name="attend",
    )(low, q, k, v, columns, kdoc, collect)


def unrope(grad, unit, gain, scale, cos, sin, sums):
    pair = cos.shape[1]
    grad_gain = jnp.sum(grad * unit, axis=0, keepdims=True)
    dy = grad * gain
    prod = dy * unit
    total = split_dot(prod[:, :pair] + prod[:, pair:], sums)
    first = scale * (dy[:, :pair] - unit[:, :pair] * total)
    second = scale * (dy[:, pair:] - unit[:, pair:] * total)
    raw = jnp.concatenate([first * cos + second * sin, second * cos - first * sin], axis=1)
    return raw.astype(BF16), grad_gain


def head_lanes(shape, head, paired):
    lane = lax.broadcasted_iota(jnp.int32, shape, 1)
    if paired:
        return lax.div(lax.rem(lane, shape[1] // 2), HALF) == head
    return lax.div(lane, DK) == head


def attend_back_kernel(
    low,
    qback,
    q_pair,
    dout,
    attended,
    k,
    k_pair,
    v,
    qdoc,
    columns,
    cosine,
    sine,
    rq,
    rk,
    gain,
    weight,
    place_plain,
    place_delta,
    sums,
    wide,
    grad_resid,
    term_out,
    grad_qkv,
    gain_out,
    dk,
    dv,
    dq,
    dox,
    q_heads,
    d_heads,
    k_heads,
    probs_all,
    scores_all,
    dq_low,
    total_qkv,
):
    heads, rows, _ = qback.shape
    steps = pl.num_programs(0) // 2
    step_at = pl.program_id(0)
    width = heads * DK
    scale = math.sqrt(DK)

    @pl.when(step_at == 0)
    def _():
        dk[...] = jnp.zeros_like(dk)
        dv[...] = jnp.zeros_like(dv)
        gain_out[...] = jnp.zeros_like(gain_out)
        keys = k_pair[...]
        for head in range(heads):
            k_heads[head] = jnp.where(head_lanes(keys.shape, head, True), keys, 0)

    @pl.when(step_at < steps)
    def _():
        index = step_at
        lane = lax.broadcasted_iota(jnp.int32, (rows, EXT), 1)
        grads = dout[...]
        queries = q_pair[...]
        spread = dot(grads, place_plain[...])
        delta = split_dot(grads.astype(F32) * attended[...].astype(F32), place_delta[...])
        for head in range(heads):
            at = slice(head * EXT, (head + 1) * EXT)
            high, middle, rest = split_three(-delta[:, at])
            dox[head] = jnp.where(
                lane < DK,
                spread[:, at],
                jnp.where(lane == DK, high, jnp.where(lane == DK + 1, middle, rest)),
            ).astype(BF16)
            stack = slice(head * rows, (head + 1) * rows)
            q_heads[stack, :] = jnp.where(head_lanes(queries.shape, head, True), queries, 0)
            d_heads[stack, :] = jnp.where(head_lanes(grads.shape, head, False), grads, 0)
        dq[...] = jnp.zeros_like(dq)

        def earlier(j, carry):
            slots = pl.ds(pl.multiple_of(j * rows, rows), rows)
            mask = columns[slots, 2:3] == qdoc[0]
            total = dq[...]
            for head in range(heads):
                scores = dot(k[head, slots, :], qback[head], NT)
                probs = jnp.where(mask, jnp.exp(scores), 0.0)
                dprobs = dot(v[head, slots, :], dox[head], NT)
                dscores = (probs * dprobs).astype(BF16)
                stack = slice(head * rows, (head + 1) * rows)
                probs_all[:, stack] = probs.astype(BF16)
                scores_all[:, stack] = dscores
                total += dot(dscores, k_heads[head, slots, :], TN)
            dq[...] = total
            dv[slots, :] += dot(probs_all[...], d_heads[...])
            dk[slots, :] += dot(scores_all[...], q_heads[...])
            return carry

        lax.fori_loop(low[index], index, earlier, 0)

        strip = max(rows // 2, min(rows, 128))
        for start in range(0, rows, strip):
            after_start = slice(start, rows)
            count = rows - start
            slots = pl.ds(pl.multiple_of(index * rows + start, strip), strip)
            key = start + lax.broadcasted_iota(jnp.int32, (strip, count), 0)
            query = start + lax.broadcasted_iota(jnp.int32, (strip, count), 1)
            mask = columns[slots, 2:3] == qdoc[0][:, after_start]
            mask = (mask & (key < query)) | (key == query)
            values, keys, queries_grad = None, None, None
            for head in range(heads):
                scores = dot(k[head, slots, :], qback[head, after_start, :], NT)
                probs = jnp.where(mask, jnp.exp(scores), 0.0)
                dprobs = dot(v[head, slots, :], dox[head, after_start, :], NT)
                dscores = (probs * dprobs).astype(BF16)
                stack = slice(head * rows + start, (head + 1) * rows)
                terms = (
                    dot(probs.astype(BF16), d_heads[stack, :]),
                    dot(dscores, q_heads[stack, :]),
                    dot(dscores, k_heads[head, slots, :], TN),
                )
                if head == 0:
                    values, keys, queries_grad = terms
                else:
                    values, keys, queries_grad = (
                        values + terms[0],
                        keys + terms[1],
                        queries_grad + terms[2],
                    )
            dv[slots, :] += values
            dk[slots, :] += keys
            dq[after_start, :] += queries_grad

        raw, grad_gain = unrope(
            dq[...] * scale,
            queries.astype(F32) * (1.0 / gain[...]),
            gain[...],
            rq[...],
            cosine[...],
            sine[...],
            sums[...],
        )
        gain_out[...] += grad_gain
        dq_low[pl.ds(pl.multiple_of(index * rows, rows), rows), :] = raw

    @pl.when(step_at >= steps)
    def _():
        index = step_at - steps
        slots = pl.ds(pl.multiple_of(index * rows, rows), rows)
        raw, grad_gain = unrope(
            dk[slots, :] * scale,
            k_pair[slots, :].astype(F32) * (1.0 / gain[...]),
            gain[...],
            rk[...],
            cosine[...],
            sine[...],
            sums[...],
        )
        gain_out[...] += grad_gain
        together = jnp.concatenate([dq_low[slots, :], raw, dv[slots, :].astype(BF16)], axis=1)
        parts, part = weight.shape[:2]
        for member in range(parts):
            term_out[member] = dot(together, weight[member], NT).astype(BF16)
            product = dot(wide[member], together, TN)

            @pl.when(index == 0)
            def _():
                total_qkv[member] = product

            @pl.when(index > 0)
            def _():
                total_qkv[member] += product

        strip = STRIP
        first = low[steps] * (grad_resid.shape[0] // strip)
        for half in range(rows // strip):
            number = index * (rows // strip) + half - first

            @pl.when((number >= 0) & (number < grad_resid.shape[0] // strip))
            def _():
                at = pl.ds(half * strip, strip)
                own = pl.ds(pl.multiple_of(number * strip, strip), strip)
                for member in range(parts):
                    term_out[member, at, :] = (
                        term_out[member, at, :].astype(F32)
                        + grad_resid[own, member * part : (member + 1) * part].astype(F32)
                    ).astype(BF16)

        @pl.when(index == steps - 1)
        def _():
            grad_qkv[...] = total_qkv[...].astype(BF16)


def attend_back(
    low,
    qback,
    q_pair,
    dout,
    attended,
    k,
    k_pair,
    v,
    qdoc,
    columns,
    cosine,
    sine,
    rq,
    rk,
    gain,
    weight,
    place_plain,
    place_delta,
    sums,
    wide,
    grad_resid,
):
    heads, tokens, _ = k.shape
    block = qdoc.shape[2]
    width = heads * DK
    steps = tokens // block
    parts, part = weight.shape[:2]

    def whole(array):
        return pl.BlockSpec(array.shape, lambda i, low: (0,) * array.ndim)

    def now(i):
        return jnp.minimum(i, steps - 1)

    def after(i):
        return jnp.maximum(i - steps, 0)

    def both(i):
        return lax.rem(i, steps)

    def rows(columns, at):
        return pl.BlockSpec((block, columns), lambda i, low: (at(i), 0))

    return pl.pallas_call(
        attend_back_kernel,
        grid_spec=pltpu.PrefetchScalarGridSpec(
            num_scalar_prefetch=1,
            grid=(2 * steps,),
            in_specs=[
                pl.BlockSpec((heads, block, EXT), lambda i, low: (0, now(i), 0)),
                rows(width, now),
                rows(width, now),
                rows(width, now),
                whole(k),
                whole(k_pair),
                whole(v),
                pl.BlockSpec((1, 1, block), lambda i, low: (now(i), 0, 0)),
                whole(columns),
                rows(width // 2, both),
                rows(width // 2, both),
                rows(width // 2, now),
                rows(width // 2, after),
                whole(gain),
                whole(weight),
                whole(place_plain),
                whole(place_delta),
                whole(sums),
                pl.BlockSpec((parts, block, part), lambda i, low: (0, after(i), 0)),
                whole(grad_resid),
            ],
            out_specs=[
                pl.BlockSpec((parts, block, part), lambda i, low: (0, after(i), 0)),
                pl.BlockSpec((parts, part, 3 * width), lambda i, low: (0, 0, 0)),
                pl.BlockSpec((1, width), lambda i, low: (0, 0)),
            ],
            scratch_shapes=[
                pltpu.VMEM((tokens, width), F32),
                pltpu.VMEM((tokens, width), F32),
                pltpu.VMEM((block, width), F32),
                pltpu.VMEM((heads, block, EXT), BF16),
                pltpu.VMEM((heads * block, width), BF16),
                pltpu.VMEM((heads * block, width), BF16),
                pltpu.VMEM((heads, tokens, width), BF16),
                pltpu.VMEM((block, heads * block), BF16),
                pltpu.VMEM((block, heads * block), BF16),
                pltpu.VMEM((tokens, width), BF16),
                pltpu.VMEM((parts, part, 3 * width), F32),
            ],
        ),
        out_shape=[
            jax.ShapeDtypeStruct((parts, tokens, part), BF16),
            jax.ShapeDtypeStruct((parts, part, 3 * width), BF16),
            jax.ShapeDtypeStruct((1, width), F32),
        ],
        compiler_params=grid_params(1),
        cost_estimate=pl.CostEstimate(
            flops=80_000_000_000, bytes_accessed=30 << 20, transcendentals=0
        ),
        name="attend_back",
    )(
        low,
        qback,
        q_pair,
        dout,
        attended,
        k,
        k_pair,
        v,
        qdoc,
        columns,
        cosine,
        sine,
        rq,
        rk,
        gain,
        weight,
        place_plain,
        place_delta,
        sums,
        wide,
        grad_resid,
    )


def row_scale(value):
    return lax.rsqrt(jnp.sum(value * value, axis=-1, keepdims=True) + EPSILON)


def residual_backward(grad_out, result, resid, unit, alpha, branch_scale, mixed_scale):
    grad_mixed = mixed_scale * (
        grad_out - result * jnp.sum(grad_out * result, axis=-1, keepdims=True)
    )
    grad_alpha = jnp.sum(grad_mixed * (unit - resid), axis=0, keepdims=True)
    grad_unit = grad_mixed * alpha
    grad_branch = branch_scale * (
        grad_unit - unit * jnp.sum(grad_unit * unit, axis=-1, keepdims=True)
    )
    return grad_mixed * (1.0 - alpha), grad_branch, grad_alpha


STRIP = 256


def strips(rows):
    strip = min(STRIP, rows)
    return [pl.ds(start, strip) for start in range(0, rows, strip)]


def core_semaphores(count):
    return [pltpu.SemaphoreType.DMA((count,)), pltpu.SemaphoreType.DMA((count,))]


def greet_pair_and_line(size):
    me, core = lax.axis_index("mp"), lax.axis_index("core")
    for k in range(1, size):
        greet({"mp": flip(me, k)})
    greet({"core": 1 - core})
    pl.semaphore_wait(pltpu.get_barrier_semaphore(), size)


def output_matrix(packed_wo, whole):
    size, chips, rows, both = packed_wo.shape
    part = both // 2
    for chip in range(chips):
        for core in range(2):
            start = (2 * chip + core) * rows
            whole[:, start : start + rows, :] = packed_wo[
                :, chip, :, core * part : (core + 1) * part
            ]


def mix_kernel(
    size,
    attended,
    packed,
    wide,
    alpha,
    cotangent,
    x,
    middle_out,
    unit_out,
    merged_out,
    full_wo_out,
    resid_out,
    cotangent_out,
    branch_scale_out,
    mixed_scale_out,
    packed_wo,
    middle_low,
    resid,
    middle_kept,
    unit_kept,
    merged,
    full_wo,
    cotangent_low,
    send,
    receive,
    local,
    own_sems,
    core_sent,
    core_got,
    out_sems,
):
    me, core = lax.axis_index("mp"), lax.axis_index("core")
    mine, width = middle_out.shape
    part = width // size
    rows = packed_wo.shape[2]
    greet_pair_and_line(size)
    every = strips(mine)

    def exchange(order):
        at = every[order]
        return Exchange(
            size,
            attended,
            merged,
            lambda ref, j: ref.at[
                pl.ds(pl.multiple_of(j * mine + at.start, at.size), at.size), :
            ],
            lambda ref, j: ref.at[at, pl.ds(pl.multiple_of(j * part, part), part)],
            send.at[order],
            receive.at[order],
            local.at[order],
        )

    exchange(0).start()
    own = [
        pltpu.make_async_copy(
            packed.at[:, :, pl.ds(packed.shape[2] - rows, rows), :], packed_wo, own_sems.at[0]
        )
    ]
    for member in range(size):
        own.append(
            pltpu.make_async_copy(
                wide.at[member, pl.ds(pl.multiple_of(me * mine, mine), mine), :],
                resid.at[:, pl.ds(member * part, part)],
                own_sems.at[1 + member],
            )
        )
    for copy in own:
        copy.start()
    for at in strips(cotangent.shape[0]):
        cotangent_low[at, :] = cotangent[at, :].astype(BF16)
    for copy in own:
        copy.wait()
    output_matrix(packed_wo, full_wo)
    leaving = [
        pltpu.make_async_copy(here, there, out_sems.at[order])
        for order, (here, there) in enumerate(
            ((full_wo, full_wo_out), (resid, resid_out), (cotangent_low, cotangent_out))
        )
    ]
    for copy in leaving:
        copy.start()

    swaps = []
    for order, at in enumerate(every):
        exchange(order).wait()
        if order + 1 < len(every):
            exchange(order + 1).start()
        branch = dot(merged[at, :part], full_wo[0], NT)
        for member in range(1, size):
            branch += dot(
                merged[at, member * part : (member + 1) * part], full_wo[member], NT
            )
        old = resid[at, :].astype(F32)
        branch_scale = row_scale(branch)
        unit = branch * branch_scale
        mixed = old + alpha[...] * (unit - old)
        mixed_scale = row_scale(mixed)
        middle = mixed * mixed_scale
        middle_kept[at, :] = middle
        unit_kept[at, :] = unit.astype(BF16)
        branch_scale_out[at, :] = branch_scale
        mixed_scale_out[at, :] = mixed_scale
        middle_low[at, :] = middle.astype(BF16)
        there = pl.ds(mine + at.start, at.size)
        swap = to_device(
            middle_low.at[at, :],
            x.at[there, :],
            core_sent.at[order],
            core_got.at[order],
            {"core": 1 - core},
        )
        swap.start()
        swaps.append(swap)
        for kind, (here, there) in enumerate(
            ((middle_kept, middle_out), (unit_kept, unit_out), (merged, merged_out))
        ):
            copy = pltpu.make_async_copy(
                here.at[at, :], there.at[at, :], out_sems.at[3 + 3 * order + kind]
            )
            copy.start()
            leaving.append(copy)
    keep = pltpu.make_async_copy(middle_low, x.at[pl.ds(0, mine), :], own_sems.at[0])
    keep.start()
    keep.wait()
    for copy in swaps + leaving:
        copy.wait()


def mix(attended, packed, rows, wide, alpha, cotangent, collective):
    size, slots, part = wide.shape
    chips = packed.shape[1]
    mine, width = slots // size, size * part
    vmem = pl.BlockSpec(memory_space=pltpu.VMEM)
    count = len(strips(mine))
    scale = jax.ShapeDtypeStruct((mine, 1), F32)
    return pl.pallas_call(
        functools.partial(mix_kernel, size),
        in_specs=[ANY, ANY, ANY, vmem, vmem],
        out_specs=[*[ANY] * 7, vmem, vmem],
        out_shape=[
            jax.ShapeDtypeStruct((2 * mine, width), BF16),
            jax.ShapeDtypeStruct((mine, width), F32),
            jax.ShapeDtypeStruct((mine, width), BF16),
            jax.ShapeDtypeStruct((mine, width), BF16),
            jax.ShapeDtypeStruct((size, width, part), BF16),
            jax.ShapeDtypeStruct((mine, width), BF16),
            jax.ShapeDtypeStruct((slots, part), BF16),
            scale,
            scale,
        ],
        scratch_shapes=[
            pltpu.VMEM((size, chips, rows, 2 * part), BF16),
            pltpu.VMEM((mine, width), BF16),
            pltpu.VMEM((mine, width), BF16),
            pltpu.VMEM((mine, width), F32),
            pltpu.VMEM((mine, width), BF16),
            pltpu.VMEM((mine, width), BF16),
            pltpu.VMEM((size, width, part), BF16),
            pltpu.VMEM((slots, part), BF16),
            pltpu.SemaphoreType.DMA((count, size)),
            pltpu.SemaphoreType.DMA((count, size)),
            pltpu.SemaphoreType.DMA((count,)),
            pltpu.SemaphoreType.DMA((1 + size,)),
            *core_semaphores(count),
            pltpu.SemaphoreType.DMA((3 + 3 * count,)),
        ],
        compiler_params=remote_params(collective),
        name="mix",
    )(attended, packed, wide, alpha, cotangent)


def whole_matrix(ref):
    _, chips, rows, units = ref.shape
    return ref[...].reshape(chips * rows, units)


def first_step():
    return (pl.program_id(0) == 0) & (pl.program_id(1) == 0)


def last_step():
    return (pl.program_id(0) == pl.num_programs(0) - 1) & (
        pl.program_id(1) == pl.num_programs(1) - 1
    )


def swap_cores(source, target, sems):
    return to_device(
        source, target, sems[0], sems[1], {"core": 1 - lax.axis_index("core")}
    )


def feed_kernel(
    size,
    x,
    w_up,
    w_gate,
    w_down,
    s_u,
    s_v,
    cotangent,
    middle,
    alpha,
    up_out,
    gate_out,
    units_out,
    result_out,
    grad_middle,
    dbranch,
    grad_alpha,
    acc,
    given,
    got,
    spread,
    low,
    send,
    receive,
    local,
    core_sent,
    core_got,
    keep_sems,
):
    exchange = Exchange(
        size,
        cotangent,
        spread,
        row_part(spread.shape[0]),
        column_part(cotangent.shape[1]),
        send,
        receive,
        local,
    )
    branch_swap = swap_cores(given, got, (core_sent.at[0], core_got.at[0]))

    @pl.when(first_step())
    def _():
        greet_pair_and_line(size)
        exchange.start()

    block, part = pl.program_id(0), pl.program_id(1)
    up = dot(x[...], whole_matrix(w_up))
    gate = dot(x[...], whole_matrix(w_gate))
    up_out[0] = up.astype(BF16)
    gate_out[0] = gate.astype(BF16)
    scaled = gate * s_v[0]
    units = (up * s_u[0] * (scaled / (1.0 + jnp.exp(-scaled)))).astype(BF16)
    units_out[0] = units
    term = dot(units, whole_matrix(w_down), NT)

    @pl.when(part == 0)
    def _():
        acc[...] = term

    @pl.when(part > 0)
    def _():
        acc[...] += term

    last = part == pl.num_programs(1) - 1

    @pl.when(last & (block == 0))
    def _():
        given[...] = acc[...].astype(BF16)
        branch_swap.start()

    @pl.when(last & (block == 1))
    def _():
        mine = acc.shape[0]
        branch_swap.wait()
        exchange.wait()
        swaps = []
        for order, at in enumerate(strips(mine)):
            branch = acc[at, :] + got[at, :].astype(F32)
            branch_scale = row_scale(branch)
            unit = branch * branch_scale
            old = middle[at, :]
            mixed = old + alpha[...] * (unit - old)
            mixed_scale = row_scale(mixed)
            result = mixed * mixed_scale
            result_out[at, :] = result.astype(BF16)
            grad_old, grad_branch, part_alpha = residual_backward(
                spread[at, :].astype(F32),
                result,
                old,
                unit,
                alpha[...],
                branch_scale,
                mixed_scale,
            )
            grad_middle[at, :] = grad_old
            if order == 0:
                grad_alpha[...] = part_alpha
            else:
                grad_alpha[...] += part_alpha
            low[at, :] = grad_branch.astype(BF16)
            there = pl.ds(mine + at.start, at.size)
            swaps.append(
                swap_cores(
                    low.at[at, :],
                    dbranch.at[there, :],
                    (core_sent.at[1 + order], core_got.at[1 + order]),
                )
            )
            swaps.append(
                pltpu.make_async_copy(low.at[at, :], dbranch.at[at, :], keep_sems.at[order])
            )
            swaps[-2].start()
            swaps[-1].start()
        for swap in swaps:
            swap.wait()


def packed_specs(packed, width):
    _, chips, _, units = packed.shape
    return [
        pl.BlockSpec((1, chips, width // chips, units), lambda t, m, w=w: (m, 0, w, 0))
        for w in range(3)
    ]


def feed(x, packed, s_u, s_v, cotangent, middle, alpha, collective):
    tokens, width = x.shape
    parts, _, _, units = packed.shape
    size = parts
    block = tokens // 2
    rows = pl.BlockSpec((block, width), lambda t, m: (1 - t, 0))
    vector = pl.BlockSpec((1, 1, units), lambda t, m: (m, 0, 0))
    piece = pl.BlockSpec((1, block, units), lambda t, m: (m, 1 - t, 0))
    vmem = pl.BlockSpec(memory_space=pltpu.VMEM)
    hidden = jax.ShapeDtypeStruct((parts, tokens, units), BF16)
    count = len(strips(block))
    low = pltpu.VMEM((block, width), BF16)
    return pl.pallas_call(
        functools.partial(feed_kernel, size),
        grid=(2, parts),
        in_specs=[rows, *packed_specs(packed, width), vector, vector, ANY, vmem, vmem],
        out_specs=[piece, piece, piece, vmem, vmem, ANY, vmem],
        out_shape=[
            hidden,
            hidden,
            hidden,
            jax.ShapeDtypeStruct((block, width), BF16),
            jax.ShapeDtypeStruct((block, width), F32),
            jax.ShapeDtypeStruct((tokens, width), BF16),
            jax.ShapeDtypeStruct((1, width), F32),
        ],
        scratch_shapes=[
            pltpu.VMEM((block, width), F32),
            low,
            low,
            low,
            low,
            *exchange_semaphores(size),
            *core_semaphores(1 + count),
            pltpu.SemaphoreType.DMA((count,)),
        ],
        compiler_params=remote_params(collective),
        cost_estimate=pl.CostEstimate(
            flops=6 * tokens * width * parts * units, bytes_accessed=60 << 20, transcendentals=0
        ),
        name="feed",
    )(x, packed, packed, packed, s_u, s_v, cotangent, middle, alpha)


def feed_back_kernel(
    size,
    dbranch,
    w_up,
    w_gate,
    w_down,
    s_u,
    s_v,
    up_in,
    gate_in,
    result,
    grad_middle_in,
    middle_in,
    resid_in,
    unit_in,
    branch_scale,
    mixed_scale,
    alpha,
    full_wo_in,
    dup_out,
    dgate_out,
    grad_u,
    grad_v,
    spread,
    grad_resid,
    dbranch_attn,
    dmerged,
    grad_alpha,
    acc,
    given,
    got,
    sum_u,
    sum_v,
    grad_middle,
    middle,
    resid,
    unit,
    full_wo,
    send,
    receive,
    local,
    core_sent,
    core_got,
    load_sems,
):
    loads = [
        pltpu.make_async_copy(there, here, load_sems.at[order])
        for order, (there, here) in enumerate(
            (
                (grad_middle_in, grad_middle),
                (middle_in, middle),
                (resid_in, resid),
                (unit_in, unit),
                (full_wo_in, full_wo),
            )
        )
    ]
    exchange = Exchange(
        size,
        result,
        spread,
        column_part(spread.shape[1]),
        row_part(result.shape[0]),
        send,
        receive,
        local,
    )
    dx_swap = swap_cores(given, got, (core_sent.at[0], core_got.at[0]))

    @pl.when(first_step())
    def _():
        for copy in loads:
            copy.start()
        greet_pair_and_line(size)
        exchange.start()

    block, part = pl.program_id(0), pl.program_id(1)
    dunits = dot(dbranch[...], whole_matrix(w_down))
    up = up_in[0].astype(F32)
    gate = gate_in[0].astype(F32)
    scaled = gate * s_v[0]
    sigmoid = 1.0 / (1.0 + jnp.exp(-scaled))
    silu = scaled * sigmoid
    slope = sigmoid * (1.0 + scaled - silu)
    through_up = dunits * silu
    through_gate = dunits * up * s_u[0] * slope
    dup = (through_up * s_u[0]).astype(BF16)
    dgate = (through_gate * s_v[0]).astype(BF16)
    dup_out[0] = dup
    dgate_out[0] = dgate
    term = dot(dup, whole_matrix(w_up), NT) + dot(dgate, whole_matrix(w_gate), NT)
    part_u = jnp.sum(through_up * up, axis=0, keepdims=True)
    part_v = jnp.sum(through_gate * gate, axis=0, keepdims=True)

    @pl.when(block == 0)
    def _():
        sum_u[part] = part_u
        sum_v[part] = part_v

    @pl.when(block > 0)
    def _():
        sum_u[part] += part_u
        sum_v[part] += part_v

    @pl.when(part == 0)
    def _():
        acc[...] = term

    @pl.when(part > 0)
    def _():
        acc[...] += term

    last = part == pl.num_programs(1) - 1

    @pl.when(last & (block == 0))
    def _():
        given[...] = acc[...].astype(BF16)
        dx_swap.start()

    @pl.when(last & (block == 1))
    def _():
        grad_u[...] = sum_u[...]
        grad_v[...] = sum_v[...]
        for copy in loads:
            copy.wait()
        dx_swap.wait()
        for order, at in enumerate(strips(acc.shape[0])):
            grad_old, grad_branch, part_alpha = residual_backward(
                grad_middle[at, :] + acc[at, :] + got[at, :].astype(F32),
                middle[at, :],
                resid[at, :].astype(F32),
                unit[at, :].astype(F32),
                alpha[...],
                branch_scale[at, :],
                mixed_scale[at, :],
            )
            grad_resid[at, :] = grad_old.astype(BF16)
            if order == 0:
                grad_alpha[...] = part_alpha
            else:
                grad_alpha[...] += part_alpha
            low = grad_branch.astype(BF16)
            dbranch_attn[at, :] = low
            columns = full_wo.shape[2]
            for member in range(size):
                dmerged[at, member * columns : (member + 1) * columns] = dot(
                    low, full_wo[member]
                ).astype(BF16)
        exchange.wait()


def feed_back(
    dbranch,
    packed,
    s_u,
    s_v,
    up,
    gate,
    result,
    grad_middle,
    middle,
    resid,
    unit,
    branch_scale,
    mixed_scale,
    alpha,
    full_wo,
    collective,
):
    tokens, width = dbranch.shape
    parts, _, _, units = packed.shape
    size = parts
    block = tokens // 2
    rows = pl.BlockSpec((block, width), lambda t, m: (1 - t, 0))
    vector = pl.BlockSpec((1, 1, units), lambda t, m: (m, 0, 0))
    piece = pl.BlockSpec((1, block, units), lambda t, m: (m, 1 - t, 0))
    vmem = pl.BlockSpec(memory_space=pltpu.VMEM)
    hidden = jax.ShapeDtypeStruct((parts, tokens, units), BF16)
    sums = jax.ShapeDtypeStruct((parts, 1, units), F32)
    state = jax.ShapeDtypeStruct((block, width), BF16)
    kept = (grad_middle, middle, resid, unit, full_wo)
    return pl.pallas_call(
        functools.partial(feed_back_kernel, size),
        grid=(2, parts),
        in_specs=[
            rows,
            *packed_specs(packed, width),
            vector,
            vector,
            piece,
            piece,
            ANY,
            *[ANY] * 4,
            *[vmem] * 3,
            ANY,
        ],
        out_specs=[piece, piece, vmem, vmem, ANY, vmem, vmem, vmem, vmem],
        out_shape=[
            hidden,
            hidden,
            sums,
            sums,
            jax.ShapeDtypeStruct((size * block, width // size), BF16),
            state,
            state,
            state,
            jax.ShapeDtypeStruct((1, width), F32),
        ],
        scratch_shapes=[
            pltpu.VMEM((block, width), F32),
            pltpu.VMEM((block, width), BF16),
            pltpu.VMEM((block, width), BF16),
            pltpu.VMEM((parts, 1, units), F32),
            pltpu.VMEM((parts, 1, units), F32),
            *[pltpu.VMEM(each.shape, each.dtype) for each in kept],
            *exchange_semaphores(size),
            *core_semaphores(1),
            pltpu.SemaphoreType.DMA((len(kept),)),
        ],
        compiler_params=remote_params(collective),
        cost_estimate=pl.CostEstimate(
            flops=6 * tokens * width * parts * units, bytes_accessed=70 << 20, transcendentals=0
        ),
        name="feed_back",
    )(
        dbranch,
        packed,
        packed,
        packed,
        s_u,
        s_v,
        up,
        gate,
        result,
        grad_middle,
        middle,
        resid,
        unit,
        branch_scale,
        mixed_scale,
        alpha,
        full_wo,
    )


def feed_grads_kernel(
    size,
    x,
    dbranch,
    dup,
    dgate,
    units,
    dbranch_attn,
    merged,
    dmerged,
    grads,
    grad_wo,
    dattended,
    x_turned,
    d_turned,
    attn_turned,
    send,
    receive,
    local,
):
    exchange = Exchange(
        size,
        dmerged,
        dattended,
        column_part(dattended.shape[1]),
        row_part(dmerged.shape[0]),
        send,
        receive,
        local,
    )

    @pl.when(first_step())
    def _():
        greet_all(size)
        exchange.start()
        x_turned[...] = x[...].T
        d_turned[...] = dbranch[...].T
        attn_turned[...] = dbranch_attn[...].T

    _, chips, rows, _ = grads.shape
    for which, left, right in (
        (0, x_turned, dup),
        (1, x_turned, dgate),
        (2, d_turned, units),
    ):

        @pl.when(pl.program_id(0) == which)
        def _():
            total = dot(left[...], right[0])
            grads[0] = total.astype(BF16).reshape(chips, rows, total.shape[1])

    @pl.when(pl.program_id(0) == 3)
    def _():
        total = dot(attn_turned[...], merged[...])
        grad_wo[...] = total.astype(BF16).reshape(grad_wo.shape)

    @pl.when(last_step())
    def _():
        exchange.wait()


def feed_grads(
    x, dbranch, dup, dgate, units_in, dbranch_attn, merged, dmerged, chips, collective
):
    tokens, width = x.shape
    parts, _, units = dup.shape
    size = parts
    rows = width // chips
    mine = dmerged.shape[0]
    part = width // size

    def whole(array):
        return pl.BlockSpec(array.shape, lambda w, m: (0, 0))

    def turn(w, m, which):
        return jnp.where(w == which, m, jnp.where(w < which, 0, parts - 1))

    def piece(which):
        return pl.BlockSpec((1, tokens, units), lambda w, m: (turn(w, m, which), 0, 0))

    return pl.pallas_call(
        functools.partial(feed_grads_kernel, size),
        grid=(4, parts),
        in_specs=[
            whole(x),
            whole(dbranch),
            piece(0),
            piece(1),
            piece(2),
            whole(dbranch_attn),
            pl.BlockSpec((mine, part), lambda w, m: (0, turn(w, m, 3))),
            ANY,
        ],
        out_specs=[
            pl.BlockSpec(
                (1, chips, rows, units),
                lambda w, m: (jnp.where(w < 3, m, parts - 1), 0, jnp.minimum(w, 2), 0),
            ),
            pl.BlockSpec(
                (1, chips, 2, rows // 2, part), lambda w, m: (turn(w, m, 3), 0, 0, 0, 0)
            ),
            ANY,
        ],
        out_shape=[
            jax.ShapeDtypeStruct((parts, chips, 3 * rows, units), BF16),
            jax.ShapeDtypeStruct((parts, chips, 2, rows // 2, part), BF16),
            jax.ShapeDtypeStruct((size * mine, part), BF16),
        ],
        scratch_shapes=[
            pltpu.VMEM((width, tokens), BF16),
            pltpu.VMEM((width, tokens), BF16),
            pltpu.VMEM((width, mine), BF16),
            *exchange_semaphores(size),
        ],
        compiler_params=remote_params(collective),
        cost_estimate=pl.CostEstimate(
            flops=6 * tokens * width * parts * units, bytes_accessed=40 << 20, transcendentals=0
        ),
        name="feed_grads",
    )(x, dbranch, dup, dgate, units_in, dbranch_attn, merged, dmerged)


def document_starts(doc_ids):
    slot_index = jnp.arange(doc_ids.shape[-1], dtype=jnp.int32)
    earlier = jnp.concatenate([doc_ids[..., :1] - 1, doc_ids[..., :-1]], axis=-1)
    starts = jnp.where(doc_ids != earlier, slot_index, jnp.zeros_like(slot_index))
    return lax.cummax(starts, axis=starts.ndim - 1)


def make_on_device(chips, size):
    def on_device(
        hidden,
        wq,
        wk,
        wv,
        wo,
        w_up,
        w_gate,
        w_down,
        s_qk,
        s_u,
        s_v,
        alpha_a,
        alpha_m,
        doc_ids,
        valid,
        cotangent,
    ):
        _, slots, part = hidden.shape
        width = part * size
        heads = s_qk.shape[0] // DK
        rows = wq.shape[0]
        units = w_up.shape[1] // 2
        mine = slots // size
        block = min(512, slots)
        me = lax.axis_index("mp")
        core = lax.axis_index("core")

        place = paired_place(heads)
        to_pair = placing_matrix(place, heads)
        to_plain = placing_matrix(np.arange(heads * DK), heads)
        turn = np.zeros((part, part), np.float32)
        turn[np.arange(part), place] = 1
        place_pair = jnp.asarray(to_pair, BF16)
        place_plain = jnp.asarray(to_plain, BF16)
        place_delta = jnp.asarray(delta_matrix(heads), BF16)
        collect_plain = jnp.asarray(to_plain.T.reshape(heads, EXT, heads * DK), BF16)
        sums = jnp.asarray(head_sum_matrix(heads), BF16)
        gain = s_qk.reshape(heads, 2, HALF).transpose(1, 0, 2).reshape(1, part)
        docs = doc_ids[0]
        starts = document_starts(docs)
        slot = jnp.arange(slots, dtype=jnp.int32)
        low = jnp.concatenate([starts[::block] // block, me[None]])
        key_docs = jnp.where(valid[0] == 1, docs, -1)
        columns = jnp.stack([slot - starts, docs, key_docs], axis=1).astype(F32)
        inverse = jnp.exp(
            jnp.arange(HALF, dtype=F32) * (-2.0 * math.log(ROPE_BASE) / DK)
        )

        vectors = jnp.concatenate([s_u, s_v * math.sqrt(width), alpha_a, alpha_m])
        (
            wide,
            full_qkv,
            packed,
            vectors,
            q,
            k,
            v,
            q_pair,
            k_pair,
            rq,
            rk,
            cosine,
            sine,
        ) = front(
            hidden[0],
            (wq, wk, wv, wo, w_up, w_gate, w_down),
            vectors[None],
            columns,
            jnp.tile(inverse, heads)[None],
            gain,
            jnp.asarray(turn, BF16),
            place_pair,
            place_plain,
            sums,
            size,
            chips,
            0,
        )
        full_qkv = full_qkv.reshape(size, part, 3 * part)
        vectors = vectors[:, 0]
        s_up = lax.dynamic_slice_in_dim(vectors[:, : 2 * units], core * units, units, 1)
        s_gate = lax.dynamic_slice_in_dim(
            vectors[:, 2 * units : 4 * units], core * units, units, 1
        )
        s_up = s_up[:, None, :]
        s_gate = s_gate[:, None, :]
        alpha_attn = vectors[:, 4 * units : 4 * units + part].reshape(1, width)
        alpha_mlp = vectors[:, 4 * units + part :].reshape(1, width)

        attended, qback = attend(
            low,
            q,
            k,
            v,
            columns,
            key_docs.astype(F32).reshape(slots // block, 1, block),
            collect_plain,
        )
        (
            x,
            middle,
            unit,
            merged,
            full_wo,
            resid,
            cotangent_low,
            branch_scale,
            mixed_scale,
        ) = mix(attended, packed, rows, wide, alpha_attn, cotangent[0], 1)

        up, gate, hidden_units, result, grad_middle, dbranch, grad_alpha_mlp = feed(
            x, packed, s_up, s_gate, cotangent_low, middle, alpha_mlp, 2
        )
        (
            dup,
            dgate,
            grad_u,
            grad_v,
            out_low,
            grad_resid,
            dbranch_attn,
            dmerged,
            grad_alpha_attn,
        ) = feed_back(
            dbranch,
            packed,
            s_up,
            s_gate,
            up,
            gate,
            result,
            grad_middle,
            middle,
            resid,
            unit,
            branch_scale,
            mixed_scale,
            alpha_attn,
            full_wo,
            3,
        )
        out_hidden = out_low.astype(F32)
        grads, grad_wo, dattended = feed_grads(
            x, dbranch, dup, dgate, hidden_units, dbranch_attn, merged, dmerged, chips, 4
        )

        term, grad_qkv, grad_gain = attend_back(
            low,
            qback,
            q_pair,
            dattended,
            attended,
            k,
            k_pair,
            v,
            docs.astype(F32).reshape(slots // block, 1, block),
            columns,
            cosine,
            sine,
            rq,
            rk,
            gain,
            full_qkv,
            place_plain,
            place_delta,
            sums,
            wide,
            grad_resid,
        )
        (
            grad_hidden,
            owned_upward,
            owned_gating,
            owned_downward,
            owned_output,
            owned_query,
            owned_keys,
            owned_values,
            summed,
        ) = sum_all(
            term,
            grads,
            grad_wo,
            grad_qkv.reshape(chips, 2, rows, 3 * part),
            (grad_u, grad_v, grad_gain, grad_alpha_attn, grad_alpha_mlp),
            jnp.asarray(turn.T, BF16),
            chips,
            5,
        )
        bounds = [2 * units, 4 * units, 4 * units + part, 4 * units + 2 * part]
        summed_up, summed_gate, summed_qk, summed_attn, summed_mlp = jnp.split(
            summed[0], bounds
        )
        return (
            out_hidden[None],
            grad_hidden[None],
            owned_query,
            owned_keys,
            owned_values,
            owned_output,
            owned_upward,
            owned_gating,
            owned_downward,
            summed_qk,
            summed_up,
            summed_gate,
            summed_attn,
            summed_mlp,
        )

    return on_device


def solution(mesh):
    rows, size = mesh.shape["dp"], mesh.shape["mp"]
    paired = Mesh(mesh.devices.reshape(rows // 2, 2, size), ("chip", "core", "mp"))
    return jax.shard_map(
        make_on_device(rows // 2, size),
        mesh=paired,
        in_specs=(
            P(DP, None, "mp"),
            P(DP, "mp"),
            P(DP, "mp"),
            P(DP, "mp"),
            P("mp", DP),
            P(DP, "mp"),
            P(DP, "mp"),
            P("mp", DP),
            P("mp"),
            P("mp"),
            P("mp"),
            P("mp"),
            P("mp"),
            P(DP, None),
            P(DP, None),
            P(DP, None, "mp"),
        ),
        out_specs=(
            P(DP, None, "mp"),
            P(DP, None, "mp"),
            P(DP, "mp"),
            P(DP, "mp"),
            P(DP, "mp"),
            P("mp", DP),
            P(DP, "mp"),
            P(DP, "mp"),
            P("mp", DP),
            P("mp"),
            P("mp"),
            P("mp"),
            P("mp"),
            P("mp"),
        ),
        check_vma=False,
    )
```

```python
import functools
import math

import jax
import jax.numpy as jnp
import numpy as np
from jax import lax
from jax.experimental import pallas as pl
from jax.experimental.pallas import tpu as pltpu
from jax.sharding import Mesh
from jax.sharding import PartitionSpec as P

DK = 64
HALF = DK // 2
EXT = 128
EPSILON = 1e-06
ROPE_BASE = 10000.0
VMEM_LIMIT = 60 * 1024 * 1024
F32 = jnp.float32
BF16 = jnp.bfloat16
DP = ("chip", "core")


def dot(left, right, dims=((1,), (0,)), precision=None):
    return lax.dot_general(
        left, right, (dims, ((), ())), precision=precision, preferred_element_type=F32
    )


NT = ((1,), (1,))
TN = ((0,), (0,))


def grid_params(dims):
    return pltpu.CompilerParams(
        dimension_semantics=("arbitrary",) * dims, vmem_limit_bytes=VMEM_LIMIT
    )


ANY = pl.BlockSpec(memory_space=pl.ANY)


def remote_params(collective, **more):
    return pltpu.CompilerParams(
        collective_id=collective,
        has_side_effects=True,
        vmem_limit_bytes=VMEM_LIMIT,
        **more,
    )


def to_device(source, target, send, receive, where):
    return pltpu.make_async_remote_copy(
        src_ref=source,
        dst_ref=target,
        send_sem=send,
        recv_sem=receive,
        device_id=where,
        device_id_type=pl.DeviceIdType.MESH,
    )


def to_member(source, target, send, receive, member):
    return to_device(source, target, send, receive, {"mp": member})


def flip(index, mask):
    bit = 1
    while bit <= mask:
        if mask & bit:
            index = index + bit - 2 * bit * lax.rem(lax.div(index, bit), 2)
        bit *= 2
    return index


def bits_below(count):
    return [1 << k for k in range(count.bit_length() - 1)]


def greet(where):
    pl.semaphore_signal(
        pltpu.get_barrier_semaphore(),
        inc=1,
        device_id=where,
        device_id_type=pl.DeviceIdType.MESH,
    )


def greet_all(size):
    me = lax.axis_index("mp")
    for k in range(1, size):
        greet({"mp": flip(me, k)})
    pl.semaphore_wait(pltpu.get_barrier_semaphore(), size - 1)


def greet_around(size, chips):
    me, chip, core = (lax.axis_index(name) for name in ("mp", "chip", "core"))
    for k in range(1, size):
        greet({"mp": flip(me, k)})
    for bit in bits_below(chips):
        greet({"chip": flip(chip, bit)})
    greet({"core": 1 - core})
    pl.semaphore_wait(pltpu.get_barrier_semaphore(), size + len(bits_below(chips)))


class Exchange:
    def __init__(self, size, source, target, piece, place, send, receive, local):
        me = lax.axis_index("mp")
        self.local = pltpu.make_async_copy(piece(source, me), place(target, me), local)
        self.remote = [
            to_member(
                piece(source, flip(me, k)),
                place(target, me),
                send.at[k],
                receive.at[k],
                flip(me, k),
            )
            for k in range(1, size)
        ]

    def start(self):
        for copy in self.remote:
            copy.start()
        self.local.start()

    def wait(self):
        self.local.wait()
        for copy in self.remote:
            copy.wait()


def exchange_semaphores(size):
    return [
        pltpu.SemaphoreType.DMA((size,)),
        pltpu.SemaphoreType.DMA((size,)),
        pltpu.SemaphoreType.DMA,
    ]


def row_part(rows):
    return lambda ref, j: ref.at[pl.ds(pl.multiple_of(j * rows, rows), rows), :]


def column_part(columns):
    return lambda ref, j: ref.at[:, pl.ds(pl.multiple_of(j * columns, columns), columns)]


class Gather:
    def __init__(self, block, index, bits, where, send, receive):
        self.block, self.index, self.bits, self.where = block, index, bits, where
        self.send, self.receive = send, receive

    def copies(self, stage, incoming):
        span = [0]
        for bit in self.bits[:stage]:
            span += [held | bit for held in span]
        bit = self.bits[stage]
        for order, held in enumerate(span):
            ref = self.block(flip(self.index, held | bit if incoming else held))
            slot = (1 << stage) - 1 + order
            yield to_device(
                ref,
                ref,
                self.send(slot),
                self.receive(slot),
                self.where(flip(self.index, bit)),
            )

    def start(self, stage):
        if stage < len(self.bits):
            for copy in self.copies(stage, False):
                copy.start()

    def arrive(self, stage):
        if stage < len(self.bits):
            for copy in self.copies(stage, True):
                copy.wait_recv()

    def close(self):
        for stage in range(len(self.bits)):
            for copy in self.copies(stage, False):
                copy.wait_send()


EARLY = 2


def front_kernel(
    size,
    chips,
    chunks,
    split,
    hidden_in,
    wq,
    wk,
    wv,
    wo,
    w_up,
    w_gate,
    w_down,
    vectors,
    columns,
    frequency,
    gain,
    in_pairs,
    place_pair,
    place_plain,
    sums,
    wide_out,
    qkv_out,
    full,
    full_vectors,
    q_out,
    k_out,
    v_out,
    q_pair_out,
    k_pair_out,
    rq_out,
    rk_out,
    cosine_out,
    sine_out,
    hidden,
    wide,
    full_qkv,
    packed,
    matrices,
    wo_turned,
    q,
    k,
    v,
    q_pair,
    k_pair,
    rq,
    rk,
    cosine,
    sine,
    local,
    out_sems,
    core_sent,
    core_got,
    hidden_up,
    hidden_down,
    hidden_got,
    packed_up,
    packed_down,
    packed_got,
    plane_sent,
    plane_got,
    qkv_sent,
    qkv_got,
    vector_sent,
    vector_got,
    load_sems,
):
    me, chip, core = (lax.axis_index(name) for name in ("mp", "chip", "core"))
    tokens, part = hidden_in.shape
    rows = tokens // chunks
    hidden_loads = [
        pltpu.make_async_copy(
            hidden_in.at[pl.ds(chunk * rows, rows), :],
            hidden.at[pl.ds(chunk * rows, rows), :],
            load_sems.at[chunk],
        )
        for chunk in range(chunks)
    ]
    for copy in hidden_loads:
        copy.start()
    height, units = packed.shape
    lines = height // 7
    owner = chip * 2 + core
    bits = bits_below(chips)
    stages = len(bits)
    greet_around(size, chips)

    def hidden_hop(origin, chunk, member, send):
        at = pl.ds(pl.multiple_of(chunk * rows, rows), rows)
        ref = wide.at[origin, at, :]
        return to_member(ref, ref, send.at[origin, chunk], hidden_got.at[origin, chunk], member)

    def send_hidden(chunk):
        @pl.when(me < size - 1)
        def _():
            hidden_hop(me, chunk, me + 1, hidden_up).start()

        @pl.when(me > 0)
        def _():
            hidden_hop(me, chunk, me - 1, hidden_down).start()

    for chunk in range(EARLY):
        at = pl.ds(chunk * rows, rows)
        hidden_loads[chunk].wait()
        wide[me, at, :] = hidden[at, :].astype(BF16)
        send_hidden(chunk)

    matrices[0] = w_up[...].astype(BF16)
    matrices[1] = w_gate[...].astype(BF16)
    matrices[2] = w_down[...].T.astype(BF16)
    wo_turned[...] = wo[...].T.astype(BF16)

    def half_of(which):
        return pl.ds(pl.multiple_of(which * units, units), units)

    def place_of(matrix):
        return pl.ds(pl.multiple_of((2 * matrix + core) * lines, lines), lines)

    wo_place = (
        pl.ds(6 * lines, lines),
        pl.ds(pl.multiple_of(core * part, part), part),
    )
    given = [
        to_device(
            matrices.at[matrix, :, half_of(1 - core)],
            packed.at[place_of(matrix), :],
            core_sent.at[matrix],
            core_got.at[matrix],
            {"core": 1 - core},
        )
        for matrix in range(3)
    ]
    given.append(
        to_device(
            wo_turned, packed.at[wo_place], core_sent.at[3], core_got.at[3], {"core": 1 - core}
        )
    )
    for copy in given:
        copy.start()
    for matrix in range(3):
        packed[place_of(matrix), :] = matrices[matrix, :, half_of(core)]
    packed[wo_place] = wo_turned[...]
    full_qkv[owner] = jnp.concatenate(
        [
            dot(wq[...].astype(BF16), in_pairs[...]).astype(BF16),
            dot(wk[...].astype(BF16), in_pairs[...]).astype(BF16),
            wv[...].astype(BF16),
        ],
        axis=1,
    )

    def packed_hop(origin, ref, member, send):
        return to_member(
            ref, full.at[origin, chip], send.at[origin], packed_got.at[origin], member
        )

    vector_copies = [
        to_member(
            vectors, full_vectors.at[me], vector_sent.at[k], vector_got.at[k], flip(me, k)
        )
        for k in range(1, size)
    ]

    def plane(origin, slot):
        return [
            Gather(
                lambda i, at=at: full.at[origin, i, at, :],
                chip,
                order,
                lambda i: {"chip": i},
                lambda k, half=half: plane_sent.at[slot, half, k],
                lambda k, half=half: plane_got.at[slot, half, k],
            )
            for half, (at, order) in enumerate(
                (
                    (pl.ds(0, split), bits),
                    (pl.ds(split, height - split), bits[::-1]),
                )
            )
        ]

    gather_qkv = Gather(
        lambda i: full_qkv.at[i],
        owner,
        [2 * bit for bit in bits] + [1],
        lambda i: {"chip": lax.div(i, 2), "core": lax.rem(i, 2)},
        lambda k: qkv_sent.at[k],
        lambda k: qkv_got.at[k],
    )

    sources = {0: [(me >= 0, me, 0, None)]}
    for distance in range(1, size):
        sources[distance] = [
            (me >= distance, me - distance, 2 * distance - 1, True),
            (me + distance < size, me + distance, 2 * distance, False),
        ]

    def pass_on(origin, ref, upward):
        if upward is not False:

            @pl.when(me < size - 1)
            def _():
                packed_hop(origin, ref, me + 1, packed_up).start()

        if not upward:

            @pl.when(me > 0)
            def _():
                packed_hop(origin, ref, me - 1, packed_down).start()

    def advance(distance, stage):
        for exists, origin, slot, _ in sources[distance]:

            @pl.when(exists)
            def _():
                for half in plane(origin, slot):
                    half.arrive(stage)
                    half.start(stage + 1)

    for copy in given:
        copy.wait_recv()
    pass_on(me, packed, None)
    own = [
        pltpu.make_async_copy(packed, full.at[me, chip], local.at[0]),
        pltpu.make_async_copy(vectors, full_vectors.at[me], local.at[1]),
    ]
    for copy in own:
        copy.start()
    gather_qkv.start(0)
    for copy in vector_copies:
        copy.start()
    for chunk in range(EARLY, chunks):
        at = pl.ds(chunk * rows, rows)
        hidden_loads[chunk].wait()
        wide[me, at, :] = hidden[at, :].astype(BF16)
    own[0].wait()
    for half in plane(me, 0):
        half.start(0)
    for chunk in range(chunks):
        at = pl.ds(chunk * rows, rows)
        angles = columns[at, 0:1] * frequency[...]
        cosine[at, :] = jnp.cos(angles)
        sine[at, :] = jnp.sin(angles)
    for stage in range(stages):
        gather_qkv.arrive(stage)
        gather_qkv.start(stage + 1)
    advance(0, 0)
    for distance in range(1, size):
        for exists, origin, slot, upward in sources[distance]:

            @pl.when(exists)
            def _():
                block = full.at[origin, chip]
                packed_hop(origin, block, me, packed_up).wait_recv()
                pass_on(origin, block, upward)
                for half in plane(origin, slot):
                    half.start(0)

        @pl.when(jnp.maximum(me, size - 1 - me) == distance)
        def _():
            for chunk in range(EARLY, chunks):
                send_hidden(chunk)

        if distance > 1:
            advance(distance - 1, 0)
    gather_qkv.arrive(stages)
    qkv_copy = pltpu.make_async_copy(full_qkv, qkv_out, local.at[2])
    qkv_copy.start()
    advance(size - 1, 0)

    def come(distance, chunk):
        for exists, origin, _, upward in sources[distance]:

            @pl.when(exists)
            def _():
                hidden_hop(origin, chunk, me, hidden_up).wait_recv()
                if upward:

                    @pl.when(me < size - 1)
                    def _():
                        hidden_hop(origin, chunk, me + 1, hidden_up).start()
                else:

                    @pl.when(me > 0)
                    def _():
                        hidden_hop(origin, chunk, me - 1, hidden_down).start()

    for distance in range(1, size - 1):
        for chunk in range(chunks):
            come(distance, chunk)

    results = (
        (q, q_out),
        (k, k_out),
        (v, v_out),
        (q_pair, q_pair_out),
        (k_pair, k_pair_out),
        (rq, rq_out),
        (rk, rk_out),
        (cosine, cosine_out),
        (sine, sine_out),
        (wide, wide_out),
    )

    def write_out(chunk):
        at = pl.ds(pl.multiple_of(chunk * rows, rows), rows)
        for order, (here, there) in enumerate(results):
            lead = (slice(None),) * (len(here.shape) - 2)
            yield pltpu.make_async_copy(
                here.at[(*lead, at)], there.at[(*lead, at)], out_sems.at[order, chunk]
            )

    each = part // lines

    def finish(chunk, carry):
        come(size - 1, chunk)
        at = pl.ds(pl.multiple_of(chunk * rows, rows), rows)
        project_block(
            [wide[member, at, :] for member in range(size)],
            [
                full_qkv[member * each : (member + 1) * each].reshape(part, 3 * part)
                for member in range(size)
            ],
            cosine[at, :],
            sine[at, :],
            gain[...],
            place_pair[...],
            place_plain[...],
            sums[...],
            at,
            [here for here, _ in results[:7]],
        )
        for copy in write_out(chunk):
            copy.start()
        return carry

    lax.fori_loop(0, chunks, finish, 0)
    for stage in range(1, stages):
        for distance in range(size):
            advance(distance, stage)

    own[1].wait()
    qkv_copy.wait()
    for copy in vector_copies:
        copy.wait()
    for copy in given:
        copy.wait_send()
    for chunk in range(chunks):
        for copy in write_out(chunk):
            copy.wait()
    gather_qkv.close()
    for distance in range(size):
        for exists, origin, slot, upward in sources[distance]:

            @pl.when(exists)
            def _():
                for half in plane(origin, slot):
                    half.close()
                block = packed if distance == 0 else full.at[origin, chip]
                if upward is not False:

                    @pl.when(me < size - 1)
                    def _():
                        packed_hop(origin, block, me, packed_up).wait_send()
                        for chunk in range(chunks):
                            hidden_hop(origin, chunk, me, hidden_up).wait_send()

                if not upward:

                    @pl.when(me > 0)
                    def _():
                        packed_hop(origin, block, me, packed_down).wait_send()
                        for chunk in range(chunks):
                            hidden_hop(origin, chunk, me, hidden_down).wait_send()


def front(
    hidden,
    weights,
    vectors,
    positions,
    frequency,
    gain,
    in_pairs,
    place_pair,
    place_plain,
    sums,
    size,
    chips,
    collective,
):
    chunks = 6
    tokens, part = hidden.shape
    lines, both = weights[4].shape
    units = both // 2
    heads = part // DK
    height = 7 * lines
    dma = pltpu.SemaphoreType.DMA
    line = dma((size, chunks))
    plane = dma((2 * size - 1, 2, max(chips - 1, 1)))
    vmem = pl.BlockSpec(memory_space=pltpu.VMEM)
    padded = ((heads, tokens, EXT), BF16)
    paired = ((tokens, part), BF16)
    scale = ((tokens, heads * HALF), F32)
    wide = ((size, tokens, part), BF16)
    qkv = ((2 * chips, lines, 3 * part), BF16)
    results = [padded, padded, padded, paired, paired, scale, scale, scale, scale]
    return pl.pallas_call(
        functools.partial(front_kernel, size, chips, chunks, height // 32 * 16),
        in_specs=[ANY, *[vmem] * 15],
        out_specs=[ANY] * 13,
        out_shape=[
            jax.ShapeDtypeStruct(*each)
            for each in [
                wide,
                qkv,
                ((size, chips, height, units), BF16),
                ((size, *vectors.shape), F32),
                *results,
            ]
        ],
        scratch_shapes=[
            pltpu.VMEM((tokens, part), F32),
            pltpu.VMEM(*wide),
            pltpu.VMEM(*qkv),
            pltpu.VMEM((height, units), BF16),
            pltpu.VMEM((3, lines, both), BF16),
            pltpu.VMEM((lines, part), BF16),
            *[pltpu.VMEM(*each) for each in results],
            dma((3,)),
            dma((10, chunks)),
            dma((4,)),
            dma((4,)),
            line,
            line,
            line,
            dma((size,)),
            dma((size,)),
            dma((size,)),
            plane,
            plane,
            dma((2 * chips - 1,)),
            dma((2 * chips - 1,)),
            dma((size,)),
            dma((size,)),
            dma((chunks,)),
        ],
        compiler_params=remote_params(collective),
        name="front",
    )(
        hidden,
        *weights,
        vectors,
        positions,
        frequency,
        gain,
        in_pairs,
        place_pair,
        place_plain,
        sums,
    )


class LineSum:
    def __init__(self, size, chunks, term, up, down, sems):
        self.size, self.chunks = size, chunks
        self.term, self.up, self.down = term, up, down
        self.sent_up, self.sent_down, self.got_up, self.got_down = sems
        self.me = lax.axis_index("mp")
        self.rows = up.shape[1] // chunks

    def at(self, chunk):
        return pl.ds(chunk * self.rows, self.rows)

    def hop(self, upward, goal, chunk, member):
        slots = self.up if upward else self.down
        send = self.sent_up if upward else self.sent_down
        receive = self.got_up if upward else self.got_down
        ref = slots.at[goal, self.at(chunk), :]
        return to_member(ref, ref, send.at[goal, chunk], receive.at[goal, chunk], member)

    def step(self, order, chunk):
        me, last, at = self.me, self.size - 1, self.at(chunk)
        for upward, goal, ahead, first, member in (
            (True, last - order, me < last - order, me == 0, me + 1),
            (False, order, me > order, me == last, me - 1),
        ):
            slots = self.up if upward else self.down

            @pl.when(ahead & first)
            def _():
                slots[goal, at, :] = self.term(goal, at)

            @pl.when(ahead & jnp.logical_not(first))
            def _():
                self.hop(upward, goal, chunk, me).wait_recv()
                slots[goal, at, :] = (
                    slots[goal, at, :].astype(F32) + self.term(goal, at).astype(F32)
                ).astype(BF16)

            if order > 0:
                older = goal + 1 if upward else goal - 1
                sent = (me < older) if upward else (me > older)

                @pl.when(sent)
                def _():
                    self.hop(upward, older, chunk, member).wait_send()

            @pl.when(ahead)
            def _():
                self.hop(upward, goal, chunk, member).start()

    def result(self, chunk, out, out_at):
        me, at = self.me, self.at(chunk)
        out[out_at, :] = self.term(me, at).astype(F32)

        @pl.when(me > 0)
        def _():
            self.hop(True, me, chunk, me).wait_recv()
            out[out_at, :] += self.up[me, at, :].astype(F32)

        @pl.when(me < self.size - 1)
        def _():
            self.hop(False, me, chunk, me).wait_recv()
            out[out_at, :] += self.down[me, at, :].astype(F32)

    def close(self):
        order = self.size - 2
        for chunk in range(self.chunks):

            @pl.when(self.me < self.size - 1 - order)
            def _():
                self.hop(True, self.size - 1 - order, chunk, self.me).wait_send()

            @pl.when(self.me > order)
            def _():
                self.hop(False, order, chunk, self.me).wait_send()


MIDDLE, LATE = 4, 5


class ChipSum:
    def __init__(self, layers, bits, source, acc, got, load, send, receive):
        self.layers, self.bits = layers, bits
        self.acc, self.got, self.chip = acc, got, lax.axis_index("chip")
        self.half = 1 << (len(bits) - 1)
        self.load = [
            pltpu.make_async_copy(
                source(layer, flip(self.chip, self.combo(slot))),
                acc.at[layer, slot],
                load.at[layer, slot],
            )
            for layer in layers
            for slot in range(self.half)
        ]
        self.source, self.sent, self.received = source, send, receive

    def combo(self, slot):
        count = len(self.bits)
        return sum(self.bits[count - 1 - j] for j in range(count - 1) if slot >> j & 1)

    def copies(self, stage):
        count = self.half >> stage
        offset = 2 * self.half - 2 * count
        where = {"chip": flip(self.chip, self.bits[stage])}
        for layer in self.layers:
            for slot in range(count):
                if stage == 0:
                    other = flip(self.chip, self.bits[0] | self.combo(slot))
                    ref = self.source(layer, other)
                else:
                    ref = self.acc.at[layer, count + slot]
                at = offset + slot
                yield layer, slot, at, to_device(
                    ref,
                    self.got.at[layer, at],
                    self.sent.at[layer, at],
                    self.received.at[layer, at],
                    where,
                )

    def start(self, stage):
        if stage == 0:
            for copy in self.load:
                copy.start()
        for _, _, _, copy in self.copies(stage):
            copy.start()

    def add(self, stage):
        if stage == 0:
            for copy in self.load:
                copy.wait()
        for layer, slot, at, copy in self.copies(stage):
            copy.wait_recv()
            self.acc[layer, slot] = (
                self.acc[layer, slot].astype(F32) + self.got[layer, at].astype(F32)
            ).astype(BF16)

    def close(self):
        for stage in range(len(self.bits)):
            for _, _, _, copy in self.copies(stage):
                copy.wait_send()


def sum_all_kernel(
    size,
    chips,
    chunks,
    split,
    term_in,
    grads,
    grad_wo,
    grad_qkv,
    grad_u,
    grad_v,
    grad_gain,
    grad_alpha_a,
    grad_alpha_m,
    out_pairs,
    out_there,
    owned_up,
    owned_gate,
    owned_down,
    owned_wo,
    owned_q,
    owned_k,
    owned_v,
    owned_vectors,
    term,
    out,
    vectors,
    term_up,
    term_down,
    acc_a,
    got_a,
    up_a,
    down_a,
    acc_b,
    got_b,
    up_b,
    down_b,
    pair_wo,
    other_wo,
    acc_wo,
    got_wo,
    up_wo,
    down_wo,
    pair_qkv,
    other_qkv,
    acc_qkv,
    got_qkv,
    whole,
    owned,
    turned_wo,
    vector_sum,
    vector_got,
    vector_line,
    local,
    core_sent,
    core_got,
    vector_sent,
    vector_received,
    term_sems,
    line_sems,
    load_sems,
    chip_sent,
    chip_got,
):
    me, chip, core = (lax.axis_index(name) for name in ("mp", "chip", "core"))
    bits = bits_below(chips)
    stages = len(bits)
    greet_around(size, chips)
    other_core_is = {"core": 1 - core}

    def sems(ref, which):
        return [ref.at[which, k] for k in range(4)]

    term_loads = [
        pltpu.make_async_copy(term_in.at[goal], term.at[goal], local.at[5 + goal])
        for goal in range(size)
    ]
    line = LineSum(
        size, chunks, lambda goal, at: term[goal, at, :], term_up, term_down, sems(term_sems, 0)
    )
    ends = sorted({0, size - 1})
    inner = [layer for layer in range(size) if layer not in ends]

    def plane_sums(layers):
        return [
            ChipSum(
                layers,
                bits,
                lambda m, c: grads.at[m, c, pl.ds(0, split), :],
                acc_a,
                got_a,
                load_sems.at[0],
                chip_sent.at[0],
                chip_got.at[0],
            ),
            ChipSum(
                layers,
                bits[::-1],
                lambda m, c: grads.at[m, c, pl.ds(split, grads.shape[2] - split), :],
                acc_b,
                got_b,
                load_sems.at[1],
                chip_sent.at[1],
                chip_got.at[1],
            ),
        ]

    sums_ends, sums_inner = plane_sums(ends), plane_sums(inner)
    sum_wo = ChipSum(
        range(size),
        bits[::-1],
        lambda m, c: pair_wo.at[m, c],
        acc_wo,
        got_wo,
        load_sems.at[2],
        chip_sent.at[2],
        chip_got.at[2],
    )
    sum_qkv = ChipSum(
        range(1),
        bits,
        lambda m, c: pair_qkv.at[c],
        acc_qkv,
        got_qkv,
        load_sems.at[3],
        chip_sent.at[3],
        chip_got.at[3],
    )
    lines = [
        LineSum(
            size,
            1,
            lambda goal, at, acc=acc: acc[goal, 0, at, :],
            up,
            down,
            sems(line_sems, which),
        )
        for which, (acc, up, down) in enumerate(
            ((acc_a, up_a, down_a), (acc_b, up_b, down_b), (acc_wo, up_wo, down_wo))
        )
    ]

    own = [
        pltpu.make_async_copy(grad_wo.at[:, :, core], pair_wo, local.at[0]),
        pltpu.make_async_copy(grad_qkv.at[:, core], pair_qkv, local.at[1]),
    ]
    given = [
        to_device(
            grad_wo.at[:, :, 1 - core], other_wo, core_sent.at[0], core_got.at[0], other_core_is
        ),
        to_device(
            grad_qkv.at[:, 1 - core], other_qkv, core_sent.at[1], core_got.at[1], other_core_is
        ),
    ]
    vector_copies = [
        to_member(
            vectors.at[flip(me, k)],
            vector_line.at[k],
            vector_sent.at[k],
            vector_received.at[k],
            flip(me, k),
        )
        for k in range(1, size)
    ]
    for copy in own + given:
        copy.start()
    for part in sums_ends:
        part.start(0)
    for copy in term_loads:
        copy.start()

    units = grad_u.shape[2]
    columns = out_pairs.shape[0]
    at_gain = 4 * units
    vectors[...] = jnp.zeros_like(vectors)
    for member in range(size):
        half = pl.multiple_of(core * units, units)
        vectors[member, :, pl.ds(half, units)] = grad_u[member]
        vectors[member, :, pl.ds(2 * units + half, units)] = grad_v[member] * math.sqrt(
            size * columns
        )
        these = slice(member * columns, (member + 1) * columns)
        vectors[member, :, at_gain + columns : at_gain + 2 * columns] = grad_alpha_a[:, these]
        vectors[member, :, at_gain + 2 * columns :] = grad_alpha_m[:, these]
    vectors[me, :, at_gain : at_gain + columns] = split_dot(grad_gain[...], out_pairs[...])
    for copy in vector_copies:
        copy.start()
    for copy in term_loads:
        copy.wait()

    owner = chip * 2 + core
    vector_bits = [1] + [2 * bit for bit in bits]

    def vector_copy(stage):
        partner = flip(owner, vector_bits[stage])
        return to_device(
            vector_sum.at[stage],
            vector_got.at[stage],
            vector_sent.at[size + stage],
            vector_received.at[size + stage],
            {"chip": lax.div(partner, 2), "core": lax.rem(partner, 2)},
        )

    def vector_step(stage):
        if stage == 0:
            total = vectors[me]
            for k, copy in enumerate(vector_copies):
                copy.wait_recv()
                total = total + vector_line[k + 1]
            vector_sum[0] = total
        else:
            vector_copy(stage - 1).wait_recv()
            vector_sum[stage] = vector_sum[stage - 1] + vector_got[stage - 1]
        if stage < len(vector_bits):
            vector_copy(stage).start()

    def add(group, stage):
        for part in group:
            part.add(stage)
            if stage + 1 < stages:
                part.start(stage + 1)

    small = [sum_wo, sum_qkv]
    rest = [*sums_inner, *small]
    vector_at = 0
    for order in range(size - 1):
        for chunk in range(chunks):
            line.step(order, chunk)
            if order == 0 and chunk >= 1 and vector_at <= len(vector_bits):
                vector_step(vector_at)
                vector_at += 1
            if order == 1 and chunk == MIDDLE:
                for stage in range(1, stages):
                    add(sums_ends, stage)
                for part in rest:
                    part.start(0)
            if order == 2 and chunk == LATE:
                add(rest, 0)
        if order == 0:
            for copy in own:
                copy.wait()
            for copy in given:
                copy.wait_recv()
            pair_wo[...] = (pair_wo[...].astype(F32) + other_wo[...].astype(F32)).astype(BF16)
            pair_qkv[...] = (pair_qkv[...].astype(F32) + other_qkv[...].astype(F32)).astype(
                BF16
            )
            add(sums_ends, 0)
        if order == 1:
            lines[0].step(0, 0)
            lines[1].step(0, 0)
    for stage in range(1, stages):
        add(rest, stage)
    for order in range(size - 1):
        if order > 0:
            lines[0].step(order, 0)
            lines[1].step(order, 0)
        lines[2].step(order, 0)
    for stage in range(vector_at, len(vector_bits) + 1):
        vector_step(stage)
    for chunk in range(chunks):
        line.result(chunk, out, line.at(chunk))
    out_copy = pltpu.make_async_copy(out, out_there, local.at[5 + size])
    out_copy.start()
    owned_vectors[...] = vector_sum[len(vector_bits)]
    part = owned_v.shape[1]
    total_qkv = acc_qkv[0, 0]
    owned_q[...] = dot(total_qkv[:, :part], out_pairs[...])
    owned_k[...] = dot(total_qkv[:, part : 2 * part], out_pairs[...])
    owned_v[...] = total_qkv[:, 2 * part :].astype(F32)
    lines[0].result(0, whole, pl.ds(0, split))
    lines[1].result(0, whole, pl.ds(split, whole.shape[0] - split))
    lines[2].result(0, turned_wo, slice(None))

    matrices, rows, columns = owned.shape
    columns = columns // 2
    place = pl.ds(pl.multiple_of(core * columns, columns), columns)
    swaps = []
    for matrix in range(matrices):
        mine = pl.ds(pl.multiple_of((2 * matrix + core) * rows, rows), rows)
        theirs = pl.ds(pl.multiple_of((2 * matrix + 1 - core) * rows, rows), rows)
        swaps.append(
            to_device(
                whole.at[theirs, :],
                owned.at[matrix, :, place],
                core_sent.at[2 + matrix],
                core_got.at[2 + matrix],
                other_core_is,
            )
        )
        swaps[-1].start()
        copy = pltpu.make_async_copy(
            whole.at[mine, :], owned.at[matrix, :, place], local.at[2 + matrix]
        )
        copy.start()
        swaps.append(copy)
    owned_wo[...] = turned_wo[...].T
    out_copy.wait()
    for copy in swaps:
        copy.wait()
    owned_up[...] = owned[0]
    owned_gate[...] = owned[1]
    owned_down[...] = owned[2].T

    for copy in given + vector_copies:
        copy.wait_send()
    for stage in range(len(vector_bits)):
        vector_copy(stage).wait_send()
    for part in [*sums_ends, *rest]:
        part.close()
    line.close()
    for part in lines:
        part.close()


def sum_all(term, grads, grad_wo, grad_qkv, shares, out_pairs, chips, collective):
    size, tokens, part = term.shape
    height, units = grads.shape[2:]
    rows = height // 6
    chunks = 6
    split = height // 32 * 16
    half, blocks = max(chips // 2, 1), max(chips - 1, 1)
    stages = chips.bit_length()
    dma = pltpu.SemaphoreType.DMA
    vmem = pl.BlockSpec(memory_space=pltpu.VMEM)
    wo_block, qkv_block = grad_wo.shape[3:], grad_qkv.shape[2:]
    long = (1, 4 * units + 3 * part)

    def sums(layers, block):
        return [
            pltpu.VMEM((layers, half, *block), BF16),
            pltpu.VMEM((layers, blocks, *block), BF16),
        ]

    def line(block):
        return [pltpu.VMEM((size, *block), BF16)] * 2

    return pl.pallas_call(
        functools.partial(sum_all_kernel, size, chips, chunks, split),
        in_specs=[ANY, ANY, ANY, ANY, *[vmem] * (len(shares) + 1)],
        out_specs=[ANY, *[vmem] * 8],
        out_shape=[
            jax.ShapeDtypeStruct((tokens, part), F32),
            jax.ShapeDtypeStruct((rows, 2 * units), F32),
            jax.ShapeDtypeStruct((rows, 2 * units), F32),
            jax.ShapeDtypeStruct((2 * units, rows), F32),
            jax.ShapeDtypeStruct(wo_block[::-1], F32),
            *[jax.ShapeDtypeStruct((qkv_block[0], part), F32)] * 3,
            jax.ShapeDtypeStruct(long, F32),
        ],
        scratch_shapes=[
            pltpu.VMEM((size, tokens, part), BF16),
            pltpu.VMEM((tokens, part), F32),
            pltpu.VMEM((size, *long), F32),
            *line((tokens, part)),
            *sums(size, (split, units)),
            *line((split, units)),
            *sums(size, (height - split, units)),
            *line((height - split, units)),
            pltpu.VMEM((size, chips, *wo_block), BF16),
            pltpu.VMEM((size, chips, *wo_block), BF16),
            *sums(size, wo_block),
            *line(wo_block),
            pltpu.VMEM((chips, *qkv_block), BF16),
            pltpu.VMEM((chips, *qkv_block), BF16),
            *sums(1, qkv_block),
            pltpu.VMEM((height, units), F32),
            pltpu.VMEM((3, rows, 2 * units), F32),
            pltpu.VMEM(wo_block, F32),
            pltpu.VMEM((stages + 1, *long), F32),
            pltpu.VMEM((stages + 1, *long), F32),
            pltpu.VMEM((size, *long), F32),
            dma((6 + size,)),
            dma((5,)),
            dma((5,)),
            dma((size + stages,)),
            dma((size + stages,)),
            dma((1, 4, size, chunks)),
            dma((3, 4, size, 1)),
            dma((4, size, half)),
            dma((4, size, blocks)),
            dma((4, size, blocks)),
        ],
        compiler_params=remote_params(collective),
        name="sum_all",
    )(term, grads, grad_wo, grad_qkv, *shares, out_pairs)


def paired_place(heads):
    head, feature = np.divmod(np.arange(heads * DK), DK)
    return (feature // HALF) * (heads * HALF) + head * HALF + feature % HALF


def placing_matrix(place, heads):
    head, feature = np.divmod(np.arange(heads * DK), DK)
    matrix = np.zeros((heads * DK, heads * EXT), np.float32)
    matrix[place, head * EXT + feature] = 1
    return matrix


def delta_matrix(heads):
    lane = np.arange(heads * EXT)
    head = np.arange(heads * DK) // DK
    return ((head[:, None] == lane[None, :] // EXT) & (lane % EXT >= DK) & (lane % EXT < DK + 3)).astype(
        np.float32
    )


def head_sum_matrix(heads):
    lane = np.arange(heads * HALF) // HALF
    return (lane[:, None] == lane[None, :]).astype(np.float32)


def split_dot(value, matrix):
    high = value.astype(BF16)
    rest = (value - high.astype(F32)).astype(BF16)
    return dot(high, matrix) + dot(rest, matrix)


def project_block(wide, weight, cos, sin, gain, place_pair, place_plain, sums, at, outs):
    q, k, v, q_pair, k_pair, rq, rk = outs
    heads = q.shape[0]
    pair, width = heads * HALF, heads * DK
    raw = dot(wide[0], weight[0])
    for part in range(1, len(wide)):
        raw += dot(wide[part], weight[part])
    lane = lax.broadcasted_iota(jnp.int32, (raw.shape[0], EXT), 1)
    for offset, out, pair_out, scale_out, factor in (
        (0, q, q_pair, rq, math.sqrt(DK)),
        (width, k, k_pair, rk, 1.0),
    ):
        first = raw[:, offset : offset + pair]
        second = raw[:, offset + pair : offset + width]
        turned_first = first * cos - second * sin
        turned_second = second * cos + first * sin
        total = split_dot(turned_first * turned_first + turned_second * turned_second, sums)
        scale = lax.rsqrt(total + EPSILON)
        scale_out[at, :] = scale
        both = jnp.concatenate(
            [
                turned_first * scale * gain[:, :pair],
                turned_second * scale * gain[:, pair:],
            ],
            axis=1,
        ).astype(BF16)
        pair_out[at, :] = both
        padded = dot(both, place_pair) * factor
        for head in range(heads):
            piece = padded[:, head * EXT : (head + 1) * EXT]
            if factor == 1.0:
                piece = jnp.where(lane < DK, piece, 1.0)
            out[head, at, :] = piece.astype(BF16)
    padded = dot(raw[:, 2 * width :].astype(BF16), place_plain)
    for head in range(heads):
        piece = padded[:, head * EXT : (head + 1) * EXT]
        v[head, at, :] = jnp.where(lane < DK, piece, 1.0).astype(BF16)


def split_three(value):
    high = value.astype(BF16).astype(F32)
    rest = value - high
    middle = rest.astype(BF16).astype(F32)
    return high, middle, rest - middle


def attend_kernel(low, q, k, v, columns, kdoc, collect, attended, qback, acc):
    heads, rows, _ = q.shape
    block = kdoc.shape[2]
    index = pl.program_id(0)
    acc[...] = jnp.zeros_like(acc)

    def earlier(j, carry):
        slots = pl.ds(pl.multiple_of(j * block, block), block)
        mask = columns[:, 1:2] == kdoc[j]
        for head in range(heads):
            scores = dot(q[head], k[head, slots, :], NT)
            weight = jnp.where(mask, jnp.exp(scores), 0.0).astype(BF16)
            acc[head] += dot(weight, v[head, slots, :])
        return carry

    lax.fori_loop(low[index], index, earlier, 0)

    strip = max(rows // 2, min(rows, 128))
    for start in range(0, rows, strip):
        at = slice(start, start + strip)
        end = start + strip
        slots = pl.ds(pl.multiple_of(index * block, block), end)
        row = start + lax.broadcasted_iota(jnp.int32, (strip, end), 0)
        column = lax.broadcasted_iota(jnp.int32, (strip, end), 1)
        mask = columns[at, 1:2] == kdoc[index][:, :end]
        mask = (mask & (column < row)) | (column == row)
        for head in range(heads):
            scores = dot(q[head, at, :], k[head, slots, :], NT)
            weight = jnp.where(mask, jnp.exp(scores), 0.0).astype(BF16)
            acc[head, at, :] += dot(weight, v[head, slots, :])

    lane = lax.broadcasted_iota(jnp.int32, (rows, EXT), 1)
    merged = jnp.zeros((rows, heads * DK), F32)
    for head in range(heads):
        both = acc[head]
        total = pltpu.roll(both, DK, 1)
        output = jnp.where(lane < DK, both / total, 0.0).astype(BF16)
        merged += dot(output, collect[head])
        high, middle, rest = split_three(-jnp.log(both))
        qback[head] = jnp.where(
            lane < DK,
            q[head].astype(F32),
            jnp.where(
                lane == DK,
                high,
                jnp.where(lane == DK + 1, middle, jnp.where(lane == DK + 2, rest, 0.0)),
            ),
        ).astype(BF16)
    attended[...] = merged.astype(BF16)


def attend(low, q, k, v, columns, kdoc, collect):
    heads, tokens, _ = q.shape
    block = kdoc.shape[2]
    width = heads * DK

    def whole(array):
        return pl.BlockSpec(array.shape, lambda i, low: (0,) * array.ndim)

    headed = pl.BlockSpec((heads, block, EXT), lambda i, low: (0, i, 0))
    return pl.pallas_call(
        attend_kernel,
        grid_spec=pltpu.PrefetchScalarGridSpec(
            num_scalar_prefetch=1,
            grid=(tokens // block,),
            in_specs=[
                headed,
                whole(k),
                whole(v),
                pl.BlockSpec((block, columns.shape[1]), lambda i, low: (i, 0)),
                whole(kdoc),
                whole(collect),
            ],
            out_specs=[pl.BlockSpec((block, width), lambda i, low: (i, 0)), headed],
            scratch_shapes=[pltpu.VMEM((heads, block, EXT), F32)],
        ),
        out_shape=[
            jax.ShapeDtypeStruct((tokens, width), BF16),
            jax.ShapeDtypeStruct((heads, tokens, EXT), BF16),
        ],
        compiler_params=grid_params(1),
        cost_estimate=pl.CostEstimate(
            flops=40_000_000_000, bytes_accessed=16 << 20, transcendentals=0
        ),
        name="attend",
    )(low, q, k, v, columns, kdoc, collect)


def unrope(grad, unit, gain, scale, cos, sin, sums):
    pair = cos.shape[1]
    grad_gain = jnp.sum(grad * unit, axis=0, keepdims=True)
    dy = grad * gain
    prod = dy * unit
    total = split_dot(prod[:, :pair] + prod[:, pair:], sums)
    first = scale * (dy[:, :pair] - unit[:, :pair] * total)
    second = scale * (dy[:, pair:] - unit[:, pair:] * total)
    raw = jnp.concatenate([first * cos + second * sin, second * cos - first * sin], axis=1)
    return raw.astype(BF16), grad_gain


def head_lanes(shape, head, paired):
    lane = lax.broadcasted_iota(jnp.int32, shape, 1)
    if paired:
        return lax.div(lax.rem(lane, shape[1] // 2), HALF) == head
    return lax.div(lane, DK) == head


def attend_back_kernel(
    low,
    qback,
    q_pair,
    dout,
    attended,
    k,
    k_pair,
    v,
    qdoc,
    columns,
    cosine,
    sine,
    rq,
    rk,
    gain,
    weight,
    place_plain,
    place_delta,
    sums,
    wide,
    grad_resid,
    out_low,
    term_out,
    grad_qkv,
    gain_out,
    out_hidden,
    dk,
    dv,
    dq,
    dox,
    q_heads,
    d_heads,
    k_heads,
    probs_all,
    scores_all,
    dq_low,
    total_qkv,
):
    heads, rows, _ = qback.shape
    steps = pl.num_programs(0) // 2
    step_at = pl.program_id(0)
    width = heads * DK
    scale = math.sqrt(DK)

    @pl.when(step_at == 0)
    def _():
        dk[...] = jnp.zeros_like(dk)
        dv[...] = jnp.zeros_like(dv)
        gain_out[...] = jnp.zeros_like(gain_out)
        keys = k_pair[...]
        for head in range(heads):
            k_heads[head] = jnp.where(head_lanes(keys.shape, head, True), keys, 0)

    @pl.when(step_at < steps)
    def _():
        index = step_at
        out_hidden[...] = out_low[...].astype(F32)
        lane = lax.broadcasted_iota(jnp.int32, (rows, EXT), 1)
        grads = dout[...]
        queries = q_pair[...]
        spread = dot(grads, place_plain[...])
        delta = split_dot(grads.astype(F32) * attended[...].astype(F32), place_delta[...])
        for head in range(heads):
            at = slice(head * EXT, (head + 1) * EXT)
            high, middle, rest = split_three(-delta[:, at])
            dox[head] = jnp.where(
                lane < DK,
                spread[:, at],
                jnp.where(lane == DK, high, jnp.where(lane == DK + 1, middle, rest)),
            ).astype(BF16)
            stack = slice(head * rows, (head + 1) * rows)
            q_heads[stack, :] = jnp.where(head_lanes(queries.shape, head, True), queries, 0)
            d_heads[stack, :] = jnp.where(head_lanes(grads.shape, head, False), grads, 0)
        dq[...] = jnp.zeros_like(dq)

        def earlier(j, carry):
            slots = pl.ds(pl.multiple_of(j * rows, rows), rows)
            mask = columns[slots, 2:3] == qdoc[0]
            total = dq[...]
            for head in range(heads):
                scores = dot(k[head, slots, :], qback[head], NT)
                probs = jnp.where(mask, jnp.exp(scores), 0.0)
                dprobs = dot(v[head, slots, :], dox[head], NT)
                dscores = (probs * dprobs).astype(BF16)
                stack = slice(head * rows, (head + 1) * rows)
                probs_all[:, stack] = probs.astype(BF16)
                scores_all[:, stack] = dscores
                total += dot(dscores, k_heads[head, slots, :], TN)
            dq[...] = total
            dv[slots, :] += dot(probs_all[...], d_heads[...])
            dk[slots, :] += dot(scores_all[...], q_heads[...])
            return carry

        lax.fori_loop(low[index], index, earlier, 0)

        strip = max(rows // 2, min(rows, 128))
        for start in range(0, rows, strip):
            after_start = slice(start, rows)
            count = rows - start
            slots = pl.ds(pl.multiple_of(index * rows + start, strip), strip)
            key = start + lax.broadcasted_iota(jnp.int32, (strip, count), 0)
            query = start + lax.broadcasted_iota(jnp.int32, (strip, count), 1)
            mask = columns[slots, 2:3] == qdoc[0][:, after_start]
            mask = (mask & (key < query)) | (key == query)
            values, keys, queries_grad = None, None, None
            for head in range(heads):
                scores = dot(k[head, slots, :], qback[head, after_start, :], NT)
                probs = jnp.where(mask, jnp.exp(scores), 0.0)
                dprobs = dot(v[head, slots, :], dox[head, after_start, :], NT)
                dscores = (probs * dprobs).astype(BF16)
                stack = slice(head * rows + start, (head + 1) * rows)
                terms = (
                    dot(probs.astype(BF16), d_heads[stack, :]),
                    dot(dscores, q_heads[stack, :]),
                    dot(dscores, k_heads[head, slots, :], TN),
                )
                if head == 0:
                    values, keys, queries_grad = terms
                else:
                    values, keys, queries_grad = (
                        values + terms[0],
                        keys + terms[1],
                        queries_grad + terms[2],
                    )
            dv[slots, :] += values
            dk[slots, :] += keys
            dq[after_start, :] += queries_grad

        raw, grad_gain = unrope(
            dq[...] * scale,
            queries.astype(F32) * (1.0 / gain[...]),
            gain[...],
            rq[...],
            cosine[...],
            sine[...],
            sums[...],
        )
        gain_out[...] += grad_gain
        dq_low[pl.ds(pl.multiple_of(index * rows, rows), rows), :] = raw

    @pl.when(step_at >= steps)
    def _():
        index = step_at - steps
        slots = pl.ds(pl.multiple_of(index * rows, rows), rows)
        raw, grad_gain = unrope(
            dk[slots, :] * scale,
            k_pair[slots, :].astype(F32) * (1.0 / gain[...]),
            gain[...],
            rk[...],
            cosine[...],
            sine[...],
            sums[...],
        )
        gain_out[...] += grad_gain
        together = jnp.concatenate([dq_low[slots, :], raw, dv[slots, :].astype(BF16)], axis=1)
        parts, part = weight.shape[:2]
        for member in range(parts):
            term_out[member] = dot(together, weight[member], NT).astype(BF16)
            product = dot(wide[member], together, TN)

            @pl.when(index == 0)
            def _():
                total_qkv[member] = product

            @pl.when(index > 0)
            def _():
                total_qkv[member] += product

        strip = STRIP
        first = low[steps] * (grad_resid.shape[0] // strip)
        for half in range(rows // strip):
            number = index * (rows // strip) + half - first

            @pl.when((number >= 0) & (number < grad_resid.shape[0] // strip))
            def _():
                at = pl.ds(half * strip, strip)
                own = pl.ds(pl.multiple_of(number * strip, strip), strip)
                for member in range(parts):
                    term_out[member, at, :] = (
                        term_out[member, at, :].astype(F32)
                        + grad_resid[own, member * part : (member + 1) * part].astype(F32)
                    ).astype(BF16)

        @pl.when(index == steps - 1)
        def _():
            grad_qkv[...] = total_qkv[...].astype(BF16)


def attend_back(
    low,
    qback,
    q_pair,
    dout,
    attended,
    k,
    k_pair,
    v,
    qdoc,
    columns,
    cosine,
    sine,
    rq,
    rk,
    gain,
    weight,
    place_plain,
    place_delta,
    sums,
    wide,
    grad_resid,
    out_low,
):
    heads, tokens, _ = k.shape
    block = qdoc.shape[2]
    width = heads * DK
    steps = tokens // block
    parts, part = weight.shape[:2]

    def whole(array):
        return pl.BlockSpec(array.shape, lambda i, low: (0,) * array.ndim)

    def now(i):
        return jnp.minimum(i, steps - 1)

    def after(i):
        return jnp.maximum(i - steps, 0)

    def both(i):
        return lax.rem(i, steps)

    def rows(columns, at):
        return pl.BlockSpec((block, columns), lambda i, low: (at(i), 0))

    return pl.pallas_call(
        attend_back_kernel,
        grid_spec=pltpu.PrefetchScalarGridSpec(
            num_scalar_prefetch=1,
            grid=(2 * steps,),
            in_specs=[
                pl.BlockSpec((heads, block, EXT), lambda i, low: (0, now(i), 0)),
                rows(width, now),
                rows(width, now),
                rows(width, now),
                whole(k),
                whole(k_pair),
                whole(v),
                pl.BlockSpec((1, 1, block), lambda i, low: (now(i), 0, 0)),
                whole(columns),
                rows(width // 2, both),
                rows(width // 2, both),
                rows(width // 2, now),
                rows(width // 2, after),
                whole(gain),
                whole(weight),
                whole(place_plain),
                whole(place_delta),
                whole(sums),
                pl.BlockSpec((parts, block, part), lambda i, low: (0, after(i), 0)),
                whole(grad_resid),
                rows(out_low.shape[1], now),
            ],
            out_specs=[
                pl.BlockSpec((parts, block, part), lambda i, low: (0, after(i), 0)),
                pl.BlockSpec((parts, part, 3 * width), lambda i, low: (0, 0, 0)),
                pl.BlockSpec((1, width), lambda i, low: (0, 0)),
                rows(out_low.shape[1], now),
            ],
            scratch_shapes=[
                pltpu.VMEM((tokens, width), F32),
                pltpu.VMEM((tokens, width), F32),
                pltpu.VMEM((block, width), F32),
                pltpu.VMEM((heads, block, EXT), BF16),
                pltpu.VMEM((heads * block, width), BF16),
                pltpu.VMEM((heads * block, width), BF16),
                pltpu.VMEM((heads, tokens, width), BF16),
                pltpu.VMEM((block, heads * block), BF16),
                pltpu.VMEM((block, heads * block), BF16),
                pltpu.VMEM((tokens, width), BF16),
                pltpu.VMEM((parts, part, 3 * width), F32),
            ],
        ),
        out_shape=[
            jax.ShapeDtypeStruct((parts, tokens, part), BF16),
            jax.ShapeDtypeStruct((parts, part, 3 * width), BF16),
            jax.ShapeDtypeStruct((1, width), F32),
            jax.ShapeDtypeStruct(out_low.shape, F32),
        ],
        compiler_params=grid_params(1),
        cost_estimate=pl.CostEstimate(
            flops=80_000_000_000, bytes_accessed=30 << 20, transcendentals=0
        ),
        name="attend_back",
    )(
        low,
        qback,
        q_pair,
        dout,
        attended,
        k,
        k_pair,
        v,
        qdoc,
        columns,
        cosine,
        sine,
        rq,
        rk,
        gain,
        weight,
        place_plain,
        place_delta,
        sums,
        wide,
        grad_resid,
        out_low,
    )


def row_scale(value):
    return lax.rsqrt(jnp.sum(value * value, axis=-1, keepdims=True) + EPSILON)


def residual_backward(grad_out, result, resid, unit, alpha, branch_scale, mixed_scale):
    grad_mixed = mixed_scale * (
        grad_out - result * jnp.sum(grad_out * result, axis=-1, keepdims=True)
    )
    grad_alpha = jnp.sum(grad_mixed * (unit - resid), axis=0, keepdims=True)
    grad_unit = grad_mixed * alpha
    grad_branch = branch_scale * (
        grad_unit - unit * jnp.sum(grad_unit * unit, axis=-1, keepdims=True)
    )
    return grad_mixed * (1.0 - alpha), grad_branch, grad_alpha


STRIP = 256


def strips(rows):
    strip = min(STRIP, rows)
    return [pl.ds(start, strip) for start in range(0, rows, strip)]


def core_semaphores(count):
    return [pltpu.SemaphoreType.DMA((count,)), pltpu.SemaphoreType.DMA((count,))]


def greet_pair_and_line(size):
    me, core = lax.axis_index("mp"), lax.axis_index("core")
    for k in range(1, size):
        greet({"mp": flip(me, k)})
    greet({"core": 1 - core})
    pl.semaphore_wait(pltpu.get_barrier_semaphore(), size)


def output_matrix(packed_wo, whole):
    size, chips, rows, both = packed_wo.shape
    part = both // 2
    for chip in range(chips):
        for core in range(2):
            start = (2 * chip + core) * rows
            whole[:, start : start + rows, :] = packed_wo[
                :, chip, :, core * part : (core + 1) * part
            ]


def mix_kernel(
    size,
    attended,
    packed,
    wide,
    alpha,
    cotangent,
    x,
    middle_out,
    unit_out,
    merged_out,
    full_wo_out,
    resid_out,
    cotangent_out,
    branch_scale_out,
    mixed_scale_out,
    packed_wo,
    middle_low,
    resid,
    middle_kept,
    unit_kept,
    merged,
    full_wo,
    cotangent_low,
    send,
    receive,
    local,
    own_sems,
    core_sent,
    core_got,
    out_sems,
):
    me, core = lax.axis_index("mp"), lax.axis_index("core")
    mine, width = middle_out.shape
    part = width // size
    rows = packed_wo.shape[2]
    greet_pair_and_line(size)
    every = strips(mine)

    def exchange(order):
        at = every[order]
        return Exchange(
            size,
            attended,
            merged,
            lambda ref, j: ref.at[
                pl.ds(pl.multiple_of(j * mine + at.start, at.size), at.size), :
            ],
            lambda ref, j: ref.at[at, pl.ds(pl.multiple_of(j * part, part), part)],
            send.at[order],
            receive.at[order],
            local.at[order],
        )

    exchange(0).start()
    own = [
        pltpu.make_async_copy(
            packed.at[:, :, pl.ds(packed.shape[2] - rows, rows), :], packed_wo, own_sems.at[0]
        )
    ]
    for member in range(size):
        own.append(
            pltpu.make_async_copy(
                wide.at[member, pl.ds(pl.multiple_of(me * mine, mine), mine), :],
                resid.at[:, pl.ds(member * part, part)],
                own_sems.at[1 + member],
            )
        )
    for copy in own:
        copy.start()
    for at in strips(cotangent.shape[0]):
        cotangent_low[at, :] = cotangent[at, :].astype(BF16)
    for copy in own:
        copy.wait()
    output_matrix(packed_wo, full_wo)
    leaving = [
        pltpu.make_async_copy(here, there, out_sems.at[order])
        for order, (here, there) in enumerate(
            ((full_wo, full_wo_out), (resid, resid_out), (cotangent_low, cotangent_out))
        )
    ]
    for copy in leaving:
        copy.start()

    swaps = []
    for order, at in enumerate(every):
        exchange(order).wait()
        if order + 1 < len(every):
            exchange(order + 1).start()
        branch = dot(merged[at, :part], full_wo[0], NT)
        for member in range(1, size):
            branch += dot(
                merged[at, member * part : (member + 1) * part], full_wo[member], NT
            )
        old = resid[at, :].astype(F32)
        branch_scale = row_scale(branch)
        unit = branch * branch_scale
        mixed = old + alpha[...] * (unit - old)
        mixed_scale = row_scale(mixed)
        middle = mixed * mixed_scale
        middle_kept[at, :] = middle
        unit_kept[at, :] = unit.astype(BF16)
        branch_scale_out[at, :] = branch_scale
        mixed_scale_out[at, :] = mixed_scale
        middle_low[at, :] = middle.astype(BF16)
        there = pl.ds(mine + at.start, at.size)
        swap = to_device(
            middle_low.at[at, :],
            x.at[there, :],
            core_sent.at[order],
            core_got.at[order],
            {"core": 1 - core},
        )
        swap.start()
        swaps.append(swap)
        for kind, (here, there) in enumerate(
            ((middle_kept, middle_out), (unit_kept, unit_out), (merged, merged_out))
        ):
            copy = pltpu.make_async_copy(
                here.at[at, :], there.at[at, :], out_sems.at[3 + 3 * order + kind]
            )
            copy.start()
            leaving.append(copy)
    keep = pltpu.make_async_copy(middle_low, x.at[pl.ds(0, mine), :], own_sems.at[0])
    keep.start()
    keep.wait()
    for copy in swaps + leaving:
        copy.wait()


def mix(attended, packed, rows, wide, alpha, cotangent, collective):
    size, slots, part = wide.shape
    chips = packed.shape[1]
    mine, width = slots // size, size * part
    vmem = pl.BlockSpec(memory_space=pltpu.VMEM)
    count = len(strips(mine))
    scale = jax.ShapeDtypeStruct((mine, 1), F32)
    return pl.pallas_call(
        functools.partial(mix_kernel, size),
        in_specs=[ANY, ANY, ANY, vmem, vmem],
        out_specs=[*[ANY] * 7, vmem, vmem],
        out_shape=[
            jax.ShapeDtypeStruct((2 * mine, width), BF16),
            jax.ShapeDtypeStruct((mine, width), F32),
            jax.ShapeDtypeStruct((mine, width), BF16),
            jax.ShapeDtypeStruct((mine, width), BF16),
            jax.ShapeDtypeStruct((size, width, part), BF16),
            jax.ShapeDtypeStruct((mine, width), BF16),
            jax.ShapeDtypeStruct((slots, part), BF16),
            scale,
            scale,
        ],
        scratch_shapes=[
            pltpu.VMEM((size, chips, rows, 2 * part), BF16),
            pltpu.VMEM((mine, width), BF16),
            pltpu.VMEM((mine, width), BF16),
            pltpu.VMEM((mine, width), F32),
            pltpu.VMEM((mine, width), BF16),
            pltpu.VMEM((mine, width), BF16),
            pltpu.VMEM((size, width, part), BF16),
            pltpu.VMEM((slots, part), BF16),
            pltpu.SemaphoreType.DMA((count, size)),
            pltpu.SemaphoreType.DMA((count, size)),
            pltpu.SemaphoreType.DMA((count,)),
            pltpu.SemaphoreType.DMA((1 + size,)),
            *core_semaphores(count),
            pltpu.SemaphoreType.DMA((3 + 3 * count,)),
        ],
        compiler_params=remote_params(collective),
        name="mix",
    )(attended, packed, wide, alpha, cotangent)


def whole_matrix(ref):
    _, chips, rows, units = ref.shape
    return ref[...].reshape(chips * rows, units)


def first_step():
    return (pl.program_id(0) == 0) & (pl.program_id(1) == 0)


def last_step():
    return (pl.program_id(0) == pl.num_programs(0) - 1) & (
        pl.program_id(1) == pl.num_programs(1) - 1
    )


def swap_cores(source, target, sems):
    return to_device(
        source, target, sems[0], sems[1], {"core": 1 - lax.axis_index("core")}
    )


def feed_kernel(
    size,
    x,
    w_up,
    w_gate,
    w_down,
    s_u,
    s_v,
    cotangent,
    middle_in,
    alpha,
    up_out,
    gate_out,
    units_out,
    result_out,
    grad_middle,
    dbranch,
    grad_alpha,
    acc,
    given,
    got,
    spread,
    low,
    middle,
    send,
    receive,
    local,
    core_sent,
    core_got,
    keep_sems,
    load_sem,
):
    load = pltpu.make_async_copy(middle_in, middle, load_sem)
    exchange = Exchange(
        size,
        cotangent,
        spread,
        row_part(spread.shape[0]),
        column_part(cotangent.shape[1]),
        send,
        receive,
        local,
    )
    branch_swap = swap_cores(given, got, (core_sent.at[0], core_got.at[0]))

    @pl.when(first_step())
    def _():
        load.start()
        greet_pair_and_line(size)
        exchange.start()

    block, part = pl.program_id(0), pl.program_id(1)
    up = dot(x[...], whole_matrix(w_up))
    gate = dot(x[...], whole_matrix(w_gate))
    up_out[0] = up.astype(BF16)
    gate_out[0] = gate.astype(BF16)
    scaled = gate * s_v[0]
    units = (up * s_u[0] * (scaled / (1.0 + jnp.exp(-scaled)))).astype(BF16)
    units_out[0] = units
    term = dot(units, whole_matrix(w_down), NT)

    @pl.when(part == 0)
    def _():
        acc[...] = term

    @pl.when(part > 0)
    def _():
        acc[...] += term

    last = part == pl.num_programs(1) - 1

    @pl.when(last & (block == 0))
    def _():
        given[...] = acc[...].astype(BF16)
        branch_swap.start()

    @pl.when(last & (block == 1))
    def _():
        mine = acc.shape[0]
        load.wait()
        branch_swap.wait()
        exchange.wait()
        swaps = []
        for order, at in enumerate(strips(mine)):
            branch = acc[at, :] + got[at, :].astype(F32)
            branch_scale = row_scale(branch)
            unit = branch * branch_scale
            old = middle[at, :]
            mixed = old + alpha[...] * (unit - old)
            mixed_scale = row_scale(mixed)
            result = mixed * mixed_scale
            result_out[at, :] = result.astype(BF16)
            grad_old, grad_branch, part_alpha = residual_backward(
                spread[at, :].astype(F32),
                result,
                old,
                unit,
                alpha[...],
                branch_scale,
                mixed_scale,
            )
            grad_middle[at, :] = grad_old
            if order == 0:
                grad_alpha[...] = part_alpha
            else:
                grad_alpha[...] += part_alpha
            low[at, :] = grad_branch.astype(BF16)
            there = pl.ds(mine + at.start, at.size)
            swaps.append(
                swap_cores(
                    low.at[at, :],
                    dbranch.at[there, :],
                    (core_sent.at[1 + order], core_got.at[1 + order]),
                )
            )
            swaps.append(
                pltpu.make_async_copy(low.at[at, :], dbranch.at[at, :], keep_sems.at[order])
            )
            swaps[-2].start()
            swaps[-1].start()
        for swap in swaps:
            swap.wait()


def packed_specs(packed, width):
    _, chips, _, units = packed.shape
    return [
        pl.BlockSpec((1, chips, width // chips, units), lambda t, m, w=w: (m, 0, w, 0))
        for w in range(3)
    ]


def feed(x, packed, s_u, s_v, cotangent, middle, alpha, collective):
    tokens, width = x.shape
    parts, _, _, units = packed.shape
    size = parts
    block = tokens // 2
    rows = pl.BlockSpec((block, width), lambda t, m: (1 - t, 0))
    vector = pl.BlockSpec((1, 1, units), lambda t, m: (m, 0, 0))
    piece = pl.BlockSpec((1, block, units), lambda t, m: (m, 1 - t, 0))
    vmem = pl.BlockSpec(memory_space=pltpu.VMEM)
    hidden = jax.ShapeDtypeStruct((parts, tokens, units), BF16)
    count = len(strips(block))
    low = pltpu.VMEM((block, width), BF16)
    return pl.pallas_call(
        functools.partial(feed_kernel, size),
        grid=(2, parts),
        in_specs=[rows, *packed_specs(packed, width), vector, vector, ANY, ANY, vmem],
        out_specs=[piece, piece, piece, vmem, vmem, ANY, vmem],
        out_shape=[
            hidden,
            hidden,
            hidden,
            jax.ShapeDtypeStruct((block, width), BF16),
            jax.ShapeDtypeStruct((block, width), F32),
            jax.ShapeDtypeStruct((tokens, width), BF16),
            jax.ShapeDtypeStruct((1, width), F32),
        ],
        scratch_shapes=[
            pltpu.VMEM((block, width), F32),
            low,
            low,
            low,
            low,
            pltpu.VMEM((block, width), F32),
            *exchange_semaphores(size),
            *core_semaphores(1 + count),
            pltpu.SemaphoreType.DMA((count,)),
            pltpu.SemaphoreType.DMA,
        ],
        compiler_params=remote_params(collective),
        cost_estimate=pl.CostEstimate(
            flops=6 * tokens * width * parts * units, bytes_accessed=60 << 20, transcendentals=0
        ),
        name="feed",
    )(x, packed, packed, packed, s_u, s_v, cotangent, middle, alpha)


def feed_back_kernel(
    size,
    dbranch,
    w_up,
    w_gate,
    w_down,
    s_u,
    s_v,
    up_in,
    gate_in,
    result,
    grad_middle_in,
    middle_in,
    resid_in,
    unit_in,
    branch_scale,
    mixed_scale,
    alpha,
    full_wo_in,
    dup_out,
    dgate_out,
    grad_u,
    grad_v,
    spread,
    grad_resid,
    dbranch_attn,
    dmerged,
    grad_alpha,
    acc,
    given,
    got,
    sum_u,
    sum_v,
    grad_middle,
    middle,
    resid,
    unit,
    full_wo,
    send,
    receive,
    local,
    core_sent,
    core_got,
    load_sems,
):
    loads = [
        pltpu.make_async_copy(there, here, load_sems.at[order])
        for order, (there, here) in enumerate(
            (
                (grad_middle_in, grad_middle),
                (middle_in, middle),
                (resid_in, resid),
                (unit_in, unit),
                (full_wo_in, full_wo),
            )
        )
    ]
    exchange = Exchange(
        size,
        result,
        spread,
        column_part(spread.shape[1]),
        row_part(result.shape[0]),
        send,
        receive,
        local,
    )
    dx_swap = swap_cores(given, got, (core_sent.at[0], core_got.at[0]))

    @pl.when(first_step())
    def _():
        for copy in loads:
            copy.start()
        greet_pair_and_line(size)
        exchange.start()

    block, part = pl.program_id(0), pl.program_id(1)
    dunits = dot(dbranch[...], whole_matrix(w_down))
    up = up_in[0].astype(F32)
    gate = gate_in[0].astype(F32)
    scaled = gate * s_v[0]
    sigmoid = 1.0 / (1.0 + jnp.exp(-scaled))
    silu = scaled * sigmoid
    slope = sigmoid * (1.0 + scaled - silu)
    through_up = dunits * silu
    through_gate = dunits * up * s_u[0] * slope
    dup = (through_up * s_u[0]).astype(BF16)
    dgate = (through_gate * s_v[0]).astype(BF16)
    dup_out[0] = dup
    dgate_out[0] = dgate
    term = dot(dup, whole_matrix(w_up), NT) + dot(dgate, whole_matrix(w_gate), NT)
    part_u = jnp.sum(through_up * up, axis=0, keepdims=True)
    part_v = jnp.sum(through_gate * gate, axis=0, keepdims=True)

    @pl.when(block == 0)
    def _():
        sum_u[part] = part_u
        sum_v[part] = part_v

    @pl.when(block > 0)
    def _():
        sum_u[part] += part_u
        sum_v[part] += part_v

    @pl.when(part == 0)
    def _():
        acc[...] = term

    @pl.when(part > 0)
    def _():
        acc[...] += term

    last = part == pl.num_programs(1) - 1

    @pl.when(last & (block == 0))
    def _():
        given[...] = acc[...].astype(BF16)
        dx_swap.start()

    @pl.when(last & (block == 1))
    def _():
        grad_u[...] = sum_u[...]
        grad_v[...] = sum_v[...]
        for copy in loads:
            copy.wait()
        dx_swap.wait()
        for order, at in enumerate(strips(acc.shape[0])):
            grad_old, grad_branch, part_alpha = residual_backward(
                grad_middle[at, :] + acc[at, :] + got[at, :].astype(F32),
                middle[at, :],
                resid[at, :].astype(F32),
                unit[at, :].astype(F32),
                alpha[...],
                branch_scale[at, :],
                mixed_scale[at, :],
            )
            grad_resid[at, :] = grad_old.astype(BF16)
            if order == 0:
                grad_alpha[...] = part_alpha
            else:
                grad_alpha[...] += part_alpha
            low = grad_branch.astype(BF16)
            dbranch_attn[at, :] = low
            columns = full_wo.shape[2]
            for member in range(size):
                dmerged[at, member * columns : (member + 1) * columns] = dot(
                    low, full_wo[member]
                ).astype(BF16)
        exchange.wait()


def feed_back(
    dbranch,
    packed,
    s_u,
    s_v,
    up,
    gate,
    result,
    grad_middle,
    middle,
    resid,
    unit,
    branch_scale,
    mixed_scale,
    alpha,
    full_wo,
    collective,
):
    tokens, width = dbranch.shape
    parts, _, _, units = packed.shape
    size = parts
    block = tokens // 2
    rows = pl.BlockSpec((block, width), lambda t, m: (1 - t, 0))
    vector = pl.BlockSpec((1, 1, units), lambda t, m: (m, 0, 0))
    piece = pl.BlockSpec((1, block, units), lambda t, m: (m, 1 - t, 0))
    vmem = pl.BlockSpec(memory_space=pltpu.VMEM)
    hidden = jax.ShapeDtypeStruct((parts, tokens, units), BF16)
    sums = jax.ShapeDtypeStruct((parts, 1, units), F32)
    state = jax.ShapeDtypeStruct((block, width), BF16)
    kept = (grad_middle, middle, resid, unit, full_wo)
    return pl.pallas_call(
        functools.partial(feed_back_kernel, size),
        grid=(2, parts),
        in_specs=[
            rows,
            *packed_specs(packed, width),
            vector,
            vector,
            piece,
            piece,
            ANY,
            *[ANY] * 4,
            *[vmem] * 3,
            ANY,
        ],
        out_specs=[piece, piece, vmem, vmem, ANY, vmem, vmem, vmem, vmem],
        out_shape=[
            hidden,
            hidden,
            sums,
            sums,
            jax.ShapeDtypeStruct((size * block, width // size), BF16),
            state,
            state,
            state,
            jax.ShapeDtypeStruct((1, width), F32),
        ],
        scratch_shapes=[
            pltpu.VMEM((block, width), F32),
            pltpu.VMEM((block, width), BF16),
            pltpu.VMEM((block, width), BF16),
            pltpu.VMEM((parts, 1, units), F32),
            pltpu.VMEM((parts, 1, units), F32),
            *[pltpu.VMEM(each.shape, each.dtype) for each in kept],
            *exchange_semaphores(size),
            *core_semaphores(1),
            pltpu.SemaphoreType.DMA((len(kept),)),
        ],
        compiler_params=remote_params(collective),
        cost_estimate=pl.CostEstimate(
            flops=6 * tokens * width * parts * units, bytes_accessed=70 << 20, transcendentals=0
        ),
        name="feed_back",
    )(
        dbranch,
        packed,
        packed,
        packed,
        s_u,
        s_v,
        up,
        gate,
        result,
        grad_middle,
        middle,
        resid,
        unit,
        branch_scale,
        mixed_scale,
        alpha,
        full_wo,
    )


def feed_grads_kernel(
    size,
    x,
    dbranch,
    dup,
    dgate,
    units,
    dbranch_attn,
    merged,
    dmerged,
    grads,
    grad_wo,
    dattended,
    x_turned,
    d_turned,
    attn_turned,
    send,
    receive,
    local,
):
    exchange = Exchange(
        size,
        dmerged,
        dattended,
        column_part(dattended.shape[1]),
        row_part(dmerged.shape[0]),
        send,
        receive,
        local,
    )

    @pl.when(first_step())
    def _():
        greet_all(size)
        exchange.start()
        x_turned[...] = x[...].T
        d_turned[...] = dbranch[...].T
        attn_turned[...] = dbranch_attn[...].T

    _, chips, rows, _ = grads.shape
    for which, left, right in (
        (0, x_turned, dup),
        (1, x_turned, dgate),
        (2, d_turned, units),
    ):

        @pl.when(pl.program_id(0) == which)
        def _():
            total = dot(left[...], right[0])
            grads[0] = total.astype(BF16).reshape(chips, rows, total.shape[1])

    @pl.when(pl.program_id(0) == 3)
    def _():
        total = dot(attn_turned[...], merged[...])
        grad_wo[...] = total.astype(BF16).reshape(grad_wo.shape)

    @pl.when(last_step())
    def _():
        exchange.wait()


def feed_grads(
    x, dbranch, dup, dgate, units_in, dbranch_attn, merged, dmerged, chips, collective
):
    tokens, width = x.shape
    parts, _, units = dup.shape
    size = parts
    rows = width // chips
    mine = dmerged.shape[0]
    part = width // size

    def whole(array):
        return pl.BlockSpec(array.shape, lambda w, m: (0, 0))

    def turn(w, m, which):
        return jnp.where(w == which, m, jnp.where(w < which, 0, parts - 1))

    def piece(which):
        return pl.BlockSpec((1, tokens, units), lambda w, m: (turn(w, m, which), 0, 0))

    return pl.pallas_call(
        functools.partial(feed_grads_kernel, size),
        grid=(4, parts),
        in_specs=[
            whole(x),
            whole(dbranch),
            piece(0),
            piece(1),
            piece(2),
            whole(dbranch_attn),
            pl.BlockSpec((mine, part), lambda w, m: (0, turn(w, m, 3))),
            ANY,
        ],
        out_specs=[
            pl.BlockSpec(
                (1, chips, rows, units),
                lambda w, m: (jnp.where(w < 3, m, parts - 1), 0, jnp.minimum(w, 2), 0),
            ),
            pl.BlockSpec(
                (1, chips, 2, rows // 2, part), lambda w, m: (turn(w, m, 3), 0, 0, 0, 0)
            ),
            ANY,
        ],
        out_shape=[
            jax.ShapeDtypeStruct((parts, chips, 3 * rows, units), BF16),
            jax.ShapeDtypeStruct((parts, chips, 2, rows // 2, part), BF16),
            jax.ShapeDtypeStruct((size * mine, part), BF16),
        ],
        scratch_shapes=[
            pltpu.VMEM((width, tokens), BF16),
            pltpu.VMEM((width, tokens), BF16),
            pltpu.VMEM((width, mine), BF16),
            *exchange_semaphores(size),
        ],
        compiler_params=remote_params(collective),
        cost_estimate=pl.CostEstimate(
            flops=6 * tokens * width * parts * units, bytes_accessed=40 << 20, transcendentals=0
        ),
        name="feed_grads",
    )(x, dbranch, dup, dgate, units_in, dbranch_attn, merged, dmerged)


def document_starts(doc_ids):
    slot_index = jnp.arange(doc_ids.shape[-1], dtype=jnp.int32)
    earlier = jnp.concatenate([doc_ids[..., :1] - 1, doc_ids[..., :-1]], axis=-1)
    starts = jnp.where(doc_ids != earlier, slot_index, jnp.zeros_like(slot_index))
    return lax.cummax(starts, axis=starts.ndim - 1)


def make_on_device(chips, size):
    def on_device(
        hidden,
        wq,
        wk,
        wv,
        wo,
        w_up,
        w_gate,
        w_down,
        s_qk,
        s_u,
        s_v,
        alpha_a,
        alpha_m,
        doc_ids,
        valid,
        cotangent,
    ):
        _, slots, part = hidden.shape
        width = part * size
        heads = s_qk.shape[0] // DK
        rows = wq.shape[0]
        units = w_up.shape[1] // 2
        mine = slots // size
        block = min(512, slots)
        me = lax.axis_index("mp")
        core = lax.axis_index("core")

        place = paired_place(heads)
        to_pair = placing_matrix(place, heads)
        to_plain = placing_matrix(np.arange(heads * DK), heads)
        turn = np.zeros((part, part), np.float32)
        turn[np.arange(part), place] = 1
        place_pair = jnp.asarray(to_pair, BF16)
        place_plain = jnp.asarray(to_plain, BF16)
        place_delta = jnp.asarray(delta_matrix(heads), BF16)
        collect_plain = jnp.asarray(to_plain.T.reshape(heads, EXT, heads * DK), BF16)
        sums = jnp.asarray(head_sum_matrix(heads), BF16)
        gain = s_qk.reshape(heads, 2, HALF).transpose(1, 0, 2).reshape(1, part)
        docs = doc_ids[0]
        starts = document_starts(docs)
        slot = jnp.arange(slots, dtype=jnp.int32)
        low = jnp.concatenate([starts[::block] // block, me[None]])
        key_docs = jnp.where(valid[0] == 1, docs, -1)
        columns = jnp.stack([slot - starts, docs, key_docs], axis=1).astype(F32)
        inverse = jnp.exp(
            jnp.arange(HALF, dtype=F32) * (-2.0 * math.log(ROPE_BASE) / DK)
        )

        vectors = jnp.concatenate([s_u, s_v * math.sqrt(width), alpha_a, alpha_m])
        (
            wide,
            full_qkv,
            packed,
            vectors,
            q,
            k,
            v,
            q_pair,
            k_pair,
            rq,
            rk,
            cosine,
            sine,
        ) = front(
            hidden[0],
            (wq, wk, wv, wo, w_up, w_gate, w_down),
            vectors[None],
            columns,
            jnp.tile(inverse, heads)[None],
            gain,
            jnp.asarray(turn, BF16),
            place_pair,
            place_plain,
            sums,
            size,
            chips,
            0,
        )
        full_qkv = full_qkv.reshape(size, part, 3 * part)
        vectors = vectors[:, 0]
        s_up = lax.dynamic_slice_in_dim(vectors[:, : 2 * units], core * units, units, 1)
        s_gate = lax.dynamic_slice_in_dim(
            vectors[:, 2 * units : 4 * units], core * units, units, 1
        )
        s_up = s_up[:, None, :]
        s_gate = s_gate[:, None, :]
        alpha_attn = vectors[:, 4 * units : 4 * units + part].reshape(1, width)
        alpha_mlp = vectors[:, 4 * units + part :].reshape(1, width)

        attended, qback = attend(
            low,
            q,
            k,
            v,
            columns,
            key_docs.astype(F32).reshape(slots // block, 1, block),
            collect_plain,
        )
        (
            x,
            middle,
            unit,
            merged,
            full_wo,
            resid,
            cotangent_low,
            branch_scale,
            mixed_scale,
        ) = mix(attended, packed, rows, wide, alpha_attn, cotangent[0], 1)

        up, gate, hidden_units, result, grad_middle, dbranch, grad_alpha_mlp = feed(
            x, packed, s_up, s_gate, cotangent_low, middle, alpha_mlp, 2
        )
        (
            dup,
            dgate,
            grad_u,
            grad_v,
            out_low,
            grad_resid,
            dbranch_attn,
            dmerged,
            grad_alpha_attn,
        ) = feed_back(
            dbranch,
            packed,
            s_up,
            s_gate,
            up,
            gate,
            result,
            grad_middle,
            middle,
            resid,
            unit,
            branch_scale,
            mixed_scale,
            alpha_attn,
            full_wo,
            3,
        )
        grads, grad_wo, dattended = feed_grads(
            x, dbranch, dup, dgate, hidden_units, dbranch_attn, merged, dmerged, chips, 4
        )

        term, grad_qkv, grad_gain, out_hidden = attend_back(
            low,
            qback,
            q_pair,
            dattended,
            attended,
            k,
            k_pair,
            v,
            docs.astype(F32).reshape(slots // block, 1, block),
            columns,
            cosine,
            sine,
            rq,
            rk,
            gain,
            full_qkv,
            place_plain,
            place_delta,
            sums,
            wide,
            grad_resid,
            out_low,
        )
        (
            grad_hidden,
            owned_upward,
            owned_gating,
            owned_downward,
            owned_output,
            owned_query,
            owned_keys,
            owned_values,
            summed,
        ) = sum_all(
            term,
            grads,
            grad_wo,
            grad_qkv.reshape(chips, 2, rows, 3 * part),
            (grad_u, grad_v, grad_gain, grad_alpha_attn, grad_alpha_mlp),
            jnp.asarray(turn.T, BF16),
            chips,
            5,
        )
        bounds = [2 * units, 4 * units, 4 * units + part, 4 * units + 2 * part]
        summed_up, summed_gate, summed_qk, summed_attn, summed_mlp = jnp.split(
            summed[0], bounds
        )
        return (
            out_hidden[None],
            grad_hidden[None],
            owned_query,
            owned_keys,
            owned_values,
            owned_output,
            owned_upward,
            owned_gating,
            owned_downward,
            summed_qk,
            summed_up,
            summed_gate,
            summed_attn,
            summed_mlp,
        )

    return on_device


def solution(mesh):
    rows, size = mesh.shape["dp"], mesh.shape["mp"]
    paired = Mesh(mesh.devices.reshape(rows // 2, 2, size), ("chip", "core", "mp"))
    return jax.shard_map(
        make_on_device(rows // 2, size),
        mesh=paired,
        in_specs=(
            P(DP, None, "mp"),
            P(DP, "mp"),
            P(DP, "mp"),
            P(DP, "mp"),
            P("mp", DP),
            P(DP, "mp"),
            P(DP, "mp"),
            P("mp", DP),
            P("mp"),
            P("mp"),
            P("mp"),
            P("mp"),
            P("mp"),
            P(DP, None),
            P(DP, None),
            P(DP, None, "mp"),
        ),
        out_specs=(
            P(DP, None, "mp"),
            P(DP, None, "mp"),
            P(DP, "mp"),
            P(DP, "mp"),
            P(DP, "mp"),
            P("mp", DP),
            P(DP, "mp"),
            P(DP, "mp"),
            P("mp", DP),
            P("mp"),
            P("mp"),
            P("mp"),
            P("mp"),
            P("mp"),
        ),
        check_vma=False,
    )
```
